32 devices in a mesh: dp: 8 (over z, y), mp: 4 (over x, core).
Axes of the slice: x: 2, y: 2, z: 4, core: 2. Of those that a mesh axis runs over, the one named last changes fastest.
Arguments:
- hidden_in: bfloat16 [4096, 1024], P('dp'), may hold values from -6 to 6
- w_query: bfloat16 [1024, 1024], P('dp', 'mp'), may hold values from -0.1875 to 0.1875
- w_key: bfloat16 [1024, 1024], P('dp', 'mp'), may hold values from -0.1875 to 0.1875
- w_value: bfloat16 [1024, 1024], P('dp', 'mp'), may hold values from -0.1875 to 0.1875
- w_out: bfloat16 [1024, 1024], P('mp', 'dp'), may hold values from -1.5 to 1.5
- w_up: bfloat16 [1024, 4096], P('dp', 'mp'), may hold values from -0.1875 to 0.1875
- w_down: bfloat16 [4096, 1024], P('mp', 'dp'), may hold values from -0.09375 to 0.09375
- w_colbert: bfloat16 [1024, 1024], P('dp', 'mp'), may hold values from -0.1875 to 0.1875
- norm1_gain: bfloat16 [1024], P('dp'), may hold values from 0.5 to 1.5
- norm1_shift: bfloat16 [1024], P('dp'), may hold values from -3 to 3
- norm2_gain: bfloat16 [1024], P('dp'), may hold values from 0.5 to 1.5
- norm2_shift: bfloat16 [1024], P('dp'), may hold values from -3 to 3
- queries: bfloat16 [8192, 1024], P('mp'), may hold values from -6 to 6
- passage: int32 [4096], replicated, may hold values from 0 to 14, as said below
- live: int32 [4096], replicated, may hold values from 0 to 1, as said below
- score_grad: float32 [256, 15], P('mp'), may hold values from -6 to 6
Outputs:
- scores: float32 [256, 15], P('mp')
- input_grad: float32 [4096, 1024], P('dp')
- query_grad: float32 [1024, 1024], P('dp', 'mp')
- key_grad: float32 [1024, 1024], P('dp', 'mp')
- value_grad: float32 [1024, 1024], P('dp', 'mp')
- out_grad: float32 [1024, 1024], P('mp', 'dp')
- up_grad: float32 [1024, 4096], P('dp', 'mp')
- down_grad: float32 [4096, 1024], P('mp', 'dp')
- colbert_grad: float32 [1024, 1024], P('dp', 'mp')
- norm1_gain_grad: float32 [1024], P('dp')
- norm1_shift_grad: float32 [1024], P('dp')
- norm2_gain_grad: float32 [1024], P('dp')
- norm2_shift_grad: float32 [1024], P('dp')
The draws below stay inside these ranges and needn't reach their ends.
Inputs may be any that keep to these rules, and one draw needn't show every extreme that they name: The tokens form 4 aligned groups of 1024, each holding one bucket whose passages all have the same padded length, the group's tokens divided by 1, 2, 4 or 8; which bucket a group holds is drawn. Within a group, token r of its shard d (shards of 512 tokens, d from 0 to 1) is the group's token r * 2 + d in passage order, and each passage is a run of that order. Passages are numbered bucket by bucket, shortest bucket first. In that passage order the live tokens of each passage come first; more than half of every passage's padded length is live, and the first passage of every bucket is live throughout.
All inputs are finite; a program needn't handle non-finite values.
Results may differ from the reference program's by a relative error of at most 0.028.
Values may be sent and summed in bfloat16 or wider, within the bound.
No kernel may reach another device: no remote copies, remote signals or barrier semaphores. Data moves between devices by JAX's collectives and lax.ppermute only.
A program may use at most 128 MiB of HBM per device.

```python
import jax
import jax.numpy as jnp
from jax import lax

D = 1024
HEADS = 16
HEAD_DIM = 64
FF = 4096
TOK_DEV = 512
NQ = 256
QLEN = 32
NBUCKET = 4
TOKENS = 4096
NQT = 8192
NPASS = 15
GROUP = 2


def layout_tables(key):
    group_span = TOKENS // NBUCKET
    order = jax.random.permutation(jax.random.fold_in(key, 7), NBUCKET).astype(jnp.int32)
    place = jnp.arange(TOKENS, dtype=jnp.int32)
    bucket = order[place // group_span]
    offset = place % group_span
    shard = offset // TOK_DEV
    row_in = offset % TOK_DEV
    ordered = row_in * GROUP + shard
    length = jnp.right_shift(jnp.full((TOKENS,), group_span, jnp.int32), (NBUCKET - 1 - bucket).astype(jnp.int32))
    within = ordered // length
    spot = ordered % length
    total_slots = 2 ** NBUCKET
    passage = total_slots - jnp.right_shift(jnp.full((TOKENS,), total_slots, jnp.int32), bucket) + within
    raw_counts = jax.random.randint(jax.random.fold_in(key, 11), (NPASS,), 0, 1048576)
    least = length // 2 + 1
    counts = least + raw_counts[passage] % (length - least + 1)
    counts = jnp.where(within == 0, length, counts)
    live = (spot < counts).astype(jnp.int32)
    return (passage.astype(jnp.int32), live)


def draw_passage(key, part):
    return layout_tables(key)[0]


def draw_live(key, part):
    return layout_tables(key)[1]


def raised(drawn, own_key, source, target, shards_of, factor):
    def block_of(axis_at):
        return (jnp.arange(drawn.shape[axis_at]) // (drawn.shape[axis_at] // shards_of)).reshape((-1,) + (1,) * (drawn.ndim - 1 - axis_at))

    one_side = jax.random.permutation(own_key, shards_of)[block_of(target)]
    second = (block_of(target) + shards_of // 2) % shards_of
    return jnp.where((block_of(source) == one_side) | (block_of(source) == second), factor * drawn, drawn)


def level_of(own_key, dims, split, low, top_value):
    factor_of = 1.0
    for dim, parts in split:
        steps = jax.random.uniform(jax.random.fold_in(jax.random.fold_in(own_key, 6), dim), (parts,), jnp.float32, low / len(split), top_value / len(split))
        factor_of = factor_of * jnp.repeat(jnp.exp(steps), dims[dim] // parts).reshape((-1,) + (1,) * (len(dims) - 1 - dim))
    return factor_of


def scatter_about(rng, shape, width, most, shards=(), kind=jnp.bfloat16):
    result = jax.random.normal(rng, shape, jnp.float32) * width
    if len(shards) > 0:
        result = level_of(rng, shape, shards, -0.22, 0.18) * result
    return jnp.clip(result, min=-most, max=most).astype(kind)


def noise_with(rng, dims, scale, reach, pieces, heavy, held_as=jnp.bfloat16):
    result = scale * jax.random.normal(rng, dims, jnp.float32)
    if pieces:
        result = result * level_of(rng, dims, pieces, -0.22, 0.18)
    return jnp.clip(raised(result, jax.random.fold_in(rng, 3), *heavy), -reach, reach).astype(held_as)


def setup_inputs(seed: int = 0) -> dict:
    keys = jax.random.split(jax.random.key(seed), 17)
    hidden_in = noise_with(keys[0], (TOKENS, D), 1.0, 6.0, ((0, 8),), (0, 1, 8, 2.0))
    w_query = scatter_about(keys[1], (D, D), D ** -0.5, 0.1875, ((0, 8), (1, 4)))
    w_key = scatter_about(keys[2], (D, D), D ** -0.5, 0.1875, ((0, 8), (1, 4)))
    w_value = scatter_about(keys[3], (D, D), D ** -0.5, 0.1875, ((0, 8), (1, 4)))
    w_out = scatter_about(keys[4], (D, D), (max(1, D // 64)) ** -0.5, 1.5, ((0, 4), (1, 8)))
    w_up = scatter_about(keys[5], (D, FF), D ** -0.5, 0.1875, ((0, 8), (1, 4)))
    w_down = scatter_about(keys[6], (FF, D), FF ** -0.5, 0.09375, ((0, 4), (1, 8)))
    w_colbert = scatter_about(keys[7], (D, D), D ** -0.5, 0.1875, ((0, 8), (1, 4)))
    norm1_gain = jnp.clip(1.0 + 0.1 * jax.random.normal(keys[8], (D,), jnp.float32), 0.5, 1.5).astype(jnp.bfloat16)
    norm1_shift = scatter_about(keys[9], (D,), 0.5, 3.0, ((0, 8),))
    norm2_gain = jnp.clip(1.0 + 0.1 * jax.random.normal(keys[10], (D,), jnp.float32), 0.5, 1.5).astype(jnp.bfloat16)
    norm2_shift = scatter_about(keys[11], (D,), 0.5, 3.0, ((0, 8),))
    queries = scatter_about(keys[12], (NQT, D), 1.0, 6.0, ((0, 4),))
    passage = draw_passage(jax.random.fold_in(keys[16], 71), 0)
    live = draw_live(jax.random.fold_in(keys[16], 71), 0)
    score_grad = scatter_about(keys[15], (NQ, NPASS), 1.0, 6.0, ((0, 4),), jnp.float32)
    return dict(hidden_in=hidden_in, w_query=w_query, w_key=w_key, w_value=w_value, w_out=w_out, w_up=w_up, w_down=w_down, w_colbert=w_colbert, norm1_gain=norm1_gain, norm1_shift=norm1_shift, norm2_gain=norm2_gain, norm2_shift=norm2_shift, queries=queries, passage=passage, live=live, score_grad=score_grad)


@jax.custom_vjp
def low(v):
    return lax.optimization_barrier(v.astype(jnp.bfloat16)).astype(jnp.float32)

@jax.custom_vjp
def low_back(v):
    return v

def low_keep(v):
    return (low(v), None)

def low_pass(kept, grad):
    return (grad,)

def back_keep(v):
    return (v, None)

def back_low(kept, grad):
    return (low(grad),)
low.defvjp(low_keep, low_pass)
low_back.defvjp(back_keep, back_low)

def matmul(left, right):
    return jnp.dot(left, right, precision=lax.Precision.HIGHEST, preferred_element_type=jnp.float32)

def layer_norm(values, gain, shift):
    centre = values - lax.optimization_barrier(jnp.mean(values, axis=-1, keepdims=True))
    spread = lax.optimization_barrier(jnp.mean(centre * centre, axis=-1, keepdims=True))
    return centre * lax.rsqrt(spread + 1e-05) * gain + shift

def attend_group(group_args):
    query_grp, key_grp, value_grp, seg_grp, live_grp = group_args
    span_rows = query_grp.shape[0]
    block_rows = min(512, span_rows)
    query_blocks = query_grp.reshape(span_rows // block_rows, block_rows, HEADS, HEAD_DIM)
    seg_blocks = seg_grp.reshape(span_rows // block_rows, block_rows)
    key_live = live_grp == 1

    def one_block(block_args):
        query_blk, seg_blk = block_args
        raw = jnp.einsum('bhd,khd->hbk', query_blk, key_grp, precision=lax.Precision.HIGHEST) * 0.125
        raw = low_back(raw)
        allowed = (seg_blk[:, None] == seg_grp[None, :]) & key_live[None, :]
        masked = jnp.where(allowed[None], raw, -1e+30)
        weights = low(jax.nn.softmax(masked, axis=-1))
        return jnp.einsum('hbk,khd->bhd', weights, value_grp, precision=lax.Precision.HIGHEST)
    attended = lax.map(jax.checkpoint(one_block), (query_blocks, seg_blocks))
    return attended.reshape(span_rows, HEADS, HEAD_DIM)

def late_scores(embedded, query_vectors, slots):
    block_rows = min(512, NQT)
    query_blocks = query_vectors.reshape(NQT // block_rows, block_rows, D)
    embed_low = low(embedded)

    def one_block(query_blk):
        dots = low_back(matmul(query_blk, embed_low.T))
        flipped = dots.T * 2.0
        best = jax.ops.segment_max(flipped, slots, num_segments=NPASS + 1)
        terms = jnp.exp(flipped - best[slots])
        total = jax.ops.segment_sum(terms, slots, num_segments=NPASS + 1)
        soft = (best[:NPASS] + jnp.log(total[:NPASS])) / 2.0
        return lax.optimization_barrier(jnp.mean(soft.T.reshape(block_rows // QLEN, QLEN, NPASS), axis=1))
    return lax.map(jax.checkpoint(one_block), query_blocks).reshape(NQ, NPASS)

def reference(hidden_in, w_query, w_key, w_value, w_out, w_up, w_down, w_colbert, norm1_gain, norm1_shift, norm2_gain, norm2_shift, queries, passage, live, score_grad):
    query_vectors = queries.astype(jnp.float32)
    slots = jnp.where(live == 1, passage, NPASS).astype(jnp.int32)
    group_span = TOKENS // NBUCKET
    seg_groups = passage.reshape(NBUCKET, group_span)
    live_groups = live.reshape(NBUCKET, group_span)

    def forward(hidden, w_q, w_k, w_v, w_o, w_u, w_d, w_c, gain_one, shift_one, gain_two, shift_two):
        query_rows = low(low_back(matmul(hidden, w_q)))
        key_rows = low(low_back(matmul(hidden, w_k)))
        value_rows = low(low_back(matmul(hidden, w_v)))
        attended = lax.map(attend_group, (query_rows.reshape(NBUCKET, group_span, HEADS, HEAD_DIM), key_rows.reshape(NBUCKET, group_span, HEADS, HEAD_DIM), value_rows.reshape(NBUCKET, group_span, HEADS, HEAD_DIM), seg_groups, live_groups))
        attended = low(low_back(attended.reshape(TOKENS, D)))
        resid_one = hidden + matmul(attended, w_o)
        normed_one = layer_norm(resid_one, gain_one, shift_one)
        inner = low_back(matmul(low(normed_one), w_u))
        active = low(jax.nn.gelu(inner, approximate=False))
        resid_two = normed_one + low_back(matmul(active, w_d))
        normed_two = layer_norm(resid_two, gain_two, shift_two)
        projected = low_back(matmul(low(normed_two), w_c))
        embedded = projected * lax.rsqrt(lax.optimization_barrier(jnp.sum(projected * projected, axis=-1, keepdims=True)) + 1e-06)
        return late_scores(embedded, query_vectors, slots)
    floats = (hidden_in.astype(jnp.float32), w_query.astype(jnp.float32), w_key.astype(jnp.float32), w_value.astype(jnp.float32), w_out.astype(jnp.float32), w_up.astype(jnp.float32), w_down.astype(jnp.float32), w_colbert.astype(jnp.float32), norm1_gain.astype(jnp.float32), norm1_shift.astype(jnp.float32), norm2_gain.astype(jnp.float32), norm2_shift.astype(jnp.float32))
    scores, pull = jax.vjp(forward, *floats)
    grads = pull(score_grad)
    return (scores, grads[0], grads[1], grads[2], grads[3], grads[4], grads[5], grads[6], grads[7], grads[8], grads[9], grads[10], grads[11])
```

```python
import functools

import jax
import jax.numpy as jnp
from jax import lax
from jax.experimental import pallas as pl
from jax.experimental.pallas import tpu as pltpu
from jax.sharding import PartitionSpec as P

HEAD_DIM = 64
QLEN = 32
NBUCKET = 4
NPASS = 15
LANES = 128

neg_big = -1e30
low_type = jnp.bfloat16
contract_rows = (((0,), (0,)), ((), ()))
contract_cols = (((1,), (1,)), ((), ()))
contract_inner = (((1,), (0,)), ((), ()))
roomy = pltpu.CompilerParams(vmem_limit_bytes=56 * 1024 * 1024)


def swap(value, axis, mask):
    pairs = [(source, source ^ mask) for source in range(lax.axis_size(axis))]
    return lax.ppermute(value, axis, pairs)


def bits_of(axis):
    return lax.axis_size(axis).bit_length() - 1


def has_bit(axis, mask):
    return lax.axis_index(axis) // mask % 2


def gather_over(value, axis, masks):
    levels = bits_of(axis)
    whole = value.reshape((1,) * levels + value.shape)
    for mask in masks:
        at = levels - 1 - (mask.bit_length() - 1)
        other = swap(whole, axis, mask)
        whole = jnp.where(
            has_bit(axis, mask) == 1,
            jnp.concatenate([other, whole], at),
            jnp.concatenate([whole, other], at),
        )
    return whole.reshape((-1,) + value.shape)


def scatter_sum(blocks, axis, masks):
    levels = bits_of(axis)
    part = blocks.reshape((2,) * levels + blocks.shape[1:])
    for mask in masks:
        at = levels - 1 - (mask.bit_length() - 1)
        mine = has_bit(axis, mask)
        keep = lax.dynamic_index_in_dim(part, mine, at, keepdims=True)
        send = lax.dynamic_index_in_dim(part, 1 - mine, at, keepdims=True)
        got = swap(send.astype(low_type), axis, mask)
        part = keep.astype(jnp.float32) + got.astype(jnp.float32)
    return part.reshape(blocks.shape[1:])


def upward(axis):
    return [2**level for level in range(bits_of(axis))]


def downward(axis):
    return upward(axis)[::-1]


def head_mask(width, head):
    lane = lax.broadcasted_iota(jnp.int32, (1, width), 1)
    return lane // HEAD_DIM == head


def only_head(rows, head):
    return jnp.where(head_mask(rows.shape[1], head), rows, jnp.zeros_like(rows))


def attend_forward_kernel(q_ref, k_ref, v_ref, segq_ref, segk_ref, o_ref, stat_ref):
    width = q_ref.shape[1]
    tile = q_ref.shape[0]
    bias = jnp.where(segq_ref[...] == segk_ref[...], 0.0, neg_big)
    out = jnp.zeros((tile, width), jnp.float32)
    stat = jnp.zeros((tile, LANES), jnp.float32)
    lane = lax.broadcasted_iota(jnp.int32, (1, LANES), 1)
    queries = q_ref[...] * jnp.asarray(0.125, low_type)
    for head in range(width // HEAD_DIM):
        raw = lax.dot_general(
            only_head(queries, head), k_ref[...], contract_cols, preferred_element_type=jnp.float32
        )
        raw = raw + bias
        top = jnp.max(raw, axis=1, keepdims=True)
        terms = jnp.exp(raw - top)
        total = jnp.sum(terms, axis=1, keepdims=True)
        probs = (terms * (1.0 / total)).astype(low_type)
        mixed = lax.dot_general(
            probs, v_ref[...], contract_inner, preferred_element_type=jnp.float32
        )
        out = jnp.where(head_mask(width, head), mixed, out)
        stat = jnp.where(lane == head, top + jnp.log(total), stat)
    o_ref[...] = out.astype(low_type)
    stat_ref[...] = stat.T


def attend_forward(query_rows, key_rows, value_rows, seg_rows, seg_keys):
    rows, width = query_rows.shape
    keys = key_rows.shape[0]
    tile = LANES
    return pl.pallas_call(
        attend_forward_kernel,
        grid=(rows // tile,),
        in_specs=[
            pl.BlockSpec((tile, width), lambda i: (i, 0)),
            pl.BlockSpec((keys, width), lambda i: (0, 0)),
            pl.BlockSpec((keys, width), lambda i: (0, 0)),
            pl.BlockSpec((tile, 1), lambda i: (i, 0)),
            pl.BlockSpec((1, keys), lambda i: (0, 0)),
        ],
        out_specs=[
            pl.BlockSpec((tile, width), lambda i: (i, 0)),
            pl.BlockSpec((LANES, tile), lambda i: (0, i)),
        ],
        out_shape=[
            jax.ShapeDtypeStruct((rows, width), low_type),
            jax.ShapeDtypeStruct((LANES, rows), jnp.float32),
        ],
        compiler_params=roomy,
        name="attend_forward",
    )(query_rows, key_rows, value_rows, seg_rows, seg_keys)


def attend_backward_kernel(
    q_ref,
    k_ref,
    v_ref,
    do_ref,
    segq_ref,
    segk_ref,
    lse_ref,
    delta_ref,
    dq_ref,
    dk_ref,
    dv_ref,
    dk_sum,
    dv_sum,
):
    width = q_ref.shape[1]
    step = pl.program_id(0)

    @pl.when(step == 0)
    def _():
        dk_sum[...] = jnp.zeros_like(dk_sum)
        dv_sum[...] = jnp.zeros_like(dv_sum)

    bias = jnp.where(segq_ref[...] == segk_ref[...], 0.0, neg_big)
    lse = lse_ref[...].T
    delta = delta_ref[...].T
    queries = q_ref[...] * jnp.asarray(0.125, low_type)
    grads = do_ref[...]
    keys = k_ref[...]
    values = v_ref[...]
    dquery = jnp.zeros(q_ref.shape, jnp.float32)
    for head in range(width // HEAD_DIM):
        q_head = only_head(queries, head)
        g_head = only_head(grads, head)
        raw = lax.dot_general(q_head, keys, contract_cols, preferred_element_type=jnp.float32)
        probs = jnp.exp(raw + bias - lse[:, head : head + 1])
        dprobs = lax.dot_general(g_head, values, contract_cols, preferred_element_type=jnp.float32)
        dscore = (probs * (dprobs - delta[:, head : head + 1])).astype(low_type)
        mixed = lax.dot_general(dscore, keys, contract_inner, preferred_element_type=jnp.float32)
        dquery = jnp.where(head_mask(width, head), mixed, dquery)
        dk_sum[...] += lax.dot_general(
            dscore, q_head, contract_rows, preferred_element_type=jnp.float32
        )
        dv_sum[...] += lax.dot_general(
            probs.astype(low_type), g_head, contract_rows, preferred_element_type=jnp.float32
        )
    dq_ref[...] = (dquery * 0.125).astype(low_type)
    dk_ref[...] = dk_sum[...].astype(low_type)
    dv_ref[...] = dv_sum[...].astype(low_type)


def attend_backward(query_rows, key_rows, value_rows, grads, seg_rows, seg_keys, lse, delta):
    rows, width = query_rows.shape
    keys = key_rows.shape[0]
    tile = LANES
    whole_keys = pl.BlockSpec((keys, width), lambda i: (0, 0))
    return pl.pallas_call(
        attend_backward_kernel,
        grid=(rows // tile,),
        in_specs=[
            pl.BlockSpec((tile, width), lambda i: (i, 0)),
            whole_keys,
            whole_keys,
            pl.BlockSpec((tile, width), lambda i: (i, 0)),
            pl.BlockSpec((tile, 1), lambda i: (i, 0)),
            pl.BlockSpec((1, keys), lambda i: (0, 0)),
            pl.BlockSpec((LANES, tile), lambda i: (0, i)),
            pl.BlockSpec((LANES, tile), lambda i: (0, i)),
        ],
        out_specs=[pl.BlockSpec((tile, width), lambda i: (i, 0)), whole_keys, whole_keys],
        out_shape=[
            jax.ShapeDtypeStruct((rows, width), low_type),
            jax.ShapeDtypeStruct((keys, width), low_type),
            jax.ShapeDtypeStruct((keys, width), low_type),
        ],
        scratch_shapes=[
            pltpu.VMEM((keys, width), jnp.float32),
            pltpu.VMEM((keys, width), jnp.float32),
        ],
        compiler_params=roomy,
        name="attend_backward",
    )(query_rows, key_rows, value_rows, grads, seg_rows, seg_keys, lse, delta)


def feed_forward_kernel(h_ref, up_ref, down_ref, out_ref, g_ref, slope_ref, total):
    step = pl.program_id(0)
    inner = jnp.dot(h_ref[...], up_ref[...], preferred_element_type=jnp.float32)
    normal = 0.5 * (1.0 + lax.erf(inner * 0.7071067811865476))
    active = (inner * normal).astype(low_type)
    g_ref[...] = active
    slope = normal + inner * jnp.exp(-0.5 * inner * inner) * 0.3989422804014327
    slope_ref[...] = slope.astype(low_type)
    term = jnp.dot(active, down_ref[...], preferred_element_type=jnp.float32)

    @pl.when(step == 0)
    def _():
        total[...] = term

    @pl.when(step > 0)
    def _():
        total[...] += term

    @pl.when(step == pl.num_programs(0) - 1)
    def _():
        out_ref[...] = total[...].astype(low_type)


def feed_forward(rows_low, w_up, w_down):
    rows, width = rows_low.shape
    units = w_up.shape[1]
    tile = min(256, units)
    return pl.pallas_call(
        feed_forward_kernel,
        grid=(units // tile,),
        in_specs=[
            pl.BlockSpec((rows, width), lambda i: (0, 0)),
            pl.BlockSpec((width, tile), lambda i: (0, i)),
            pl.BlockSpec((tile, width), lambda i: (i, 0)),
        ],
        out_specs=[
            pl.BlockSpec((rows, width), lambda i: (0, 0)),
            pl.BlockSpec((rows, tile), lambda i: (0, i)),
            pl.BlockSpec((rows, tile), lambda i: (0, i)),
        ],
        out_shape=[
            jax.ShapeDtypeStruct((rows, width), low_type),
            jax.ShapeDtypeStruct((rows, units), low_type),
            jax.ShapeDtypeStruct((rows, units), low_type),
        ],
        scratch_shapes=[pltpu.VMEM((rows, width), jnp.float32)],
        compiler_params=roomy,
        name="feed_forward",
    )(rows_low, w_up, w_down)


def feed_backward_kernel(d_ref, up_ref, down_ref, slope_ref, out_ref, dz_ref, total):
    step = pl.program_id(0)
    dactive = lax.dot_general(
        d_ref[...], down_ref[...], contract_cols, preferred_element_type=jnp.float32
    )
    dinner = (dactive * slope_ref[...].astype(jnp.float32)).astype(low_type)
    dz_ref[...] = dinner
    term = lax.dot_general(dinner, up_ref[...], contract_cols, preferred_element_type=jnp.float32)

    @pl.when(step == 0)
    def _():
        total[...] = term

    @pl.when(step > 0)
    def _():
        total[...] += term

    @pl.when(step == pl.num_programs(0) - 1)
    def _():
        out_ref[...] = total[...].astype(low_type)


def feed_backward(grad_low, w_up, w_down, slope):
    rows, width = grad_low.shape
    units = w_up.shape[1]
    tile = min(256, units)
    return pl.pallas_call(
        feed_backward_kernel,
        grid=(units // tile,),
        in_specs=[
            pl.BlockSpec((rows, width), lambda i: (0, 0)),
            pl.BlockSpec((width, tile), lambda i: (0, i)),
            pl.BlockSpec((tile, width), lambda i: (i, 0)),
            pl.BlockSpec((rows, tile), lambda i: (0, i)),
        ],
        out_specs=[
            pl.BlockSpec((rows, width), lambda i: (0, 0)),
            pl.BlockSpec((rows, tile), lambda i: (0, i)),
        ],
        out_shape=[
            jax.ShapeDtypeStruct((rows, width), low_type),
            jax.ShapeDtypeStruct((rows, units), low_type),
        ],
        scratch_shapes=[pltpu.VMEM((rows, width), jnp.float32)],
        compiler_params=roomy,
        name="feed_backward",
    )(grad_low, w_up, w_down, slope)


def late_forward_kernel(e_ref, q_ref, live_ref, sharp_ref, soft_ref):
    dots = lax.dot_general(
        e_ref[...], q_ref[...], contract_cols, preferred_element_type=jnp.float32
    )
    sharp = dots * 2.0 + live_ref[...]
    sharp_ref[...] = sharp
    blocks = soft_ref.shape[0]
    rows = sharp.shape[0] // blocks
    cube = sharp.reshape(blocks, rows, sharp.shape[1])
    top = jnp.max(cube, axis=1)
    total = jnp.sum(jnp.exp(cube - top[:, None, :]), axis=1)
    soft_ref[...] = jnp.where(top > 0.5 * neg_big, top + jnp.log(total), neg_big)


def late_forward(embed_low, queries, live_bias, blocks):
    rows, width = embed_low.shape
    count = queries.shape[0]
    tile = 256
    return pl.pallas_call(
        late_forward_kernel,
        grid=(count // tile,),
        in_specs=[
            pl.BlockSpec((rows, width), lambda i: (0, 0)),
            pl.BlockSpec((tile, width), lambda i: (i, 0)),
            pl.BlockSpec((rows, 1), lambda i: (0, 0)),
        ],
        out_specs=[
            pl.BlockSpec((rows, tile), lambda i: (0, i)),
            pl.BlockSpec((blocks, tile), lambda i: (0, i)),
        ],
        out_shape=[
            jax.ShapeDtypeStruct((rows, count), jnp.float32),
            jax.ShapeDtypeStruct((blocks, count), jnp.float32),
        ],
        compiler_params=roomy,
        name="late_forward",
    )(embed_low, queries, live_bias)


def late_backward_kernel(sharp_ref, soft_ref, weight_ref, q_ref, out_ref, total):
    step = pl.program_id(0)
    blocks = soft_ref.shape[0]
    rows, tile = sharp_ref.shape
    cube = sharp_ref[...].reshape(blocks, rows // blocks, tile)
    pulled = weight_ref[...][:, None, :] * jnp.exp(cube - soft_ref[...][:, None, :])
    pulled = pulled.reshape(rows, tile).astype(low_type)
    term = jnp.dot(pulled, q_ref[...], preferred_element_type=jnp.float32)

    @pl.when(step == 0)
    def _():
        total[...] = term

    @pl.when(step > 0)
    def _():
        total[...] += term

    @pl.when(step == pl.num_programs(0) - 1)
    def _():
        out_ref[...] = total[...].astype(low_type)


def late_backward(sharp, soft, weight, queries):
    rows, count = sharp.shape
    width = queries.shape[1]
    blocks = soft.shape[0]
    tile = 256
    return pl.pallas_call(
        late_backward_kernel,
        grid=(count // tile,),
        in_specs=[
            pl.BlockSpec((rows, tile), lambda i: (0, i)),
            pl.BlockSpec((blocks, tile), lambda i: (0, i)),
            pl.BlockSpec((blocks, tile), lambda i: (0, i)),
            pl.BlockSpec((tile, width), lambda i: (i, 0)),
        ],
        out_specs=pl.BlockSpec((rows, width), lambda i: (0, 0)),
        out_shape=jax.ShapeDtypeStruct((rows, width), low_type),
        scratch_shapes=[pltpu.VMEM((rows, width), jnp.float32)],
        compiler_params=roomy,
        name="late_backward",
    )(sharp, soft, weight, queries)


def norm_stats(values):
    centre = values - jnp.mean(values, axis=-1, keepdims=True)
    spread = jnp.mean(centre * centre, axis=-1, keepdims=True)
    scale = lax.rsqrt(spread + 1e-05)
    return centre * scale, scale


def norm_backward(unit, scale, gain, grad):
    dunit = grad * gain
    dvalues = scale * (
        dunit
        - jnp.mean(dunit, axis=-1, keepdims=True)
        - unit * jnp.mean(dunit * unit, axis=-1, keepdims=True)
    )
    return dvalues, jnp.sum(grad * unit, axis=0), jnp.sum(grad, axis=0)


def low_dot(left, right, dims):
    return lax.dot_general(left, right, dims, preferred_element_type=jnp.float32)


def body(
    hidden_in,
    w_query,
    w_key,
    w_value,
    w_out,
    w_up,
    w_down,
    w_colbert,
    norm1_gain,
    norm1_shift,
    norm2_gain,
    norm2_shift,
    queries,
    passage,
    live,
    score_grad,
):
    tok_rows, width = hidden_in.shape
    device = lax.axis_index("dp")
    column = lax.axis_index("mp")
    dp_size = lax.axis_size("dp")
    mp_size = lax.axis_size("mp")
    group_size = dp_size // NBUCKET
    own_rows = tok_rows // mp_size
    head_width = w_query.shape[1]
    dp_up, dp_down = upward("dp"), downward("dp")
    mp_up, mp_down = upward("mp"), downward("mp")

    def my_rows(value):
        return lax.dynamic_slice_in_dim(value, column * own_rows, own_rows, 0)

    def gather_rows(value):
        return gather_over(value, "mp", mp_down).reshape((-1,) + value.shape[1:])

    def scatter_rows(value):
        blocks = value.reshape((mp_size, own_rows) + value.shape[1:])
        return scatter_sum(blocks, "mp", mp_up)

    seg_rows = lax.dynamic_slice_in_dim(passage, device * tok_rows, tok_rows)
    live_rows = lax.dynamic_slice_in_dim(live, device * tok_rows, tok_rows)
    seg_keys, live_keys = [seg_rows], [live_rows]
    for apart in range(1, group_size):
        start = (device ^ apart) * tok_rows
        seg_keys.append(lax.dynamic_slice_in_dim(passage, start, tok_rows))
        live_keys.append(lax.dynamic_slice_in_dim(live, start, tok_rows))
    seg_others = jnp.concatenate(seg_keys[1:])
    slot_own = jnp.where(live_rows == 1, seg_rows, -1)
    slot_keys = jnp.where(jnp.concatenate(live_keys) == 1, jnp.concatenate(seg_keys), -1)

    half = w_query.shape[1] * 3 // 2
    pack = jnp.concatenate([w_query, w_key, w_value], axis=1)
    full_a = gather_over(pack[:, :half], "dp", dp_down).reshape(width, half)
    full_b = gather_over(pack[:, half:], "dp", dp_up[:1] + dp_down[:-1]).reshape(width, half)
    full_qkv = jnp.concatenate([full_a, full_b], axis=1)

    others = my_rows(hidden_in)[None]
    for level in range(group_size.bit_length() - 1):
        others = jnp.concatenate([others, swap(others, "dp", 2**level)], 0)
    others = gather_over(others[1:], "mp", mp_down)
    others = jnp.swapaxes(others, 0, 1).reshape(-1, width)

    norms = jnp.stack([norm1_gain, norm1_shift, norm2_gain, norm2_shift])
    out_pack = jnp.concatenate(
        [w_out, norms, jnp.zeros((16 - norms.shape[0], w_out.shape[1]), low_type)], axis=0
    )
    out_full = jnp.swapaxes(gather_over(out_pack, "dp", dp_down), 0, 1).reshape(-1, width)
    full_out = out_full[: w_out.shape[0]]
    gain_one, shift_one, gain_two, shift_two = [
        out_full[w_out.shape[0] + row].astype(jnp.float32) for row in range(4)
    ]
    full_up = gather_over(w_up, "dp", dp_down).reshape(width, -1)
    full_down = jnp.swapaxes(gather_over(w_down, "dp", dp_down), 0, 1).reshape(-1, width)
    col_mp = jnp.swapaxes(
        gather_over(gather_over(w_colbert, "dp", dp_down).reshape(width, -1), "mp", mp_down), 0, 1
    )
    full_col = col_mp.reshape(width, width)

    both = jnp.concatenate([hidden_in, others], 0)
    qkv_own = low_dot(hidden_in, full_qkv, contract_inner).astype(low_type)
    qkv_others = low_dot(others, full_qkv, contract_inner).astype(low_type)
    query_rows = qkv_own[:, :head_width]
    query_others = qkv_others[:, :head_width]
    qkv_all = jnp.concatenate([qkv_own, qkv_others], 0)
    key_all = qkv_all[:, head_width : 2 * head_width]
    value_all = qkv_all[:, 2 * head_width :]
    attended_low, lse = attend_forward(
        query_rows, key_all, value_all, seg_rows[:, None], slot_keys[None, :]
    )
    mixed = scatter_rows(low_dot(attended_low, full_out, contract_inner).astype(low_type))
    resid_one = my_rows(hidden_in).astype(jnp.float32) + mixed
    unit_one, scale_one = norm_stats(resid_one)
    normed_one = unit_one * gain_one + shift_one
    normed_low = gather_rows(normed_one.astype(low_type))
    part_two, active_low, slope_low = feed_forward(normed_low, full_up, full_down)
    resid_two = normed_one + scatter_rows(part_two)
    unit_two, scale_two = norm_stats(resid_two)
    normed_two_low = (unit_two * gain_two + shift_two).astype(low_type)
    projected = low_dot(normed_two_low, full_col, contract_inner)
    inv_length = lax.rsqrt(jnp.sum(projected * projected, axis=-1, keepdims=True) + 1e-06)
    embedded = projected * inv_length
    embed_low = gather_rows(embedded.astype(low_type))

    blocks = 2 ** (NBUCKET - 1)
    seg_block = seg_rows.reshape(blocks, -1)[:, 0]
    live_bias = jnp.where(live_rows == 1, 0.0, neg_big)[:, None]
    sharp, soft_block = late_forward(embed_low, queries, live_bias, blocks)
    soft_group = soft_block[None]
    for level in range(group_size.bit_length() - 1):
        soft_group = jnp.concatenate([soft_group, swap(soft_group, "dp", 2**level)], 0)
    same = seg_block[:, None] == seg_block[None, :]
    terms = jnp.where(same[:, None, :, None], soft_group[None], neg_big)
    top = jnp.max(terms, axis=(1, 2))
    soft = top + jnp.log(jnp.sum(jnp.exp(terms - top[:, None, None]), axis=(1, 2)))
    passages = jnp.arange(NPASS, dtype=jnp.int32)
    first = jnp.concatenate([jnp.ones((1,), bool), seg_block[1:] != seg_block[:-1]])
    place = ((seg_block[:, None] == passages[None, :]) & first[:, None]).astype(jnp.float32)
    query_means = jnp.mean(soft.reshape(blocks, -1, QLEN), axis=2) * 0.5
    scores = jnp.sum(query_means[:, :, None] * place[:, None, :], axis=0)
    for mask in dp_up[group_size.bit_length() - 1 :]:
        scores = scores + swap(scores, "dp", mask)

    grad_block = jnp.sum(
        jnp.where(
            (seg_block[:, None] == passages[None, :])[:, None, :], score_grad[None], 0.0
        ),
        axis=2,
    )
    weight = jnp.repeat(grad_block / QLEN, QLEN, axis=1)
    dembed = scatter_rows(late_backward(sharp, soft, weight, queries))
    along = jnp.sum(embedded * dembed, axis=-1, keepdims=True)
    dproj_low = (inv_length * (dembed - embedded * along)).astype(low_type)
    dnormed_two = low_dot(dproj_low, full_col, contract_cols)
    dresid_two, dgain_two, dshift_two = norm_backward(unit_two, scale_two, gain_two, dnormed_two)
    dffn_low = gather_rows(dresid_two.astype(low_type))
    part_one, dinner_low = feed_backward(dffn_low, full_up, full_down, slope_low)
    dnormed_one = dresid_two + scatter_rows(part_one)
    dresid_one, dgain_one, dshift_one = norm_backward(unit_one, scale_one, gain_one, dnormed_one)
    norm_rows = jnp.stack([dgain_one, dshift_one, dgain_two, dshift_two])
    norm_high = norm_rows.astype(low_type)
    norm_rest = (norm_rows - norm_high.astype(jnp.float32)).astype(low_type)
    mixed_pack = jnp.concatenate(
        [dresid_one.astype(low_type), norm_high, norm_rest, jnp.zeros((8, width), low_type)], 0
    )
    mixed_pack = gather_over(mixed_pack, "mp", mp_down)
    dmixed_low = mixed_pack[:, :own_rows].reshape(tok_rows, width)
    norm_pair = mixed_pack[:, own_rows : own_rows + 8].astype(jnp.float32)
    norm_sum = jnp.sum(norm_pair[:, :4] + norm_pair[:, 4:], axis=0)
    dattended = low_dot(dmixed_low, full_out, contract_cols)
    dattended_low = dattended.astype(low_type)
    heads = head_width // HEAD_DIM
    delta = jnp.sum(
        (dattended * attended_low.astype(jnp.float32)).reshape(tok_rows, heads, HEAD_DIM), axis=-1
    ).T
    delta = jnp.concatenate([delta, jnp.zeros((8 - heads, tok_rows), jnp.float32)], 0)
    stats = jnp.concatenate([lse[:8], delta], 0)
    grads_group = dattended_low[None]
    stats_group = stats[None]
    for level in range(group_size.bit_length() - 1):
        grads_group = jnp.concatenate([grads_group, swap(grads_group, "dp", 2**level)], 0)
        stats_group = jnp.concatenate([stats_group, swap(stats_group, "dp", 2**level)], 0)
    pad = jnp.zeros((LANES - 8, tok_rows), jnp.float32)
    dquery_low, dkey_all, dvalue_all = attend_backward(
        query_rows,
        key_all,
        value_all,
        dattended_low,
        seg_rows[:, None],
        slot_keys[None, :],
        lse,
        jnp.concatenate([delta, pad], 0),
    )
    other_stats = jnp.swapaxes(stats_group[1:], 0, 1).reshape(16, -1)
    pad = jnp.zeros((LANES - 8, other_stats.shape[1]), jnp.float32)
    _, dkey_more, dvalue_more = attend_backward(
        query_others,
        key_all[:tok_rows],
        value_all[:tok_rows],
        grads_group[1:].reshape(-1, head_width),
        seg_others[:, None],
        slot_own[None, :],
        jnp.concatenate([other_stats[:8], pad], 0),
        jnp.concatenate([other_stats[8:], pad], 0),
    )
    dkey_low = (
        dkey_all[:tok_rows].astype(jnp.float32) + dkey_more.astype(jnp.float32)
    ).astype(low_type)
    dvalue_low = (
        dvalue_all[:tok_rows].astype(jnp.float32) + dvalue_more.astype(jnp.float32)
    ).astype(low_type)
    dqkv = jnp.concatenate([dquery_low, dkey_low, dvalue_low], axis=1)
    dhidden = low_dot(dqkv, full_qkv, contract_cols).astype(low_type)
    input_own = dresid_one + scatter_rows(dhidden)
    input_grad = gather_rows(input_own.astype(low_type)).astype(jnp.float32)

    def row_blocks(value):
        return value.reshape((dp_size, -1) + value.shape[1:])

    def col_blocks(value):
        return jnp.swapaxes(value.reshape(value.shape[0], dp_size, -1), 0, 1)

    col_width = w_colbert.shape[1]
    h2_pack = gather_rows(normed_two_low)
    du_cols = gather_rows(dproj_low)
    du_own = lax.dynamic_slice_in_dim(du_cols, column * col_width, col_width, 1)
    grad_colbert = scatter_sum(
        row_blocks(low_dot(h2_pack, du_own, contract_rows).astype(low_type)), "dp", dp_up
    )
    grad_down = scatter_sum(
        col_blocks(low_dot(active_low, dffn_low, contract_rows).astype(low_type)), "dp", dp_up
    )
    grad_up = scatter_sum(
        row_blocks(low_dot(normed_low, dinner_low, contract_rows).astype(low_type)), "dp", dp_up
    )
    out_part = low_dot(attended_low, dmixed_low, contract_rows).astype(low_type)
    norm_high = norm_sum.astype(low_type)
    norm_rest = (norm_sum - norm_high.astype(jnp.float32)).astype(low_type)
    out_part = jnp.concatenate(
        [out_part, norm_high, norm_rest, jnp.zeros((8, width), low_type)], 0
    )
    grad_out = scatter_sum(col_blocks(out_part), "dp", dp_up)
    norm_grads = grad_out[w_out.shape[0] : w_out.shape[0] + 8]
    norm_grads = norm_grads[:4] + norm_grads[4:]
    grad_qkv = low_dot(hidden_in, dqkv, contract_rows).astype(low_type)
    grad_a = scatter_sum(row_blocks(grad_qkv[:, :half]), "dp", dp_up)
    grad_b = scatter_sum(row_blocks(grad_qkv[:, half:]), "dp", dp_up[1:] + dp_up[:1])
    grad_qkv = jnp.concatenate([grad_a, grad_b], 1)
    return (
        scores,
        input_grad,
        grad_qkv[:, :head_width],
        grad_qkv[:, head_width : 2 * head_width],
        grad_qkv[:, 2 * head_width :],
        grad_out[: w_out.shape[0]],
        grad_up,
        grad_down,
        grad_colbert,
        norm_grads[0],
        norm_grads[1],
        norm_grads[2],
        norm_grads[3],
    )


def solution(mesh):
    return jax.shard_map(
        body,
        mesh=mesh,
        in_specs=(
            P("dp", None),
            P("dp", "mp"),
            P("dp", "mp"),
            P("dp", "mp"),
            P("mp", "dp"),
            P("dp", "mp"),
            P("mp", "dp"),
            P("dp", "mp"),
            P("dp"),
            P("dp"),
            P("dp"),
            P("dp"),
            P("mp", None),
            P(),
            P(),
            P("mp", None),
        ),
        out_specs=(
            P("mp", None),
            P("dp", None),
            P("dp", "mp"),
            P("dp", "mp"),
            P("dp", "mp"),
            P("mp", "dp"),
            P("dp", "mp"),
            P("mp", "dp"),
            P("dp", "mp"),
            P("dp"),
            P("dp"),
            P("dp"),
            P("dp"),
        ),
        check_vma=False,
    )
```

```python
import jax
import jax.numpy as jnp
from jax import lax
from jax.experimental import pallas as pl
from jax.experimental.pallas import tpu as pltpu
from jax.sharding import PartitionSpec as P

HEAD_DIM = 64
QLEN = 32
NBUCKET = 4
NPASS = 15
LANES = 128
SPARE = 16

neg_big = -1e30
low_type = jnp.bfloat16
full_type = jnp.float32
contract_rows = (((0,), (0,)), ((), ()))
contract_cols = (((1,), (1,)), ((), ()))
contract_inner = (((1,), (0,)), ((), ()))


def room(mebibytes):
    return pltpu.CompilerParams(vmem_limit_bytes=mebibytes * 1024 * 1024)


def room_for_keys(keys):
    return room(min(56, 4 + keys // 128))


brief = pl.CostEstimate(flops=1, bytes_accessed=1, transcendentals=0)


def low_dot(left, right, dims=contract_inner):
    return lax.dot_general(left, right, dims, preferred_element_type=full_type)


def shape_of(shape, dtype=low_type):
    return jax.ShapeDtypeStruct(shape, dtype)


def whole_call(kernel, outs, name, *args):
    vmem = pl.BlockSpec(memory_space=pltpu.VMEM)
    return pl.pallas_call(
        kernel,
        in_specs=[vmem] * len(args),
        out_specs=[vmem] * len(outs),
        out_shape=outs,
        compiler_params=room(12),
        cost_estimate=brief,
        name=name,
    )(*args)


def swap(value, axis, mask):
    pairs = [(source, source ^ mask) for source in range(lax.axis_size(axis))]
    return lax.ppermute(value, axis, pairs)


def bits_of(axis):
    return lax.axis_size(axis).bit_length() - 1


def has_bit(axis, mask):
    return lax.axis_index(axis) // mask % 2 == 1


def upward(axis):
    return [2**level for level in range(bits_of(axis))]


def downward(axis):
    return upward(axis)[::-1]


def offsets_of(masks):
    order = [0]
    for mask in masks:
        order = order + [at ^ mask for at in order]
    return order


def arrange(blocks, axis, masks):
    levels = bits_of(axis)
    cube = blocks.reshape((2,) * levels + blocks.shape[1:])
    for mask in masks:
        at = levels - mask.bit_length()
        cube = jnp.where(has_bit(axis, mask), jnp.flip(cube, at), cube)
    front = [levels - mask.bit_length() for mask in masks]
    cube = jnp.transpose(cube, front + list(range(levels, cube.ndim)))
    return cube.reshape(blocks.shape)


def tie(*values):
    return lax.optimization_barrier(values)


class Gather:
    def __init__(self, value, axis, masks):
        self.axis, self.masks = axis, list(masks)
        self.levels, self.shape = bits_of(axis), value.shape
        self.whole = value.reshape((1,) * self.levels + value.shape)

    def start(self, main):
        if self.masks:
            self.whole, main = tie(self.whole, main)
            self.other = swap(self.whole, self.axis, self.masks[0])
        return main

    def finish(self, main):
        if self.masks:
            mask = self.masks.pop(0)
            other, main = tie(self.other, main)
            at = self.levels - mask.bit_length()
            self.whole = jnp.where(
                has_bit(self.axis, mask),
                jnp.concatenate([other, self.whole], at),
                jnp.concatenate([self.whole, other], at),
            )
        return main

    def step(self, main):
        return self.start(self.finish(main))

    def drain(self, main):
        main = self.finish(main)
        while self.masks:
            main = self.finish(self.start(main))
        return main

    def value(self):
        return self.whole.reshape((-1,) + self.shape)


class Scatter:
    def __init__(self, keep, send, axis, masks):
        self.axis, self.masks = axis, list(masks)
        self.keep, self.send = keep, send

    def start(self, main):
        if self.masks:
            self.send, main = tie(self.send, main)
            self.other = swap(self.send, self.axis, self.masks[0])
        return main

    def finish(self, main):
        if self.masks:
            self.masks.pop(0)
            other, main = tie(self.other, main)
            total = self.keep.astype(full_type) + other.astype(full_type)
            half = total.shape[0] // 2
            if self.masks:
                self.keep, self.send = total[:half], total[half:].astype(low_type)
            else:
                self.keep = total
        return main

    def step(self, main):
        return self.start(self.finish(main))

    def drain(self, main):
        main = self.finish(main)
        while self.masks:
            main = self.finish(self.start(main))
        return main

    def value(self):
        return self.keep[0]


def rows_gather(block):
    blocks = [block]
    for mask in downward("mp"):
        blocks = blocks + [swap(each, "mp", mask) for each in blocks]
    return blocks


def rows_scatter(keep, send, main=None, between=None):
    masks = upward("mp")
    terms = [keep, swap(send, "mp", masks[0])]
    for mask in masks[1:]:
        terms = terms + [swap(rows_fold(*terms), "mp", mask)]
    return terms


def add_up(refs):
    rows = refs[-1].shape[0]
    total = refs[0][0:rows, :].astype(full_type)
    for ref in refs[1:]:
        total = total + ref[0:rows, :].astype(full_type)
    return total


def head_mask(width, head):
    lane = lax.broadcasted_iota(jnp.int32, (1, width), 1)
    return lane // HEAD_DIM == head


def only_head(rows, head):
    return jnp.where(head_mask(rows.shape[1], head), rows, jnp.zeros_like(rows))


def attend_forward_kernel(q_ref, k_ref, v_ref, segq_ref, segk_ref, o_ref, stat_ref):
    tile, width = q_ref.shape
    bias = jnp.where(segq_ref[...] == segk_ref[...], 0.0, neg_big)
    out = jnp.zeros((tile, width), full_type)
    stat = jnp.zeros((tile, LANES), full_type)
    lane = lax.broadcasted_iota(jnp.int32, (1, LANES), 1)
    queries = q_ref[...] * jnp.asarray(0.125, low_type)
    for head in range(width // HEAD_DIM):
        raw = low_dot(only_head(queries, head), k_ref[...], contract_cols) + bias
        top = jnp.max(raw, axis=1, keepdims=True)
        terms = jnp.exp(raw - top)
        total = jnp.sum(terms, axis=1, keepdims=True)
        mixed = low_dot(terms.astype(low_type), v_ref[...]) * (1.0 / total)
        out = jnp.where(head_mask(width, head), mixed, out)
        stat = jnp.where(lane == head, top + jnp.log(total), stat)
    o_ref[...] = out.astype(low_type)
    stat_ref[...] = stat.T[: stat_ref.shape[0]]


def attend_forward(query_key, value_rows, seg_rows, seg_keys):
    rows = seg_rows.shape[0]
    keys, width = value_rows.shape
    tile = LANES
    return pl.pallas_call(
        attend_forward_kernel,
        grid=(rows // tile,),
        in_specs=[
            pl.BlockSpec((tile, width), lambda i: (i, 0)),
            pl.BlockSpec((keys, width), lambda i: (0, 1)),
            pl.BlockSpec((keys, width), lambda i: (0, 0)),
            pl.BlockSpec((tile, 1), lambda i: (i, 0)),
            pl.BlockSpec((1, keys), lambda i: (0, 0)),
        ],
        out_specs=[
            pl.BlockSpec((tile, width), lambda i: (i, 0)),
            pl.BlockSpec((8, tile), lambda i: (0, i)),
        ],
        out_shape=[shape_of((rows, width)), shape_of((8, rows), full_type)],
        compiler_params=room_for_keys(keys),
        cost_estimate=brief,
        name="attend_forward",
    )(query_key, query_key, value_rows, seg_rows, seg_keys)


def attend_terms(q_ref, k_ref, v_ref, do_ref, o_ref, segq_ref, segk_ref, lse_ref):
    tile, width = q_ref.shape
    bias = jnp.where(segq_ref[...] == segk_ref[...], 0.0, neg_big)
    pad = jnp.zeros((LANES - lse_ref.shape[0], tile), full_type)
    lse = jnp.concatenate([lse_ref[...], pad], 0).T
    queries = q_ref[...] * jnp.asarray(0.125, low_type)
    grads = do_ref[...]
    both = grads.astype(full_type) * o_ref[...].astype(full_type)
    for head in range(width // HEAD_DIM):
        q_head = only_head(queries, head)
        g_head = only_head(grads, head)
        delta = jnp.sum(only_head(both, head), axis=1, keepdims=True)
        raw = low_dot(q_head, k_ref[...], contract_cols)
        probs = jnp.exp(raw + (bias - lse[:, head : head + 1]))
        dprobs = low_dot(g_head, v_ref[...], contract_cols)
        dscore = (probs * (dprobs - delta)).astype(low_type)
        yield head, q_head, g_head, probs.astype(low_type), dscore


def attend_own_kernel(
    q_ref, k_ref, v_ref, do_ref, o_ref, segq_ref, segk_ref, lse_ref, dq_ref, dk_ref, dv_ref
):
    tile, width = q_ref.shape
    own = dk_ref.shape[0]

    @pl.when(pl.program_id(0) == 0)
    def _():
        dk_ref[...] = jnp.zeros_like(dk_ref)
        dv_ref[...] = jnp.zeros_like(dv_ref)

    dquery = jnp.zeros((tile, width), full_type)
    for head, q_head, g_head, probs, dscore in attend_terms(
        q_ref, k_ref, v_ref, do_ref, o_ref, segq_ref, segk_ref, lse_ref
    ):
        dquery = jnp.where(head_mask(width, head), low_dot(dscore, k_ref[...]), dquery)
        dk_ref[...] += low_dot(dscore[:, :own], q_head, contract_rows)
        dv_ref[...] += low_dot(probs[:, :own], g_head, contract_rows)
    dq_ref[...] = (dquery * 0.125).astype(low_type)


def attend_own(query_key, value_rows, grads, attended, seg_rows, seg_keys, lse):
    rows, width = grads.shape
    keys = value_rows.shape[0]
    tile = LANES
    return pl.pallas_call(
        attend_own_kernel,
        grid=(rows // tile,),
        in_specs=[
            pl.BlockSpec((tile, width), lambda i: (i, 0)),
            pl.BlockSpec((keys, width), lambda i: (0, 1)),
            pl.BlockSpec((keys, width), lambda i: (0, 0)),
            pl.BlockSpec((tile, width), lambda i: (i, 0)),
            pl.BlockSpec((tile, width), lambda i: (i, 0)),
            pl.BlockSpec((tile, 1), lambda i: (i, 0)),
            pl.BlockSpec((1, keys), lambda i: (0, 0)),
            pl.BlockSpec((8, tile), lambda i: (0, i)),
        ],
        out_specs=[
            pl.BlockSpec((tile, width), lambda i: (i, 0)),
            pl.BlockSpec((rows, width), lambda i: (0, 0)),
            pl.BlockSpec((rows, width), lambda i: (0, 0)),
        ],
        out_shape=[
            shape_of((rows, width)),
            shape_of((rows, width), full_type),
            shape_of((rows, width), full_type),
        ],
        compiler_params=room_for_keys(keys),
        cost_estimate=brief,
        name="attend_own",
    )(query_key, query_key, value_rows, grads, attended, seg_rows, seg_keys, lse)


def attend_other_kernel(
    q_ref,
    k_ref,
    v_ref,
    do_ref,
    o_ref,
    segq_ref,
    segk_ref,
    lse_ref,
    dq_ref,
    dk_ref,
    dv_ref,
    dqk_out,
    dv_out,
    dk_sum,
    dv_sum,
):
    width = q_ref.shape[1]

    @pl.when(pl.program_id(0) == 0)
    def _():
        dk_sum[...] = dk_ref[...]
        dv_sum[...] = dv_ref[...]

    for _, q_head, g_head, probs, dscore in attend_terms(
        q_ref, k_ref, v_ref, do_ref, o_ref, segq_ref, segk_ref, lse_ref
    ):
        dk_sum[...] += low_dot(dscore, q_head, contract_rows)
        dv_sum[...] += low_dot(probs, g_head, contract_rows)

    @pl.when(pl.program_id(0) == pl.num_programs(0) - 1)
    def _():
        dqk_out[:, :width] = dq_ref[...]
        dqk_out[:, width:] = dk_sum[...].astype(low_type)
        dv_out[...] = dv_sum[...].astype(low_type)


def attend_other(query_key, value_rows, grads, attended, seg_rows, seg_keys, lse, dq, dk, dv):
    rows, width = grads.shape
    own = dq.shape[0]
    tile = LANES
    first = own // tile
    held = pl.BlockSpec((own, width), lambda i: (0, 0))
    return pl.pallas_call(
        attend_other_kernel,
        grid=(rows // tile,),
        in_specs=[
            pl.BlockSpec((tile, width), lambda i: (i + first, 0)),
            pl.BlockSpec((own, width), lambda i: (0, 1)),
            held,
            pl.BlockSpec((tile, width), lambda i: (i, 0)),
            pl.BlockSpec((tile, width), lambda i: (i, 0)),
            pl.BlockSpec((tile, 1), lambda i: (i, 0)),
            pl.BlockSpec((1, own), lambda i: (0, 0)),
            pl.BlockSpec((8, tile), lambda i: (0, i)),
            held,
            held,
            held,
        ],
        out_specs=[pl.BlockSpec((own, 2 * width), lambda i: (0, 0)), held],
        out_shape=[shape_of((own, 2 * width)), shape_of((own, width))],
        scratch_shapes=[pltpu.VMEM((own, width), full_type)] * 2,
        compiler_params=room_for_keys(own),
        cost_estimate=brief,
        name="attend_other",
    )(query_key, query_key, value_rows, grads, attended, seg_rows, seg_keys, lse, dq, dk, dv)


def lanes_of(ref):
    return jnp.concatenate([ref[at] for at in range(ref.shape[0])], axis=1)


def rows_of(refs):
    return jnp.concatenate([ref[...] for ref in refs], axis=0)


def feed_up_kernel(*refs):
    *row_refs, up_ref, g_ref, slope_ref = refs
    for at, ref in enumerate(row_refs):
        place = pl.ds(at * ref.shape[0], ref.shape[0])
        inner = low_dot(ref[...], up_ref[...])
        normal = 0.5 * (1.0 + lax.erf(inner * 0.7071067811865476))
        g_ref[place, :] = (inner * normal).astype(low_type)
        slope = normal + inner * jnp.exp(-0.5 * inner * inner) * 0.3989422804014327
        slope_ref[place, :] = slope.astype(low_type)


def feed_up(blocks, w_up, units):
    own, width = blocks[0].shape
    rows = own * len(blocks)
    tile = 256
    return pl.pallas_call(
        feed_up_kernel,
        grid=(units // tile,),
        in_specs=[pl.BlockSpec((own, width), lambda i: (0, 0))] * len(blocks)
        + [pl.BlockSpec((width, tile), lambda i: (0, i))],
        out_specs=[pl.BlockSpec((rows, tile), lambda i: (0, i))] * 2,
        out_shape=[shape_of((rows, units))] * 2,
        compiler_params=room(10),
        cost_estimate=brief,
        name="feed_up",
    )(*blocks, w_up)


def store_halves(total, keep_ref, send_ref):
    half = total.shape[0] // 2
    keep_ref[...] = total[:half]
    send_ref[...] = total[half:].astype(low_type)


def halves_of(rows, width):
    return [shape_of((rows // 2, width), full_type), shape_of((rows // 2, width))]


def feed_down_kernel(g_ref, down_ref, keep_ref, send_ref):
    store_halves(low_dot(g_ref[...], lanes_of(down_ref)), keep_ref, send_ref)


def feed_down(active, w_down):
    rows, units = active.shape
    blocks, _, lanes = w_down.shape
    tile = 2
    return pl.pallas_call(
        feed_down_kernel,
        grid=(blocks // tile,),
        in_specs=[
            pl.BlockSpec((rows, units), lambda i: (0, 0)),
            pl.BlockSpec((tile, units, lanes), lambda i: (i, 0, 0)),
        ],
        out_specs=[pl.BlockSpec((rows // 2, tile * lanes), lambda i: (0, i))] * 2,
        out_shape=halves_of(rows, blocks * lanes),
        compiler_params=room(10),
        cost_estimate=brief,
        name="feed_down",
    )(active, w_down)


def feed_inner_kernel(*refs):
    *row_refs, down_ref, slope_ref, dz_ref = refs
    weight = lanes_of(down_ref)
    for at, ref in enumerate(row_refs):
        place = pl.ds(at * ref.shape[0], ref.shape[0])
        dactive = low_dot(ref[...], weight, contract_cols)
        dz_ref[place, :] = (dactive * slope_ref[place, :].astype(full_type)).astype(low_type)


def feed_inner(blocks, w_down, slope):
    own, width = blocks[0].shape
    rows, units = slope.shape
    tile = 256
    lanes = w_down.shape[2]
    return pl.pallas_call(
        feed_inner_kernel,
        grid=(units // tile,),
        in_specs=[pl.BlockSpec((own, width), lambda i: (0, 0))] * len(blocks)
        + [
            pl.BlockSpec((w_down.shape[0], tile, lanes), lambda i: (0, i, 0)),
            pl.BlockSpec((rows, tile), lambda i: (0, i)),
        ],
        out_specs=pl.BlockSpec((rows, tile), lambda i: (0, i)),
        out_shape=shape_of((rows, units)),
        compiler_params=room(10),
        cost_estimate=brief,
        name="feed_inner",
    )(*blocks, w_down, slope)


def feed_back_kernel(dz_ref, up_ref, keep_ref, send_ref):
    store_halves(low_dot(dz_ref[...], up_ref[...], contract_cols), keep_ref, send_ref)


def feed_back(dinner, w_up):
    rows, units = dinner.shape
    width = w_up.shape[0]
    tile = 256
    return pl.pallas_call(
        feed_back_kernel,
        grid=(width // tile,),
        in_specs=[
            pl.BlockSpec((rows, units), lambda i: (0, 0)),
            pl.BlockSpec((tile, units), lambda i: (i, 0)),
        ],
        out_specs=[pl.BlockSpec((rows // 2, tile), lambda i: (0, i))] * 2,
        out_shape=halves_of(rows, width),
        compiler_params=room(10),
        cost_estimate=brief,
        name="feed_back",
    )(dinner, w_up)


def late_forward_kernel(*refs):
    *e_refs, q_ref, live_ref, sharp_ref, soft_ref = refs
    blocks = soft_ref.shape[0]
    per = blocks // len(e_refs)
    for at, e_ref in enumerate(e_refs):
        rows = e_ref.shape[0]
        place = pl.ds(at * rows, rows)
        sharp = low_dot(e_ref[...], q_ref[...], contract_cols) * 2.0 + live_ref[place, :]
        sharp_ref[place, :] = sharp
        cube = sharp.reshape(per, rows // per, sharp.shape[1])
        top = jnp.max(cube, axis=1)
        total = jnp.sum(jnp.exp(cube - top[:, None, :]), axis=1)
        soft = jnp.where(top > 0.5 * neg_big, top + jnp.log(total), neg_big)
        soft_ref[pl.ds(at * per, per), :] = soft


def late_forward(e_blocks, queries, live_bias, blocks):
    own, width = e_blocks[0].shape
    rows = own * len(e_blocks)
    count = queries.shape[0]
    tile = 512
    return pl.pallas_call(
        late_forward_kernel,
        grid=(count // tile,),
        in_specs=[pl.BlockSpec((own, width), lambda i: (0, 0))] * len(e_blocks)
        + [
            pl.BlockSpec((tile, width), lambda i: (i, 0)),
            pl.BlockSpec((rows, 1), lambda i: (0, 0)),
        ],
        out_specs=[
            pl.BlockSpec((rows, tile), lambda i: (0, i)),
            pl.BlockSpec((blocks, tile), lambda i: (0, i)),
        ],
        out_shape=[shape_of((rows, count), full_type), shape_of((blocks, count), full_type)],
        compiler_params=room(14),
        cost_estimate=brief,
        name="late_forward",
    )(*e_blocks, queries, live_bias)


def late_backward_kernel(sharp_ref, soft_ref, weight_ref, q_ref, keep_ref, send_ref, total):
    step = pl.program_id(0)
    blocks = soft_ref.shape[0]
    rows, tile = sharp_ref.shape
    cube = sharp_ref[...].reshape(blocks, rows // blocks, tile)
    pulled = weight_ref[...][:, None, :] * jnp.exp(cube - soft_ref[...][:, None, :])
    term = low_dot(pulled.reshape(rows, tile).astype(low_type), q_ref[...])

    @pl.when(step == 0)
    def _():
        total[...] = term

    @pl.when(step > 0)
    def _():
        total[...] += term

    @pl.when(step == pl.num_programs(0) - 1)
    def _():
        store_halves(total[...], keep_ref, send_ref)


def late_backward(sharp, soft, weight, queries):
    rows, count = sharp.shape
    width = queries.shape[1]
    blocks = soft.shape[0]
    tile = 512
    held = pl.BlockSpec((rows // 2, width), lambda i: (0, 0))
    return pl.pallas_call(
        late_backward_kernel,
        grid=(count // tile,),
        in_specs=[
            pl.BlockSpec((rows, tile), lambda i: (0, i)),
            pl.BlockSpec((blocks, tile), lambda i: (0, i)),
            pl.BlockSpec((blocks, tile), lambda i: (0, i)),
            pl.BlockSpec((tile, width), lambda i: (i, 0)),
        ],
        out_specs=[held, held],
        out_shape=halves_of(rows, width),
        scratch_shapes=[pltpu.VMEM((rows, width), full_type)],
        compiler_params=room(16),
        cost_estimate=brief,
        name="late_backward",
    )(sharp, soft, weight, queries)


def norm_stats(values):
    centre = values - jnp.mean(values, axis=-1, keepdims=True)
    spread = jnp.mean(centre * centre, axis=-1, keepdims=True)
    scale = lax.rsqrt(spread + 1e-05)
    return centre * scale, scale


def norm_backward(unit, scale, gain, grad):
    dunit = grad * gain
    dvalues = scale * (
        dunit
        - jnp.mean(dunit, axis=-1, keepdims=True)
        - unit * jnp.mean(dunit * unit, axis=-1, keepdims=True)
    )
    return (
        dvalues,
        jnp.sum(grad * unit, axis=0, keepdims=True),
        jnp.sum(grad, axis=0, keepdims=True),
    )


def norm_one_kernel(*refs):
    *terms, norm_ref, h_ref, low_ref, unit_ref, scale_ref = refs
    unit, scale = norm_stats(add_up(terms))
    normed = unit * norm_ref[0:1] + norm_ref[1:2]
    h_ref[...] = normed
    low_ref[...] = normed.astype(low_type)
    unit_ref[...] = unit
    scale_ref[...] = scale


def lanes_at(order_ref, at, span):
    return pl.ds(pl.multiple_of(order_ref[at] * span, span), span)


def norm_two_kernel(order_ref, *refs):
    *rest, low_ref, unit_ref, scale_ref, e_ref, elow_ref, inv_ref = refs
    parts = order_ref.shape[0]
    *terms, norm_ref = rest[:-parts]
    col_refs = rest[-parts:]
    unit, scale = norm_stats(add_up(terms))
    normed_low = (unit * norm_ref[2:3] + norm_ref[3:4]).astype(low_type)
    low_ref[...] = normed_low
    unit_ref[...] = unit
    scale_ref[...] = scale
    span = col_refs[0].shape[1]
    squares = 0.0
    for at, ref in enumerate(col_refs):
        projected = low_dot(normed_low, ref[...])
        e_ref[:, lanes_at(order_ref, at, span)] = projected
        squares = squares + jnp.sum(projected * projected, axis=-1, keepdims=True)
    inv = lax.rsqrt(squares + 1e-06)
    embedded = e_ref[...] * inv
    e_ref[...] = embedded
    elow_ref[...] = embedded.astype(low_type)
    inv_ref[...] = inv


def norm_two_back_kernel(order_ref, *refs):
    *rest, du_ref, dr_ref, low_ref, g_ref = refs
    parts = order_ref.shape[0]
    *terms, norm_ref, unit_ref, scale_ref, e_ref, inv_ref = rest[:-parts]
    col_refs = rest[-parts:]
    dembed = add_up(terms)
    embedded = e_ref[...]
    along = jnp.sum(embedded * dembed, axis=-1, keepdims=True)
    du_ref[...] = (inv_ref[...] * (dembed - embedded * along)).astype(low_type)
    span = col_refs[0].shape[1]
    dnormed = 0.0
    for at, ref in enumerate(col_refs):
        dproj = du_ref[:, lanes_at(order_ref, at, span)]
        dnormed = dnormed + low_dot(dproj, ref[...], contract_cols)
    dresid, dgain, dshift = norm_backward(
        unit_ref[...], scale_ref[...], norm_ref[2:3], dnormed
    )
    dr_ref[...] = dresid
    low_ref[...] = dresid.astype(low_type)
    g_ref[...] = jnp.concatenate([dgain, dshift], 0)


def split_sums(sums):
    high = sums.astype(low_type).astype(full_type)
    zeros = jnp.zeros((SPARE - 8, sums.shape[1]), full_type)
    return jnp.concatenate([high, sums - high, zeros], 0).astype(low_type)


def norm_one_back_kernel(*refs):
    *terms, norm_ref, unit_ref, scale_ref, two_ref, dr_ref, pack_ref = refs
    dresid, dgain, dshift = norm_backward(
        unit_ref[...], scale_ref[...], norm_ref[0:1], add_up(terms)
    )
    dr_ref[...] = dresid
    rows = dresid.shape[0]
    pack_ref[0:rows, :] = dresid.astype(low_type)
    pack_ref[rows : rows + SPARE, :] = split_sums(
        jnp.concatenate([dgain, dshift, two_ref[...]], 0)
    )


def fold_kernel(keep_ref, got_ref, low_ref):
    half = low_ref.shape[0]
    total = keep_ref[half:, :] + got_ref[half:, :].astype(full_type)
    low_ref[...] = total.astype(low_type)


def rows_fold(keep, got):
    return whole_call(fold_kernel, [shape_of((got.shape[0] // 2, got.shape[1]))], "fold", keep, got)[0]


def mix_kernel(o_ref, out_ref, keep_ref, send_ref):
    rows = o_ref.shape[1]
    weight = jnp.concatenate([out_ref[at, 0:rows, :] for at in range(out_ref.shape[0])], axis=1)
    store_halves(low_dot(o_ref[...], weight), keep_ref, send_ref)


def unmix_kernel(*refs):
    *packs, out_ref, do_ref, sums_ref = refs
    rows = do_ref.shape[1]
    weight = jnp.concatenate([out_ref[at, 0:rows, :] for at in range(out_ref.shape[0])], axis=1)
    own = packs[0].shape[0] - SPARE
    sums = jnp.zeros((8, weight.shape[1]), full_type)
    for at, ref in enumerate(packs):
        do = low_dot(ref[0:own, :], weight, contract_cols)
        do_ref[at * own : (at + 1) * own, :] = do.astype(low_type)
        sums = sums + ref[own : own + SPARE, :].astype(full_type)[:8]
    sums_ref[...] = split_sums(sums[:4] + sums[4:])


def block_order(masks):
    return lax.axis_index("dp") ^ jnp.asarray(offsets_of(masks[::-1]), jnp.int32)


def ordered_call(kernel, outs, scratch, name, order, *args):
    vmem = pl.BlockSpec(memory_space=pltpu.VMEM)
    return pl.pallas_call(
        kernel,
        in_specs=[pl.BlockSpec(memory_space=pltpu.SMEM)] + [vmem] * len(args),
        out_specs=[vmem] * len(outs),
        out_shape=outs,
        scratch_shapes=[pltpu.VMEM(*each) for each in scratch],
        compiler_params=room(12),
        cost_estimate=brief,
        name=name,
    )(order, *args)


def stored(place_ref, left, right):
    turned = left.T
    cols = right.shape[1]
    for start in range(0, cols, 256):
        stop = min(start + 256, cols)
        place_ref[:, start:stop] = low_dot(turned, right[:, start:stop]).astype(low_type)


def deal(order_ref, keep_ref, send_ref, write):
    half = keep_ref.shape[0]
    for at in range(2 * half):
        write(keep_ref.at[at] if at < half else send_ref.at[at - half], order_ref[at])


def rows_in(ref, block, count):
    return ref[pl.ds(pl.multiple_of(block * count, count), count), :]


def lanes_in(ref, block):
    return ref[:, pl.ds(pl.multiple_of(block * LANES, LANES), LANES)]


def halves_like(count, block):
    return [shape_of((count // 2,) + block)] * 2


def grad_down_kernel(order_ref, active_ref, *refs):
    *row_refs, keep_ref, send_ref, total = refs
    stored(total, active_ref[...], rows_of(row_refs))

    def write(ref, block):
        ref[...] = lanes_in(total, block)

    deal(order_ref, keep_ref, send_ref, write)


def grad_down(active, row_blocks, masks):
    count = lax.axis_size("dp")
    units, width = active.shape[1], row_blocks[0].shape[1]
    if width // count == LANES:
        return ordered_call(
            grad_down_kernel,
            halves_like(count, (units, LANES)),
            [((units, width), low_type)],
            "grad_down",
            block_order(masks),
            active,
            *row_blocks,
        )
    whole = low_dot(active, jnp.concatenate(row_blocks, 0), contract_rows).astype(low_type)
    return halves(arrange(jnp.swapaxes(whole.reshape(units, count, -1), 0, 1), "dp", masks))


def halves(blocks):
    half = blocks.shape[0] // 2
    return blocks[:half], blocks[half:]


def grad_up_kernel(order_ref, dinner_ref, *refs):
    *row_refs, keep_ref, send_ref, total = refs
    parts = len(row_refs) // 3
    units = dinner_ref.shape[1]
    block_rows = keep_ref.shape[1]
    cols = keep_ref.shape[2] - units
    stored(total.at[:, 0:units], rows_of(row_refs[:parts]), dinner_ref[...])
    mine = pl.ds(pl.multiple_of(order_ref[order_ref.shape[0] - 1] * cols, cols), cols)
    dproj = jnp.concatenate([ref[:, mine] for ref in row_refs[2 * parts :]], axis=0)
    stored(total.at[:, units:], rows_of(row_refs[parts : 2 * parts]), dproj)

    def write(ref, block):
        ref[...] = rows_in(total, block, block_rows)

    deal(order_ref, keep_ref, send_ref, write)


def grad_up(dinner, one_blocks, two_blocks, du_blocks, col_width, masks):
    count = lax.axis_size("dp")
    units, width = dinner.shape[1], one_blocks[0].shape[1]
    column = lax.axis_index("mp")
    rows = width // count
    if rows == LANES:
        order = jnp.concatenate([block_order(masks), column.reshape(1)])
        return ordered_call(
            grad_up_kernel,
            halves_like(count, (rows, units + col_width)),
            [((width, units + col_width), low_type)],
            "grad_up",
            order,
            dinner,
            *one_blocks,
            *two_blocks,
            *du_blocks,
        )
    dproj = lax.dynamic_slice_in_dim(
        jnp.concatenate(du_blocks, 0), column * col_width, col_width, 1
    )
    up = low_dot(jnp.concatenate(one_blocks, 0), dinner, contract_rows)
    col = low_dot(jnp.concatenate(two_blocks, 0), dproj, contract_rows)
    whole = jnp.concatenate([up, col], 1).astype(low_type)
    return halves(arrange(whole.reshape(count, rows, -1), "dp", masks))


def grad_qk_kernel(order_ref, left_ref, right_ref, keep_ref, send_ref, total):
    block_rows = keep_ref.shape[1]
    stored(total, left_ref[...], right_ref[...])

    def write(ref, block):
        ref[...] = rows_in(total, block, block_rows)

    deal(order_ref, keep_ref, send_ref, write)


def grad_qk(left, right, masks):
    count = lax.axis_size("dp")
    width, cols = left.shape[1], right.shape[1]
    rows = width // count
    if rows == LANES:
        return ordered_call(
            grad_qk_kernel,
            halves_like(count, (rows, cols)),
            [((width, cols), low_type)],
            "grad_qk",
            block_order(masks),
            left,
            right,
        )
    whole = low_dot(left, right, contract_rows).astype(low_type)
    return halves(arrange(whole.reshape(count, rows, cols), "dp", masks))


def grad_vo_kernel(order_ref, hidden_ref, dv_ref, o_ref, *refs):
    *packs, sums_ref, keep_ref, send_ref, total_v, total_o = refs
    rows = packs[0].shape[0] - SPARE
    cols = dv_ref.shape[1]
    heads = o_ref.shape[1]
    stored(total_v, hidden_ref[...], dv_ref[...])
    mixed = jnp.concatenate([ref[0:rows, :] for ref in packs], axis=0)
    stored(total_o.at[0:heads, :], o_ref[...], mixed)
    total_o[heads : heads + SPARE, :] = sums_ref[...]

    def write(ref, block):
        value = rows_in(total_v, block, LANES)
        for at in range(cols // LANES):
            ref[at * LANES : (at + 1) * LANES, :] = value[:, at * LANES : (at + 1) * LANES]
        ref[cols:, :] = lanes_in(total_o, block)

    deal(order_ref, keep_ref, send_ref, write)


def pack_vo(value, out):
    cols = value.shape[-1]
    parts = [value[..., at : at + LANES] for at in range(0, cols, LANES)]
    return jnp.concatenate(parts + [out.reshape(out.shape[:-2] + (-1, LANES))], axis=-2)


def unpack_vo(packed, rows, cols, out_shape):
    high = rows * cols // LANES
    value = jnp.concatenate(
        [packed[..., at : at + rows, :] for at in range(0, high, rows)], axis=-1
    )
    return value, packed[..., high:, :].reshape(packed.shape[:-2] + out_shape)


def grad_vo(hidden, dvalue, attended, packs, sums, masks):
    count = lax.axis_size("dp")
    width, cols = hidden.shape[1], dvalue.shape[1]
    heads = attended.shape[1]
    rows = width // count
    if rows == LANES:
        block = (cols * rows // LANES + heads + SPARE, LANES)
        return ordered_call(
            grad_vo_kernel,
            halves_like(count, block),
            [((width, cols), low_type), ((heads + SPARE, width), low_type)],
            "grad_vo",
            block_order(masks),
            hidden,
            dvalue,
            attended,
            *packs,
            sums,
        )
    value = low_dot(hidden, dvalue, contract_rows).astype(low_type).reshape(count, rows, cols)
    mixed = jnp.concatenate([each[:-SPARE] for each in packs], 0)
    out = low_dot(attended, mixed, contract_rows).astype(low_type)
    out = jnp.concatenate([out, sums], 0).reshape(heads + SPARE, count, rows)
    return halves(arrange(pack_vo(value, jnp.swapaxes(out, 0, 1)), "dp", masks))


def to_lanes(blocks):
    if blocks.shape[2] == LANES:
        return blocks
    whole = jnp.swapaxes(blocks, 0, 1).reshape(blocks.shape[1], -1, LANES)
    return jnp.swapaxes(whole, 0, 1)


def place_kernel(at_ref, *refs):
    *blocks, out_ref = refs
    rows = blocks[0].shape[0]
    for at, ref in enumerate(blocks):
        start = pl.multiple_of(at_ref[at] * rows, rows)
        out_ref[pl.ds(start, rows), :] = ref[...].astype(full_type)


def place_rows(order, blocks):
    rows, width = blocks[0].shape
    outs = [shape_of((rows * len(blocks), width), full_type)]
    return ordered_call(place_kernel, outs, [], "place_rows", order, *blocks)[0]


def unproject_kernel(dqk_ref, dv_ref, a_ref, b_ref, keep_ref, send_ref):
    total = low_dot(dqk_ref[...], a_ref[...], contract_cols)
    store_halves(total + low_dot(dv_ref[...], b_ref[...], contract_cols), keep_ref, send_ref)


def unproject(dqk, dvalue, w_qk, w_v):
    outs = halves_of(dqk.shape[0], w_qk.shape[0])
    return whole_call(unproject_kernel, outs, "unproject", dqk, dvalue, w_qk, w_v)


def close_kernel(*refs):
    *terms, out_ref = refs
    out_ref[...] = add_up(terms).astype(low_type)


def pack_kernel(
    order_ref,
    hidden_ref,
    q_ref,
    k_ref,
    v_ref,
    o_ref,
    norm_ref,
    up_ref,
    col_ref,
    a_out,
    u_out,
    b_out,
    own_out,
):
    heads = q_ref.shape[1]
    a_out[:, :heads] = q_ref[...]
    a_out[:, heads:] = k_ref[...]
    units = up_ref.shape[1]
    u_out[:, :units] = up_ref[...]
    u_out[:, units:] = col_ref[...]
    for at in range(heads // LANES):
        b_out[at * LANES : (at + 1) * LANES, :] = v_ref[:, at * LANES : (at + 1) * LANES]
    rest = v_ref.shape[0] * heads // LANES
    b_out[rest : rest + o_ref.shape[0], :] = o_ref[...]
    b_out[rest + o_ref.shape[0] :, :] = norm_ref[...]
    parts = order_ref.shape[0]
    rows = hidden_ref.shape[0] // parts
    for at in range(parts):
        own_out[at * rows : (at + 1) * rows, :] = rows_in(hidden_ref, order_ref[at], rows)


def pack_inputs(order, hidden, w_query, w_key, w_value, w_out, norms, w_up, w_colbert):
    rows, heads = w_query.shape
    if w_out.shape[1] == LANES and rows == LANES:
        packed = (rows * heads // LANES + w_out.shape[0] + SPARE, LANES)
        outs = [
            shape_of((rows, 2 * heads)),
            shape_of((rows, w_up.shape[1] + w_colbert.shape[1])),
            shape_of(packed),
            shape_of(hidden.shape),
        ]
        args = (hidden, w_query, w_key, w_value, w_out, norms, w_up, w_colbert)
        return ordered_call(pack_kernel, outs, [], "pack", order, *args)
    span = hidden.shape[0] // order.shape[0]
    return (
        jnp.concatenate([w_query, w_key], axis=1),
        jnp.concatenate([w_up, w_colbert], axis=1),
        pack_vo(w_value, jnp.concatenate([w_out, norms], axis=0)),
        jnp.concatenate(
            [
                lax.dynamic_slice_in_dim(hidden, order[at] * span, span, 0)
                for at in range(order.shape[0])
            ]
        ),
    )


def body(
    hidden_in,
    w_query,
    w_key,
    w_value,
    w_out,
    w_up,
    w_down,
    w_colbert,
    norm1_gain,
    norm1_shift,
    norm2_gain,
    norm2_shift,
    queries,
    passage,
    live,
    score_grad,
):
    tok_rows, width = hidden_in.shape
    device = lax.axis_index("dp")
    column = lax.axis_index("mp")
    dp_size = lax.axis_size("dp")
    mp_size = lax.axis_size("mp")
    group_size = dp_size // NBUCKET
    group_levels = group_size.bit_length() - 1
    own_rows = tok_rows // mp_size
    head_width = w_query.shape[1]
    dp_up, dp_down = upward("dp"), downward("dp")
    turned = dp_up[:1] + dp_down[:-1]
    row_order = offsets_of(downward("mp"))

    def ordered(value, owner, span=own_rows):
        return jnp.concatenate(
            [
                lax.dynamic_slice_in_dim(value, (owner * mp_size + (column ^ at)) * span, span, 0)
                for at in row_order
            ]
        )

    def group_gather(value):
        for level in range(group_levels):
            value = jnp.concatenate([value, swap(value, "dp", 2**level)], 0)
        return value

    across = dp_up[-1:] + dp_up[:-1]
    turned_back, across_back = turned[::-1], across[::-1]
    col_order = column ^ jnp.asarray(row_order, jnp.int32)
    norms = jnp.stack([norm1_gain, norm1_shift, norm2_gain, norm2_shift])
    norms = jnp.concatenate([norms, jnp.zeros((SPARE - 4, w_out.shape[1]), low_type)], 0)
    out_shape = (w_out.shape[0] + SPARE, w_out.shape[1])
    packed_a, packed_u, packed_b, hidden_own = pack_inputs(
        col_order, hidden_in, w_query, w_key, w_value, w_out, norms, w_up, w_colbert
    )
    own_hidden = hidden_own[:own_rows]
    pack_a = Gather(packed_a, "dp", dp_down)
    pack_u = Gather(packed_u, "dp", dp_down)
    pack_b = Gather(packed_b, "dp", turned)
    pack_d = Gather(w_down, "dp", dp_down)

    main = (hidden_own, own_hidden)
    main = pack_a.start(main)
    main = pack_u.start(main)
    main = pack_b.start(main)
    others = group_gather(main[1][None])[1:]
    seg_own = ordered(passage, device)
    live_own = ordered(live, device)
    seg_others = jnp.concatenate([ordered(passage, device ^ at) for at in range(1, group_size)])
    live_others = jnp.concatenate([ordered(live, device ^ at) for at in range(1, group_size)])
    slot_own = jnp.where(live_own == 1, seg_own, -1)
    slot_keys = jnp.concatenate([slot_own, jnp.where(live_others == 1, seg_others, -1)])
    seg_column, seg_far, slot_row = seg_own[:, None], seg_others[:, None], slot_keys[None, :]
    blocks = 2 ** (NBUCKET - 1)
    seg_block = seg_own.reshape(blocks, -1)[:, 0]
    live_bias = jnp.where(live_own == 1, 0.0, neg_big)[:, None]
    same = seg_block[:, None] == seg_block[None, :]
    passages = jnp.arange(NPASS, dtype=jnp.int32)
    place = (seg_block[:, None] == passages[None, :]).astype(full_type)
    grad_block = jnp.sum(place[:, None, :] * score_grad[None], axis=2)
    weight = jnp.repeat(grad_block / QLEN, QLEN, axis=1)
    early = (seg_column, seg_far, slot_own, slot_row, live_bias, weight, same, place)
    early, main = tie(early, main)
    seg_column, seg_far, slot_own, slot_row, live_bias, weight, same, place = early
    main = pack_a.step(main)
    others, main = tie(others, main)
    far_others = swap(others, "mp", 2)
    main = pack_u.step(main)
    main = pack_b.step(main)
    main = pack_a.step(main)
    main = pack_d.start(main)
    far_others, main = tie(far_others, main)
    others = [others, far_others]
    others = others + [swap(each, "mp", 1) for each in others]
    others = jnp.stack(others, 1).reshape(-1, width)
    hidden_own, own_hidden = main
    hidden_all = jnp.concatenate([hidden_own, others], 0)
    main = (hidden_own, own_hidden, hidden_all)
    main = pack_b.step(main)
    main = pack_u.step(main)
    main = pack_a.drain(main)
    full_a = pack_a.value().reshape(width, -1)
    full_a, main = tie(full_a, main)
    hidden_own, own_hidden, hidden_all = main

    query_key = low_dot(hidden_all, full_a).astype(low_type)
    main = (query_key, hidden_all)
    main = pack_d.step(main)
    main = pack_b.drain(main)
    full_b, full_out = unpack_vo(pack_b.value(), w_value.shape[0], head_width, out_shape)
    full_b = full_b.reshape(width, head_width)
    full_out = to_lanes(full_out)
    (full_b, full_out), main = tie((full_b, full_out), main)
    query_key, hidden_all = main
    value_rows = low_dot(hidden_all, full_b).astype(low_type)
    norm_rows = jnp.swapaxes(full_out[:, head_width : head_width + 4], 0, 1).reshape(4, width)
    norm_rows = norm_rows.astype(full_type)
    attended, lse = attend_forward(query_key, value_rows, seg_column, slot_row)
    norm_rows, attended = tie(norm_rows, attended)
    attended = pack_d.step(attended)
    terms = rows_scatter(*whole_call(mix_kernel, halves_of(tok_rows, width), "mix", attended, full_out))
    terms = pack_u.drain(terms)
    square = shape_of((own_rows, width), full_type)
    low_square = shape_of((own_rows, width))
    narrow = shape_of((own_rows, 1), full_type)
    normed_one, normed_low, unit_one, scale_one = whole_call(
        norm_one_kernel,
        [square, low_square, square, narrow],
        "norm_one",
        own_hidden,
        *terms,
        norm_rows,
    )

    units = w_up.shape[1]
    rows_one = rows_gather(normed_low)
    full_up = pack_u.value().reshape(width, -1)
    col_own = full_up[:, units:]
    (full_up, col_own), rows_one = tie((full_up, col_own), rows_one)
    far_col = swap(col_own, "mp", 2)
    active, slope = feed_up(rows_one, full_up, units)
    main = pack_d.drain((active, slope))
    full_down = to_lanes(pack_d.value())
    full_down, (active, slope) = tie(full_down, main)
    keep, send = feed_down(active, full_down)
    far_col, (keep, send) = tie(far_col, (keep, send))
    terms = rows_scatter(keep, send)
    col_blocks = [col_own, far_col]
    col_blocks = col_blocks + [swap(each, "mp", 1) for each in col_blocks]
    normed_two_low, unit_two, scale_two, embedded, embed_low, inv_length = ordered_call(
        norm_two_kernel,
        [low_square, square, narrow, square, low_square, narrow],
        [],
        "norm_two",
        col_order,
        normed_one,
        *terms,
        norm_rows,
        *col_blocks,
    )

    e_blocks = rows_gather(embed_low)
    sharp, soft_block = late_forward(e_blocks, queries, live_bias, blocks)
    two_blocks, soft_block = tie(normed_two_low, soft_block)
    soft_group = group_gather(soft_block[None])
    terms = jnp.where(same[:, None, :, None], soft_group[None], neg_big)
    top = jnp.max(terms, axis=(1, 2))
    soft = top + jnp.log(jnp.sum(jnp.exp(terms - top[:, None, None]), axis=(1, 2)))
    two_blocks = rows_gather(two_blocks)
    far = group_gather(jnp.stack([attended]))[1:]
    far_lse = group_gather(lse[None])[1:]
    keep, send = late_backward(sharp, soft, weight, queries)
    (far, far_lse, two_blocks), (keep, send) = tie((far, far_lse, two_blocks), (keep, send))
    far_attended = far.reshape(-1, head_width)
    far_lse = jnp.swapaxes(far_lse, 0, 1).reshape(8, -1)

    query_means = jnp.mean(soft.reshape(blocks, -1, QLEN), axis=2) * 0.5
    shared = jnp.sum(same.astype(full_type), axis=1)
    scores = jnp.sum(query_means[:, :, None] * (place / shared[:, None])[:, None, :], axis=0)
    scores, keep = tie(scores, keep)

    terms = rows_scatter(keep, send)
    dproj_low, dresid_two, dresid_low, two_sums = ordered_call(
        norm_two_back_kernel,
        [low_square, square, low_square, shape_of((2, width), full_type)],
        [],
        "norm_two_back",
        col_order,
        *terms,
        norm_rows,
        unit_two,
        scale_two,
        embedded,
        inv_length,
        *col_blocks,
    )
    dresid_blocks = rows_gather(dresid_low)

    dproj_low, dresid_blocks = tie(dproj_low, dresid_blocks)
    du_far = swap(dproj_low, "mp", 2)
    if group_size < dp_size:
        masks = dp_up[group_levels:]
        scores = scores + swap(scores, "dp", masks[0])
    dinner = feed_inner(dresid_blocks, full_down, slope)
    (scores, keep_up), dinner = tie((scores, full_up), dinner)
    for mask in masks[1:]:
        scores = scores + swap(scores, "dp", mask)
    keep, send = feed_back(dinner, keep_up)
    got = swap(send, "mp", 1)
    du_blocks = [dproj_low, du_far]
    du_blocks = du_blocks + [swap(each, "mp", 1) for each in du_blocks]
    terms = [keep, got]
    low = rows_fold(*terms)
    (scores, active, dinner), low = tie((scores, active, dinner), low)
    far_low = swap(low, "mp", 2)
    grad_d = Scatter(*grad_down(active, dresid_blocks, across_back), "dp", across_back)
    dinner = grad_d.start(dinner)
    grad_u = Scatter(
        *grad_up(dinner, rows_one, two_blocks, du_blocks, w_colbert.shape[1], dp_up), "dp", dp_up
    )
    far_low = grad_u.start(far_low)
    dresid_one, mixed_pack = whole_call(
        norm_one_back_kernel,
        [square, shape_of((own_rows + SPARE, width))],
        "norm_one_back",
        dresid_two,
        *terms,
        far_low,
        norm_rows,
        unit_one,
        scale_one,
        two_sums,
    )
    packs = rows_gather(mixed_pack)

    dattended, norm_sums = whole_call(
        unmix_kernel,
        [shape_of((tok_rows, head_width)), shape_of((SPARE, width))],
        "unmix",
        *packs,
        full_out,
    )
    far_grads = group_gather(dattended[None])[1:].reshape(-1, head_width)
    main = grad_d.step(dattended)
    dquery, dkey, dvalue = attend_own(
        query_key, value_rows, main, attended, seg_column, slot_row, lse
    )
    far_grads, dquery = tie(far_grads, dquery)
    main = (far_grads, dquery)
    main = grad_u.step(main)
    main = grad_d.step(main)
    far_grads, dquery = main
    dqk, dvalue_low = attend_other(
        query_key,
        value_rows,
        far_grads,
        far_attended,
        seg_far,
        slot_own[None, :],
        far_lse,
        dquery,
        dkey,
        dvalue,
    )
    main = grad_d.finish((dqk, dvalue_low))
    main = grad_u.step(main)
    dqk, dvalue_low = main
    grad_b = Scatter(
        *grad_vo(hidden_own, dvalue_low, attended, packs, norm_sums, turned_back), "dp", turned_back
    )
    dqk = grad_b.start(dqk)
    grad_a = Scatter(*grad_qk(hidden_own, dqk, dp_up), "dp", dp_up)
    dqk = grad_a.start(dqk)
    keep, send = unproject(dqk, dvalue_low, full_a, full_b)
    terms = rows_scatter(keep, send)
    terms = grad_a.step(terms)
    terms = grad_b.step(terms)
    input_own = whole_call(close_kernel, [low_square], "close", dresid_one, *terms)[0]
    input_own = grad_u.finish(input_own)
    input_blocks = rows_gather(input_own)
    input_blocks = grad_a.step(input_blocks)
    input_grad = place_rows(col_order, input_blocks)
    input_grad = grad_b.step(input_grad)
    input_grad = grad_b.drain(grad_a.drain(input_grad))

    grad_qk_rows = grad_a.value()
    value_grad, out_rows = unpack_vo(grad_b.value(), w_value.shape[0], head_width, out_shape)
    norm_grads = out_rows[head_width : head_width + 4] + out_rows[head_width + 4 : head_width + 8]
    up_rows = grad_u.value()
    return (
        scores,
        input_grad,
        grad_qk_rows[:, :head_width],
        grad_qk_rows[:, head_width:],
        value_grad,
        out_rows[:head_width],
        up_rows[:, :units],
        grad_d.value(),
        up_rows[:, units:],
        norm_grads[0],
        norm_grads[1],
        norm_grads[2],
        norm_grads[3],
    )


def solution(mesh):
    rows, both, across = P("dp", None), P("dp", "mp"), P("mp", "dp")
    return jax.shard_map(
        body,
        mesh=mesh,
        in_specs=(
            (rows, both, both, both, across, both, across, both)
            + (P("dp"),) * 4
            + (P("mp", None), P(), P(), P("mp", None))
        ),
        out_specs=(
            (P("mp", None), rows, both, both, both, across, both, across, both)
            + (P("dp"),) * 4
        ),
        check_vma=False,
    )
```

```python
import jax
import jax.numpy as jnp
from jax import lax
from jax.experimental import pallas as pl
from jax.experimental.pallas import tpu as pltpu
from jax.sharding import PartitionSpec as P

HEAD_DIM = 64
QLEN = 32
NBUCKET = 4
NPASS = 15
LANES = 128
SPARE = 16

neg_big = -1e30
low_type = jnp.bfloat16
full_type = jnp.float32
contract_rows = (((0,), (0,)), ((), ()))
contract_cols = (((1,), (1,)), ((), ()))
contract_inner = (((1,), (0,)), ((), ()))


def room(mebibytes):
    return pltpu.CompilerParams(vmem_limit_bytes=mebibytes * 1024 * 1024)


def room_for_keys(keys):
    return room(min(56, 4 + keys // 128))


brief = pl.CostEstimate(flops=1, bytes_accessed=1, transcendentals=0)


def low_dot(left, right, dims=contract_inner):
    return lax.dot_general(left, right, dims, preferred_element_type=full_type)


def shape_of(shape, dtype=low_type):
    return jax.ShapeDtypeStruct(shape, dtype)


def whole_block(shape):
    return pl.BlockSpec(shape, lambda i: (0,) * len(shape))


def whole_call(kernel, outs, name, *args):
    return pl.pallas_call(
        kernel,
        grid=(1,),
        in_specs=[whole_block(each.shape) for each in args],
        out_specs=[whole_block(each.shape) for each in outs],
        out_shape=outs,
        compiler_params=room(12),
        cost_estimate=brief,
        name=name,
    )(*args)


def swap(value, axis, mask):
    pairs = [(source, source ^ mask) for source in range(lax.axis_size(axis))]
    return lax.ppermute(value, axis, pairs)


def bits_of(axis):
    return lax.axis_size(axis).bit_length() - 1


def has_bit(axis, mask):
    return lax.axis_index(axis) // mask % 2 == 1


def upward(axis):
    return [2**level for level in range(bits_of(axis))]


def downward(axis):
    return upward(axis)[::-1]


def offsets_of(masks):
    order = [0]
    for mask in masks:
        order = order + [at ^ mask for at in order]
    return order


def arrange(blocks, axis, masks):
    levels = bits_of(axis)
    cube = blocks.reshape((2,) * levels + blocks.shape[1:])
    for mask in masks:
        at = levels - mask.bit_length()
        cube = jnp.where(has_bit(axis, mask), jnp.flip(cube, at), cube)
    front = [levels - mask.bit_length() for mask in masks]
    cube = jnp.transpose(cube, front + list(range(levels, cube.ndim)))
    return cube.reshape(blocks.shape)


def tie(*values):
    return lax.optimization_barrier(values)


class Gather:
    def __init__(self, value, axis, masks):
        self.axis, self.masks = axis, list(masks)
        self.levels, self.shape = bits_of(axis), value.shape
        self.whole = value.reshape((1,) * self.levels + value.shape)

    def start(self, main):
        if self.masks:
            self.whole, main = tie(self.whole, main)
            self.other = swap(self.whole, self.axis, self.masks[0])
        return main

    def finish(self, main):
        if self.masks:
            mask = self.masks.pop(0)
            other, main = tie(self.other, main)
            at = self.levels - mask.bit_length()
            self.whole = jnp.where(
                has_bit(self.axis, mask),
                jnp.concatenate([other, self.whole], at),
                jnp.concatenate([self.whole, other], at),
            )
        return main

    def step(self, main):
        return self.start(self.finish(main))

    def drain(self, main):
        main = self.finish(main)
        while self.masks:
            main = self.finish(self.start(main))
        return main

    def value(self):
        return self.whole.reshape((-1,) + self.shape)


class Scatter:
    def __init__(self, keep, send, axis, masks):
        self.axis, self.masks = axis, list(masks)
        self.keep, self.send = keep, send

    def start(self, main):
        if self.masks:
            self.send, main = tie(self.send, main)
            self.other = swap(self.send, self.axis, self.masks[0])
        return main

    def finish(self, main):
        if self.masks:
            self.masks.pop(0)
            other, main = tie(self.other, main)
            if self.masks:
                self.keep, self.send = halve(self.keep, other)
            else:
                self.other = other
        return main

    def step(self, main):
        return self.start(self.finish(main))

    def drain(self, main):
        main = self.finish(main)
        while self.masks:
            main = self.finish(self.start(main))
        return main

    def value(self):
        return self.keep[0].astype(full_type) + self.other[0].astype(full_type)


def halve_kernel(keep_low, keep_high, other_low, other_high, low_ref, high_ref):
    for keep, other, out in (
        (keep_low, other_low, low_ref),
        (keep_high, other_high, high_ref),
    ):
        total = keep[...].astype(full_type) + other[...].astype(full_type)
        out[...] = total.astype(low_type)


def halve(keep, other):
    half = keep.shape[0] // 2
    block = (1,) + keep.shape[1:]
    low = pl.BlockSpec(block, lambda i: (i, 0, 0))
    high = pl.BlockSpec(block, lambda i: (half + i, 0, 0))
    return pl.pallas_call(
        halve_kernel,
        grid=(half,),
        in_specs=[low, high, low, high],
        out_specs=[low, low],
        out_shape=[shape_of((half,) + keep.shape[1:])] * 2,
        compiler_params=room(8),
        cost_estimate=brief,
        name="halve",
    )(keep, keep, other, other)


def rows_gather(block):
    blocks = [block]
    for mask in downward("mp"):
        blocks = blocks + [swap(each, "mp", mask) for each in blocks]
    return blocks


def rows_scatter(keep, send, main=None, between=None):
    masks = upward("mp")
    terms = [keep, swap(send, "mp", masks[0])]
    for mask in masks[1:]:
        terms = terms + [swap(rows_fold(*terms), "mp", mask)]
    return terms


def add_up(refs):
    rows = refs[-1].shape[0]
    total = refs[0][0:rows, :].astype(full_type)
    for ref in refs[1:]:
        total = total + ref[0:rows, :].astype(full_type)
    return total


def head_mask(width, head):
    lane = lax.broadcasted_iota(jnp.int32, (1, width), 1)
    return lane // HEAD_DIM == head


def only_head(rows, head):
    return jnp.where(head_mask(rows.shape[1], head), rows, jnp.zeros_like(rows))


def attend_forward_kernel(q_ref, k_ref, v_ref, segq_ref, segk_ref, o_ref, stat_ref):
    tile, width = q_ref.shape
    bias = jnp.where(segq_ref[...] == segk_ref[...], 0.0, neg_big)
    out = jnp.zeros((tile, width), full_type)
    stat = jnp.zeros((tile, LANES), full_type)
    lane = lax.broadcasted_iota(jnp.int32, (1, LANES), 1)
    queries = q_ref[...] * jnp.asarray(0.125, low_type)
    for head in range(width // HEAD_DIM):
        raw = low_dot(only_head(queries, head), k_ref[...], contract_cols) + bias
        top = jnp.max(raw, axis=1, keepdims=True)
        terms = jnp.exp(raw - top)
        total = jnp.sum(terms, axis=1, keepdims=True)
        mixed = low_dot(terms.astype(low_type), v_ref[...]) * (1.0 / total)
        out = jnp.where(head_mask(width, head), mixed, out)
        stat = jnp.where(lane == head, top + jnp.log(total), stat)
    o_ref[...] = out.astype(low_type)
    stat_ref[...] = stat.T[: stat_ref.shape[0]]


def attend_forward(query_key, value_rows, seg_rows, seg_keys):
    rows = seg_rows.shape[0]
    keys, width = value_rows.shape
    tile = LANES
    return pl.pallas_call(
        attend_forward_kernel,
        grid=(rows // tile,),
        in_specs=[
            pl.BlockSpec((tile, width), lambda i: (i, 0)),
            pl.BlockSpec((keys, width), lambda i: (0, 1)),
            pl.BlockSpec((keys, width), lambda i: (0, 0)),
            pl.BlockSpec((tile, 1), lambda i: (i, 0)),
            pl.BlockSpec((1, keys), lambda i: (0, 0)),
        ],
        out_specs=[
            pl.BlockSpec((tile, width), lambda i: (i, 0)),
            pl.BlockSpec((8, tile), lambda i: (0, i)),
        ],
        out_shape=[shape_of((rows, width)), shape_of((8, rows), full_type)],
        compiler_params=room_for_keys(keys),
        cost_estimate=brief,
        name="attend_forward",
    )(query_key, query_key, value_rows, seg_rows, seg_keys)


def attend_terms(q_ref, k_ref, v_ref, do_ref, o_ref, segq_ref, segk_ref, lse_ref):
    tile, width = q_ref.shape
    bias = jnp.where(segq_ref[...] == segk_ref[...], 0.0, neg_big)
    pad = jnp.zeros((LANES - lse_ref.shape[0], tile), full_type)
    lse = jnp.concatenate([lse_ref[...], pad], 0).T
    queries = q_ref[...] * jnp.asarray(0.125, low_type)
    grads = do_ref[...]
    both = grads.astype(full_type) * o_ref[...].astype(full_type)
    for head in range(width // HEAD_DIM):
        q_head = only_head(queries, head)
        g_head = only_head(grads, head)
        delta = jnp.sum(only_head(both, head), axis=1, keepdims=True)
        raw = low_dot(q_head, k_ref[...], contract_cols)
        probs = jnp.exp(raw + (bias - lse[:, head : head + 1]))
        dprobs = low_dot(g_head, v_ref[...], contract_cols)
        dscore = (probs * (dprobs - delta)).astype(low_type)
        yield head, q_head, g_head, probs.astype(low_type), dscore


def attend_back(rows_of_q, part, keys, masks, sums, wants_dq, dq_parts=()):
    query_key, first_row, grads, attended, lse, seg_rows = rows_of_q
    value_rows, seg_keys, own = masks
    width = value_rows.shape[1]
    tile = LANES
    parts_of = 1 if part is None else 2
    steps = grads.shape[0] // tile // parts_of
    shift = steps if part == 1 else 0
    first = first_row // tile + shift
    closing = len(dq_parts) > 0

    def kernel(*refs):
        base, refs = refs[:8], refs[8:]
        q_ref, k_ref = base[:2]
        before, refs = (refs[:2], refs[2:]) if sums else (None, refs)
        parts, refs = refs[: len(dq_parts)], refs[len(dq_parts) :]
        if closing:
            dqk_out, dv_out, dk_sum, dv_sum = refs
        else:
            dk_sum, dv_sum = refs[:2]
        step = pl.program_id(0)

        @pl.when(step == 0)
        def _():
            dk_sum[...] = before[0][...] if sums else jnp.zeros_like(dk_sum)
            dv_sum[...] = before[1][...] if sums else jnp.zeros_like(dv_sum)

        dquery = jnp.zeros((tile, width), full_type)
        for head, q_head, g_head, probs, dscore in attend_terms(*base):
            if wants_dq:
                dquery = jnp.where(head_mask(width, head), low_dot(dscore, k_ref[...]), dquery)
            dk_sum[...] += low_dot(dscore[:, :own], q_head, contract_rows)
            dv_sum[...] += low_dot(probs[:, :own], g_head, contract_rows)
        if wants_dq:
            refs[2][...] = (dquery * 0.125).astype(low_type)
        if closing:

            @pl.when(step == steps - 1)
            def _():
                rows = own // len(parts)
                for at, ref in enumerate(parts):
                    dqk_out[at * rows : (at + 1) * rows, :width] = ref[...]
                dqk_out[:, width:] = dk_sum[...].astype(low_type)
                dv_out[...] = dv_sum[...].astype(low_type)

    tile_rows = pl.BlockSpec((tile, width), lambda i: (shift + i, 0))
    held = whole_block((own, width))
    in_specs = [
        pl.BlockSpec((tile, width), lambda i: (first + i, 0)),
        pl.BlockSpec((keys, width), lambda i: (0, 1)),
        pl.BlockSpec((keys, width), lambda i: (0, 0)),
        tile_rows,
        tile_rows,
        pl.BlockSpec((tile, 1), lambda i: (shift + i, 0)),
        pl.BlockSpec((1, keys), lambda i: (0, 0)),
        pl.BlockSpec((8, tile), lambda i: (0, shift + i)),
    ]
    args = [query_key, query_key, value_rows, grads, attended, seg_rows, seg_keys, lse]
    if sums:
        in_specs, args = in_specs + [held, held], args + list(sums)
    in_specs = in_specs + [whole_block(each.shape) for each in dq_parts]
    args = args + list(dq_parts)
    if closing:
        outs = [shape_of((own, 2 * width)), shape_of((own, width))]
        out_specs = [whole_block(each.shape) for each in outs]
        scratch = [pltpu.VMEM((own, width), full_type)] * 2
    else:
        outs = [shape_of((own, width), full_type)] * 2
        out_specs, scratch = [held, held], []
        if wants_dq:
            outs = outs + [shape_of((steps * tile, width))]
            out_specs = out_specs + [pl.BlockSpec((tile, width), lambda i: (i, 0))]
    return pl.pallas_call(
        kernel,
        grid=(steps,),
        in_specs=in_specs,
        out_specs=out_specs,
        out_shape=outs,
        scratch_shapes=scratch,
        compiler_params=room_for_keys(keys),
        cost_estimate=brief,
        name="attend_back",
    )(*args)


def lanes_of(ref):
    return jnp.concatenate([ref[at] for at in range(ref.shape[0])], axis=1)


def rows_of(refs):
    return jnp.concatenate([ref[...] for ref in refs], axis=0)


def feed_up_kernel(*refs):
    *row_refs, up_ref, g_ref, slope_ref = refs
    for at, ref in enumerate(row_refs):
        place = pl.ds(at * ref.shape[0], ref.shape[0])
        inner = low_dot(ref[...], up_ref[...])
        normal = 0.5 * (1.0 + lax.erf(inner * 0.7071067811865476))
        g_ref[place, :] = (inner * normal).astype(low_type)
        slope = normal + inner * jnp.exp(-0.5 * inner * inner) * 0.3989422804014327
        slope_ref[place, :] = slope.astype(low_type)


def feed_up(blocks, w_up, units):
    own, width = blocks[0].shape
    rows = own * len(blocks)
    tile = 256
    return pl.pallas_call(
        feed_up_kernel,
        grid=(units // tile,),
        in_specs=[pl.BlockSpec((own, width), lambda i: (0, 0))] * len(blocks)
        + [pl.BlockSpec((width, tile), lambda i: (0, i))],
        out_specs=[pl.BlockSpec((rows, tile), lambda i: (0, i))] * 2,
        out_shape=[shape_of((rows, units))] * 2,
        compiler_params=room(10),
        cost_estimate=brief,
        name="feed_up",
    )(*blocks, w_up)


def store_halves(total, keep_ref, send_ref):
    half = total.shape[0] // 2
    keep_ref[...] = total[:half]
    send_ref[...] = total[half:].astype(low_type)


def halves_of(rows, width):
    return [shape_of((rows // 2, width), full_type), shape_of((rows // 2, width))]


def feed_down_kernel(g_ref, down_ref, keep_ref, send_ref):
    store_halves(low_dot(g_ref[...], lanes_of(down_ref)), keep_ref, send_ref)


def feed_down(active, w_down):
    rows, units = active.shape
    blocks, _, lanes = w_down.shape
    tile = 2
    return pl.pallas_call(
        feed_down_kernel,
        grid=(blocks // tile,),
        in_specs=[
            pl.BlockSpec((rows, units), lambda i: (0, 0)),
            pl.BlockSpec((tile, units, lanes), lambda i: (i, 0, 0)),
        ],
        out_specs=[pl.BlockSpec((rows // 2, tile * lanes), lambda i: (0, i))] * 2,
        out_shape=halves_of(rows, blocks * lanes),
        compiler_params=room(10),
        cost_estimate=brief,
        name="feed_down",
    )(active, w_down)


def feed_inner_kernel(*refs):
    *row_refs, down_ref, slope_ref, dz_ref = refs
    weight = lanes_of(down_ref)
    for at, ref in enumerate(row_refs):
        place = pl.ds(at * ref.shape[0], ref.shape[0])
        dactive = low_dot(ref[...], weight, contract_cols)
        dz_ref[place, :] = (dactive * slope_ref[place, :].astype(full_type)).astype(low_type)


def feed_inner(blocks, w_down, slope):
    own, width = blocks[0].shape
    rows, units = slope.shape
    tile = 256
    lanes = w_down.shape[2]
    return pl.pallas_call(
        feed_inner_kernel,
        grid=(units // tile,),
        in_specs=[pl.BlockSpec((own, width), lambda i: (0, 0))] * len(blocks)
        + [
            pl.BlockSpec((w_down.shape[0], tile, lanes), lambda i: (0, i, 0)),
            pl.BlockSpec((rows, tile), lambda i: (0, i)),
        ],
        out_specs=pl.BlockSpec((rows, tile), lambda i: (0, i)),
        out_shape=shape_of((rows, units)),
        compiler_params=room(10),
        cost_estimate=brief,
        name="feed_inner",
    )(*blocks, w_down, slope)


def feed_back_kernel(dz_ref, up_ref, keep_ref, send_ref):
    store_halves(low_dot(dz_ref[...], up_ref[...], contract_cols), keep_ref, send_ref)


def feed_back(dinner, w_up):
    rows, units = dinner.shape
    width = w_up.shape[0]
    tile = 256
    return pl.pallas_call(
        feed_back_kernel,
        grid=(width // tile,),
        in_specs=[
            pl.BlockSpec((rows, units), lambda i: (0, 0)),
            pl.BlockSpec((tile, units), lambda i: (i, 0)),
        ],
        out_specs=[pl.BlockSpec((rows // 2, tile), lambda i: (0, i))] * 2,
        out_shape=halves_of(rows, width),
        compiler_params=room(10),
        cost_estimate=brief,
        name="feed_back",
    )(dinner, w_up)


def late_forward_kernel(*refs):
    *e_refs, q_ref, live_ref, sharp_ref, soft_ref = refs
    blocks = soft_ref.shape[0]
    per = blocks // len(e_refs)
    for at, e_ref in enumerate(e_refs):
        rows = e_ref.shape[0]
        place = pl.ds(at * rows, rows)
        sharp = low_dot(e_ref[...], q_ref[...], contract_cols) * 2.0 + live_ref[place, :]
        sharp_ref[place, :] = sharp
        cube = sharp.reshape(per, rows // per, sharp.shape[1])
        top = jnp.max(cube, axis=1)
        total = jnp.sum(jnp.exp(cube - top[:, None, :]), axis=1)
        soft = jnp.where(top > 0.5 * neg_big, top + jnp.log(total), neg_big)
        soft_ref[pl.ds(at * per, per), :] = soft


def late_forward(e_blocks, queries, live_bias, blocks):
    own, width = e_blocks[0].shape
    rows = own * len(e_blocks)
    count = queries.shape[0]
    tile = 512
    return pl.pallas_call(
        late_forward_kernel,
        grid=(count // tile,),
        in_specs=[pl.BlockSpec((own, width), lambda i: (0, 0))] * len(e_blocks)
        + [
            pl.BlockSpec((tile, width), lambda i: (i, 0)),
            pl.BlockSpec((rows, 1), lambda i: (0, 0)),
        ],
        out_specs=[
            pl.BlockSpec((rows, tile), lambda i: (0, i)),
            pl.BlockSpec((blocks, tile), lambda i: (0, i)),
        ],
        out_shape=[shape_of((rows, count), full_type), shape_of((blocks, count), full_type)],
        compiler_params=room(14),
        cost_estimate=brief,
        name="late_forward",
    )(*e_blocks, queries, live_bias)


def join_soft(soft, far, same):
    top = soft
    for at in range(far.shape[0]):
        top = jnp.maximum(top, far[at])
    total = jnp.exp(soft - top)
    for at in range(far.shape[0]):
        total = total + jnp.exp(far[at] - top)
    blocks = soft.shape[0]
    most = jnp.full(soft.shape, neg_big, full_type)
    for at in range(blocks):
        shared = same[:, at : at + 1] > 0.0
        most = jnp.maximum(most, jnp.where(shared, top[at : at + 1], neg_big))
    sums = jnp.zeros(soft.shape, full_type)
    for at in range(blocks):
        shared = same[:, at : at + 1] > 0.0
        term = jnp.where(shared, top[at : at + 1], neg_big)
        sums = sums + jnp.exp(term - most) * total[at : at + 1]
    return most + jnp.log(sums)


def late_backward_kernel(
    sharp_ref, soft_ref, far_ref, same_ref, place_ref, weight_ref, q_ref, *refs
):
    keep_ref, send_ref, score_ref, total = refs
    step = pl.program_id(0)
    blocks = soft_ref.shape[0]
    rows, tile = sharp_ref.shape
    soft = join_soft(soft_ref[...], far_ref[...], same_ref[...])
    cube = sharp_ref[...].reshape(blocks, rows // blocks, tile)
    pulled = weight_ref[...][:, None, :] * jnp.exp(cube - soft[:, None, :])
    term = low_dot(pulled.reshape(rows, tile).astype(low_type), q_ref[...])
    query = lax.broadcasted_iota(jnp.int32, (tile, score_ref.shape[0]), 0) // QLEN
    count = lax.broadcasted_iota(jnp.int32, (tile, score_ref.shape[0]), 1)
    pool = jnp.where(query == count, 0.5 / QLEN, 0.0)
    exact = lax.Precision.HIGHEST
    means = lax.dot_general(pool, soft, (((0,), (1,)), ((), ())), precision=exact)
    score_ref[...] = lax.dot_general(means, place_ref[...], contract_inner, precision=exact)

    @pl.when(step == 0)
    def _():
        total[...] = term

    @pl.when(step > 0)
    def _():
        total[...] += term

    @pl.when(step == pl.num_programs(0) - 1)
    def _():
        store_halves(total[...], keep_ref, send_ref)


def late_backward(sharp, soft, far, same, place, weight, queries):
    rows, count = sharp.shape
    width = queries.shape[1]
    blocks = soft.shape[0]
    tile = 512
    held = whole_block((rows // 2, width))
    return pl.pallas_call(
        late_backward_kernel,
        grid=(count // tile,),
        in_specs=[
            pl.BlockSpec((rows, tile), lambda i: (0, i)),
            pl.BlockSpec((blocks, tile), lambda i: (0, i)),
            pl.BlockSpec((far.shape[0], blocks, tile), lambda i: (0, 0, i)),
            whole_block(same.shape),
            whole_block(place.shape),
            pl.BlockSpec((blocks, tile), lambda i: (0, i)),
            pl.BlockSpec((tile, width), lambda i: (i, 0)),
        ],
        out_specs=[held, held, pl.BlockSpec((tile // QLEN, NPASS), lambda i: (i, 0))],
        out_shape=halves_of(rows, width) + [shape_of((count // QLEN, NPASS), full_type)],
        scratch_shapes=[pltpu.VMEM((rows, width), full_type)],
        compiler_params=room(16),
        cost_estimate=brief,
        name="late_backward",
    )(sharp, soft, far, same, place, weight, queries)


def norm_stats(values):
    centre = values - jnp.mean(values, axis=-1, keepdims=True)
    spread = jnp.mean(centre * centre, axis=-1, keepdims=True)
    scale = lax.rsqrt(spread + 1e-05)
    return centre * scale, scale


def norm_backward(unit, scale, gain, grad):
    dunit = grad * gain
    dvalues = scale * (
        dunit
        - jnp.mean(dunit, axis=-1, keepdims=True)
        - unit * jnp.mean(dunit * unit, axis=-1, keepdims=True)
    )
    return (
        dvalues,
        jnp.sum(grad * unit, axis=0, keepdims=True),
        jnp.sum(grad, axis=0, keepdims=True),
    )


def norm_one_kernel(*refs):
    *terms, norm_ref, h_ref, low_ref, unit_ref, scale_ref = refs
    unit, scale = norm_stats(add_up(terms))
    normed = unit * norm_ref[0:1] + norm_ref[1:2]
    h_ref[...] = normed
    low_ref[...] = normed.astype(low_type)
    unit_ref[...] = unit
    scale_ref[...] = scale


def lanes_at(order_ref, at, span):
    return pl.ds(pl.multiple_of(order_ref[at] * span, span), span)


def norm_two_kernel(order_ref, *refs):
    *rest, low_ref, unit_ref, scale_ref, e_ref, elow_ref, inv_ref = refs
    parts = order_ref.shape[0]
    *terms, norm_ref = rest[:-parts]
    col_refs = rest[-parts:]
    unit, scale = norm_stats(add_up(terms))
    normed_low = (unit * norm_ref[2:3] + norm_ref[3:4]).astype(low_type)
    low_ref[...] = normed_low
    unit_ref[...] = unit
    scale_ref[...] = scale
    span = col_refs[0].shape[1]
    squares = 0.0
    for at, ref in enumerate(col_refs):
        projected = low_dot(normed_low, ref[...])
        e_ref[:, lanes_at(order_ref, at, span)] = projected
        squares = squares + jnp.sum(projected * projected, axis=-1, keepdims=True)
    inv = lax.rsqrt(squares + 1e-06)
    embedded = e_ref[...] * inv
    e_ref[...] = embedded
    elow_ref[...] = embedded.astype(low_type)
    inv_ref[...] = inv


def norm_two_back_kernel(order_ref, *refs):
    *rest, du_ref, dr_ref, low_ref, g_ref = refs
    parts = order_ref.shape[0]
    *terms, norm_ref, unit_ref, scale_ref, e_ref, inv_ref = rest[:-parts]
    col_refs = rest[-parts:]
    dembed = add_up(terms)
    embedded = e_ref[...]
    along = jnp.sum(embedded * dembed, axis=-1, keepdims=True)
    du_ref[...] = (inv_ref[...] * (dembed - embedded * along)).astype(low_type)
    span = col_refs[0].shape[1]
    dnormed = 0.0
    for at, ref in enumerate(col_refs):
        dproj = du_ref[:, lanes_at(order_ref, at, span)]
        dnormed = dnormed + low_dot(dproj, ref[...], contract_cols)
    dresid, dgain, dshift = norm_backward(
        unit_ref[...], scale_ref[...], norm_ref[2:3], dnormed
    )
    dr_ref[...] = dresid
    low_ref[...] = dresid.astype(low_type)
    g_ref[...] = jnp.concatenate([dgain, dshift], 0)


def split_sums(sums):
    high = sums.astype(low_type).astype(full_type)
    zeros = jnp.zeros((SPARE - 8, sums.shape[1]), full_type)
    return jnp.concatenate([high, sums - high, zeros], 0).astype(low_type)


def norm_one_back_kernel(*refs):
    *terms, norm_ref, unit_ref, scale_ref, two_ref, dr_ref, pack_ref = refs
    dresid, dgain, dshift = norm_backward(
        unit_ref[...], scale_ref[...], norm_ref[0:1], add_up(terms)
    )
    dr_ref[...] = dresid
    rows = dresid.shape[0]
    pack_ref[0:rows, :] = dresid.astype(low_type)
    pack_ref[rows : rows + SPARE, :] = split_sums(
        jnp.concatenate([dgain, dshift, two_ref[...]], 0)
    )


def fold_kernel(keep_ref, got_ref, low_ref):
    half = low_ref.shape[0]
    total = keep_ref[half:, :] + got_ref[half:, :].astype(full_type)
    low_ref[...] = total.astype(low_type)


def rows_fold(keep, got):
    return whole_call(fold_kernel, [shape_of((got.shape[0] // 2, got.shape[1]))], "fold", keep, got)[0]


def mix_kernel(o_ref, out_ref, keep_ref, send_ref):
    rows = o_ref.shape[1]
    weight = jnp.concatenate([out_ref[at, 0:rows, :] for at in range(out_ref.shape[0])], axis=1)
    store_halves(low_dot(o_ref[...], weight), keep_ref, send_ref)


def unmix_kernel(*refs):
    *packs, out_ref, do_ref, sums_ref = refs
    rows = do_ref.shape[1]
    weight = jnp.concatenate([out_ref[at, 0:rows, :] for at in range(out_ref.shape[0])], axis=1)
    own = packs[0].shape[0] - SPARE
    sums = jnp.zeros((8, weight.shape[1]), full_type)
    for at, ref in enumerate(packs):
        do = low_dot(ref[0:own, :], weight, contract_cols)
        do_ref[at * own : (at + 1) * own, :] = do.astype(low_type)
        sums = sums + ref[own : own + SPARE, :].astype(full_type)[:8]
    sums_ref[...] = split_sums(sums[:4] + sums[4:])


def block_order(masks):
    return lax.axis_index("dp") ^ jnp.asarray(offsets_of(masks[::-1]), jnp.int32)


def ordered_call(kernel, outs, scratch, name, order, *args, grant=20):
    return pl.pallas_call(
        kernel,
        grid=(1,),
        in_specs=[pl.BlockSpec(memory_space=pltpu.SMEM)]
        + [whole_block(each.shape) for each in args],
        out_specs=[whole_block(each.shape) for each in outs],
        out_shape=outs,
        scratch_shapes=[pltpu.VMEM(*each) for each in scratch],
        compiler_params=room(grant),
        cost_estimate=brief,
        name=name,
    )(order, *args)


def stored(place_ref, left, right):
    turned = left.T
    cols = right.shape[1]
    for start in range(0, cols, 256):
        stop = min(start + 256, cols)
        place_ref[:, start:stop] = low_dot(turned, right[:, start:stop]).astype(low_type)


def deal(order_ref, keep_ref, send_ref, write):
    half = keep_ref.shape[0]
    for at in range(2 * half):
        write(keep_ref.at[at] if at < half else send_ref.at[at - half], order_ref[at])


def rows_in(ref, block, count):
    return ref[pl.ds(pl.multiple_of(block * count, count), count), :]


def lanes_in(ref, block):
    return ref[:, pl.ds(pl.multiple_of(block * LANES, LANES), LANES)]


def halves_like(count, block):
    return [shape_of((count // 2,) + block)] * 2


def grad_down_kernel(order_ref, active_ref, *refs):
    *row_refs, keep_ref, send_ref, total = refs
    stored(total, active_ref[...], rows_of(row_refs))

    def write(ref, block):
        ref[...] = lanes_in(total, block)

    deal(order_ref, keep_ref, send_ref, write)


def grad_down(active, row_blocks, masks):
    count = lax.axis_size("dp")
    units, width = active.shape[1], row_blocks[0].shape[1]
    if width // count == LANES:
        return ordered_call(
            grad_down_kernel,
            halves_like(count, (units, LANES)),
            [((units, width), low_type)],
            "grad_down",
            block_order(masks),
            active,
            *row_blocks,
        )
    whole = low_dot(active, jnp.concatenate(row_blocks, 0), contract_rows).astype(low_type)
    return halves(arrange(jnp.swapaxes(whole.reshape(units, count, -1), 0, 1), "dp", masks))


def halves(blocks):
    half = blocks.shape[0] // 2
    return blocks[:half], blocks[half:]


def grad_up_kernel(order_ref, dinner_ref, *refs):
    *row_refs, keep_ref, send_ref, total = refs
    parts = len(row_refs) // 3
    units = dinner_ref.shape[1]
    block_rows = keep_ref.shape[1]
    cols = keep_ref.shape[2] - units
    stored(total.at[:, 0:units], rows_of(row_refs[:parts]), dinner_ref[...])
    mine = pl.ds(pl.multiple_of(order_ref[order_ref.shape[0] - 1] * cols, cols), cols)
    dproj = jnp.concatenate([ref[:, mine] for ref in row_refs[2 * parts :]], axis=0)
    stored(total.at[:, units:], rows_of(row_refs[parts : 2 * parts]), dproj)

    def write(ref, block):
        ref[...] = rows_in(total, block, block_rows)

    deal(order_ref, keep_ref, send_ref, write)


def grad_up(dinner, one_blocks, two_blocks, du_blocks, col_width, masks):
    count = lax.axis_size("dp")
    units, width = dinner.shape[1], one_blocks[0].shape[1]
    column = lax.axis_index("mp")
    rows = width // count
    if rows == LANES:
        order = jnp.concatenate([block_order(masks), column.reshape(1)])
        return ordered_call(
            grad_up_kernel,
            halves_like(count, (rows, units + col_width)),
            [((width, units + col_width), low_type)],
            "grad_up",
            order,
            dinner,
            *one_blocks,
            *two_blocks,
            *du_blocks,
        )
    dproj = lax.dynamic_slice_in_dim(
        jnp.concatenate(du_blocks, 0), column * col_width, col_width, 1
    )
    up = low_dot(jnp.concatenate(one_blocks, 0), dinner, contract_rows)
    col = low_dot(jnp.concatenate(two_blocks, 0), dproj, contract_rows)
    whole = jnp.concatenate([up, col], 1).astype(low_type)
    return halves(arrange(whole.reshape(count, rows, -1), "dp", masks))


def grad_qk_kernel(order_ref, left_ref, right_ref, keep_ref, send_ref, total):
    block_rows = keep_ref.shape[1]
    stored(total, left_ref[...], right_ref[...])

    def write(ref, block):
        ref[...] = rows_in(total, block, block_rows)

    deal(order_ref, keep_ref, send_ref, write)


def grad_qk(left, right, masks):
    count = lax.axis_size("dp")
    width, cols = left.shape[1], right.shape[1]
    rows = width // count
    if rows == LANES:
        return ordered_call(
            grad_qk_kernel,
            halves_like(count, (rows, cols)),
            [((width, cols), low_type)],
            "grad_qk",
            block_order(masks),
            left,
            right,
        )
    whole = low_dot(left, right, contract_rows).astype(low_type)
    return halves(arrange(whole.reshape(count, rows, cols), "dp", masks))


def grad_vo_kernel(order_ref, hidden_ref, dv_ref, o_ref, *refs):
    *packs, sums_ref, keep_ref, send_ref, total_v, total_o = refs
    rows = packs[0].shape[0] - SPARE
    cols = dv_ref.shape[1]
    heads = o_ref.shape[1]
    stored(total_v, hidden_ref[...], dv_ref[...])
    mixed = jnp.concatenate([ref[0:rows, :] for ref in packs], axis=0)
    stored(total_o.at[0:heads, :], o_ref[...], mixed)
    total_o[heads : heads + SPARE, :] = sums_ref[...]

    def write(ref, block):
        value = rows_in(total_v, block, LANES)
        for at in range(cols // LANES):
            ref[at * LANES : (at + 1) * LANES, :] = value[:, at * LANES : (at + 1) * LANES]
        ref[cols:, :] = lanes_in(total_o, block)

    deal(order_ref, keep_ref, send_ref, write)


def finish_pair_kernel(keep_ref, other_ref, left_ref, right_ref):
    total = keep_ref[...].astype(full_type) + other_ref[...].astype(full_type)
    cols = left_ref.shape[1]
    left_ref[...] = total[:, :cols]
    right_ref[...] = total[:, cols:]


def finish_pair(scatter, cols):
    rows, both = scatter.keep.shape[1:]
    outs = [shape_of((rows, cols), full_type), shape_of((rows, both - cols), full_type)]
    return whole_call(finish_pair_kernel, outs, "finish_pair", scatter.keep[0], scatter.other[0])


def finish_vo_kernel(keep_ref, other_ref, value_ref, out_ref, *norm_refs):
    total = keep_ref[...].astype(full_type) + other_ref[...].astype(full_type)
    rows, cols = value_ref.shape
    row = 0
    for at in range(0, cols, LANES):
        value_ref[:, at : at + LANES] = total[row : row + rows]
        row += rows
    out_ref[...] = total[row : row + out_ref.shape[0]]
    row += out_ref.shape[0]
    for at, ref in enumerate(norm_refs):
        ref[...] = total[row + at : row + at + 1] + total[row + 4 + at : row + 5 + at]


def finish_vo(keep, other, value_shape, out_shape):
    rows, cols = out_shape
    if cols == LANES:
        outs = [shape_of(value_shape, full_type), shape_of(out_shape, full_type)]
        outs = outs + [shape_of((1, cols), full_type)] * 4
        value, out, *norms = whole_call(finish_vo_kernel, outs, "finish_vo", keep, other)
        return value, out, norms
    total = keep.astype(full_type) + other.astype(full_type)
    value, out = unpack_vo(total, *value_shape, (rows + SPARE, cols))
    return value, out[:rows], out[rows : rows + 4] + out[rows + 4 : rows + 8]


def pack_vo(value, out):
    cols = value.shape[-1]
    parts = [value[..., at : at + LANES] for at in range(0, cols, LANES)]
    return jnp.concatenate(parts + [out.reshape(out.shape[:-2] + (-1, LANES))], axis=-2)


def unpack_vo(packed, rows, cols, out_shape):
    high = rows * cols // LANES
    value = jnp.concatenate(
        [packed[..., at : at + rows, :] for at in range(0, high, rows)], axis=-1
    )
    return value, packed[..., high:, :].reshape(packed.shape[:-2] + out_shape)


def grad_vo(hidden, dvalue, attended, packs, sums, masks):
    count = lax.axis_size("dp")
    width, cols = hidden.shape[1], dvalue.shape[1]
    heads = attended.shape[1]
    rows = width // count
    if rows == LANES:
        block = (cols * rows // LANES + heads + SPARE, LANES)
        return ordered_call(
            grad_vo_kernel,
            halves_like(count, block),
            [((width, cols), low_type), ((heads + SPARE, width), low_type)],
            "grad_vo",
            block_order(masks),
            hidden,
            dvalue,
            attended,
            *packs,
            sums,
        )
    value = low_dot(hidden, dvalue, contract_rows).astype(low_type).reshape(count, rows, cols)
    mixed = jnp.concatenate([each[:-SPARE] for each in packs], 0)
    out = low_dot(attended, mixed, contract_rows).astype(low_type)
    out = jnp.concatenate([out, sums], 0).reshape(heads + SPARE, count, rows)
    return halves(arrange(pack_vo(value, jnp.swapaxes(out, 0, 1)), "dp", masks))


def to_lanes(blocks):
    if blocks.shape[2] == LANES:
        return blocks
    whole = jnp.swapaxes(blocks, 0, 1).reshape(blocks.shape[1], -1, LANES)
    return jnp.swapaxes(whole, 0, 1)


def place_kernel(at_ref, *refs):
    *blocks, out_ref = refs
    rows = blocks[0].shape[0]
    for at, ref in enumerate(blocks):
        start = pl.multiple_of(at_ref[at] * rows, rows)
        out_ref[pl.ds(start, rows), :] = ref[...].astype(full_type)


def place_rows(order, blocks):
    rows, width = blocks[0].shape
    outs = [shape_of((rows * len(blocks), width), full_type)]
    return ordered_call(place_kernel, outs, [], "place_rows", order, *blocks)[0]


def unproject_kernel(dqk_ref, dv_ref, a_ref, b_ref, keep_ref, send_ref):
    total = low_dot(dqk_ref[...], a_ref[...], contract_cols)
    store_halves(total + low_dot(dv_ref[...], b_ref[...], contract_cols), keep_ref, send_ref)


def unproject(dqk, dvalue, w_qk, w_v):
    outs = halves_of(dqk.shape[0], w_qk.shape[0])
    return whole_call(unproject_kernel, outs, "unproject", dqk, dvalue, w_qk, w_v)


def close_kernel(*refs):
    *terms, out_ref = refs
    out_ref[...] = add_up(terms).astype(low_type)


def pack_kernel(order_ref, *refs):
    hidden_ref, q_ref, k_ref, v_ref, o_ref, up_ref, col_ref, *norm_refs = refs[:11]
    a_out, u_out, b_out, own_out, block_out = refs[11:]
    heads, units = q_ref.shape[1], up_ref.shape[1]
    a_out[:, :heads] = q_ref[...]
    a_out[:, heads:] = k_ref[...]
    u_out[:, :units] = up_ref[...]
    u_out[:, units:] = col_ref[...]
    row = 0
    for at in range(0, heads, LANES):
        b_out[row : row + v_ref.shape[0], :] = v_ref[:, at : at + LANES]
        row += v_ref.shape[0]
    b_out[row : row + o_ref.shape[0], :] = o_ref[...]
    row += o_ref.shape[0]
    norms = [ref[...].astype(full_type).reshape(1, -1) for ref in norm_refs]
    norms = jnp.concatenate(norms + [jnp.zeros((SPARE - 4, LANES), full_type)], axis=0)
    b_out[row : row + SPARE, :] = norms.astype(low_type)
    parts = order_ref.shape[0]
    rows = hidden_ref.shape[0] // parts
    for at in range(parts):
        own_out[at * rows : (at + 1) * rows, :] = rows_in(hidden_ref, order_ref[at], rows)
    block_out[...] = own_out[0:rows, :]


def pack_inputs(order, hidden, w_query, w_key, w_value, w_out, w_up, w_colbert, *norms):
    rows, heads = w_query.shape
    span = hidden.shape[0] // order.shape[0]
    if w_out.shape[1] == LANES and rows == LANES:
        packed = (rows * heads // LANES + w_out.shape[0] + SPARE, LANES)
        outs = [
            shape_of((rows, 2 * heads)),
            shape_of((rows, w_up.shape[1] + w_colbert.shape[1])),
            shape_of(packed),
            shape_of(hidden.shape),
            shape_of((span, hidden.shape[1])),
        ]
        args = (hidden, w_query, w_key, w_value, w_out, w_up, w_colbert) + norms
        return ordered_call(pack_kernel, outs, [], "pack", order, *args, grant=60)
    norms = jnp.concatenate([jnp.stack(norms), jnp.zeros((SPARE - 4, w_out.shape[1]), low_type)], 0)
    blocks = [
        lax.dynamic_slice_in_dim(hidden, order[at] * span, span, 0)
        for at in range(order.shape[0])
    ]
    return (
        jnp.concatenate([w_query, w_key], axis=1),
        jnp.concatenate([w_up, w_colbert], axis=1),
        pack_vo(w_value, jnp.concatenate([w_out, norms], axis=0)),
        jnp.concatenate(blocks),
        blocks[0],
    )


def body(
    hidden_in,
    w_query,
    w_key,
    w_value,
    w_out,
    w_up,
    w_down,
    w_colbert,
    norm1_gain,
    norm1_shift,
    norm2_gain,
    norm2_shift,
    queries,
    passage,
    live,
    score_grad,
):
    tok_rows, width = hidden_in.shape
    device = lax.axis_index("dp")
    column = lax.axis_index("mp")
    dp_size = lax.axis_size("dp")
    mp_size = lax.axis_size("mp")
    group_size = dp_size // NBUCKET
    group_levels = group_size.bit_length() - 1
    own_rows = tok_rows // mp_size
    head_width = w_query.shape[1]
    dp_up, dp_down = upward("dp"), downward("dp")
    turned = dp_up[:1] + dp_down[:-1]
    row_order = offsets_of(downward("mp"))

    def ordered(value, owner, span=own_rows):
        return jnp.concatenate(
            [
                lax.dynamic_slice_in_dim(value, (owner * mp_size + (column ^ at)) * span, span, 0)
                for at in row_order
            ]
        )

    def group_gather(value):
        for level in range(group_levels):
            value = jnp.concatenate([value, swap(value, "dp", 2**level)], 0)
        return value

    across = dp_up[-1:] + dp_up[:-1]
    turned_back, across_back = turned[::-1], across[::-1]
    col_order = column ^ jnp.asarray(row_order, jnp.int32)
    norms = (norm1_gain, norm1_shift, norm2_gain, norm2_shift)
    out_shape = (w_out.shape[0] + SPARE, w_out.shape[1])
    packed_a, packed_u, packed_b, hidden_own, own_hidden = pack_inputs(
        col_order, hidden_in, w_query, w_key, w_value, w_out, w_up, w_colbert, *norms
    )
    pack_a = Gather(packed_a, "dp", dp_down)
    pack_u = Gather(packed_u, "dp", dp_down)
    pack_b = Gather(packed_b, "dp", turned)
    pack_d = Gather(w_down, "dp", dp_down)

    main = (hidden_own, own_hidden)
    main = pack_a.start(main)
    main = pack_u.start(main)
    main = pack_b.start(main)
    others = group_gather(main[1][None])[1:]
    seg_own = ordered(passage, device)
    live_own = ordered(live, device)
    seg_others = jnp.concatenate([ordered(passage, device ^ at) for at in range(1, group_size)])
    live_others = jnp.concatenate([ordered(live, device ^ at) for at in range(1, group_size)])
    slot_own = jnp.where(live_own == 1, seg_own, -1)
    slot_keys = jnp.concatenate([slot_own, jnp.where(live_others == 1, seg_others, -1)])
    seg_column, seg_far, slot_row = seg_own[:, None], seg_others[:, None], slot_keys[None, :]
    blocks = 2 ** (NBUCKET - 1)
    seg_block = seg_own.reshape(blocks, -1)[:, 0]
    live_bias = jnp.where(live_own == 1, 0.0, neg_big)[:, None]
    same = seg_block[:, None] == seg_block[None, :]
    passages = jnp.arange(NPASS, dtype=jnp.int32)
    place = (seg_block[:, None] == passages[None, :]).astype(full_type)
    grad_block = jnp.sum(place[:, None, :] * score_grad[None], axis=2)
    weight = jnp.repeat(grad_block / QLEN, QLEN, axis=1)
    same = same.astype(full_type)
    place = place / jnp.sum(same, axis=1, keepdims=True)
    slot_own = slot_own[None, :]
    early = (seg_column, seg_far, slot_own, slot_row, live_bias, weight, same, place)
    early, main = tie(early, main)
    seg_column, seg_far, slot_own, slot_row, live_bias, weight, same, place = early
    main = pack_a.step(main)
    others, main = tie(others, main)
    far_others = swap(others, "mp", 2)
    main = pack_u.step(main)
    main = pack_b.finish(main)
    main = pack_a.step(main)
    main = pack_b.start(main)
    far_others, main = tie(far_others, main)
    others = [others, far_others]
    others = others + [swap(each, "mp", 1) for each in others]
    others = jnp.stack(others, 1).reshape(-1, width)
    hidden_own, own_hidden = main
    hidden_all = jnp.concatenate([hidden_own, others], 0)
    main = (hidden_own, own_hidden, hidden_all)
    main = pack_u.step(main)
    main = pack_b.step(main)
    main = pack_d.start(main)
    main = pack_a.drain(main)
    full_a = pack_a.value().reshape(width, -1)
    full_a, main = tie(full_a, main)
    hidden_own, own_hidden, hidden_all = main

    query_key = low_dot(hidden_all, full_a).astype(low_type)
    main = (query_key, hidden_all)
    main = pack_b.drain(main)
    full_b, full_out = unpack_vo(pack_b.value(), w_value.shape[0], head_width, out_shape)
    full_b = full_b.reshape(width, head_width)
    full_out = to_lanes(full_out)
    (full_b, full_out), main = tie((full_b, full_out), main)
    query_key, hidden_all = main
    value_rows = low_dot(hidden_all, full_b).astype(low_type)
    value_rows = pack_d.step(value_rows)
    norm_rows = jnp.swapaxes(full_out[:, head_width : head_width + 4], 0, 1).reshape(4, width)
    norm_rows = norm_rows.astype(full_type)
    attended, lse = attend_forward(query_key, value_rows, seg_column, slot_row)
    norm_rows, attended = tie(norm_rows, attended)
    attended = pack_u.drain(attended)
    keep, send = whole_call(mix_kernel, halves_of(tok_rows, width), "mix", attended, full_out)
    keep, send = pack_d.step((keep, send))
    terms = rows_scatter(keep, send)
    square = shape_of((own_rows, width), full_type)
    low_square = shape_of((own_rows, width))
    narrow = shape_of((own_rows, 1), full_type)
    normed_one, normed_low, unit_one, scale_one = whole_call(
        norm_one_kernel,
        [square, low_square, square, narrow],
        "norm_one",
        own_hidden,
        *terms,
        norm_rows,
    )

    units = w_up.shape[1]
    rows_one = rows_gather(normed_low)
    full_up = pack_u.value().reshape(width, -1)
    col_own = full_up[:, units:]
    (full_up, col_own), rows_one = tie((full_up, col_own), rows_one)
    far_col = swap(col_own, "mp", 2)
    active, slope = feed_up(rows_one, full_up, units)
    main = pack_d.drain((active, slope))
    full_down = to_lanes(pack_d.value())
    full_down, (active, slope) = tie(full_down, main)
    keep, send = feed_down(active, full_down)
    (far, far_lse), send = tie((attended, lse), send)
    far = group_gather(far[None])[1:]
    far_lse = group_gather(far_lse[None])[1:]
    terms = rows_scatter(keep, send)
    (far, far_lse), terms = tie((far, far_lse), terms)
    col_blocks = [col_own, far_col]
    col_blocks = col_blocks + [swap(each, "mp", 1) for each in col_blocks]
    normed_two_low, unit_two, scale_two, embedded, embed_low, inv_length = ordered_call(
        norm_two_kernel,
        [low_square, square, narrow, square, low_square, narrow],
        [],
        "norm_two",
        col_order,
        normed_one,
        *terms,
        norm_rows,
        *col_blocks,
    )

    e_blocks = rows_gather(embed_low)
    two_low, e_blocks = tie(normed_two_low, e_blocks)
    far_two = swap(two_low, "mp", 2)
    sharp, soft_block = late_forward(e_blocks, queries, live_bias, blocks)
    soft_far = group_gather(soft_block[None])[1:]
    keep, send, scores = late_backward(
        sharp, soft_block, soft_far, same, place, weight, queries
    )
    far_two, (keep, send) = tie(far_two, (keep, send))
    far_attended = far.reshape(-1, head_width)
    far_lse = jnp.swapaxes(far_lse, 0, 1).reshape(8, -1)

    score_masks = dp_up[group_levels:]
    scores, send = tie(scores, send)
    scores_far = swap(scores, "dp", score_masks[0])
    terms = rows_scatter(keep, send)
    scores_far, terms = tie(scores_far, terms)
    scores, terms = tie(scores + scores_far, terms)
    scores_far = swap(scores, "dp", score_masks[1])
    dproj_low, dresid_two, dresid_low, two_sums = ordered_call(
        norm_two_back_kernel,
        [low_square, square, low_square, shape_of((2, width), full_type)],
        [],
        "norm_two_back",
        col_order,
        *terms,
        norm_rows,
        unit_two,
        scale_two,
        embedded,
        inv_length,
        *col_blocks,
    )
    dresid_blocks = [dresid_low, swap(dresid_low, "mp", 2)]
    scores_far, dresid_blocks = tie(scores_far, dresid_blocks)
    dresid_blocks = dresid_blocks + [swap(each, "mp", 1) for each in dresid_blocks]
    two_blocks = [normed_two_low, far_two]
    two_blocks = two_blocks + [swap(each, "mp", 1) for each in two_blocks]
    two_blocks, dresid_blocks = tie(two_blocks, dresid_blocks)
    scores = scores + scores_far
    for mask in score_masks[2:]:
        scores = scores + swap(scores, "dp", mask)

    dproj_low, dresid_blocks = tie(dproj_low, dresid_blocks)
    du_far = swap(dproj_low, "mp", 2)
    dinner = feed_inner(dresid_blocks, full_down, slope)
    du_far, dinner = tie(du_far, dinner)
    keep, send = feed_back(dinner, full_up)
    got = swap(send, "mp", 1)
    du_blocks = [dproj_low, du_far]
    du_blocks = du_blocks + [swap(each, "mp", 1) for each in du_blocks]
    terms = [keep, got]
    low = rows_fold(*terms)
    (active, dinner), low = tie((active, dinner), low)
    far_low = swap(low, "mp", 2)
    grad_d = Scatter(*grad_down(active, dresid_blocks, dp_up), "dp", dp_up)
    dinner = grad_d.start(dinner)
    grad_u = Scatter(
        *grad_up(dinner, rows_one, two_blocks, du_blocks, w_colbert.shape[1], across_back),
        "dp",
        across_back,
    )
    far_low = grad_u.start(far_low)
    dresid_one, mixed_pack = whole_call(
        norm_one_back_kernel,
        [square, shape_of((own_rows + SPARE, width))],
        "norm_one_back",
        dresid_two,
        *terms,
        far_low,
        norm_rows,
        unit_one,
        scale_one,
        two_sums,
    )
    packs = rows_gather(mixed_pack)

    dattended, norm_sums = whole_call(
        unmix_kernel,
        [shape_of((tok_rows, head_width)), shape_of((SPARE, width))],
        "unmix",
        *packs,
        full_out,
    )
    far_grads = group_gather(dattended[None])[1:].reshape(-1, head_width)
    own_q = (query_key, 0, dattended, attended, lse, seg_column)
    all_keys = (value_rows, slot_row, tok_rows)
    keys = value_rows.shape[0]
    *sums, dquery = attend_back(own_q, None, keys, all_keys, None, True)
    dquery = grad_d.step(dquery)
    far_grads, dquery = tie(far_grads, dquery)
    far_q = (query_key, tok_rows, far_grads, far_attended, far_lse, seg_far)
    own_keys = (value_rows, slot_own, tok_rows)
    sums = attend_back(far_q, 0, tok_rows, own_keys, sums, False)
    sums = grad_u.step(sums)
    dqk, dvalue_low = attend_back(far_q, 1, tok_rows, own_keys, sums, False, (dquery,))
    grad_b = Scatter(
        *grad_vo(hidden_own, dvalue_low, attended, packs, norm_sums, across_back),
        "dp",
        across_back,
    )
    dqk = grad_b.start(dqk)
    grad_a = Scatter(*grad_qk(hidden_own, dqk, dp_up), "dp", dp_up)
    dqk = grad_a.start(dqk)
    keep, send = unproject(dqk, dvalue_low, full_a, full_b)
    got = swap(send, "mp", 1)
    low = rows_fold(keep, got)
    terms = [keep, got, swap(low, "mp", 2)]
    terms = grad_d.step(terms)
    input_own = whole_call(close_kernel, [low_square], "close", dresid_one, *terms)[0]
    far_own = swap(input_own, "mp", 2)
    far_own = grad_u.step(grad_a.step(far_own))
    far_own = grad_b.step(far_own)
    input_blocks = [input_own, far_own]
    input_blocks = input_blocks + [swap(each, "mp", 1) for each in input_blocks]
    input_grad = place_rows(col_order, input_blocks)
    input_grad = grad_d.finish(grad_a.step(input_grad))
    down_grad = grad_d.value()
    input_grad = grad_b.step(input_grad)
    input_grad = grad_u.finish(input_grad)
    up_grad, colbert_grad = finish_pair(grad_u, units)
    ends = (input_grad, down_grad, up_grad, colbert_grad)
    ends = grad_a.finish(ends)
    query_grad, key_grad = finish_pair(grad_a, head_width)
    ends, (query_grad, key_grad) = grad_b.finish((ends, (query_grad, key_grad)))
    input_grad, down_grad, up_grad, colbert_grad = ends
    value_grad, out_grad, norm_grads = finish_vo(
        grad_b.keep[0], grad_b.other[0], w_value.shape, w_out.shape
    )
    return (
        scores,
        input_grad,
        query_grad,
        key_grad,
        value_grad,
        out_grad,
        up_grad,
        down_grad,
        colbert_grad,
        norm_grads[0].reshape(-1),
        norm_grads[1].reshape(-1),
        norm_grads[2].reshape(-1),
        norm_grads[3].reshape(-1),
    )


def solution(mesh):
    rows, both, across = P("dp", None), P("dp", "mp"), P("mp", "dp")
    return jax.shard_map(
        body,
        mesh=mesh,
        in_specs=(
            (rows, both, both, both, across, both, across, both)
            + (P("dp"),) * 4
            + (P("mp", None), P(), P(), P("mp", None))
        ),
        out_specs=(
            (P("mp", None), rows, both, both, both, across, both, across, both)
            + (P("dp"),) * 4
        ),
        check_vma=False,
    )
```

```python
import jax
import jax.numpy as jnp
from jax import lax
from jax.experimental import pallas as pl
from jax.experimental.pallas import tpu as pltpu
from jax.sharding import PartitionSpec as P

HEAD_DIM = 64
QLEN = 32
NBUCKET = 4
NPASS = 15
LANES = 128
SPARE = 16

neg_big = -1e30
low_type = jnp.bfloat16
full_type = jnp.float32
contract_rows = (((0,), (0,)), ((), ()))
contract_cols = (((1,), (1,)), ((), ()))
contract_inner = (((1,), (0,)), ((), ()))


def room(mebibytes):
    return pltpu.CompilerParams(vmem_limit_bytes=mebibytes * 1024 * 1024)


def room_for_keys(keys):
    return room(min(56, 4 + keys // 128))


brief = pl.CostEstimate(flops=1, bytes_accessed=1, transcendentals=0)


def low_dot(left, right, dims=contract_inner):
    return lax.dot_general(left, right, dims, preferred_element_type=full_type)


def shape_of(shape, dtype=low_type):
    return jax.ShapeDtypeStruct(shape, dtype)


def whole_block(shape):
    return pl.BlockSpec(shape, lambda i: (0,) * len(shape))


def whole_call(kernel, outs, name, *args):
    return pl.pallas_call(
        kernel,
        grid=(1,),
        in_specs=[whole_block(each.shape) for each in args],
        out_specs=[whole_block(each.shape) for each in outs],
        out_shape=outs,
        compiler_params=room(12),
        cost_estimate=brief,
        name=name,
    )(*args)


def swap(value, axis, mask):
    pairs = [(source, source ^ mask) for source in range(lax.axis_size(axis))]
    return lax.ppermute(value, axis, pairs)


def bits_of(axis):
    return lax.axis_size(axis).bit_length() - 1


def has_bit(axis, mask):
    return lax.axis_index(axis) // mask % 2 == 1


def upward(axis):
    return [2**level for level in range(bits_of(axis))]


def downward(axis):
    return upward(axis)[::-1]


def offsets_of(masks):
    order = [0]
    for mask in masks:
        order = order + [at ^ mask for at in order]
    return order


def arrange(blocks, axis, masks):
    levels = bits_of(axis)
    cube = blocks.reshape((2,) * levels + blocks.shape[1:])
    for mask in masks:
        at = levels - mask.bit_length()
        cube = jnp.where(has_bit(axis, mask), jnp.flip(cube, at), cube)
    front = [levels - mask.bit_length() for mask in masks]
    cube = jnp.transpose(cube, front + list(range(levels, cube.ndim)))
    return cube.reshape(blocks.shape)


def tie(*values):
    return lax.optimization_barrier(values)


class Gather:
    def __init__(self, value, axis, masks):
        self.axis, self.masks = axis, list(masks)
        self.levels, self.shape = bits_of(axis), value.shape
        self.whole = value.reshape((1,) * self.levels + value.shape)

    def start(self, main):
        if self.masks:
            self.whole, main = tie(self.whole, main)
            self.other = swap(self.whole, self.axis, self.masks[0])
        return main

    def finish(self, main):
        if self.masks:
            mask = self.masks.pop(0)
            other, main = tie(self.other, main)
            at = self.levels - mask.bit_length()
            self.whole = jnp.where(
                has_bit(self.axis, mask),
                jnp.concatenate([other, self.whole], at),
                jnp.concatenate([self.whole, other], at),
            )
        return main

    def step(self, main):
        return self.start(self.finish(main))

    def drain(self, main):
        main = self.finish(main)
        while self.masks:
            main = self.finish(self.start(main))
        return main

    def value(self):
        return self.whole.reshape((-1,) + self.shape)


class Scatter:
    def __init__(self, keep, send, axis, masks):
        self.axis, self.masks = axis, list(masks)
        self.keep, self.send = keep, send

    def start(self, main):
        if self.masks:
            self.send, main = tie(self.send, main)
            self.other = swap(self.send, self.axis, self.masks[0])
        return main

    def finish(self, main):
        if self.masks:
            self.masks.pop(0)
            other, main = tie(self.other, main)
            if self.masks:
                self.keep, self.send = halve(self.keep, other)
            else:
                self.other = other
        return main

    def step(self, main):
        return self.start(self.finish(main))

    def drain(self, main):
        main = self.finish(main)
        while self.masks:
            main = self.finish(self.start(main))
        return main

    def value(self):
        return self.keep[0].astype(full_type) + self.other[0].astype(full_type)


def halve_kernel(keep_low, keep_high, other_low, other_high, low_ref, high_ref):
    for keep, other, out in (
        (keep_low, other_low, low_ref),
        (keep_high, other_high, high_ref),
    ):
        total = keep[...].astype(full_type) + other[...].astype(full_type)
        out[...] = total.astype(low_type)


def halve(keep, other):
    half = keep.shape[0] // 2
    block = (1,) + keep.shape[1:]
    low = pl.BlockSpec(block, lambda i: (i, 0, 0))
    high = pl.BlockSpec(block, lambda i: (half + i, 0, 0))
    return pl.pallas_call(
        halve_kernel,
        grid=(half,),
        in_specs=[low, high, low, high],
        out_specs=[low, low],
        out_shape=[shape_of((half,) + keep.shape[1:])] * 2,
        compiler_params=room(8),
        cost_estimate=brief,
        name="halve",
    )(keep, keep, other, other)


def rows_gather(block):
    blocks = [block]
    for mask in downward("mp"):
        blocks = blocks + [swap(each, "mp", mask) for each in blocks]
    return blocks


def rows_scatter(blocks):
    masks = upward("mp")
    terms = [[block] for block in blocks]
    for mask in masks:
        half = len(terms) // 2
        sends = [each[0] if len(each) == 1 else rows_fold(each) for each in terms[half:]]
        order = range(half)[::-1]
        got = {at: swap(sends[at], "mp", mask) for at in order}
        terms = [terms[at] + [got[at]] for at in range(half)]
    return terms[0]


def add_up(refs):
    total = refs[0][...].astype(full_type)
    for ref in refs[1:]:
        total = total + ref[...].astype(full_type)
    return total


def head_mask(width, head):
    lane = lax.broadcasted_iota(jnp.int32, (1, width), 1)
    return lane // HEAD_DIM == head


def only_head(rows, head):
    return jnp.where(head_mask(rows.shape[1], head), rows, jnp.zeros_like(rows))


def attend_forward_kernel(q_ref, k_ref, v_ref, segq_ref, segk_ref, o_ref, stat_ref):
    tile, width = q_ref.shape
    bias = jnp.where(segq_ref[...] == segk_ref[...], 0.0, neg_big)
    out = jnp.zeros((tile, width), full_type)
    stat = jnp.zeros((tile, LANES), full_type)
    lane = lax.broadcasted_iota(jnp.int32, (1, LANES), 1)
    queries = q_ref[...] * jnp.asarray(0.125, low_type)
    for head in range(width // HEAD_DIM):
        raw = low_dot(only_head(queries, head), k_ref[...], contract_cols) + bias
        top = jnp.max(raw, axis=1, keepdims=True)
        terms = jnp.exp(raw - top)
        total = jnp.sum(terms, axis=1, keepdims=True)
        mixed = low_dot(terms.astype(low_type), v_ref[...]) * (1.0 / total)
        out = jnp.where(head_mask(width, head), mixed, out)
        stat = jnp.where(lane == head, top + jnp.log(total), stat)
    o_ref[...] = out.astype(low_type)
    stat_ref[...] = stat.T[: stat_ref.shape[0]]


def attend_forward(query_key, value_rows, seg_rows, seg_keys):
    rows = seg_rows.shape[0]
    keys, width = value_rows.shape
    tile = LANES
    return pl.pallas_call(
        attend_forward_kernel,
        grid=(rows // tile,),
        in_specs=[
            pl.BlockSpec((tile, width), lambda i: (i, 0)),
            pl.BlockSpec((keys, width), lambda i: (0, 1)),
            pl.BlockSpec((keys, width), lambda i: (0, 0)),
            pl.BlockSpec((tile, 1), lambda i: (i, 0)),
            pl.BlockSpec((1, keys), lambda i: (0, 0)),
        ],
        out_specs=[
            pl.BlockSpec((tile, width), lambda i: (i, 0)),
            pl.BlockSpec((8, tile), lambda i: (0, i)),
        ],
        out_shape=[shape_of((rows, width)), shape_of((8, rows), full_type)],
        compiler_params=room_for_keys(keys),
        cost_estimate=brief,
        name="attend_forward",
    )(query_key, query_key, value_rows, seg_rows, seg_keys)


def attend_terms(q_ref, k_ref, v_ref, do_ref, o_ref, segq_ref, segk_ref, lse_ref):
    tile, width = q_ref.shape
    bias = jnp.where(segq_ref[...] == segk_ref[...], 0.0, neg_big)
    pad = jnp.zeros((LANES - lse_ref.shape[0], tile), full_type)
    lse = jnp.concatenate([lse_ref[...], pad], 0).T
    queries = q_ref[...] * jnp.asarray(0.125, low_type)
    grads = do_ref[...]
    both = grads.astype(full_type) * o_ref[...].astype(full_type)
    for head in range(width // HEAD_DIM):
        q_head = only_head(queries, head)
        g_head = only_head(grads, head)
        delta = jnp.sum(only_head(both, head), axis=1, keepdims=True)
        raw = low_dot(q_head, k_ref[...], contract_cols)
        probs = jnp.exp(raw + (bias - lse[:, head : head + 1]))
        dprobs = low_dot(g_head, v_ref[...], contract_cols)
        dscore = (probs * (dprobs - delta)).astype(low_type)
        yield head, q_head, g_head, probs.astype(low_type), dscore


def attend_back(rows_of_q, part, keys, masks, sums, wants_dq, dq_parts=()):
    query_key, first_row, grads, attended, lse, seg_rows = rows_of_q
    value_rows, seg_keys, own = masks
    width = value_rows.shape[1]
    tile = LANES
    parts_of = 1 if part is None else 2
    steps = grads.shape[0] // tile // parts_of
    shift = steps if part == 1 else 0
    first = first_row // tile + shift
    closing = len(dq_parts) > 0

    def kernel(*refs):
        base, refs = refs[:8], refs[8:]
        q_ref, k_ref = base[:2]
        before, refs = (refs[:2], refs[2:]) if sums else (None, refs)
        parts, refs = refs[: len(dq_parts)], refs[len(dq_parts) :]
        if closing:
            dqk_out, dv_out, dk_sum, dv_sum = refs
        else:
            dk_sum, dv_sum = refs[:2]
        step = pl.program_id(0)

        @pl.when(step == 0)
        def _():
            dk_sum[...] = before[0][...] if sums else jnp.zeros_like(dk_sum)
            dv_sum[...] = before[1][...] if sums else jnp.zeros_like(dv_sum)

        dquery = jnp.zeros((tile, width), full_type)
        for head, q_head, g_head, probs, dscore in attend_terms(*base):
            if wants_dq:
                dquery = jnp.where(head_mask(width, head), low_dot(dscore, k_ref[...]), dquery)
            dk_sum[...] += low_dot(dscore[:, :own], q_head, contract_rows)
            dv_sum[...] += low_dot(probs[:, :own], g_head, contract_rows)
        if wants_dq:
            refs[2][...] = (dquery * 0.125).astype(low_type)
        if closing:

            @pl.when(step == steps - 1)
            def _():
                rows = own // len(parts)
                for at, ref in enumerate(parts):
                    dqk_out[at * rows : (at + 1) * rows, :width] = ref[...]
                dqk_out[:, width:] = dk_sum[...].astype(low_type)
                dv_out[...] = dv_sum[...].astype(low_type)

    tile_rows = pl.BlockSpec((tile, width), lambda i: (shift + i, 0))
    held = whole_block((own, width))
    in_specs = [
        pl.BlockSpec((tile, width), lambda i: (first + i, 0)),
        pl.BlockSpec((keys, width), lambda i: (0, 1)),
        pl.BlockSpec((keys, width), lambda i: (0, 0)),
        tile_rows,
        tile_rows,
        pl.BlockSpec((tile, 1), lambda i: (shift + i, 0)),
        pl.BlockSpec((1, keys), lambda i: (0, 0)),
        pl.BlockSpec((8, tile), lambda i: (0, shift + i)),
    ]
    args = [query_key, query_key, value_rows, grads, attended, seg_rows, seg_keys, lse]
    if sums:
        in_specs, args = in_specs + [held, held], args + list(sums)
    in_specs = in_specs + [whole_block(each.shape) for each in dq_parts]
    args = args + list(dq_parts)
    if closing:
        outs = [shape_of((own, 2 * width)), shape_of((own, width))]
        out_specs = [whole_block(each.shape) for each in outs]
        scratch = [pltpu.VMEM((own, width), full_type)] * 2
    else:
        outs = [shape_of((own, width), full_type)] * 2
        out_specs, scratch = [held, held], []
        if wants_dq:
            outs = outs + [shape_of((steps * tile, width))]
            out_specs = out_specs + [pl.BlockSpec((tile, width), lambda i: (i, 0))]
    return pl.pallas_call(
        kernel,
        grid=(steps,),
        in_specs=in_specs,
        out_specs=out_specs,
        out_shape=outs,
        scratch_shapes=scratch,
        compiler_params=room_for_keys(keys),
        cost_estimate=brief,
        name="attend_back",
    )(*args)


def lanes_of(ref):
    return jnp.concatenate([ref[at] for at in range(ref.shape[0])], axis=1)


def rows_of(refs):
    return jnp.concatenate([ref[...] for ref in refs], axis=0)


def feed_up_kernel(*refs):
    *row_refs, up_ref, g_ref, slope_ref = refs
    for at, ref in enumerate(row_refs):
        place = pl.ds(at * ref.shape[0], ref.shape[0])
        inner = low_dot(ref[...], up_ref[...])
        normal = 0.5 * (1.0 + lax.erf(inner * 0.7071067811865476))
        g_ref[place, :] = (inner * normal).astype(low_type)
        slope = normal + inner * jnp.exp(-0.5 * inner * inner) * 0.3989422804014327
        slope_ref[place, :] = slope.astype(low_type)


def feed_up(blocks, w_up, units):
    own, width = blocks[0].shape
    rows = own * len(blocks)
    tile = 256
    return pl.pallas_call(
        feed_up_kernel,
        grid=(units // tile,),
        in_specs=[pl.BlockSpec((own, width), lambda i: (0, 0))] * len(blocks)
        + [pl.BlockSpec((width, tile), lambda i: (0, i))],
        out_specs=[pl.BlockSpec((rows, tile), lambda i: (0, i))] * 2,
        out_shape=[shape_of((rows, units))] * 2,
        compiler_params=room(10),
        cost_estimate=brief,
        name="feed_up",
    )(*blocks, w_up)


def store_blocks(total, block_refs):
    rows = total.shape[0] // len(block_refs)
    for at, ref in enumerate(block_refs):
        ref[...] = total[at * rows : (at + 1) * rows].astype(ref.dtype)


def blocks_of(rows, width):
    count = lax.axis_size("mp")
    kept = [shape_of((rows // count, width), full_type)] * (count // 2)
    return kept + [shape_of((rows // count, width))] * (count // 2)


def feed_down_kernel(g_ref, down_ref, *block_refs):
    store_blocks(low_dot(g_ref[...], lanes_of(down_ref)), block_refs)


def feed_down(active, w_down):
    rows, units = active.shape
    blocks, _, lanes = w_down.shape
    tile = 2
    return pl.pallas_call(
        feed_down_kernel,
        grid=(blocks // tile,),
        in_specs=[
            pl.BlockSpec((rows, units), lambda i: (0, 0)),
            pl.BlockSpec((tile, units, lanes), lambda i: (i, 0, 0)),
        ],
        out_specs=[
            pl.BlockSpec((each.shape[0], tile * lanes), lambda i: (0, i))
            for each in blocks_of(rows, blocks * lanes)
        ],
        out_shape=blocks_of(rows, blocks * lanes),
        compiler_params=room(10),
        cost_estimate=brief,
        name="feed_down",
    )(active, w_down)


def feed_inner_kernel(*refs):
    *row_refs, down_ref, slope_ref, dz_ref = refs
    weight = lanes_of(down_ref)
    for at, ref in enumerate(row_refs):
        place = pl.ds(at * ref.shape[0], ref.shape[0])
        dactive = low_dot(ref[...], weight, contract_cols)
        dz_ref[place, :] = (dactive * slope_ref[place, :].astype(full_type)).astype(low_type)


def feed_inner(blocks, w_down, slope):
    own, width = blocks[0].shape
    rows, units = slope.shape
    tile = 256
    lanes = w_down.shape[2]
    return pl.pallas_call(
        feed_inner_kernel,
        grid=(units // tile,),
        in_specs=[pl.BlockSpec((own, width), lambda i: (0, 0))] * len(blocks)
        + [
            pl.BlockSpec((w_down.shape[0], tile, lanes), lambda i: (0, i, 0)),
            pl.BlockSpec((rows, tile), lambda i: (0, i)),
        ],
        out_specs=pl.BlockSpec((rows, tile), lambda i: (0, i)),
        out_shape=shape_of((rows, units)),
        compiler_params=room(10),
        cost_estimate=brief,
        name="feed_inner",
    )(*blocks, w_down, slope)


def feed_back_kernel(dz_ref, up_ref, *block_refs):
    store_blocks(low_dot(dz_ref[...], up_ref[...], contract_cols), block_refs)


def feed_back(dinner, w_up):
    rows, units = dinner.shape
    width = w_up.shape[0]
    tile = 256
    return pl.pallas_call(
        feed_back_kernel,
        grid=(width // tile,),
        in_specs=[
            pl.BlockSpec((rows, units), lambda i: (0, 0)),
            pl.BlockSpec((tile, units), lambda i: (i, 0)),
        ],
        out_specs=[
            pl.BlockSpec((each.shape[0], tile), lambda i: (0, i))
            for each in blocks_of(rows, width)
        ],
        out_shape=blocks_of(rows, width),
        compiler_params=room(10),
        cost_estimate=brief,
        name="feed_back",
    )(dinner, w_up)


def late_forward_kernel(*refs):
    *e_refs, q_ref, live_ref, sharp_ref, soft_ref = refs
    blocks = soft_ref.shape[0]
    per = blocks // len(e_refs)
    for at, e_ref in enumerate(e_refs):
        rows = e_ref.shape[0]
        place = pl.ds(at * rows, rows)
        sharp = low_dot(e_ref[...], q_ref[...], contract_cols) * 2.0 + live_ref[place, :]
        sharp_ref[place, :] = sharp
        cube = sharp.reshape(per, rows // per, sharp.shape[1])
        top = jnp.max(cube, axis=1)
        total = jnp.sum(jnp.exp(cube - top[:, None, :]), axis=1)
        soft = jnp.where(top > 0.5 * neg_big, top + jnp.log(total), neg_big)
        soft_ref[pl.ds(at * per, per), :] = soft


def late_forward(e_blocks, queries, live_bias, blocks):
    own, width = e_blocks[0].shape
    rows = own * len(e_blocks)
    count = queries.shape[0]
    tile = 512
    return pl.pallas_call(
        late_forward_kernel,
        grid=(count // tile,),
        in_specs=[pl.BlockSpec((own, width), lambda i: (0, 0))] * len(e_blocks)
        + [
            pl.BlockSpec((tile, width), lambda i: (i, 0)),
            pl.BlockSpec((rows, 1), lambda i: (0, 0)),
        ],
        out_specs=[
            pl.BlockSpec((rows, tile), lambda i: (0, i)),
            pl.BlockSpec((blocks, tile), lambda i: (0, i)),
        ],
        out_shape=[shape_of((rows, count), full_type), shape_of((blocks, count), full_type)],
        compiler_params=room(14),
        cost_estimate=brief,
        name="late_forward",
    )(*e_blocks, queries, live_bias)


def join_soft(soft, far, same):
    top = soft
    for at in range(far.shape[0]):
        top = jnp.maximum(top, far[at])
    total = jnp.exp(soft - top)
    for at in range(far.shape[0]):
        total = total + jnp.exp(far[at] - top)
    blocks = soft.shape[0]
    most = jnp.full(soft.shape, neg_big, full_type)
    for at in range(blocks):
        shared = same[:, at : at + 1] > 0.0
        most = jnp.maximum(most, jnp.where(shared, top[at : at + 1], neg_big))
    sums = jnp.zeros(soft.shape, full_type)
    for at in range(blocks):
        shared = same[:, at : at + 1] > 0.0
        term = jnp.where(shared, top[at : at + 1], neg_big)
        sums = sums + jnp.exp(term - most) * total[at : at + 1]
    return most + jnp.log(sums)


def late_backward_kernel(
    sharp_ref, soft_ref, far_ref, same_ref, place_ref, weight_ref, q_ref, *refs
):
    *block_refs, score_ref, total = refs
    step = pl.program_id(0)
    blocks = soft_ref.shape[0]
    rows, tile = sharp_ref.shape
    soft = join_soft(soft_ref[...], far_ref[...], same_ref[...])
    cube = sharp_ref[...].reshape(blocks, rows // blocks, tile)
    pulled = weight_ref[...][:, None, :] * jnp.exp(cube - soft[:, None, :])
    term = low_dot(pulled.reshape(rows, tile).astype(low_type), q_ref[...])
    query = lax.broadcasted_iota(jnp.int32, (tile, score_ref.shape[0]), 0) // QLEN
    count = lax.broadcasted_iota(jnp.int32, (tile, score_ref.shape[0]), 1)
    pool = jnp.where(query == count, 0.5 / QLEN, 0.0)
    exact = lax.Precision.HIGHEST
    means = lax.dot_general(pool, soft, (((0,), (1,)), ((), ())), precision=exact)
    score_ref[...] = lax.dot_general(means, place_ref[...], contract_inner, precision=exact)

    @pl.when(step == 0)
    def _():
        total[...] = term

    @pl.when(step > 0)
    def _():
        total[...] += term

    @pl.when(step == pl.num_programs(0) - 1)
    def _():
        store_blocks(total[...], block_refs)


def late_backward(sharp, soft, far, same, place, weight, queries):
    rows, count = sharp.shape
    width = queries.shape[1]
    blocks = soft.shape[0]
    tile = 512
    outs = blocks_of(rows, width)
    return pl.pallas_call(
        late_backward_kernel,
        grid=(count // tile,),
        in_specs=[
            pl.BlockSpec((rows, tile), lambda i: (0, i)),
            pl.BlockSpec((blocks, tile), lambda i: (0, i)),
            pl.BlockSpec((far.shape[0], blocks, tile), lambda i: (0, 0, i)),
            whole_block(same.shape),
            whole_block(place.shape),
            pl.BlockSpec((blocks, tile), lambda i: (0, i)),
            pl.BlockSpec((tile, width), lambda i: (i, 0)),
        ],
        out_specs=[whole_block(each.shape) for each in outs]
        + [pl.BlockSpec((tile // QLEN, NPASS), lambda i: (i, 0))],
        out_shape=outs + [shape_of((count // QLEN, NPASS), full_type)],
        scratch_shapes=[pltpu.VMEM((rows, width), full_type)],
        compiler_params=room(16),
        cost_estimate=brief,
        name="late_backward",
    )(sharp, soft, far, same, place, weight, queries)


def norm_stats(values):
    centre = values - jnp.mean(values, axis=-1, keepdims=True)
    spread = jnp.mean(centre * centre, axis=-1, keepdims=True)
    scale = lax.rsqrt(spread + 1e-05)
    return centre * scale, scale


def norm_backward(unit, scale, gain, grad):
    dunit = grad * gain
    dvalues = scale * (
        dunit
        - jnp.mean(dunit, axis=-1, keepdims=True)
        - unit * jnp.mean(dunit * unit, axis=-1, keepdims=True)
    )
    return (
        dvalues,
        jnp.sum(grad * unit, axis=0, keepdims=True),
        jnp.sum(grad, axis=0, keepdims=True),
    )


def norm_one_kernel(*refs):
    *terms, norm_ref, h_ref, low_ref, unit_ref, scale_ref = refs
    unit, scale = norm_stats(add_up(terms))
    normed = unit * norm_ref[0:1] + norm_ref[1:2]
    h_ref[...] = normed
    low_ref[...] = normed.astype(low_type)
    unit_ref[...] = unit
    scale_ref[...] = scale


def lanes_at(order_ref, at, span):
    return pl.ds(pl.multiple_of(order_ref[at] * span, span), span)


def norm_two_kernel(order_ref, *refs):
    *rest, low_ref, unit_ref, scale_ref, e_ref, elow_ref, inv_ref = refs
    parts = order_ref.shape[0]
    *terms, norm_ref = rest[:-parts]
    col_refs = rest[-parts:]
    unit, scale = norm_stats(add_up(terms))
    normed_low = (unit * norm_ref[2:3] + norm_ref[3:4]).astype(low_type)
    low_ref[...] = normed_low
    unit_ref[...] = unit
    scale_ref[...] = scale
    span = col_refs[0].shape[1]
    squares = 0.0
    for at, ref in enumerate(col_refs):
        projected = low_dot(normed_low, ref[...])
        e_ref[:, lanes_at(order_ref, at, span)] = projected
        squares = squares + jnp.sum(projected * projected, axis=-1, keepdims=True)
    inv = lax.rsqrt(squares + 1e-06)
    embedded = e_ref[...] * inv
    e_ref[...] = embedded
    elow_ref[...] = embedded.astype(low_type)
    inv_ref[...] = inv


def norm_two_back_kernel(order_ref, *refs):
    *rest, own_ref, far_ref, dr_ref, low_ref, g_ref, du_ref = refs
    parts = order_ref.shape[0]
    *terms, norm_ref, unit_ref, scale_ref, e_ref, inv_ref = rest[:-parts]
    col_refs = rest[-parts:]
    dembed = add_up(terms)
    embedded = e_ref[...]
    along = jnp.sum(embedded * dembed, axis=-1, keepdims=True)
    du_ref[...] = (inv_ref[...] * (dembed - embedded * along)).astype(low_type)
    span = col_refs[0].shape[1]
    dnormed = 0.0
    for at, ref in enumerate(col_refs):
        dproj = du_ref[:, lanes_at(order_ref, at, span)]
        dnormed = dnormed + low_dot(dproj, ref[...], contract_cols)
    half = own_ref.shape[1]
    mine = order_ref[0] // (parts // 2)
    own_ref[...] = du_ref[:, pl.ds(pl.multiple_of(mine * half, half), half)]
    far_ref[...] = du_ref[:, pl.ds(pl.multiple_of((1 - mine) * half, half), half)]
    dresid, dgain, dshift = norm_backward(
        unit_ref[...], scale_ref[...], norm_ref[2:3], dnormed
    )
    dr_ref[...] = dresid
    low_ref[...] = dresid.astype(low_type)
    g_ref[...] = jnp.concatenate([dgain, dshift], 0)


def split_sums(sums):
    high = sums.astype(low_type).astype(full_type)
    zeros = jnp.zeros((SPARE - 8, sums.shape[1]), full_type)
    return jnp.concatenate([high, sums - high, zeros], 0).astype(low_type)


def norm_one_back_kernel(*refs):
    *terms, norm_ref, unit_ref, scale_ref, two_ref, dr_ref, pack_ref = refs
    dresid, dgain, dshift = norm_backward(
        unit_ref[...], scale_ref[...], norm_ref[0:1], add_up(terms)
    )
    dr_ref[...] = dresid
    rows = dresid.shape[0]
    pack_ref[0:rows, :] = dresid.astype(low_type)
    pack_ref[rows : rows + SPARE, :] = split_sums(
        jnp.concatenate([dgain, dshift, two_ref[...]], 0)
    )


def fold_kernel(*refs):
    *terms, low_ref = refs
    low_ref[...] = add_up(terms).astype(low_type)


def rows_fold(terms):
    return whole_call(fold_kernel, [shape_of(terms[0].shape)], "fold", *terms)[0]


def mix_kernel(o_ref, out_ref, *block_refs):
    rows = o_ref.shape[1]
    weight = jnp.concatenate([out_ref[at, 0:rows, :] for at in range(out_ref.shape[0])], axis=1)
    store_blocks(low_dot(o_ref[...], weight), block_refs)


def unmix_kernel(*refs):
    *packs, out_ref, do_ref, sums_ref = refs
    rows = do_ref.shape[1]
    weight = jnp.concatenate([out_ref[at, 0:rows, :] for at in range(out_ref.shape[0])], axis=1)
    own = packs[0].shape[0] - SPARE
    sums = jnp.zeros((8, weight.shape[1]), full_type)
    for at, ref in enumerate(packs):
        do = low_dot(ref[0:own, :], weight, contract_cols)
        do_ref[at * own : (at + 1) * own, :] = do.astype(low_type)
        sums = sums + ref[own : own + SPARE, :].astype(full_type)[:8]
    sums_ref[...] = split_sums(sums[:4] + sums[4:])


def block_order(masks):
    return lax.axis_index("dp") ^ jnp.asarray(offsets_of(masks[::-1]), jnp.int32)


def ordered_call(kernel, outs, scratch, name, order, *args, grant=20):
    return pl.pallas_call(
        kernel,
        grid=(1,),
        in_specs=[pl.BlockSpec(memory_space=pltpu.SMEM)]
        + [whole_block(each.shape) for each in args],
        out_specs=[whole_block(each.shape) for each in outs],
        out_shape=outs,
        scratch_shapes=[pltpu.VMEM(*each) for each in scratch],
        compiler_params=room(grant),
        cost_estimate=brief,
        name=name,
    )(order, *args)


def stored(place_ref, left, right):
    turned = left.T
    cols = right.shape[1]
    for start in range(0, cols, 256):
        stop = min(start + 256, cols)
        place_ref[:, start:stop] = low_dot(turned, right[:, start:stop]).astype(low_type)


def deal(order_ref, keep_ref, send_ref, write):
    half = keep_ref.shape[0]
    for at in range(2 * half):
        write(keep_ref.at[at] if at < half else send_ref.at[at - half], order_ref[at])


def rows_in(ref, block, count):
    return ref[pl.ds(pl.multiple_of(block * count, count), count), :]


def lanes_in(ref, block):
    return ref[:, pl.ds(pl.multiple_of(block * LANES, LANES), LANES)]


def halves_like(count, block):
    return [shape_of((count // 2,) + block)] * 2


def grad_down_kernel(order_ref, active_ref, *refs):
    *row_refs, keep_ref, send_ref, total = refs
    stored(total, active_ref[...], rows_of(row_refs))

    def write(ref, block):
        ref[...] = lanes_in(total, block)

    deal(order_ref, keep_ref, send_ref, write)


def grad_down(active, row_blocks, masks):
    count = lax.axis_size("dp")
    units, width = active.shape[1], row_blocks[0].shape[1]
    if width // count == LANES:
        return ordered_call(
            grad_down_kernel,
            halves_like(count, (units, LANES)),
            [((units, width), low_type)],
            "grad_down",
            block_order(masks),
            active,
            *row_blocks,
        )
    whole = low_dot(active, jnp.concatenate(row_blocks, 0), contract_rows).astype(low_type)
    return halves(arrange(jnp.swapaxes(whole.reshape(units, count, -1), 0, 1), "dp", masks))


def halves(blocks):
    half = blocks.shape[0] // 2
    return blocks[:half], blocks[half:]


def grad_up_kernel(order_ref, dinner_ref, *refs):
    *row_refs, keep_ref, send_ref, total = refs
    parts = len(row_refs) // 3
    units = dinner_ref.shape[1]
    block_rows = keep_ref.shape[1]
    cols = keep_ref.shape[2] - units
    stored(total.at[:, 0:units], rows_of(row_refs[:parts]), dinner_ref[...])
    mine = order_ref[order_ref.shape[0] - 1] % (row_refs[-1].shape[1] // cols)
    mine = pl.ds(pl.multiple_of(mine * cols, cols), cols)
    dproj = jnp.concatenate([ref[:, mine] for ref in row_refs[2 * parts :]], axis=0)
    stored(total.at[:, units:], rows_of(row_refs[parts : 2 * parts]), dproj)

    def write(ref, block):
        ref[...] = rows_in(total, block, block_rows)

    deal(order_ref, keep_ref, send_ref, write)


def grad_up(dinner, one_blocks, two_blocks, du_blocks, col_width, masks):
    count = lax.axis_size("dp")
    units, width = dinner.shape[1], one_blocks[0].shape[1]
    column = lax.axis_index("mp")
    rows = width // count
    if rows == LANES:
        order = jnp.concatenate([block_order(masks), column.reshape(1)])
        return ordered_call(
            grad_up_kernel,
            halves_like(count, (rows, units + col_width)),
            [((width, units + col_width), low_type)],
            "grad_up",
            order,
            dinner,
            *one_blocks,
            *two_blocks,
            *du_blocks,
        )
    column = column % (du_blocks[0].shape[1] // col_width)
    dproj = lax.dynamic_slice_in_dim(
        jnp.concatenate(du_blocks, 0), column * col_width, col_width, 1
    )
    up = low_dot(jnp.concatenate(one_blocks, 0), dinner, contract_rows)
    col = low_dot(jnp.concatenate(two_blocks, 0), dproj, contract_rows)
    whole = jnp.concatenate([up, col], 1).astype(low_type)
    return halves(arrange(whole.reshape(count, rows, -1), "dp", masks))


def grad_qk_kernel(order_ref, left_ref, right_ref, keep_ref, send_ref, total):
    block_rows = keep_ref.shape[1]
    stored(total, left_ref[...], right_ref[...])

    def write(ref, block):
        ref[...] = rows_in(total, block, block_rows)

    deal(order_ref, keep_ref, send_ref, write)


def grad_qk(left, right, masks):
    count = lax.axis_size("dp")
    width, cols = left.shape[1], right.shape[1]
    rows = width // count
    if rows == LANES:
        return ordered_call(
            grad_qk_kernel,
            halves_like(count, (rows, cols)),
            [((width, cols), low_type)],
            "grad_qk",
            block_order(masks),
            left,
            right,
        )
    whole = low_dot(left, right, contract_rows).astype(low_type)
    return halves(arrange(whole.reshape(count, rows, cols), "dp", masks))


def grad_vo_kernel(order_ref, hidden_ref, dv_ref, o_ref, *refs):
    *packs, sums_ref, keep_ref, send_ref, total_v, total_o = refs
    rows = packs[0].shape[0] - SPARE
    cols = dv_ref.shape[1]
    heads = o_ref.shape[1]
    stored(total_v, hidden_ref[...], dv_ref[...])
    mixed = jnp.concatenate([ref[0:rows, :] for ref in packs], axis=0)
    stored(total_o.at[0:heads, :], o_ref[...], mixed)
    total_o[heads : heads + SPARE, :] = sums_ref[...]

    def write(ref, block):
        value = rows_in(total_v, block, LANES)
        for at in range(cols // LANES):
            ref[at * LANES : (at + 1) * LANES, :] = value[:, at * LANES : (at + 1) * LANES]
        ref[cols:, :] = lanes_in(total_o, block)

    deal(order_ref, keep_ref, send_ref, write)


def finish_pair_kernel(keep_ref, other_ref, left_ref, right_ref):
    total = keep_ref[...].astype(full_type) + other_ref[...].astype(full_type)
    cols = left_ref.shape[1]
    left_ref[...] = total[:, :cols]
    right_ref[...] = total[:, cols:]


def finish_pair(scatter, cols):
    rows, both = scatter.keep.shape[1:]
    outs = [shape_of((rows, cols), full_type), shape_of((rows, both - cols), full_type)]
    return whole_call(finish_pair_kernel, outs, "finish_pair", scatter.keep[0], scatter.other[0])


def finish_vo_kernel(keep_ref, other_ref, value_ref, out_ref, *norm_refs):
    total = keep_ref[...].astype(full_type) + other_ref[...].astype(full_type)
    rows, cols = value_ref.shape
    row = 0
    for at in range(0, cols, LANES):
        value_ref[:, at : at + LANES] = total[row : row + rows]
        row += rows
    out_ref[...] = total[row : row + out_ref.shape[0]]
    row += out_ref.shape[0]
    for at, ref in enumerate(norm_refs):
        ref[...] = total[row + at : row + at + 1] + total[row + 4 + at : row + 5 + at]


def finish_vo(keep, other, value_shape, out_shape):
    rows, cols = out_shape
    if cols == LANES:
        outs = [shape_of(value_shape, full_type), shape_of(out_shape, full_type)]
        outs = outs + [shape_of((1, cols), full_type)] * 4
        value, out, *norms = whole_call(finish_vo_kernel, outs, "finish_vo", keep, other)
        return value, out, norms
    total = keep.astype(full_type) + other.astype(full_type)
    value, out = unpack_vo(total, *value_shape, (rows + SPARE, cols))
    return value, out[:rows], out[rows : rows + 4] + out[rows + 4 : rows + 8]


def pack_vo(value, out):
    cols = value.shape[-1]
    parts = [value[..., at : at + LANES] for at in range(0, cols, LANES)]
    return jnp.concatenate(parts + [out.reshape(out.shape[:-2] + (-1, LANES))], axis=-2)


def unpack_vo(packed, rows, cols, out_shape):
    high = rows * cols // LANES
    value = jnp.concatenate(
        [packed[..., at : at + rows, :] for at in range(0, high, rows)], axis=-1
    )
    return value, packed[..., high:, :].reshape(packed.shape[:-2] + out_shape)


def grad_vo(hidden, dvalue, attended, packs, sums, masks):
    count = lax.axis_size("dp")
    width, cols = hidden.shape[1], dvalue.shape[1]
    heads = attended.shape[1]
    rows = width // count
    if rows == LANES:
        block = (cols * rows // LANES + heads + SPARE, LANES)
        return ordered_call(
            grad_vo_kernel,
            halves_like(count, block),
            [((width, cols), low_type), ((heads + SPARE, width), low_type)],
            "grad_vo",
            block_order(masks),
            hidden,
            dvalue,
            attended,
            *packs,
            sums,
        )
    value = low_dot(hidden, dvalue, contract_rows).astype(low_type).reshape(count, rows, cols)
    mixed = jnp.concatenate([each[:-SPARE] for each in packs], 0)
    out = low_dot(attended, mixed, contract_rows).astype(low_type)
    out = jnp.concatenate([out, sums], 0).reshape(heads + SPARE, count, rows)
    return halves(arrange(pack_vo(value, jnp.swapaxes(out, 0, 1)), "dp", masks))


def to_lanes(blocks):
    if blocks.shape[2] == LANES:
        return blocks
    whole = jnp.swapaxes(blocks, 0, 1).reshape(blocks.shape[1], -1, LANES)
    return jnp.swapaxes(whole, 0, 1)


def place_kernel(at_ref, *refs):
    *blocks, out_ref = refs
    rows = blocks[0].shape[0]
    for at, ref in enumerate(blocks):
        start = pl.multiple_of(at_ref[at] * rows, rows)
        out_ref[pl.ds(start, rows), :] = ref[...].astype(full_type)


def place_rows(order, blocks):
    rows, width = blocks[0].shape
    outs = [shape_of((rows * len(blocks), width), full_type)]
    return ordered_call(place_kernel, outs, [], "place_rows", order, *blocks)[0]


def unproject_kernel(dqk_ref, dv_ref, a_ref, b_ref, *block_refs):
    total = low_dot(dqk_ref[...], a_ref[...], contract_cols)
    store_blocks(total + low_dot(dv_ref[...], b_ref[...], contract_cols), block_refs)


def unproject(dqk, dvalue, w_qk, w_v):
    outs = blocks_of(dqk.shape[0], w_qk.shape[0])
    return whole_call(unproject_kernel, outs, "unproject", dqk, dvalue, w_qk, w_v)


def close_kernel(*refs):
    *terms, out_ref = refs
    out_ref[...] = add_up(terms).astype(low_type)


def pack_kernel(order_ref, *refs):
    hidden_ref, q_ref, k_ref, v_ref, o_ref, up_ref, col_ref, *norm_refs = refs[:11]
    a_out, u_out, b_out, own_out, block_out = refs[11:]
    heads, units = q_ref.shape[1], up_ref.shape[1]
    a_out[:, :heads] = q_ref[...]
    a_out[:, heads:] = k_ref[...]
    u_out[:, :units] = up_ref[...]
    u_out[:, units:] = col_ref[...]
    row = 0
    for at in range(0, heads, LANES):
        b_out[row : row + v_ref.shape[0], :] = v_ref[:, at : at + LANES]
        row += v_ref.shape[0]
    b_out[row : row + o_ref.shape[0], :] = o_ref[...]
    row += o_ref.shape[0]
    norms = [ref[...].astype(full_type).reshape(1, -1) for ref in norm_refs]
    norms = jnp.concatenate(norms + [jnp.zeros((SPARE - 4, LANES), full_type)], axis=0)
    b_out[row : row + SPARE, :] = norms.astype(low_type)
    parts = order_ref.shape[0]
    rows = hidden_ref.shape[0] // parts
    for at in range(parts):
        own_out[at * rows : (at + 1) * rows, :] = rows_in(hidden_ref, order_ref[at], rows)
    block_out[...] = own_out[0:rows, :]


def pack_inputs(order, hidden, w_query, w_key, w_value, w_out, w_up, w_colbert, *norms):
    rows, heads = w_query.shape
    span = hidden.shape[0] // order.shape[0]
    if w_out.shape[1] == LANES and rows == LANES:
        packed = (rows * heads // LANES + w_out.shape[0] + SPARE, LANES)
        outs = [
            shape_of((rows, 2 * heads)),
            shape_of((rows, w_up.shape[1] + w_colbert.shape[1])),
            shape_of(packed),
            shape_of(hidden.shape),
            shape_of((span, hidden.shape[1])),
        ]
        args = (hidden, w_query, w_key, w_value, w_out, w_up, w_colbert) + norms
        return ordered_call(pack_kernel, outs, [], "pack", order, *args, grant=60)
    norms = jnp.concatenate([jnp.stack(norms), jnp.zeros((SPARE - 4, w_out.shape[1]), low_type)], 0)
    blocks = [
        lax.dynamic_slice_in_dim(hidden, order[at] * span, span, 0)
        for at in range(order.shape[0])
    ]
    return (
        jnp.concatenate([w_query, w_key], axis=1),
        jnp.concatenate([w_up, w_colbert], axis=1),
        pack_vo(w_value, jnp.concatenate([w_out, norms], axis=0)),
        jnp.concatenate(blocks),
        blocks[0],
    )


def body(
    hidden_in,
    w_query,
    w_key,
    w_value,
    w_out,
    w_up,
    w_down,
    w_colbert,
    norm1_gain,
    norm1_shift,
    norm2_gain,
    norm2_shift,
    queries,
    passage,
    live,
    score_grad,
):
    tok_rows, width = hidden_in.shape
    device = lax.axis_index("dp")
    column = lax.axis_index("mp")
    dp_size = lax.axis_size("dp")
    mp_size = lax.axis_size("mp")
    group_size = dp_size // NBUCKET
    group_levels = group_size.bit_length() - 1
    own_rows = tok_rows // mp_size
    head_width = w_query.shape[1]
    dp_up, dp_down = upward("dp"), downward("dp")
    turned = dp_up[:1] + dp_down[:-1]
    row_order = offsets_of(downward("mp"))

    def ordered(value, owner, span=own_rows):
        return jnp.concatenate(
            [
                lax.dynamic_slice_in_dim(value, (owner * mp_size + (column ^ at)) * span, span, 0)
                for at in row_order
            ]
        )

    def group_gather(value):
        for level in range(group_levels):
            value = jnp.concatenate([value, swap(value, "dp", 2**level)], 0)
        return value

    across = dp_up[-1:] + dp_up[:-1]
    turned_back, across_back = turned[::-1], across[::-1]
    col_order = column ^ jnp.asarray(row_order, jnp.int32)
    norms = (norm1_gain, norm1_shift, norm2_gain, norm2_shift)
    out_shape = (w_out.shape[0] + SPARE, w_out.shape[1])
    packed_a, packed_u, packed_b, hidden_own, own_hidden = pack_inputs(
        col_order, hidden_in, w_query, w_key, w_value, w_out, w_up, w_colbert, *norms
    )
    pack_a = Gather(packed_a, "dp", dp_down)
    pack_u = Gather(packed_u, "dp", dp_down)
    pack_b = Gather(packed_b, "dp", dp_down)
    pack_d = Gather(w_down, "dp", turned)

    main = (hidden_own, own_hidden)
    main = pack_a.start(main)
    main = pack_b.start(main)
    main = pack_u.start(main)
    main = pack_d.start(main)
    others = group_gather(main[1][None])[1:]
    seg_own = ordered(passage, device)
    live_own = ordered(live, device)
    seg_others = jnp.concatenate([ordered(passage, device ^ at) for at in range(1, group_size)])
    live_others = jnp.concatenate([ordered(live, device ^ at) for at in range(1, group_size)])
    slot_own = jnp.where(live_own == 1, seg_own, -1)
    slot_keys = jnp.concatenate([slot_own, jnp.where(live_others == 1, seg_others, -1)])
    seg_column, seg_far, slot_row = seg_own[:, None], seg_others[:, None], slot_keys[None, :]
    blocks = 2 ** (NBUCKET - 1)
    seg_block = seg_own.reshape(blocks, -1)[:, 0]
    live_bias = jnp.where(live_own == 1, 0.0, neg_big)[:, None]
    same = seg_block[:, None] == seg_block[None, :]
    passages = jnp.arange(NPASS, dtype=jnp.int32)
    place = (seg_block[:, None] == passages[None, :]).astype(full_type)
    grad_block = jnp.sum(place[:, None, :] * score_grad[None], axis=2)
    weight = jnp.repeat(grad_block / QLEN, QLEN, axis=1)
    same = same.astype(full_type)
    place = place / jnp.sum(same, axis=1, keepdims=True)
    slot_own = slot_own[None, :]
    early = (seg_column, seg_far, slot_own, slot_row, live_bias, weight, same, place)
    early, main = tie(early, main)
    seg_column, seg_far, slot_own, slot_row, live_bias, weight, same, place = early
    main = pack_a.step(main)
    main = pack_b.step(main)
    others, main = tie(others, main)
    far_others = swap(others, "mp", 2)
    main = pack_d.finish(main)
    main = pack_u.step(main)
    main = pack_d.start(main)
    main = pack_a.step(main)
    main = pack_b.step(main)
    far_others, main = tie(far_others, main)
    main = pack_u.step(main)
    others = [others, far_others]
    others = others + [swap(each, "mp", 1) for each in others]
    others = jnp.stack(others, 1).reshape(-1, width)
    hidden_own, own_hidden = main
    hidden_all = jnp.concatenate([hidden_own, others], 0)
    main = (hidden_own, own_hidden, hidden_all)
    main = pack_a.drain(main)
    full_a = pack_a.value().reshape(width, -1)
    full_a, main = tie(full_a, main)
    hidden_own, own_hidden, hidden_all = main

    query_key = low_dot(hidden_all, full_a).astype(low_type)
    main = (query_key, hidden_all)
    main = pack_b.drain(main)
    full_b, full_out = unpack_vo(pack_b.value(), w_value.shape[0], head_width, out_shape)
    full_b = full_b.reshape(width, head_width)
    full_out = to_lanes(full_out)
    (full_b, full_out), main = tie((full_b, full_out), main)
    main = pack_d.step(main)
    query_key, hidden_all = main
    value_rows = low_dot(hidden_all, full_b).astype(low_type)
    norm_rows = jnp.swapaxes(full_out[:, head_width : head_width + 4], 0, 1).reshape(4, width)
    norm_rows = norm_rows.astype(full_type)
    attended, lse = attend_forward(query_key, value_rows, seg_column, slot_row)
    norm_rows, attended = tie(norm_rows, attended)
    parts = whole_call(mix_kernel, blocks_of(tok_rows, width), "mix", attended, full_out)
    terms = rows_scatter(parts)
    terms = pack_u.drain(terms)
    full_up = pack_u.value().reshape(width, -1)
    units = w_up.shape[1]
    col_own = full_up[:, units:]
    col_own, terms = tie(col_own, terms)
    square = shape_of((own_rows, width), full_type)
    low_square = shape_of((own_rows, width))
    narrow = shape_of((own_rows, 1), full_type)
    normed_one, normed_low, unit_one, scale_one = whole_call(
        norm_one_kernel,
        [square, low_square, square, narrow],
        "norm_one",
        own_hidden,
        *terms,
        norm_rows,
    )

    rows_one = [normed_low, swap(normed_low, "mp", 2)]
    rows_one = pack_d.drain(rows_one)
    rows_one = rows_one + [swap(each, "mp", 1) for each in rows_one]
    full_down = to_lanes(pack_d.value())
    far_col = swap(col_own, "mp", 2)
    active, slope = feed_up(rows_one, full_up, units)
    parts = feed_down(active, full_down)
    (far, far_lse), parts = tie((attended, lse), parts)
    far = group_gather(far[None])[1:]
    far_lse = group_gather(far_lse[None])[1:]
    far_col, parts = tie(far_col, parts)
    terms = rows_scatter(parts)
    (far, far_lse), terms = tie((far, far_lse), terms)
    col_blocks = [col_own, far_col]
    col_blocks = col_blocks + [swap(each, "mp", 1) for each in col_blocks]
    normed_two_low, unit_two, scale_two, embedded, embed_low, inv_length = ordered_call(
        norm_two_kernel,
        [low_square, square, narrow, square, low_square, narrow],
        [],
        "norm_two",
        col_order,
        normed_one,
        *terms,
        norm_rows,
        *col_blocks,
    )

    e_blocks = rows_gather(embed_low)
    two_low, e_blocks = tie(normed_two_low, e_blocks)
    far_two = swap(two_low, "mp", 2)
    sharp, soft_block = late_forward(e_blocks, queries, live_bias, blocks)
    soft_far = group_gather(soft_block[None])[1:]
    *parts, scores = late_backward(
        sharp, soft_block, soft_far, same, place, weight, queries
    )
    far_two, parts = tie(far_two, parts)
    far_attended = far.reshape(-1, head_width)
    far_lse = jnp.swapaxes(far_lse, 0, 1).reshape(8, -1)

    score_masks = dp_up[group_levels:]
    scores, parts = tie(scores, parts)
    scores_far = swap(scores, "dp", score_masks[0])
    terms = rows_scatter(parts)
    scores_far, terms = tie(scores_far, terms)
    scores, terms = tie(scores + scores_far, terms)
    scores_far = swap(scores, "dp", score_masks[1])
    low_half = shape_of((own_rows, width // 2))
    du_own, du_far, dresid_two, dresid_low, two_sums = ordered_call(
        norm_two_back_kernel,
        [low_half, low_half, square, low_square, shape_of((2, width), full_type)],
        [((own_rows, width), low_type)],
        "norm_two_back",
        col_order,
        *terms,
        norm_rows,
        unit_two,
        scale_two,
        embedded,
        inv_length,
        *col_blocks,
    )
    dresid_blocks = [dresid_low, swap(dresid_low, "mp", 2)]
    scores_far, dresid_blocks = tie(scores_far, dresid_blocks)
    dresid_blocks = dresid_blocks + [swap(each, "mp", 1) for each in dresid_blocks]
    two_blocks = [normed_two_low, far_two]
    two_blocks = two_blocks + [swap(each, "mp", 1) for each in two_blocks]
    two_blocks, dresid_blocks = tie(two_blocks, dresid_blocks)
    scores = scores + scores_far
    for mask in score_masks[2:]:
        scores = scores + swap(scores, "dp", mask)

    (du_own, du_far), dresid_blocks = tie((du_own, du_far), dresid_blocks)
    du_far = swap(du_far, "mp", 2)
    dinner = feed_inner(dresid_blocks, full_down, slope)
    du_far, dinner = tie(du_far, dinner)
    parts = feed_back(dinner, full_up)
    got_far, got = swap(parts[3], "mp", 1), swap(parts[2], "mp", 1)
    du_blocks = [du_own, du_far]
    du_blocks = du_blocks + [swap(each, "mp", 1) for each in du_blocks]
    low = rows_fold([parts[1], got_far])
    (active, dinner), low = tie((active, dinner), low)
    far_low = swap(low, "mp", 2)
    grad_d = Scatter(*grad_down(active, dresid_blocks, turned), "dp", turned)
    dinner = grad_d.start(dinner)
    grad_u = Scatter(
        *grad_up(dinner, rows_one, two_blocks, du_blocks, w_colbert.shape[1], across_back),
        "dp",
        across_back,
    )
    far_low = grad_u.start(far_low)
    dresid_one, mixed_pack = whole_call(
        norm_one_back_kernel,
        [square, shape_of((own_rows + SPARE, width))],
        "norm_one_back",
        dresid_two,
        parts[0],
        got,
        far_low,
        norm_rows,
        unit_one,
        scale_one,
        two_sums,
    )
    packs = rows_gather(mixed_pack)

    dattended, norm_sums = whole_call(
        unmix_kernel,
        [shape_of((tok_rows, head_width)), shape_of((SPARE, width))],
        "unmix",
        *packs,
        full_out,
    )
    far_grads = group_gather(dattended[None])[1:].reshape(-1, head_width)
    own_q = (query_key, 0, dattended, attended, lse, seg_column)
    all_keys = (value_rows, slot_row, tok_rows)
    keys = value_rows.shape[0]
    *sums, dquery = attend_back(own_q, None, keys, all_keys, None, True)
    dquery = grad_d.step(dquery)
    far_grads, dquery = tie(far_grads, dquery)
    far_q = (query_key, tok_rows, far_grads, far_attended, far_lse, seg_far)
    own_keys = (value_rows, slot_own, tok_rows)
    sums = attend_back(far_q, 0, tok_rows, own_keys, sums, False)
    sums = grad_u.step(sums)
    dqk, dvalue_low = attend_back(far_q, 1, tok_rows, own_keys, sums, False, (dquery,))
    parts = unproject(dqk, dvalue_low, full_a, full_b)
    got_far, got = swap(parts[3], "mp", 1), swap(parts[2], "mp", 1)
    low = rows_fold([parts[1], got_far])
    (dqk, dvalue_low), low = tie((dqk, dvalue_low), low)
    far_low = swap(low, "mp", 2)
    grad_b = Scatter(
        *grad_vo(hidden_own, dvalue_low, attended, packs, norm_sums, across_back),
        "dp",
        across_back,
    )
    dqk = grad_b.start(dqk)
    dqk = grad_d.step(dqk)
    grad_a = Scatter(*grad_qk(hidden_own, dqk, dp_up), "dp", dp_up)
    last = grad_a.start(parts[0])
    last = grad_u.step(last)
    terms = [dresid_one, last, got, far_low]
    input_own = whole_call(close_kernel, [low_square], "close", *terms)[0]
    far_own = swap(input_own, "mp", 2)
    far_own = grad_a.step(grad_b.step(far_own))
    input_blocks = [input_own, far_own]
    input_blocks = input_blocks + [swap(each, "mp", 1) for each in input_blocks]
    input_grad = place_rows(col_order, input_blocks)
    input_grad = grad_a.step(grad_b.step(input_grad))
    input_grad = grad_d.finish(grad_u.finish(input_grad))
    down_grad = grad_d.value()
    up_grad, colbert_grad = finish_pair(grad_u, units)
    ends = (input_grad, down_grad, up_grad, colbert_grad)
    ends = grad_a.finish(ends)
    query_grad, key_grad = finish_pair(grad_a, head_width)
    ends, (query_grad, key_grad) = grad_b.finish((ends, (query_grad, key_grad)))
    input_grad, down_grad, up_grad, colbert_grad = ends
    value_grad, out_grad, norm_grads = finish_vo(
        grad_b.keep[0], grad_b.other[0], w_value.shape, w_out.shape
    )
    return (
        scores,
        input_grad,
        query_grad,
        key_grad,
        value_grad,
        out_grad,
        up_grad,
        down_grad,
        colbert_grad,
        norm_grads[0].reshape(-1),
        norm_grads[1].reshape(-1),
        norm_grads[2].reshape(-1),
        norm_grads[3].reshape(-1),
    )


def solution(mesh):
    rows, both, across = P("dp", None), P("dp", "mp"), P("mp", "dp")
    return jax.shard_map(
        body,
        mesh=mesh,
        in_specs=(
            (rows, both, both, both, across, both, across, both)
            + (P("dp"),) * 4
            + (P("mp", None), P(), P(), P("mp", None))
        ),
        out_specs=(
            (P("mp", None), rows, both, both, both, across, both, across, both)
            + (P("dp"),) * 4
        ),
        check_vma=False,
    )
```

```python
import jax
import jax.numpy as jnp
from jax import lax
from jax.experimental import pallas as pl
from jax.experimental.pallas import tpu as pltpu
from jax.sharding import PartitionSpec as P

HEAD_DIM = 64
QLEN = 32
NBUCKET = 4
NPASS = 15
LANES = 128
SPARE = 16

neg_big = -1e30
low_type = jnp.bfloat16
full_type = jnp.float32
contract_rows = (((0,), (0,)), ((), ()))
contract_cols = (((1,), (1,)), ((), ()))
contract_inner = (((1,), (0,)), ((), ()))


def room(mebibytes):
    return pltpu.CompilerParams(vmem_limit_bytes=mebibytes * 1024 * 1024)


def rows_for_keys(keys):
    return 256 if keys <= 2048 else LANES


def room_for_keys(keys):
    return room(min(56, 4 + keys * rows_for_keys(keys) // 16384))


brief = pl.CostEstimate(flops=1, bytes_accessed=1, transcendentals=0)


def low_dot(left, right, dims=contract_inner):
    return lax.dot_general(left, right, dims, preferred_element_type=full_type)


def shape_of(shape, dtype=low_type):
    return jax.ShapeDtypeStruct(shape, dtype)


def whole_block(shape):
    return pl.BlockSpec(shape, lambda i: (0,) * len(shape))


def whole_call(kernel, outs, name, *args):
    return pl.pallas_call(
        kernel,
        grid=(1,),
        in_specs=[whole_block(each.shape) for each in args],
        out_specs=[whole_block(each.shape) for each in outs],
        out_shape=outs,
        compiler_params=room(12),
        cost_estimate=brief,
        name=name,
    )(*args)


def swap(value, axis, mask):
    pairs = [(source, source ^ mask) for source in range(lax.axis_size(axis))]
    return lax.ppermute(value, axis, pairs)


def bits_of(axis):
    return lax.axis_size(axis).bit_length() - 1


def has_bit(axis, mask):
    return lax.axis_index(axis) // mask % 2 == 1


def upward(axis):
    return [2**level for level in range(bits_of(axis))]


def downward(axis):
    return upward(axis)[::-1]


def offsets_of(masks):
    order = [0]
    for mask in masks:
        order = order + [at ^ mask for at in order]
    return order


def arrange(blocks, axis, masks):
    levels = bits_of(axis)
    cube = blocks.reshape((2,) * levels + blocks.shape[1:])
    for mask in masks:
        at = levels - mask.bit_length()
        cube = jnp.where(has_bit(axis, mask), jnp.flip(cube, at), cube)
    front = [levels - mask.bit_length() for mask in masks]
    cube = jnp.transpose(cube, front + list(range(levels, cube.ndim)))
    return cube.reshape(blocks.shape)


def tie(*values):
    return lax.optimization_barrier(values)


class Gather:
    def __init__(self, value, axis, masks):
        self.axis, self.masks = axis, list(masks)
        self.levels, self.shape = bits_of(axis), value.shape
        self.whole = value.reshape((1,) * self.levels + value.shape)

    def start(self, main):
        if self.masks:
            self.whole, main = tie(self.whole, main)
            self.other = swap(self.whole, self.axis, self.masks[0])
        return main

    def finish(self, main):
        if self.masks:
            mask = self.masks.pop(0)
            other, main = tie(self.other, main)
            at = self.levels - mask.bit_length()
            self.whole = jnp.where(
                has_bit(self.axis, mask),
                jnp.concatenate([other, self.whole], at),
                jnp.concatenate([self.whole, other], at),
            )
        return main

    def step(self, main):
        return self.start(self.finish(main))

    def drain(self, main):
        main = self.finish(main)
        while self.masks:
            main = self.finish(self.start(main))
        return main

    def value(self):
        return self.whole.reshape((-1,) + self.shape)


class Scatter:
    def __init__(self, keep, send, axis, masks):
        self.axis, self.masks = axis, list(masks)
        self.keep, self.send = keep, send

    def start(self, main):
        if self.masks:
            self.send, main = tie(self.send, main)
            self.other = swap(self.send, self.axis, self.masks[0])
        return main

    def finish(self, main):
        if self.masks:
            self.masks.pop(0)
            other, main = tie(self.other, main)
            if self.masks:
                self.keep, self.send = halve(self.keep, other)
            else:
                self.other = other
        return main

    def step(self, main):
        return self.start(self.finish(main))

    def drain(self, main):
        main = self.finish(main)
        while self.masks:
            main = self.finish(self.start(main))
        return main

    def value(self):
        return self.keep[0].astype(full_type) + self.other[0].astype(full_type)


def halve_kernel(keep_low, keep_high, other_low, other_high, low_ref, high_ref):
    for keep, other, out in (
        (keep_low, other_low, low_ref),
        (keep_high, other_high, high_ref),
    ):
        total = keep[...].astype(full_type) + other[...].astype(full_type)
        out[...] = total.astype(low_type)


def halve(keep, other):
    half = keep.shape[0] // 2
    block = (1,) + keep.shape[1:]
    low = pl.BlockSpec(block, lambda i: (i, 0, 0))
    high = pl.BlockSpec(block, lambda i: (half + i, 0, 0))
    return pl.pallas_call(
        halve_kernel,
        grid=(half,),
        in_specs=[low, high, low, high],
        out_specs=[low, low],
        out_shape=[shape_of((half,) + keep.shape[1:])] * 2,
        compiler_params=room(8),
        cost_estimate=brief,
        name="halve",
    )(keep, keep, other, other)


def rows_gather(block):
    blocks = [block]
    for mask in downward("mp"):
        blocks = blocks + [swap(each, "mp", mask) for each in blocks]
    return blocks


def rows_scatter(blocks):
    masks = upward("mp")
    terms = [[block] for block in blocks]
    for mask in masks:
        half = len(terms) // 2
        sends = [each[0] if len(each) == 1 else rows_fold(each) for each in terms[half:]]
        order = range(half)[::-1]
        got = {at: swap(sends[at], "mp", mask) for at in order}
        terms = [terms[at] + [got[at]] for at in range(half)]
    return terms[0]


def add_up(refs):
    total = refs[0][...].astype(full_type)
    for ref in refs[1:]:
        total = total + ref[...].astype(full_type)
    return total


def head_mask(width, head):
    lane = lax.broadcasted_iota(jnp.int32, (1, width), 1)
    return lane // HEAD_DIM == head


def only_head(rows, head):
    return jnp.where(head_mask(rows.shape[1], head), rows, jnp.zeros_like(rows))


def attend_forward_kernel(q_ref, k_ref, v_ref, segq_ref, segk_ref, o_ref, stat_ref):
    tile, width = q_ref.shape
    stat = jnp.broadcast_to(segq_ref[...], (LANES, tile)).T
    bias = jnp.where(stat[:, 0:1] == segk_ref[...], 0.0, neg_big)
    out = jnp.zeros((tile, width), full_type)
    lane = lax.broadcasted_iota(jnp.int32, (1, LANES), 1)
    queries = q_ref[...] * jnp.asarray(0.125, low_type)
    for head in range(width // HEAD_DIM):
        raw = low_dot(only_head(queries, head), k_ref[...], contract_cols) + bias
        top = jnp.max(raw, axis=1, keepdims=True)
        terms = jnp.exp(raw - top)
        total = jnp.sum(terms, axis=1, keepdims=True)
        mixed = low_dot(terms.astype(low_type), v_ref[...]) * (1.0 / total)
        out = jnp.where(head_mask(width, head), mixed, out)
        stat = jnp.where(lane == head, top + jnp.log(total), stat)
    o_ref[...] = out.astype(low_type)
    stat_ref[...] = stat.T[: stat_ref.shape[0]]


def attend_forward(query_key, value_rows, seg_rows, seg_keys):
    rows = seg_rows.shape[1]
    keys, width = value_rows.shape
    tile = rows_for_keys(keys)
    return pl.pallas_call(
        attend_forward_kernel,
        grid=(rows // tile,),
        in_specs=[
            pl.BlockSpec((tile, width), lambda i: (i, 0)),
            pl.BlockSpec((keys, width), lambda i: (0, 1)),
            pl.BlockSpec((keys, width), lambda i: (0, 0)),
            pl.BlockSpec((1, tile), lambda i: (0, i)),
            pl.BlockSpec((1, keys), lambda i: (0, 0)),
        ],
        out_specs=[
            pl.BlockSpec((tile, width), lambda i: (i, 0)),
            pl.BlockSpec((8, tile), lambda i: (0, i)),
        ],
        out_shape=[shape_of((rows, width)), shape_of((8, rows), full_type)],
        compiler_params=room_for_keys(keys),
        cost_estimate=brief,
        name="attend_forward",
    )(query_key, query_key, value_rows, seg_rows, seg_keys)


def attend_terms(q_ref, k_ref, v_ref, do_ref, o_ref, segk_ref, lse_ref):
    tile, width = q_ref.shape
    pad = jnp.zeros((LANES - lse_ref.shape[0], tile), full_type)
    lse = jnp.concatenate([lse_ref[...], pad], 0).T
    heads = width // HEAD_DIM
    bias = jnp.where(lse[:, heads : heads + 1] == segk_ref[...], 0.0, neg_big)
    queries = q_ref[...] * jnp.asarray(0.125, low_type)
    grads = do_ref[...]
    both = grads.astype(full_type) * o_ref[...].astype(full_type)
    for head in range(width // HEAD_DIM):
        q_head = only_head(queries, head)
        g_head = only_head(grads, head)
        delta = jnp.sum(only_head(both, head), axis=1, keepdims=True)
        raw = low_dot(q_head, k_ref[...], contract_cols)
        probs = jnp.exp(raw + (bias - lse[:, head : head + 1]))
        dprobs = low_dot(g_head, v_ref[...], contract_cols)
        dscore = (probs * (dprobs - delta)).astype(low_type)
        yield head, q_head, g_head, probs.astype(low_type), dscore


def attend_back(rows_of_q, part, keys, masks, sums, wants_dq, dq_parts=()):
    query_key, first_row, grads, attended, lse = rows_of_q
    value_rows, seg_keys, own = masks
    width = value_rows.shape[1]
    tile = rows_for_keys(keys)
    parts_of = 1 if part is None else 2
    steps = grads.shape[0] // tile // parts_of
    shift = steps if part == 1 else 0
    first = first_row // tile + shift
    closing = len(dq_parts) > 0

    def kernel(*refs):
        base, refs = refs[:7], refs[7:]
        q_ref, k_ref = base[:2]
        before, refs = (refs[:2], refs[2:]) if sums else (None, refs)
        parts, refs = refs[: len(dq_parts)], refs[len(dq_parts) :]
        if closing:
            dqk_out, dv_out, dk_sum, dv_sum = refs
        else:
            dk_sum, dv_sum = refs[:2]
        step = pl.program_id(0)

        @pl.when(step == 0)
        def _():
            dk_sum[...] = before[0][...] if sums else jnp.zeros_like(dk_sum)
            dv_sum[...] = before[1][...] if sums else jnp.zeros_like(dv_sum)

        dquery = jnp.zeros((tile, width), full_type)
        for head, q_head, g_head, probs, dscore in attend_terms(*base):
            if wants_dq:
                dquery = jnp.where(head_mask(width, head), low_dot(dscore, k_ref[...]), dquery)
            dk_sum[...] += low_dot(dscore[:, :own], q_head, contract_rows)
            dv_sum[...] += low_dot(probs[:, :own], g_head, contract_rows)
        if wants_dq:
            refs[2][...] = (dquery * 0.125).astype(low_type)
        if closing:

            @pl.when(step == steps - 1)
            def _():
                rows = own // len(parts)
                for at, ref in enumerate(parts):
                    dqk_out[at * rows : (at + 1) * rows, :width] = ref[...]
                dqk_out[:, width:] = dk_sum[...].astype(low_type)
                dv_out[...] = dv_sum[...].astype(low_type)

    tile_rows = pl.BlockSpec((tile, width), lambda i: (shift + i, 0))
    held = whole_block((own, width))
    in_specs = [
        pl.BlockSpec((tile, width), lambda i: (first + i, 0)),
        pl.BlockSpec((keys, width), lambda i: (0, 1)),
        pl.BlockSpec((keys, width), lambda i: (0, 0)),
        tile_rows,
        tile_rows,
        pl.BlockSpec((1, keys), lambda i: (0, 0)),
        pl.BlockSpec((8, tile), lambda i: (0, shift + i)),
    ]
    args = [query_key, query_key, value_rows, grads, attended, seg_keys, lse]
    if sums:
        in_specs, args = in_specs + [held, held], args + list(sums)
    in_specs = in_specs + [whole_block(each.shape) for each in dq_parts]
    args = args + list(dq_parts)
    if closing:
        outs = [shape_of((own, 2 * width)), shape_of((own, width))]
        out_specs = [whole_block(each.shape) for each in outs]
        scratch = [pltpu.VMEM((own, width), full_type)] * 2
    else:
        outs = [shape_of((own, width), full_type)] * 2
        out_specs, scratch = [held, held], []
        if wants_dq:
            outs = outs + [shape_of((steps * tile, width))]
            out_specs = out_specs + [pl.BlockSpec((tile, width), lambda i: (i, 0))]
    return pl.pallas_call(
        kernel,
        grid=(steps,),
        in_specs=in_specs,
        out_specs=out_specs,
        out_shape=outs,
        scratch_shapes=scratch,
        compiler_params=room_for_keys(keys),
        cost_estimate=brief,
        name="attend_back",
    )(*args)


def lanes_of(ref):
    return jnp.concatenate([ref[at] for at in range(ref.shape[0])], axis=1)


def rows_of(refs):
    return jnp.concatenate([ref[...] for ref in refs], axis=0)


def gather_blocks(block_refs, rows):
    @pl.when(pl.program_id(0) == 0)
    def _():
        span = block_refs[0].shape[0]
        for at, ref in enumerate(block_refs):
            rows[at * span : (at + 1) * span, :] = ref[...]


def feed_up_kernel(*refs):
    *row_refs, up_ref, g_ref, slope_ref, rows = refs
    gather_blocks(row_refs, rows)
    whole = low_dot(rows[...], up_ref[...])
    span = row_refs[0].shape[0]
    for at in range(len(row_refs)):
        place = pl.ds(at * span, span)
        inner = whole[at * span : (at + 1) * span]
        normal = 0.5 * (1.0 + lax.erf(inner * 0.7071067811865476))
        g_ref[place, :] = (inner * normal).astype(low_type)
        slope = normal + inner * jnp.exp(-0.5 * inner * inner) * 0.3989422804014327
        slope_ref[place, :] = slope.astype(low_type)


def feed_up(blocks, w_up, units):
    own, width = blocks[0].shape
    rows = own * len(blocks)
    tile = 256
    return pl.pallas_call(
        feed_up_kernel,
        grid=(units // tile,),
        in_specs=[pl.BlockSpec((own, width), lambda i: (0, 0))] * len(blocks)
        + [pl.BlockSpec((width, tile), lambda i: (0, i))],
        out_specs=[pl.BlockSpec((rows, tile), lambda i: (0, i))] * 2,
        out_shape=[shape_of((rows, units))] * 2,
        scratch_shapes=[pltpu.VMEM((rows, width), low_type)],
        compiler_params=room(10),
        cost_estimate=brief,
        name="feed_up",
    )(*blocks, w_up)


def store_blocks(total, block_refs):
    rows = total.shape[0] // len(block_refs)
    for at, ref in enumerate(block_refs):
        ref[...] = total[at * rows : (at + 1) * rows].astype(ref.dtype)


def blocks_of(rows, width):
    count = lax.axis_size("mp")
    kept = [shape_of((rows // count, width), full_type)] * (count // 2)
    return kept + [shape_of((rows // count, width))] * (count // 2)


def feed_down_kernel(g_ref, down_ref, *block_refs):
    store_blocks(low_dot(g_ref[...], lanes_of(down_ref)), block_refs)


def feed_down(active, w_down):
    rows, units = active.shape
    blocks, _, lanes = w_down.shape
    tile = 2
    return pl.pallas_call(
        feed_down_kernel,
        grid=(blocks // tile,),
        in_specs=[
            pl.BlockSpec((rows, units), lambda i: (0, 0)),
            pl.BlockSpec((tile, units, lanes), lambda i: (i, 0, 0)),
        ],
        out_specs=[
            pl.BlockSpec((each.shape[0], tile * lanes), lambda i: (0, i))
            for each in blocks_of(rows, blocks * lanes)
        ],
        out_shape=blocks_of(rows, blocks * lanes),
        compiler_params=room(10),
        cost_estimate=brief,
        name="feed_down",
    )(active, w_down)


def feed_inner_kernel(*refs):
    *row_refs, down_ref, slope_ref, dz_ref, rows = refs
    gather_blocks(row_refs, rows)
    dactive = low_dot(rows[...], lanes_of(down_ref), contract_cols)
    dz_ref[...] = (dactive * slope_ref[...].astype(full_type)).astype(low_type)


def feed_inner(blocks, w_down, slope):
    own, width = blocks[0].shape
    rows, units = slope.shape
    tile = 256
    lanes = w_down.shape[2]
    return pl.pallas_call(
        feed_inner_kernel,
        grid=(units // tile,),
        in_specs=[pl.BlockSpec((own, width), lambda i: (0, 0))] * len(blocks)
        + [
            pl.BlockSpec((w_down.shape[0], tile, lanes), lambda i: (0, i, 0)),
            pl.BlockSpec((rows, tile), lambda i: (0, i)),
        ],
        out_specs=pl.BlockSpec((rows, tile), lambda i: (0, i)),
        out_shape=shape_of((rows, units)),
        scratch_shapes=[pltpu.VMEM((rows, width), low_type)],
        compiler_params=room(10),
        cost_estimate=brief,
        name="feed_inner",
    )(*blocks, w_down, slope)


def feed_back_kernel(dz_ref, up_ref, *block_refs):
    store_blocks(low_dot(dz_ref[...], up_ref[...], contract_cols), block_refs)


def feed_back(dinner, w_up):
    rows, units = dinner.shape
    width = w_up.shape[0]
    tile = 256
    return pl.pallas_call(
        feed_back_kernel,
        grid=(width // tile,),
        in_specs=[
            pl.BlockSpec((rows, units), lambda i: (0, 0)),
            pl.BlockSpec((tile, units), lambda i: (i, 0)),
        ],
        out_specs=[
            pl.BlockSpec((each.shape[0], tile), lambda i: (0, i))
            for each in blocks_of(rows, width)
        ],
        out_shape=blocks_of(rows, width),
        compiler_params=room(10),
        cost_estimate=brief,
        name="feed_back",
    )(dinner, w_up)


def late_forward_kernel(*refs):
    *e_refs, q_ref, live_ref, sharp_ref, soft_ref, e_rows = refs
    gather_blocks(e_refs, e_rows)
    blocks = soft_ref.shape[0]
    per = blocks // len(e_refs)
    whole = low_dot(e_rows[...], q_ref[...], contract_cols)
    rows = e_refs[0].shape[0]
    for at in range(len(e_refs)):
        place = pl.ds(at * rows, rows)
        sharp = whole[at * rows : (at + 1) * rows] * 2.0 + live_ref[place, :]
        sharp_ref[place, :] = sharp
        cube = sharp.reshape(per, rows // per, sharp.shape[1])
        top = jnp.max(cube, axis=1)
        total = jnp.sum(jnp.exp(cube - top[:, None, :]), axis=1)
        soft = jnp.where(top > 0.5 * neg_big, top + jnp.log(total), neg_big)
        soft_ref[pl.ds(at * per, per), :] = soft


def late_forward(e_blocks, queries, live_bias, blocks):
    own, width = e_blocks[0].shape
    rows = own * len(e_blocks)
    count = queries.shape[0]
    tile = 512
    return pl.pallas_call(
        late_forward_kernel,
        grid=(count // tile,),
        in_specs=[pl.BlockSpec((own, width), lambda i: (0, 0))] * len(e_blocks)
        + [
            pl.BlockSpec((tile, width), lambda i: (i, 0)),
            pl.BlockSpec((rows, 1), lambda i: (0, 0)),
        ],
        out_specs=[
            pl.BlockSpec((rows, tile), lambda i: (0, i)),
            pl.BlockSpec((blocks, tile), lambda i: (0, i)),
        ],
        out_shape=[shape_of((rows, count), full_type), shape_of((blocks, count), full_type)],
        scratch_shapes=[pltpu.VMEM((rows, width), low_type)],
        compiler_params=room(14),
        cost_estimate=brief,
        name="late_forward",
    )(*e_blocks, queries, live_bias)


def join_soft(soft, far, same):
    top = soft
    for at in range(far.shape[0]):
        top = jnp.maximum(top, far[at])
    total = jnp.exp(soft - top)
    for at in range(far.shape[0]):
        total = total + jnp.exp(far[at] - top)
    blocks = soft.shape[0]
    most = jnp.full(soft.shape, neg_big, full_type)
    for at in range(blocks):
        shared = same[:, at : at + 1] > 0.0
        most = jnp.maximum(most, jnp.where(shared, top[at : at + 1], neg_big))
    sums = jnp.zeros(soft.shape, full_type)
    for at in range(blocks):
        shared = same[:, at : at + 1] > 0.0
        term = jnp.where(shared, top[at : at + 1], neg_big)
        sums = sums + jnp.exp(term - most) * total[at : at + 1]
    return most + jnp.log(sums)


def late_backward_kernel(
    sharp_ref, soft_ref, far_ref, same_ref, place_ref, weight_ref, q_ref, *refs
):
    *block_refs, score_ref, total = refs
    step = pl.program_id(0)
    blocks = soft_ref.shape[0]
    rows, tile = sharp_ref.shape
    soft = join_soft(soft_ref[...], far_ref[...], same_ref[...])
    cube = sharp_ref[...].reshape(blocks, rows // blocks, tile)
    pulled = weight_ref[...][:, None, :] * jnp.exp(cube - soft[:, None, :])
    term = low_dot(pulled.reshape(rows, tile).astype(low_type), q_ref[...])
    query = lax.broadcasted_iota(jnp.int32, (tile, score_ref.shape[0]), 0) // QLEN
    count = lax.broadcasted_iota(jnp.int32, (tile, score_ref.shape[0]), 1)
    pool = jnp.where(query == count, 0.5 / QLEN, 0.0)
    exact = lax.Precision.HIGHEST
    means = lax.dot_general(pool, soft, (((0,), (1,)), ((), ())), precision=exact)
    score_ref[...] = lax.dot_general(means, place_ref[...], contract_inner, precision=exact)

    @pl.when(step == 0)
    def _():
        total[...] = term

    @pl.when(step > 0)
    def _():
        total[...] += term

    @pl.when(step == pl.num_programs(0) - 1)
    def _():
        store_blocks(total[...], block_refs)


def late_backward(sharp, soft, far, same, place, weight, queries):
    rows, count = sharp.shape
    width = queries.shape[1]
    blocks = soft.shape[0]
    tile = min(1024, count)
    outs = blocks_of(rows, width)
    return pl.pallas_call(
        late_backward_kernel,
        grid=(count // tile,),
        in_specs=[
            pl.BlockSpec((rows, tile), lambda i: (0, i)),
            pl.BlockSpec((blocks, tile), lambda i: (0, i)),
            pl.BlockSpec((far.shape[0], blocks, tile), lambda i: (0, 0, i)),
            whole_block(same.shape),
            whole_block(place.shape),
            pl.BlockSpec((blocks, tile), lambda i: (0, i)),
            pl.BlockSpec((tile, width), lambda i: (i, 0)),
        ],
        out_specs=[whole_block(each.shape) for each in outs]
        + [pl.BlockSpec((tile // QLEN, NPASS), lambda i: (i, 0))],
        out_shape=outs + [shape_of((count // QLEN, NPASS), full_type)],
        scratch_shapes=[pltpu.VMEM((rows, width), full_type)],
        compiler_params=room(24),
        cost_estimate=brief,
        name="late_backward",
    )(sharp, soft, far, same, place, weight, queries)


def norm_stats(values):
    centre = values - jnp.mean(values, axis=-1, keepdims=True)
    spread = jnp.mean(centre * centre, axis=-1, keepdims=True)
    scale = lax.rsqrt(spread + 1e-05)
    return centre * scale, scale


def norm_backward(unit, scale, gain, grad):
    dunit = grad * gain
    dvalues = scale * (
        dunit
        - jnp.mean(dunit, axis=-1, keepdims=True)
        - unit * jnp.mean(dunit * unit, axis=-1, keepdims=True)
    )
    return (
        dvalues,
        jnp.sum(grad * unit, axis=0, keepdims=True),
        jnp.sum(grad, axis=0, keepdims=True),
    )


def norm_one_kernel(*refs):
    *terms, norm_ref, h_ref, low_ref, unit_ref, scale_ref = refs
    unit, scale = norm_stats(add_up(terms))
    normed = unit * norm_ref[0:1] + norm_ref[1:2]
    h_ref[...] = normed
    low_ref[...] = normed.astype(low_type)
    unit_ref[...] = unit
    scale_ref[...] = scale


def lanes_at(order_ref, at, span):
    return pl.ds(pl.multiple_of(order_ref[at] * span, span), span)


def norm_two_kernel(order_ref, *refs):
    *rest, low_ref, unit_ref, scale_ref, e_ref, elow_ref, inv_ref = refs
    parts = order_ref.shape[0]
    *terms, norm_ref = rest[:-parts]
    col_refs = rest[-parts:]
    unit, scale = norm_stats(add_up(terms))
    normed_low = (unit * norm_ref[2:3] + norm_ref[3:4]).astype(low_type)
    low_ref[...] = normed_low
    unit_ref[...] = unit
    scale_ref[...] = scale
    span = col_refs[0].shape[1]
    squares = 0.0
    for at, ref in enumerate(col_refs):
        projected = low_dot(normed_low, ref[...])
        e_ref[:, lanes_at(order_ref, at, span)] = projected
        squares = squares + jnp.sum(projected * projected, axis=-1, keepdims=True)
    inv = lax.rsqrt(squares + 1e-06)
    embedded = e_ref[...] * inv
    e_ref[...] = embedded
    elow_ref[...] = embedded.astype(low_type)
    inv_ref[...] = inv


def norm_two_back_kernel(order_ref, *refs):
    *rest, own_ref, far_ref, dr_ref, low_ref, g_ref, du_ref = refs
    parts = order_ref.shape[0]
    *terms, norm_ref, unit_ref, scale_ref, e_ref, inv_ref = rest[:-parts]
    col_refs = rest[-parts:]
    dembed = add_up(terms)
    embedded = e_ref[...]
    along = jnp.sum(embedded * dembed, axis=-1, keepdims=True)
    du_ref[...] = (inv_ref[...] * (dembed - embedded * along)).astype(low_type)
    span = col_refs[0].shape[1]
    dnormed = 0.0
    for at, ref in enumerate(col_refs):
        dproj = du_ref[:, lanes_at(order_ref, at, span)]
        dnormed = dnormed + low_dot(dproj, ref[...], contract_cols)
    half = own_ref.shape[1]
    mine = order_ref[0] // (parts // 2)
    own_ref[...] = du_ref[:, pl.ds(pl.multiple_of(mine * half, half), half)]
    far_ref[...] = du_ref[:, pl.ds(pl.multiple_of((1 - mine) * half, half), half)]
    dresid, dgain, dshift = norm_backward(
        unit_ref[...], scale_ref[...], norm_ref[2:3], dnormed
    )
    dr_ref[...] = dresid
    low_ref[...] = dresid.astype(low_type)
    g_ref[...] = jnp.concatenate([dgain, dshift], 0)


def split_sums(sums):
    high = sums.astype(low_type).astype(full_type)
    zeros = jnp.zeros((SPARE - 8, sums.shape[1]), full_type)
    return jnp.concatenate([high, sums - high, zeros], 0).astype(low_type)


def norm_one_back_kernel(*refs):
    *terms, norm_ref, unit_ref, scale_ref, two_ref, dr_ref, pack_ref = refs
    dresid, dgain, dshift = norm_backward(
        unit_ref[...], scale_ref[...], norm_ref[0:1], add_up(terms)
    )
    dr_ref[...] = dresid
    rows = dresid.shape[0]
    pack_ref[0:rows, :] = dresid.astype(low_type)
    pack_ref[rows : rows + SPARE, :] = split_sums(
        jnp.concatenate([dgain, dshift, two_ref[...]], 0)
    )


def fold_kernel(*refs):
    *terms, low_ref = refs
    low_ref[...] = add_up(terms).astype(low_type)


def rows_fold(terms):
    return whole_call(fold_kernel, [shape_of(terms[0].shape)], "fold", *terms)[0]


def mix_kernel(o_ref, out_ref, *block_refs):
    rows = o_ref.shape[1]
    weight = jnp.concatenate([out_ref[at, 0:rows, :] for at in range(out_ref.shape[0])], axis=1)
    store_blocks(low_dot(o_ref[...], weight), block_refs)


def unmix_kernel(*refs):
    *packs, out_ref, do_ref, sums_ref = refs
    rows = do_ref.shape[1]
    weight = jnp.concatenate([out_ref[at, 0:rows, :] for at in range(out_ref.shape[0])], axis=1)
    own = packs[0].shape[0] - SPARE
    sums = jnp.zeros((8, weight.shape[1]), full_type)
    mixed = jnp.concatenate([ref[0:own, :] for ref in packs], axis=0)
    do_ref[...] = low_dot(mixed, weight, contract_cols).astype(low_type)
    for ref in packs:
        sums = sums + ref[own : own + SPARE, :].astype(full_type)[:8]
    sums_ref[...] = split_sums(sums[:4] + sums[4:])


def block_order(masks):
    return lax.axis_index("dp") ^ jnp.asarray(offsets_of(masks[::-1]), jnp.int32)


def ordered_call(kernel, outs, scratch, name, order, *args, grant=20):
    return pl.pallas_call(
        kernel,
        grid=(1,),
        in_specs=[pl.BlockSpec(memory_space=pltpu.SMEM)]
        + [whole_block(each.shape) for each in args],
        out_specs=[whole_block(each.shape) for each in outs],
        out_shape=outs,
        scratch_shapes=[pltpu.VMEM(*each) for each in scratch],
        compiler_params=room(grant),
        cost_estimate=brief,
        name=name,
    )(order, *args)


def stored(place_ref, left, right):
    turned = left.T
    cols = right.shape[1]
    for start in range(0, cols, 256):
        stop = min(start + 256, cols)
        place_ref[:, start:stop] = low_dot(turned, right[:, start:stop]).astype(low_type)


def deal(order_ref, keep_ref, send_ref, write):
    half = keep_ref.shape[0]
    for at in range(2 * half):
        write(keep_ref.at[at] if at < half else send_ref.at[at - half], order_ref[at])


def rows_in(ref, block, count):
    return ref[pl.ds(pl.multiple_of(block * count, count), count), :]


def lanes_in(ref, block):
    return ref[:, pl.ds(pl.multiple_of(block * LANES, LANES), LANES)]


def halves_like(count, block):
    return [shape_of((count // 2,) + block)] * 2


def grad_down_kernel(order_ref, active_ref, *refs):
    *row_refs, keep_ref, send_ref, total = refs
    stored(total, active_ref[...], rows_of(row_refs))

    def write(ref, block):
        ref[...] = lanes_in(total, block)

    deal(order_ref, keep_ref, send_ref, write)


def grad_down(active, row_blocks, masks):
    count = lax.axis_size("dp")
    units, width = active.shape[1], row_blocks[0].shape[1]
    if width // count == LANES:
        return ordered_call(
            grad_down_kernel,
            halves_like(count, (units, LANES)),
            [((units, width), low_type)],
            "grad_down",
            block_order(masks),
            active,
            *row_blocks,
        )
    whole = low_dot(active, jnp.concatenate(row_blocks, 0), contract_rows).astype(low_type)
    return halves(arrange(jnp.swapaxes(whole.reshape(units, count, -1), 0, 1), "dp", masks))


def halves(blocks):
    half = blocks.shape[0] // 2
    return blocks[:half], blocks[half:]


def grad_up_kernel(order_ref, dinner_ref, *refs):
    *row_refs, keep_ref, send_ref, total = refs
    parts = len(row_refs) // 3
    units = dinner_ref.shape[1]
    block_rows = keep_ref.shape[1]
    cols = keep_ref.shape[2] - units
    stored(total.at[:, 0:units], rows_of(row_refs[:parts]), dinner_ref[...])
    mine = order_ref[order_ref.shape[0] - 1] % (row_refs[-1].shape[1] // cols)
    mine = pl.ds(pl.multiple_of(mine * cols, cols), cols)
    dproj = jnp.concatenate([ref[:, mine] for ref in row_refs[2 * parts :]], axis=0)
    stored(total.at[:, units:], rows_of(row_refs[parts : 2 * parts]), dproj)

    def write(ref, block):
        ref[...] = rows_in(total, block, block_rows)

    deal(order_ref, keep_ref, send_ref, write)


def grad_up(dinner, one_blocks, two_blocks, du_blocks, col_width, masks):
    count = lax.axis_size("dp")
    units, width = dinner.shape[1], one_blocks[0].shape[1]
    column = lax.axis_index("mp")
    rows = width // count
    if rows == LANES:
        order = jnp.concatenate([block_order(masks), column.reshape(1)])
        return ordered_call(
            grad_up_kernel,
            halves_like(count, (rows, units + col_width)),
            [((width, units + col_width), low_type)],
            "grad_up",
            order,
            dinner,
            *one_blocks,
            *two_blocks,
            *du_blocks,
        )
    column = column % (du_blocks[0].shape[1] // col_width)
    dproj = lax.dynamic_slice_in_dim(
        jnp.concatenate(du_blocks, 0), column * col_width, col_width, 1
    )
    up = low_dot(jnp.concatenate(one_blocks, 0), dinner, contract_rows)
    col = low_dot(jnp.concatenate(two_blocks, 0), dproj, contract_rows)
    whole = jnp.concatenate([up, col], 1).astype(low_type)
    return halves(arrange(whole.reshape(count, rows, -1), "dp", masks))


def grad_qk_kernel(order_ref, left_ref, right_ref, keep_ref, send_ref, total):
    block_rows = keep_ref.shape[1]
    stored(total, left_ref[...], right_ref[...])

    def write(ref, block):
        ref[...] = rows_in(total, block, block_rows)

    deal(order_ref, keep_ref, send_ref, write)


def grad_qk(left, right, masks):
    count = lax.axis_size("dp")
    width, cols = left.shape[1], right.shape[1]
    rows = width // count
    if rows == LANES:
        return ordered_call(
            grad_qk_kernel,
            halves_like(count, (rows, cols)),
            [((width, cols), low_type)],
            "grad_qk",
            block_order(masks),
            left,
            right,
        )
    whole = low_dot(left, right, contract_rows).astype(low_type)
    return halves(arrange(whole.reshape(count, rows, cols), "dp", masks))


def grad_vo_kernel(order_ref, hidden_ref, dv_ref, o_ref, *refs):
    *packs, sums_ref, keep_ref, send_ref, total_v, total_o = refs
    rows = packs[0].shape[0] - SPARE
    cols = dv_ref.shape[1]
    heads = o_ref.shape[1]
    stored(total_v, hidden_ref[...], dv_ref[...])
    mixed = jnp.concatenate([ref[0:rows, :] for ref in packs], axis=0)
    stored(total_o.at[0:heads, :], o_ref[...], mixed)
    total_o[heads : heads + SPARE, :] = sums_ref[...]

    def write(ref, block):
        value = rows_in(total_v, block, LANES)
        for at in range(cols // LANES):
            ref[at * LANES : (at + 1) * LANES, :] = value[:, at * LANES : (at + 1) * LANES]
        ref[cols:, :] = lanes_in(total_o, block)

    deal(order_ref, keep_ref, send_ref, write)


def finish_pair_kernel(keep_ref, other_ref, left_ref, right_ref):
    total = keep_ref[...].astype(full_type) + other_ref[...].astype(full_type)
    cols = left_ref.shape[1]
    left_ref[...] = total[:, :cols]
    right_ref[...] = total[:, cols:]


def finish_pair(scatter, cols):
    rows, both = scatter.keep.shape[1:]
    outs = [shape_of((rows, cols), full_type), shape_of((rows, both - cols), full_type)]
    return whole_call(finish_pair_kernel, outs, "finish_pair", scatter.keep[0], scatter.other[0])


def finish_vo_kernel(keep_ref, other_ref, value_ref, out_ref, *norm_refs):
    total = keep_ref[...].astype(full_type) + other_ref[...].astype(full_type)
    rows, cols = value_ref.shape
    row = 0
    for at in range(0, cols, LANES):
        value_ref[:, at : at + LANES] = total[row : row + rows]
        row += rows
    out_ref[...] = total[row : row + out_ref.shape[0]]
    row += out_ref.shape[0]
    for at, ref in enumerate(norm_refs):
        ref[...] = total[row + at : row + at + 1] + total[row + 4 + at : row + 5 + at]


def finish_vo(keep, other, value_shape, out_shape):
    rows, cols = out_shape
    if cols == LANES:
        outs = [shape_of(value_shape, full_type), shape_of(out_shape, full_type)]
        outs = outs + [shape_of((1, cols), full_type)] * 4
        value, out, *norms = whole_call(finish_vo_kernel, outs, "finish_vo", keep, other)
        return value, out, norms
    total = keep.astype(full_type) + other.astype(full_type)
    value, out = unpack_vo(total, *value_shape, (rows + SPARE, cols))
    return value, out[:rows], out[rows : rows + 4] + out[rows + 4 : rows + 8]


def pack_vo(value, out):
    cols = value.shape[-1]
    parts = [value[..., at : at + LANES] for at in range(0, cols, LANES)]
    return jnp.concatenate(parts + [out.reshape(out.shape[:-2] + (-1, LANES))], axis=-2)


def unpack_vo(packed, rows, cols, out_shape):
    high = rows * cols // LANES
    value = jnp.concatenate(
        [packed[..., at : at + rows, :] for at in range(0, high, rows)], axis=-1
    )
    return value, packed[..., high:, :].reshape(packed.shape[:-2] + out_shape)


def grad_vo(hidden, dvalue, attended, packs, sums, masks):
    count = lax.axis_size("dp")
    width, cols = hidden.shape[1], dvalue.shape[1]
    heads = attended.shape[1]
    rows = width // count
    if rows == LANES:
        block = (cols * rows // LANES + heads + SPARE, LANES)
        return ordered_call(
            grad_vo_kernel,
            halves_like(count, block),
            [((width, cols), low_type), ((heads + SPARE, width), low_type)],
            "grad_vo",
            block_order(masks),
            hidden,
            dvalue,
            attended,
            *packs,
            sums,
        )
    value = low_dot(hidden, dvalue, contract_rows).astype(low_type).reshape(count, rows, cols)
    mixed = jnp.concatenate([each[:-SPARE] for each in packs], 0)
    out = low_dot(attended, mixed, contract_rows).astype(low_type)
    out = jnp.concatenate([out, sums], 0).reshape(heads + SPARE, count, rows)
    return halves(arrange(pack_vo(value, jnp.swapaxes(out, 0, 1)), "dp", masks))


def to_lanes(blocks):
    if blocks.shape[2] == LANES:
        return blocks
    whole = jnp.swapaxes(blocks, 0, 1).reshape(blocks.shape[1], -1, LANES)
    return jnp.swapaxes(whole, 0, 1)


def place_kernel(at_ref, *refs):
    *blocks, out_ref = refs
    rows = blocks[0].shape[0]
    for at, ref in enumerate(blocks):
        start = pl.multiple_of(at_ref[at] * rows, rows)
        out_ref[pl.ds(start, rows), :] = ref[...].astype(full_type)


def place_rows(order, blocks):
    rows, width = blocks[0].shape
    outs = [shape_of((rows * len(blocks), width), full_type)]
    return ordered_call(place_kernel, outs, [], "place_rows", order, *blocks)[0]


def unproject_kernel(dqk_ref, dv_ref, a_ref, b_ref, *block_refs):
    total = low_dot(dqk_ref[...], a_ref[...], contract_cols)
    store_blocks(total + low_dot(dv_ref[...], b_ref[...], contract_cols), block_refs)


def unproject(dqk, dvalue, w_qk, w_v):
    outs = blocks_of(dqk.shape[0], w_qk.shape[0])
    return whole_call(unproject_kernel, outs, "unproject", dqk, dvalue, w_qk, w_v)


def fold_pair_kernel(keep_ref, got_ref, *low_refs):
    total = keep_ref[...] + got_ref[...].astype(full_type)
    rows = low_refs[0].shape[0]
    for at, ref in enumerate(low_refs):
        ref[...] = total[at * rows : (at + 1) * rows].astype(low_type)


def close_kernel(*refs):
    *terms, low_far, high_far, out_ref = refs
    total = add_up(terms)
    half = low_far.shape[0]
    for at, ref in enumerate((low_far, high_far)):
        place = pl.ds(at * half, half)
        part = total[at * half : (at + 1) * half] + ref[...].astype(full_type)
        out_ref[place, :] = part.astype(low_type)


def pack_kernel(order_ref, *refs):
    hidden_ref, q_ref, k_ref, v_ref, o_ref, up_ref, col_ref, *norm_refs = refs[:11]
    a_out, u_out, b_out, own_out, block_out = refs[11:]
    heads, units = q_ref.shape[1], up_ref.shape[1]
    a_out[:, :heads] = q_ref[...]
    a_out[:, heads:] = k_ref[...]
    u_out[:, :units] = up_ref[...]
    u_out[:, units:] = col_ref[...]
    row = 0
    for at in range(0, heads, LANES):
        b_out[row : row + v_ref.shape[0], :] = v_ref[:, at : at + LANES]
        row += v_ref.shape[0]
    b_out[row : row + o_ref.shape[0], :] = o_ref[...]
    row += o_ref.shape[0]
    norms = [ref[...].astype(full_type).reshape(1, -1) for ref in norm_refs]
    norms = jnp.concatenate(norms + [jnp.zeros((SPARE - 4, LANES), full_type)], axis=0)
    b_out[row : row + SPARE, :] = norms.astype(low_type)
    parts = order_ref.shape[0]
    rows = hidden_ref.shape[0] // parts
    for at in range(parts):
        own_out[at * rows : (at + 1) * rows, :] = rows_in(hidden_ref, order_ref[at], rows)
    block_out[...] = own_out[0:rows, :]


def pack_inputs(order, hidden, w_query, w_key, w_value, w_out, w_up, w_colbert, *norms):
    rows, heads = w_query.shape
    span = hidden.shape[0] // order.shape[0]
    if w_out.shape[1] == LANES and rows == LANES:
        packed = (rows * heads // LANES + w_out.shape[0] + SPARE, LANES)
        outs = [
            shape_of((rows, 2 * heads)),
            shape_of((rows, w_up.shape[1] + w_colbert.shape[1])),
            shape_of(packed),
            shape_of(hidden.shape),
            shape_of((span, hidden.shape[1])),
        ]
        args = (hidden, w_query, w_key, w_value, w_out, w_up, w_colbert) + norms
        return ordered_call(pack_kernel, outs, [], "pack", order, *args, grant=60)
    norms = jnp.concatenate([jnp.stack(norms), jnp.zeros((SPARE - 4, w_out.shape[1]), low_type)], 0)
    blocks = [
        lax.dynamic_slice_in_dim(hidden, order[at] * span, span, 0)
        for at in range(order.shape[0])
    ]
    return (
        jnp.concatenate([w_query, w_key], axis=1),
        jnp.concatenate([w_up, w_colbert], axis=1),
        pack_vo(w_value, jnp.concatenate([w_out, norms], axis=0)),
        jnp.concatenate(blocks),
        blocks[0],
    )


def body(
    hidden_in,
    w_query,
    w_key,
    w_value,
    w_out,
    w_up,
    w_down,
    w_colbert,
    norm1_gain,
    norm1_shift,
    norm2_gain,
    norm2_shift,
    queries,
    passage,
    live,
    score_grad,
):
    tok_rows, width = hidden_in.shape
    device = lax.axis_index("dp")
    column = lax.axis_index("mp")
    dp_size = lax.axis_size("dp")
    mp_size = lax.axis_size("mp")
    group_size = dp_size // NBUCKET
    group_levels = group_size.bit_length() - 1
    own_rows = tok_rows // mp_size
    head_width = w_query.shape[1]
    dp_up, dp_down = upward("dp"), downward("dp")
    turned = dp_up[:1] + dp_down[:-1]
    row_order = offsets_of(downward("mp"))

    def ordered(value, owner, span=own_rows):
        return jnp.concatenate(
            [
                lax.dynamic_slice_in_dim(value, (owner * mp_size + (column ^ at)) * span, span, 0)
                for at in row_order
            ]
        )

    def group_gather(value):
        for level in range(group_levels):
            value = jnp.concatenate([value, swap(value, "dp", 2**level)], 0)
        return value

    across = dp_up[-1:] + dp_up[:-1]
    turned_back, across_back = turned[::-1], across[::-1]
    col_order = column ^ jnp.asarray(row_order, jnp.int32)
    norms = (norm1_gain, norm1_shift, norm2_gain, norm2_shift)
    out_shape = (w_out.shape[0] + SPARE, w_out.shape[1])
    packed_a, packed_u, packed_b, hidden_own, own_hidden = pack_inputs(
        col_order, hidden_in, w_query, w_key, w_value, w_out, w_up, w_colbert, *norms
    )
    pack_a = Gather(packed_a, "dp", dp_down)
    pack_u = Gather(packed_u, "dp", dp_down)
    pack_b = Gather(packed_b, "dp", dp_down)
    pack_d = Gather(w_down, "dp", turned)

    main = (hidden_own, own_hidden)
    main = pack_a.start(main)
    main = pack_b.start(main)
    main = pack_u.start(main)
    main = pack_d.start(main)
    others = group_gather(main[1][None])[1:]
    seg_own = ordered(passage, device)
    live_own = ordered(live, device)
    seg_others = jnp.concatenate([ordered(passage, device ^ at) for at in range(1, group_size)])
    live_others = jnp.concatenate([ordered(live, device ^ at) for at in range(1, group_size)])
    slot_own = jnp.where(live_own == 1, seg_own, -1)
    slot_keys = jnp.concatenate([slot_own, jnp.where(live_others == 1, seg_others, -1)])
    seg_row = seg_own.astype(full_type)[None, :]
    slot_row = slot_keys.astype(full_type)[None, :]
    blocks = 2 ** (NBUCKET - 1)
    seg_block = seg_own.reshape(blocks, -1)[:, 0]
    live_bias = jnp.where(live_own == 1, 0.0, neg_big)[:, None]
    same = seg_block[:, None] == seg_block[None, :]
    passages = jnp.arange(NPASS, dtype=jnp.int32)
    place = (seg_block[:, None] == passages[None, :]).astype(full_type)
    grad_block = jnp.sum(place[:, None, :] * score_grad[None], axis=2)
    weight = jnp.repeat(grad_block / QLEN, QLEN, axis=1)
    same = same.astype(full_type)
    place = place / jnp.sum(same, axis=1, keepdims=True)
    slot_own = slot_own.astype(full_type)[None, :]
    early = (seg_row, slot_own, slot_row, live_bias, weight, same, place)
    early, main = tie(early, main)
    seg_row, slot_own, slot_row, live_bias, weight, same, place = early
    main = pack_a.step(main)
    main = pack_b.step(main)
    others, main = tie(others, main)
    far_others = swap(others, "mp", 2)
    main = pack_d.finish(main)
    main = pack_u.step(main)
    main = pack_d.start(main)
    main = pack_a.step(main)
    main = pack_b.step(main)
    far_others, main = tie(far_others, main)
    main = pack_u.step(main)
    others = [others, far_others]
    others = others + [swap(each, "mp", 1) for each in others]
    others = jnp.stack(others, 1).reshape(-1, width)
    hidden_own, own_hidden = main
    hidden_all = jnp.concatenate([hidden_own, others], 0)
    main = (hidden_own, own_hidden, hidden_all)
    main = pack_a.drain(main)
    full_a = pack_a.value().reshape(width, -1)
    full_a, main = tie(full_a, main)
    hidden_own, own_hidden, hidden_all = main

    query_key = low_dot(hidden_all, full_a).astype(low_type)
    main = (query_key, hidden_all)
    main = pack_b.drain(main)
    full_b, full_out = unpack_vo(pack_b.value(), w_value.shape[0], head_width, out_shape)
    full_b = full_b.reshape(width, head_width)
    full_out = to_lanes(full_out)
    (full_b, full_out), main = tie((full_b, full_out), main)
    main = pack_d.step(main)
    query_key, hidden_all = main
    value_rows = low_dot(hidden_all, full_b).astype(low_type)
    norm_rows = jnp.swapaxes(full_out[:, head_width : head_width + 4], 0, 1).reshape(4, width)
    norm_rows = norm_rows.astype(full_type)
    attended, lse = attend_forward(query_key, value_rows, seg_row, slot_row)
    norm_rows, attended = tie(norm_rows, attended)
    parts = whole_call(mix_kernel, blocks_of(tok_rows, width), "mix", attended, full_out)
    terms = rows_scatter(parts)
    units = w_up.shape[1]
    square = shape_of((own_rows, width), full_type)
    low_square = shape_of((own_rows, width))
    narrow = shape_of((own_rows, 1), full_type)
    normed_one, normed_low, unit_one, scale_one = whole_call(
        norm_one_kernel,
        [square, low_square, square, narrow],
        "norm_one",
        own_hidden,
        *terms,
        norm_rows,
    )

    rows_one = [normed_low, swap(normed_low, "mp", 2)]
    rows_one = pack_u.drain(rows_one)
    full_up = pack_u.value().reshape(width, -1)
    col_own = full_up[:, units:]
    (full_up, col_own), rows_one = tie((full_up, col_own), rows_one)
    rows_one = rows_one + [swap(each, "mp", 1) for each in rows_one]
    far_col = swap(col_own, "mp", 2)
    active, slope = feed_up(rows_one, full_up, units)
    active = pack_d.drain(active)
    full_down = to_lanes(pack_d.value())
    parts = feed_down(active, full_down)
    far_col, parts = tie(far_col, parts)
    terms = rows_scatter(parts)
    col_blocks = [col_own, far_col]
    col_blocks = col_blocks + [swap(each, "mp", 1) for each in col_blocks]
    normed_two_low, unit_two, scale_two, embedded, embed_low, inv_length = ordered_call(
        norm_two_kernel,
        [low_square, square, narrow, square, low_square, narrow],
        [],
        "norm_two",
        col_order,
        normed_one,
        *terms,
        norm_rows,
        *col_blocks,
    )

    (far, far_lse), embed_low = tie((attended, lse), embed_low)
    far = group_gather(far[None])[1:]
    far_lse = group_gather(far_lse[None])[1:]
    e_blocks = rows_gather(embed_low)
    two_low, e_blocks = tie(normed_two_low, e_blocks)
    far_two = swap(two_low, "mp", 2)
    sharp, soft_block = late_forward(e_blocks, queries, live_bias, blocks)
    (far, far_lse), soft_block = tie((far, far_lse), soft_block)
    soft_far = group_gather(soft_block[None])[1:]
    *parts, scores = late_backward(
        sharp, soft_block, soft_far, same, place, weight, queries
    )
    far_two, parts = tie(far_two, parts)
    far_attended = far.reshape(-1, head_width)
    far_lse = jnp.swapaxes(far_lse, 0, 1).reshape(8, -1)

    score_masks = dp_up[group_levels:]
    scores, parts = tie(scores, parts)
    scores_far = swap(scores, "dp", score_masks[0])
    terms = rows_scatter(parts)
    scores_far, terms = tie(scores_far, terms)
    scores, terms = tie(scores + scores_far, terms)
    scores_far = swap(scores, "dp", score_masks[1])
    low_half = shape_of((own_rows, width // 2))
    du_own, du_far, dresid_two, dresid_low, two_sums = ordered_call(
        norm_two_back_kernel,
        [low_half, low_half, square, low_square, shape_of((2, width), full_type)],
        [((own_rows, width), low_type)],
        "norm_two_back",
        col_order,
        *terms,
        norm_rows,
        unit_two,
        scale_two,
        embedded,
        inv_length,
        *col_blocks,
    )
    dresid_blocks = [dresid_low, swap(dresid_low, "mp", 2)]
    scores_far, dresid_blocks = tie(scores_far, dresid_blocks)
    dresid_blocks = dresid_blocks + [swap(each, "mp", 1) for each in dresid_blocks]
    two_blocks = [normed_two_low, far_two]
    two_blocks = two_blocks + [swap(each, "mp", 1) for each in two_blocks]
    two_blocks, dresid_blocks = tie(two_blocks, dresid_blocks)
    scores = scores + scores_far
    for mask in score_masks[2:]:
        scores = scores + swap(scores, "dp", mask)

    (du_own, du_far), dresid_blocks = tie((du_own, du_far), dresid_blocks)
    du_far = swap(du_far, "mp", 2)
    dinner = feed_inner(dresid_blocks, full_down, slope)
    du_far, dinner = tie(du_far, dinner)
    parts = feed_back(dinner, full_up)
    got_far, got = swap(parts[3], "mp", 1), swap(parts[2], "mp", 1)
    du_blocks = [du_own, du_far]
    du_blocks = du_blocks + [swap(each, "mp", 1) for each in du_blocks]
    low = rows_fold([parts[1], got_far])
    (active, dinner, got), low = tie((active, dinner, got), low)
    far_low = swap(low, "mp", 2)
    grad_d = Scatter(*grad_down(active, dresid_blocks, dp_up), "dp", dp_up)
    dinner = grad_d.start(dinner)
    grad_u = Scatter(
        *grad_up(dinner, rows_one, two_blocks, du_blocks, w_colbert.shape[1], across_back),
        "dp",
        across_back,
    )
    far_low = grad_u.start(far_low)
    dresid_one, mixed_pack = whole_call(
        norm_one_back_kernel,
        [square, shape_of((own_rows + SPARE, width))],
        "norm_one_back",
        dresid_two,
        parts[0],
        got,
        far_low,
        norm_rows,
        unit_one,
        scale_one,
        two_sums,
    )
    packs = rows_gather(mixed_pack)

    dattended, norm_sums = whole_call(
        unmix_kernel,
        [shape_of((tok_rows, head_width)), shape_of((SPARE, width))],
        "unmix",
        *packs,
        full_out,
    )
    far_grads = group_gather(dattended[None])[1:].reshape(-1, head_width)
    own_q = (query_key, 0, dattended, attended, lse)
    all_keys = (value_rows, slot_row, tok_rows)
    keys = value_rows.shape[0]
    *sums, dquery = attend_back(own_q, None, keys, all_keys, None, True)
    far_grads, dquery = tie(far_grads, dquery)
    dquery = grad_d.step(grad_u.step(dquery))
    far_q = (query_key, tok_rows, far_grads, far_attended, far_lse)
    own_keys = (value_rows, slot_own, tok_rows)
    dqk, dvalue_low = attend_back(far_q, None, tok_rows, own_keys, sums, False, (dquery,))
    parts = unproject(dqk, dvalue_low, full_a, full_b)
    got_far, got = swap(parts[3], "mp", 1), swap(parts[2], "mp", 1)
    low = whole_call(
        fold_pair_kernel,
        [shape_of((own_rows // 2, width))] * 2,
        "fold_pair",
        parts[1],
        got_far,
    )
    (dqk, dvalue_low), low = tie((dqk, dvalue_low), low)
    far_low = [swap(each, "mp", 2) for each in low]
    grad_b = Scatter(
        *grad_vo(hidden_own, dvalue_low, attended, packs, norm_sums, across_back),
        "dp",
        across_back,
    )
    dqk = grad_b.start(dqk)
    dqk = grad_d.step(dqk)
    grad_a = Scatter(*grad_qk(hidden_own, dqk, dp_up), "dp", dp_up)
    last = grad_a.start(parts[0])
    far_low = grad_u.step(far_low)
    terms = [dresid_one, last, got, *far_low]
    input_own = whole_call(close_kernel, [low_square], "close", *terms)[0]
    far_own = swap(input_own, "mp", 2)
    far_own = grad_a.step(grad_b.step(far_own))
    input_blocks = [input_own, far_own]
    input_blocks = input_blocks + [swap(each, "mp", 1) for each in input_blocks]
    input_grad = place_rows(col_order, input_blocks)
    input_grad = grad_b.step(grad_a.step(input_grad))
    input_grad = grad_d.finish(grad_u.finish(input_grad))
    down_grad = grad_d.value()
    up_grad, colbert_grad = finish_pair(grad_u, units)
    ends = (input_grad, down_grad, up_grad, colbert_grad)
    ends = grad_a.finish(ends)
    query_grad, key_grad = finish_pair(grad_a, head_width)
    ends, (query_grad, key_grad) = grad_b.finish((ends, (query_grad, key_grad)))
    input_grad, down_grad, up_grad, colbert_grad = ends
    value_grad, out_grad, norm_grads = finish_vo(
        grad_b.keep[0], grad_b.other[0], w_value.shape, w_out.shape
    )
    return (
        scores,
        input_grad,
        query_grad,
        key_grad,
        value_grad,
        out_grad,
        up_grad,
        down_grad,
        colbert_grad,
        norm_grads[0].reshape(-1),
        norm_grads[1].reshape(-1),
        norm_grads[2].reshape(-1),
        norm_grads[3].reshape(-1),
    )


def solution(mesh):
    rows, both, across = P("dp", None), P("dp", "mp"), P("mp", "dp")
    return jax.shard_map(
        body,
        mesh=mesh,
        in_specs=(
            (rows, both, both, both, across, both, across, both)
            + (P("dp"),) * 4
            + (P("mp", None), P(), P(), P("mp", None))
        ),
        out_specs=(
            (P("mp", None), rows, both, both, both, across, both, across, both)
            + (P("dp"),) * 4
        ),
        check_vma=False,
    )
```

```python
import jax
import jax.numpy as jnp
from jax import lax
from jax.experimental import pallas as pl
from jax.experimental.pallas import tpu as pltpu
from jax.sharding import PartitionSpec as P

HEAD_DIM = 64
QLEN = 32
NBUCKET = 4
NPASS = 15
LANES = 128
SPARE = 16

neg_big = -1e30
low_type = jnp.bfloat16
full_type = jnp.float32
contract_rows = (((0,), (0,)), ((), ()))
contract_cols = (((1,), (1,)), ((), ()))
contract_inner = (((1,), (0,)), ((), ()))


def room(mebibytes):
    return pltpu.CompilerParams(vmem_limit_bytes=mebibytes * 1024 * 1024)


def rows_for_keys(keys):
    return 256 if keys <= 2048 else LANES


def room_for_keys(keys):
    return room(min(56, 4 + keys * rows_for_keys(keys) // 16384))


brief = pl.CostEstimate(flops=1, bytes_accessed=1, transcendentals=0)


def low_dot(left, right, dims=contract_inner):
    return lax.dot_general(left, right, dims, preferred_element_type=full_type)


def shape_of(shape, dtype=low_type):
    return jax.ShapeDtypeStruct(shape, dtype)


def whole_block(shape):
    return pl.BlockSpec(shape, lambda i: (0,) * len(shape))


def whole_call(kernel, outs, name, *args):
    return pl.pallas_call(
        kernel,
        grid=(1,),
        in_specs=[whole_block(each.shape) for each in args],
        out_specs=[whole_block(each.shape) for each in outs],
        out_shape=outs,
        compiler_params=room(12),
        cost_estimate=brief,
        name=name,
    )(*args)


def swap(value, axis, mask):
    pairs = [(source, source ^ mask) for source in range(lax.axis_size(axis))]
    return lax.ppermute(value, axis, pairs)


def bits_of(axis):
    return lax.axis_size(axis).bit_length() - 1


def has_bit(axis, mask):
    return lax.axis_index(axis) // mask % 2 == 1


def upward(axis):
    return [2**level for level in range(bits_of(axis))]


def downward(axis):
    return upward(axis)[::-1]


def offsets_of(masks):
    order = [0]
    for mask in masks:
        order = order + [at ^ mask for at in order]
    return order


def arrange(blocks, axis, masks):
    levels = bits_of(axis)
    cube = blocks.reshape((2,) * levels + blocks.shape[1:])
    for mask in masks:
        at = levels - mask.bit_length()
        cube = jnp.where(has_bit(axis, mask), jnp.flip(cube, at), cube)
    front = [levels - mask.bit_length() for mask in masks]
    cube = jnp.transpose(cube, front + list(range(levels, cube.ndim)))
    return cube.reshape(blocks.shape)


def tie(*values):
    return lax.optimization_barrier(values)


class Gather:
    def __init__(self, value, axis, masks):
        self.axis, self.masks = axis, list(masks)
        self.levels, self.shape = bits_of(axis), value.shape
        self.whole = value.reshape((1,) * self.levels + value.shape)

    def start(self, main):
        if self.masks:
            self.whole, main = tie(self.whole, main)
            self.other = swap(self.whole, self.axis, self.masks[0])
        return main

    def finish(self, main):
        if self.masks:
            mask = self.masks.pop(0)
            other, main = tie(self.other, main)
            at = self.levels - mask.bit_length()
            self.whole = jnp.where(
                has_bit(self.axis, mask),
                jnp.concatenate([other, self.whole], at),
                jnp.concatenate([self.whole, other], at),
            )
        return main

    def step(self, main):
        return self.start(self.finish(main))

    def drain(self, main):
        main = self.finish(main)
        while self.masks:
            main = self.finish(self.start(main))
        return main

    def value(self):
        return self.whole.reshape((-1,) + self.shape)


class Scatter:
    def __init__(self, keep, send, axis, masks):
        self.axis, self.masks = axis, list(masks)
        self.keep, self.send = keep, send

    def start(self, main):
        if self.masks:
            self.send, main = tie(self.send, main)
            self.other = swap(self.send, self.axis, self.masks[0])
        return main

    def finish(self, main):
        if self.masks:
            self.masks.pop(0)
            other, main = tie(self.other, main)
            if self.masks:
                self.keep, self.send = halve(self.keep, other)
            else:
                self.other = other
        return main

    def step(self, main):
        return self.start(self.finish(main))

    def drain(self, main):
        main = self.finish(main)
        while self.masks:
            main = self.finish(self.start(main))
        return main

    def value(self):
        return self.keep[0].astype(full_type) + self.other[0].astype(full_type)


def halve_kernel(keep_low, keep_high, other_low, other_high, low_ref, high_ref):
    for keep, other, out in (
        (keep_low, other_low, low_ref),
        (keep_high, other_high, high_ref),
    ):
        total = keep[...].astype(full_type) + other[...].astype(full_type)
        out[...] = total.astype(low_type)


def halve(keep, other):
    half = keep.shape[0] // 2
    block = (1,) + keep.shape[1:]
    low = pl.BlockSpec(block, lambda i: (i, 0, 0))
    high = pl.BlockSpec(block, lambda i: (half + i, 0, 0))
    return pl.pallas_call(
        halve_kernel,
        grid=(half,),
        in_specs=[low, high, low, high],
        out_specs=[low, low],
        out_shape=[shape_of((half,) + keep.shape[1:])] * 2,
        compiler_params=room(8),
        cost_estimate=brief,
        name="halve",
    )(keep, keep, other, other)


def rows_gather(block):
    blocks = [block]
    for mask in downward("mp"):
        blocks = blocks + [swap(each, "mp", mask) for each in blocks]
    return blocks


def rows_scatter(blocks):
    masks = upward("mp")
    terms = [[block] for block in blocks]
    for mask in masks:
        half = len(terms) // 2
        sends = [each[0] if len(each) == 1 else rows_fold(each) for each in terms[half:]]
        order = range(half)[::-1]
        got = {at: swap(sends[at], "mp", mask) for at in order}
        terms = [terms[at] + [got[at]] for at in range(half)]
    return terms[0]


def add_up(refs):
    total = refs[0][...].astype(full_type)
    for ref in refs[1:]:
        total = total + ref[...].astype(full_type)
    return total


def head_mask(width, head):
    lane = lax.broadcasted_iota(jnp.int32, (1, width), 1)
    return lane // HEAD_DIM == head


def only_head(rows, head):
    return jnp.where(head_mask(rows.shape[1], head), rows, jnp.zeros_like(rows))


def attend_forward_kernel(q_ref, k_ref, v_ref, segq_ref, segk_ref, o_ref, stat_ref):
    tile, width = q_ref.shape
    stat = jnp.broadcast_to(segq_ref[...], (LANES, tile)).T
    bias = jnp.where(stat[:, 0:1] == segk_ref[...], 0.0, neg_big)
    out = jnp.zeros((tile, width), full_type)
    lane = lax.broadcasted_iota(jnp.int32, (1, LANES), 1)
    queries = q_ref[...] * jnp.asarray(0.125, low_type)
    for head in range(width // HEAD_DIM):
        raw = low_dot(only_head(queries, head), k_ref[...], contract_cols) + bias
        top = jnp.max(raw, axis=1, keepdims=True)
        terms = jnp.exp(raw - top)
        total = jnp.sum(terms, axis=1, keepdims=True)
        mixed = low_dot(terms.astype(low_type), v_ref[...]) * (1.0 / total)
        out = jnp.where(head_mask(width, head), mixed, out)
        stat = jnp.where(lane == head, top + jnp.log(total), stat)
    o_ref[...] = out.astype(low_type)
    stat_ref[...] = stat.T[: stat_ref.shape[0]]


def attend_forward(query_key, value_rows, seg_rows, seg_keys):
    rows = seg_rows.shape[1]
    keys, width = value_rows.shape
    tile = rows_for_keys(keys)
    return pl.pallas_call(
        attend_forward_kernel,
        grid=(rows // tile,),
        in_specs=[
            pl.BlockSpec((tile, width), lambda i: (i, 0)),
            pl.BlockSpec((keys, width), lambda i: (0, 1)),
            pl.BlockSpec((keys, width), lambda i: (0, 0)),
            pl.BlockSpec((1, tile), lambda i: (0, i)),
            pl.BlockSpec((1, keys), lambda i: (0, 0)),
        ],
        out_specs=[
            pl.BlockSpec((tile, width), lambda i: (i, 0)),
            pl.BlockSpec((8, tile), lambda i: (0, i)),
        ],
        out_shape=[shape_of((rows, width)), shape_of((8, rows), full_type)],
        compiler_params=room_for_keys(keys),
        cost_estimate=brief,
        name="attend_forward",
    )(query_key, query_key, value_rows, seg_rows, seg_keys)


def attend_terms(q_ref, k_ref, v_ref, do_ref, o_ref, segk_ref, lse_ref):
    tile, width = q_ref.shape
    pad = jnp.zeros((LANES - lse_ref.shape[0], tile), full_type)
    lse = jnp.concatenate([lse_ref[...], pad], 0).T
    heads = width // HEAD_DIM
    bias = jnp.where(lse[:, heads : heads + 1] == segk_ref[...], 0.0, neg_big)
    queries = q_ref[...] * jnp.asarray(0.125, low_type)
    grads = do_ref[...]
    both = grads.astype(full_type) * o_ref[...].astype(full_type)
    for head in range(width // HEAD_DIM):
        q_head = only_head(queries, head)
        g_head = only_head(grads, head)
        delta = jnp.sum(only_head(both, head), axis=1, keepdims=True)
        raw = low_dot(q_head, k_ref[...], contract_cols)
        probs = jnp.exp(raw + (bias - lse[:, head : head + 1]))
        dprobs = low_dot(g_head, v_ref[...], contract_cols)
        dscore = (probs * (dprobs - delta)).astype(low_type)
        yield head, q_head, g_head, probs.astype(low_type), dscore


def attend_back(rows_of_q, part, keys, masks, sums, wants_dq, dq_parts=()):
    query_key, first_row, grads, attended, lse = rows_of_q
    value_rows, seg_keys, own = masks
    width = value_rows.shape[1]
    tile = rows_for_keys(keys)
    parts_of = 1 if part is None else 2
    steps = grads.shape[0] // tile // parts_of
    shift = steps if part == 1 else 0
    first = first_row // tile + shift
    closing = len(dq_parts) > 0

    def kernel(*refs):
        base, refs = refs[:7], refs[7:]
        q_ref, k_ref = base[:2]
        before, refs = (refs[:2], refs[2:]) if sums else (None, refs)
        parts, refs = refs[: len(dq_parts)], refs[len(dq_parts) :]
        if closing:
            dqk_out, dv_out, dk_sum, dv_sum = refs
        else:
            dk_sum, dv_sum = refs[:2]
        step = pl.program_id(0)

        @pl.when(step == 0)
        def _():
            dk_sum[...] = before[0][...] if sums else jnp.zeros_like(dk_sum)
            dv_sum[...] = before[1][...] if sums else jnp.zeros_like(dv_sum)

        dquery = jnp.zeros((tile, width), full_type)
        for head, q_head, g_head, probs, dscore in attend_terms(*base):
            if wants_dq:
                dquery = jnp.where(head_mask(width, head), low_dot(dscore, k_ref[...]), dquery)
            dk_sum[...] += low_dot(dscore[:, :own], q_head, contract_rows)
            dv_sum[...] += low_dot(probs[:, :own], g_head, contract_rows)
        if wants_dq:
            refs[2][...] = (dquery * 0.125).astype(low_type)
        if closing:

            @pl.when(step == steps - 1)
            def _():
                rows = own // len(parts)
                for at, ref in enumerate(parts):
                    dqk_out[at * rows : (at + 1) * rows, :width] = ref[...]
                dqk_out[:, width:] = dk_sum[...].astype(low_type)
                dv_out[...] = dv_sum[...].astype(low_type)

    tile_rows = pl.BlockSpec((tile, width), lambda i: (shift + i, 0))
    held = whole_block((own, width))
    in_specs = [
        pl.BlockSpec((tile, width), lambda i: (first + i, 0)),
        pl.BlockSpec((keys, width), lambda i: (0, 1)),
        pl.BlockSpec((keys, width), lambda i: (0, 0)),
        tile_rows,
        tile_rows,
        pl.BlockSpec((1, keys), lambda i: (0, 0)),
        pl.BlockSpec((8, tile), lambda i: (0, shift + i)),
    ]
    args = [query_key, query_key, value_rows, grads, attended, seg_keys, lse]
    if sums:
        in_specs, args = in_specs + [held, held], args + list(sums)
    in_specs = in_specs + [whole_block(each.shape) for each in dq_parts]
    args = args + list(dq_parts)
    if closing:
        outs = [shape_of((own, 2 * width)), shape_of((own, width))]
        out_specs = [whole_block(each.shape) for each in outs]
        scratch = [pltpu.VMEM((own, width), full_type)] * 2
    else:
        outs = [shape_of((own, width), full_type)] * 2
        out_specs, scratch = [held, held], []
        if wants_dq:
            outs = outs + [shape_of((steps * tile, width))]
            out_specs = out_specs + [pl.BlockSpec((tile, width), lambda i: (i, 0))]
    return pl.pallas_call(
        kernel,
        grid=(steps,),
        in_specs=in_specs,
        out_specs=out_specs,
        out_shape=outs,
        scratch_shapes=scratch,
        compiler_params=room_for_keys(keys),
        cost_estimate=brief,
        name="attend_back",
    )(*args)


def lanes_of(ref):
    return jnp.concatenate([ref[at] for at in range(ref.shape[0])], axis=1)


def rows_of(refs):
    return jnp.concatenate([ref[...] for ref in refs], axis=0)


def gather_blocks(block_refs, rows):
    @pl.when(pl.program_id(0) == 0)
    def _():
        span = block_refs[0].shape[0]
        for at, ref in enumerate(block_refs):
            rows[at * span : (at + 1) * span, :] = ref[...]


def feed_up_kernel(*refs):
    *row_refs, up_ref, g_ref, slope_ref, rows = refs
    gather_blocks(row_refs, rows)
    whole = low_dot(rows[...], up_ref[...])
    span = row_refs[0].shape[0]
    for at in range(len(row_refs)):
        place = pl.ds(at * span, span)
        inner = whole[at * span : (at + 1) * span]
        normal = 0.5 * (1.0 + lax.erf(inner * 0.7071067811865476))
        g_ref[place, :] = (inner * normal).astype(low_type)
        slope = normal + inner * jnp.exp(-0.5 * inner * inner) * 0.3989422804014327
        slope_ref[place, :] = slope.astype(low_type)


def feed_up(blocks, w_up, units):
    own, width = blocks[0].shape
    rows = own * len(blocks)
    tile = 256
    return pl.pallas_call(
        feed_up_kernel,
        grid=(units // tile,),
        in_specs=[pl.BlockSpec((own, width), lambda i: (0, 0))] * len(blocks)
        + [pl.BlockSpec((width, tile), lambda i: (0, i))],
        out_specs=[pl.BlockSpec((rows, tile), lambda i: (0, i))] * 2,
        out_shape=[shape_of((rows, units))] * 2,
        scratch_shapes=[pltpu.VMEM((rows, width), low_type)],
        compiler_params=room(10),
        cost_estimate=brief,
        name="feed_up",
    )(*blocks, w_up)


def store_blocks(total, block_refs):
    rows = total.shape[0] // len(block_refs)
    for at, ref in enumerate(block_refs):
        ref[...] = total[at * rows : (at + 1) * rows].astype(ref.dtype)


def blocks_of(rows, width):
    count = lax.axis_size("mp")
    kept = [shape_of((rows // count, width), full_type)] * (count // 2)
    return kept + [shape_of((rows // count, width))] * (count // 2)


def feed_down_kernel(g_ref, down_ref, *block_refs):
    store_blocks(low_dot(g_ref[...], lanes_of(down_ref)), block_refs)


def feed_down(active, w_down):
    rows, units = active.shape
    blocks, _, lanes = w_down.shape
    tile = 2
    return pl.pallas_call(
        feed_down_kernel,
        grid=(blocks // tile,),
        in_specs=[
            pl.BlockSpec((rows, units), lambda i: (0, 0)),
            pl.BlockSpec((tile, units, lanes), lambda i: (i, 0, 0)),
        ],
        out_specs=[
            pl.BlockSpec((each.shape[0], tile * lanes), lambda i: (0, i))
            for each in blocks_of(rows, blocks * lanes)
        ],
        out_shape=blocks_of(rows, blocks * lanes),
        compiler_params=room(10),
        cost_estimate=brief,
        name="feed_down",
    )(active, w_down)


def feed_inner_kernel(*refs):
    *row_refs, down_ref, slope_ref, dz_ref, rows = refs
    gather_blocks(row_refs, rows)
    dactive = low_dot(rows[...], lanes_of(down_ref), contract_cols)
    dz_ref[...] = (dactive * slope_ref[...].astype(full_type)).astype(low_type)


def feed_inner(blocks, w_down, slope):
    own, width = blocks[0].shape
    rows, units = slope.shape
    tile = 256
    lanes = w_down.shape[2]
    return pl.pallas_call(
        feed_inner_kernel,
        grid=(units // tile,),
        in_specs=[pl.BlockSpec((own, width), lambda i: (0, 0))] * len(blocks)
        + [
            pl.BlockSpec((w_down.shape[0], tile, lanes), lambda i: (0, i, 0)),
            pl.BlockSpec((rows, tile), lambda i: (0, i)),
        ],
        out_specs=pl.BlockSpec((rows, tile), lambda i: (0, i)),
        out_shape=shape_of((rows, units)),
        scratch_shapes=[pltpu.VMEM((rows, width), low_type)],
        compiler_params=room(10),
        cost_estimate=brief,
        name="feed_inner",
    )(*blocks, w_down, slope)


def feed_back_kernel(dz_ref, up_ref, *block_refs):
    store_blocks(low_dot(dz_ref[...], up_ref[...], contract_cols), block_refs)


def feed_back(dinner, w_up):
    rows, units = dinner.shape
    width = w_up.shape[0]
    tile = 256
    return pl.pallas_call(
        feed_back_kernel,
        grid=(width // tile,),
        in_specs=[
            pl.BlockSpec((rows, units), lambda i: (0, 0)),
            pl.BlockSpec((tile, units), lambda i: (i, 0)),
        ],
        out_specs=[
            pl.BlockSpec((each.shape[0], tile), lambda i: (0, i))
            for each in blocks_of(rows, width)
        ],
        out_shape=blocks_of(rows, width),
        compiler_params=room(10),
        cost_estimate=brief,
        name="feed_back",
    )(dinner, w_up)


def late_forward_kernel(*refs):
    *e_refs, q_ref, live_ref, sharp_ref, soft_ref, e_rows = refs
    gather_blocks(e_refs, e_rows)
    blocks = soft_ref.shape[0]
    per = blocks // len(e_refs)
    whole = low_dot(e_rows[...], q_ref[...], contract_cols)
    rows = e_refs[0].shape[0]
    for at in range(len(e_refs)):
        place = pl.ds(at * rows, rows)
        sharp = whole[at * rows : (at + 1) * rows] * 2.0 + live_ref[place, :]
        sharp_ref[place, :] = sharp
        cube = sharp.reshape(per, rows // per, sharp.shape[1])
        top = jnp.max(cube, axis=1)
        total = jnp.sum(jnp.exp(cube - top[:, None, :]), axis=1)
        soft = jnp.where(top > 0.5 * neg_big, top + jnp.log(total), neg_big)
        soft_ref[pl.ds(at * per, per), :] = soft


def late_forward(e_blocks, queries, live_bias, blocks):
    own, width = e_blocks[0].shape
    rows = own * len(e_blocks)
    count = queries.shape[0]
    tile = 512
    return pl.pallas_call(
        late_forward_kernel,
        grid=(count // tile,),
        in_specs=[pl.BlockSpec((own, width), lambda i: (0, 0))] * len(e_blocks)
        + [
            pl.BlockSpec((tile, width), lambda i: (i, 0)),
            pl.BlockSpec((rows, 1), lambda i: (0, 0)),
        ],
        out_specs=[
            pl.BlockSpec((rows, tile), lambda i: (0, i)),
            pl.BlockSpec((blocks, tile), lambda i: (0, i)),
        ],
        out_shape=[shape_of((rows, count), full_type), shape_of((blocks, count), full_type)],
        scratch_shapes=[pltpu.VMEM((rows, width), low_type)],
        compiler_params=room(14),
        cost_estimate=brief,
        name="late_forward",
    )(*e_blocks, queries, live_bias)


def join_soft(soft, far, same):
    top = soft
    for at in range(far.shape[0]):
        top = jnp.maximum(top, far[at])
    total = jnp.exp(soft - top)
    for at in range(far.shape[0]):
        total = total + jnp.exp(far[at] - top)
    blocks = soft.shape[0]
    most = jnp.full(soft.shape, neg_big, full_type)
    for at in range(blocks):
        shared = same[:, at : at + 1] > 0.0
        most = jnp.maximum(most, jnp.where(shared, top[at : at + 1], neg_big))
    sums = jnp.zeros(soft.shape, full_type)
    for at in range(blocks):
        shared = same[:, at : at + 1] > 0.0
        term = jnp.where(shared, top[at : at + 1], neg_big)
        sums = sums + jnp.exp(term - most) * total[at : at + 1]
    return most + jnp.log(sums)


def late_backward_kernel(
    sharp_ref, soft_ref, far_ref, same_ref, place_ref, weight_ref, q_ref, *refs
):
    *block_refs, score_ref, total = refs
    step = pl.program_id(0)
    blocks = soft_ref.shape[0]
    rows, tile = sharp_ref.shape
    soft = join_soft(soft_ref[...], far_ref[...], same_ref[...])
    cube = sharp_ref[...].reshape(blocks, rows // blocks, tile)
    pulled = weight_ref[...][:, None, :] * jnp.exp(cube - soft[:, None, :])
    term = low_dot(pulled.reshape(rows, tile).astype(low_type), q_ref[...])
    query = lax.broadcasted_iota(jnp.int32, (tile, score_ref.shape[0]), 0) // QLEN
    count = lax.broadcasted_iota(jnp.int32, (tile, score_ref.shape[0]), 1)
    pool = jnp.where(query == count, 0.5 / QLEN, 0.0)
    exact = lax.Precision.HIGHEST
    means = lax.dot_general(pool, soft, (((0,), (1,)), ((), ())), precision=exact)
    score_ref[...] = lax.dot_general(means, place_ref[...], contract_inner, precision=exact)

    @pl.when(step == 0)
    def _():
        total[...] = term

    @pl.when(step > 0)
    def _():
        total[...] += term

    @pl.when(step == pl.num_programs(0) - 1)
    def _():
        store_blocks(total[...], block_refs)


def late_backward(sharp, soft, far, same, place, weight, queries):
    rows, count = sharp.shape
    width = queries.shape[1]
    blocks = soft.shape[0]
    tile = min(1024, count)
    outs = blocks_of(rows, width)
    return pl.pallas_call(
        late_backward_kernel,
        grid=(count // tile,),
        in_specs=[
            pl.BlockSpec((rows, tile), lambda i: (0, i)),
            pl.BlockSpec((blocks, tile), lambda i: (0, i)),
            pl.BlockSpec((far.shape[0], blocks, tile), lambda i: (0, 0, i)),
            whole_block(same.shape),
            whole_block(place.shape),
            pl.BlockSpec((blocks, tile), lambda i: (0, i)),
            pl.BlockSpec((tile, width), lambda i: (i, 0)),
        ],
        out_specs=[whole_block(each.shape) for each in outs]
        + [pl.BlockSpec((tile // QLEN, NPASS), lambda i: (i, 0))],
        out_shape=outs + [shape_of((count // QLEN, NPASS), full_type)],
        scratch_shapes=[pltpu.VMEM((rows, width), full_type)],
        compiler_params=room(24),
        cost_estimate=brief,
        name="late_backward",
    )(sharp, soft, far, same, place, weight, queries)


def norm_stats(values):
    centre = values - jnp.mean(values, axis=-1, keepdims=True)
    spread = jnp.mean(centre * centre, axis=-1, keepdims=True)
    scale = lax.rsqrt(spread + 1e-05)
    return centre * scale, scale


def norm_backward(unit, scale, gain, grad):
    dunit = grad * gain
    dvalues = scale * (
        dunit
        - jnp.mean(dunit, axis=-1, keepdims=True)
        - unit * jnp.mean(dunit * unit, axis=-1, keepdims=True)
    )
    return (
        dvalues,
        jnp.sum(grad * unit, axis=0, keepdims=True),
        jnp.sum(grad, axis=0, keepdims=True),
    )


def norm_one_kernel(*refs):
    *terms, norm_ref, h_ref, low_ref, unit_ref, scale_ref = refs
    unit, scale = norm_stats(add_up(terms))
    normed = unit * norm_ref[0:1] + norm_ref[1:2]
    h_ref[...] = normed
    low_ref[...] = normed.astype(low_type)
    unit_ref[...] = unit
    scale_ref[...] = scale


def lanes_at(order_ref, at, span):
    return pl.ds(pl.multiple_of(order_ref[at] * span, span), span)


def norm_two_kernel(order_ref, *refs):
    *rest, low_ref, unit_ref, scale_ref, e_ref, elow_ref, inv_ref = refs
    parts = order_ref.shape[0]
    *terms, norm_ref = rest[:-parts]
    col_refs = rest[-parts:]
    unit, scale = norm_stats(add_up(terms))
    normed_low = (unit * norm_ref[2:3] + norm_ref[3:4]).astype(low_type)
    low_ref[...] = normed_low
    unit_ref[...] = unit
    scale_ref[...] = scale
    span = col_refs[0].shape[1]
    squares = 0.0
    for at, ref in enumerate(col_refs):
        projected = low_dot(normed_low, ref[...])
        e_ref[:, lanes_at(order_ref, at, span)] = projected
        squares = squares + jnp.sum(projected * projected, axis=-1, keepdims=True)
    inv = lax.rsqrt(squares + 1e-06)
    embedded = e_ref[...] * inv
    e_ref[...] = embedded
    elow_ref[...] = embedded.astype(low_type)
    inv_ref[...] = inv


def norm_two_back_kernel(order_ref, *refs):
    *rest, own_ref, far_ref, dr_ref, low_ref, g_ref, du_ref = refs
    parts = order_ref.shape[0]
    *terms, norm_ref, unit_ref, scale_ref, e_ref, inv_ref = rest[:-parts]
    col_refs = rest[-parts:]
    dembed = add_up(terms)
    embedded = e_ref[...]
    along = jnp.sum(embedded * dembed, axis=-1, keepdims=True)
    du_ref[...] = (inv_ref[...] * (dembed - embedded * along)).astype(low_type)
    span = col_refs[0].shape[1]
    dnormed = 0.0
    for at, ref in enumerate(col_refs):
        dproj = du_ref[:, lanes_at(order_ref, at, span)]
        dnormed = dnormed + low_dot(dproj, ref[...], contract_cols)
    half = own_ref.shape[1]
    mine = order_ref[0] // (parts // 2)
    own_ref[...] = du_ref[:, pl.ds(pl.multiple_of(mine * half, half), half)]
    far_ref[...] = du_ref[:, pl.ds(pl.multiple_of((1 - mine) * half, half), half)]
    dresid, dgain, dshift = norm_backward(
        unit_ref[...], scale_ref[...], norm_ref[2:3], dnormed
    )
    dr_ref[...] = dresid
    low_ref[...] = dresid.astype(low_type)
    g_ref[...] = jnp.concatenate([dgain, dshift], 0)


def split_sums(sums):
    high = sums.astype(low_type).astype(full_type)
    zeros = jnp.zeros((SPARE - 8, sums.shape[1]), full_type)
    return jnp.concatenate([high, sums - high, zeros], 0).astype(low_type)


def norm_one_back_kernel(*refs):
    *terms, norm_ref, unit_ref, scale_ref, two_ref, dr_ref, pack_ref = refs
    dresid, dgain, dshift = norm_backward(
        unit_ref[...], scale_ref[...], norm_ref[0:1], add_up(terms)
    )
    dr_ref[...] = dresid
    rows = dresid.shape[0]
    pack_ref[0:rows, :] = dresid.astype(low_type)
    pack_ref[rows : rows + SPARE, :] = split_sums(
        jnp.concatenate([dgain, dshift, two_ref[...]], 0)
    )


def fold_kernel(*refs):
    *terms, low_ref = refs
    low_ref[...] = add_up(terms).astype(low_type)


def rows_fold(terms):
    return whole_call(fold_kernel, [shape_of(terms[0].shape)], "fold", *terms)[0]


def mix_kernel(o_ref, out_ref, *block_refs):
    rows = o_ref.shape[1]
    weight = jnp.concatenate([out_ref[at, 0:rows, :] for at in range(out_ref.shape[0])], axis=1)
    store_blocks(low_dot(o_ref[...], weight), block_refs)


def unmix_kernel(*refs):
    *packs, out_ref, do_ref, sums_ref = refs
    rows = do_ref.shape[1]
    weight = jnp.concatenate([out_ref[at, 0:rows, :] for at in range(out_ref.shape[0])], axis=1)
    own = packs[0].shape[0] - SPARE
    sums = jnp.zeros((8, weight.shape[1]), full_type)
    mixed = jnp.concatenate([ref[0:own, :] for ref in packs], axis=0)
    do_ref[...] = low_dot(mixed, weight, contract_cols).astype(low_type)
    for ref in packs:
        sums = sums + ref[own : own + SPARE, :].astype(full_type)[:8]
    sums_ref[...] = split_sums(sums[:4] + sums[4:])


def block_order(masks):
    return lax.axis_index("dp") ^ jnp.asarray(offsets_of(masks[::-1]), jnp.int32)


def ordered_call(kernel, outs, scratch, name, order, *args, grant=20):
    return pl.pallas_call(
        kernel,
        grid=(1,),
        in_specs=[pl.BlockSpec(memory_space=pltpu.SMEM)]
        + [whole_block(each.shape) for each in args],
        out_specs=[whole_block(each.shape) for each in outs],
        out_shape=outs,
        scratch_shapes=[pltpu.VMEM(*each) for each in scratch],
        compiler_params=room(grant),
        cost_estimate=brief,
        name=name,
    )(order, *args)


def stored(place_ref, left, right):
    turned = left.T
    cols = right.shape[1]
    for start in range(0, cols, 256):
        stop = min(start + 256, cols)
        place_ref[:, start:stop] = low_dot(turned, right[:, start:stop]).astype(low_type)


def deal(order_ref, keep_ref, send_ref, write):
    half = keep_ref.shape[0]
    for at in range(2 * half):
        write(keep_ref.at[at] if at < half else send_ref.at[at - half], order_ref[at])


def rows_in(ref, block, count):
    return ref[pl.ds(pl.multiple_of(block * count, count), count), :]


def lanes_in(ref, block):
    return ref[:, pl.ds(pl.multiple_of(block * LANES, LANES), LANES)]


def halves_like(count, block):
    return [shape_of((count // 2,) + block)] * 2


def grad_down_kernel(order_ref, active_ref, *refs):
    *row_refs, keep_ref, send_ref, total = refs
    stored(total, active_ref[...], rows_of(row_refs))

    def write(ref, block):
        ref[...] = lanes_in(total, block)

    deal(order_ref, keep_ref, send_ref, write)


def grad_down(active, row_blocks, masks):
    count = lax.axis_size("dp")
    units, width = active.shape[1], row_blocks[0].shape[1]
    if width // count == LANES:
        return ordered_call(
            grad_down_kernel,
            halves_like(count, (units, LANES)),
            [((units, width), low_type)],
            "grad_down",
            block_order(masks),
            active,
            *row_blocks,
        )
    whole = low_dot(active, jnp.concatenate(row_blocks, 0), contract_rows).astype(low_type)
    return halves(arrange(jnp.swapaxes(whole.reshape(units, count, -1), 0, 1), "dp", masks))


def halves(blocks):
    half = blocks.shape[0] // 2
    return blocks[:half], blocks[half:]


def grad_up_kernel(order_ref, dinner_ref, *refs):
    *row_refs, keep_ref, send_ref, total = refs
    parts = len(row_refs) // 3
    units = dinner_ref.shape[1]
    block_rows = keep_ref.shape[1]
    cols = keep_ref.shape[2] - units
    stored(total.at[:, 0:units], rows_of(row_refs[:parts]), dinner_ref[...])
    mine = order_ref[order_ref.shape[0] - 1] % (row_refs[-1].shape[1] // cols)
    mine = pl.ds(pl.multiple_of(mine * cols, cols), cols)
    dproj = jnp.concatenate([ref[:, mine] for ref in row_refs[2 * parts :]], axis=0)
    stored(total.at[:, units:], rows_of(row_refs[parts : 2 * parts]), dproj)

    def write(ref, block):
        ref[...] = rows_in(total, block, block_rows)

    deal(order_ref, keep_ref, send_ref, write)


def grad_up(dinner, one_blocks, two_blocks, du_blocks, col_width, masks):
    count = lax.axis_size("dp")
    units, width = dinner.shape[1], one_blocks[0].shape[1]
    column = lax.axis_index("mp")
    rows = width // count
    if rows == LANES:
        order = jnp.concatenate([block_order(masks), column.reshape(1)])
        return ordered_call(
            grad_up_kernel,
            halves_like(count, (rows, units + col_width)),
            [((width, units + col_width), low_type)],
            "grad_up",
            order,
            dinner,
            *one_blocks,
            *two_blocks,
            *du_blocks,
        )
    column = column % (du_blocks[0].shape[1] // col_width)
    dproj = lax.dynamic_slice_in_dim(
        jnp.concatenate(du_blocks, 0), column * col_width, col_width, 1
    )
    up = low_dot(jnp.concatenate(one_blocks, 0), dinner, contract_rows)
    col = low_dot(jnp.concatenate(two_blocks, 0), dproj, contract_rows)
    whole = jnp.concatenate([up, col], 1).astype(low_type)
    return halves(arrange(whole.reshape(count, rows, -1), "dp", masks))


def grad_qk_kernel(order_ref, left_ref, right_ref, keep_ref, send_ref, total):
    block_rows = keep_ref.shape[1]
    stored(total, left_ref[...], right_ref[...])

    def write(ref, block):
        ref[...] = rows_in(total, block, block_rows)

    deal(order_ref, keep_ref, send_ref, write)


def grad_qk(left, right, masks):
    count = lax.axis_size("dp")
    width, cols = left.shape[1], right.shape[1]
    rows = width // count
    if rows == LANES:
        return ordered_call(
            grad_qk_kernel,
            halves_like(count, (rows, cols)),
            [((width, cols), low_type)],
            "grad_qk",
            block_order(masks),
            left,
            right,
        )
    whole = low_dot(left, right, contract_rows).astype(low_type)
    return halves(arrange(whole.reshape(count, rows, cols), "dp", masks))


def grad_vo_kernel(order_ref, hidden_ref, dv_ref, o_ref, *refs):
    *packs, sums_ref, keep_ref, send_ref, total_v, total_o = refs
    rows = packs[0].shape[0] - SPARE
    cols = dv_ref.shape[1]
    heads = o_ref.shape[1]
    stored(total_v, hidden_ref[...], dv_ref[...])
    mixed = jnp.concatenate([ref[0:rows, :] for ref in packs], axis=0)
    stored(total_o.at[0:heads, :], o_ref[...], mixed)
    total_o[heads : heads + SPARE, :] = sums_ref[...]

    def write(ref, block):
        value = rows_in(total_v, block, LANES)
        for at in range(cols // LANES):
            ref[at * LANES : (at + 1) * LANES, :] = value[:, at * LANES : (at + 1) * LANES]
        ref[cols:, :] = lanes_in(total_o, block)

    deal(order_ref, keep_ref, send_ref, write)


def finish_pair_kernel(keep_ref, other_ref, left_ref, right_ref):
    total = keep_ref[...].astype(full_type) + other_ref[...].astype(full_type)
    cols = left_ref.shape[1]
    left_ref[...] = total[:, :cols]
    right_ref[...] = total[:, cols:]


def finish_pair(scatter, cols):
    rows, both = scatter.keep.shape[1:]
    outs = [shape_of((rows, cols), full_type), shape_of((rows, both - cols), full_type)]
    return whole_call(finish_pair_kernel, outs, "finish_pair", scatter.keep[0], scatter.other[0])


def finish_vo_kernel(keep_ref, other_ref, value_ref, out_ref, *norm_refs):
    total = keep_ref[...].astype(full_type) + other_ref[...].astype(full_type)
    rows, cols = value_ref.shape
    row = 0
    for at in range(0, cols, LANES):
        value_ref[:, at : at + LANES] = total[row : row + rows]
        row += rows
    out_ref[...] = total[row : row + out_ref.shape[0]]
    row += out_ref.shape[0]
    for at, ref in enumerate(norm_refs):
        ref[...] = total[row + at : row + at + 1] + total[row + 4 + at : row + 5 + at]


def finish_vo(keep, other, value_shape, out_shape):
    rows, cols = out_shape
    if cols == LANES:
        outs = [shape_of(value_shape, full_type), shape_of(out_shape, full_type)]
        outs = outs + [shape_of((1, cols), full_type)] * 4
        value, out, *norms = whole_call(finish_vo_kernel, outs, "finish_vo", keep, other)
        return value, out, norms
    total = keep.astype(full_type) + other.astype(full_type)
    value, out = unpack_vo(total, *value_shape, (rows + SPARE, cols))
    return value, out[:rows], out[rows : rows + 4] + out[rows + 4 : rows + 8]


def pack_vo(value, out):
    cols = value.shape[-1]
    parts = [value[..., at : at + LANES] for at in range(0, cols, LANES)]
    return jnp.concatenate(parts + [out.reshape(out.shape[:-2] + (-1, LANES))], axis=-2)


def unpack_vo(packed, rows, cols, out_shape):
    high = rows * cols // LANES
    value = jnp.concatenate(
        [packed[..., at : at + rows, :] for at in range(0, high, rows)], axis=-1
    )
    return value, packed[..., high:, :].reshape(packed.shape[:-2] + out_shape)


def grad_vo(hidden, dvalue, attended, packs, sums, masks):
    count = lax.axis_size("dp")
    width, cols = hidden.shape[1], dvalue.shape[1]
    heads = attended.shape[1]
    rows = width // count
    if rows == LANES:
        block = (cols * rows // LANES + heads + SPARE, LANES)
        return ordered_call(
            grad_vo_kernel,
            halves_like(count, block),
            [((width, cols), low_type), ((heads + SPARE, width), low_type)],
            "grad_vo",
            block_order(masks),
            hidden,
            dvalue,
            attended,
            *packs,
            sums,
        )
    value = low_dot(hidden, dvalue, contract_rows).astype(low_type).reshape(count, rows, cols)
    mixed = jnp.concatenate([each[:-SPARE] for each in packs], 0)
    out = low_dot(attended, mixed, contract_rows).astype(low_type)
    out = jnp.concatenate([out, sums], 0).reshape(heads + SPARE, count, rows)
    return halves(arrange(pack_vo(value, jnp.swapaxes(out, 0, 1)), "dp", masks))


def to_lanes(blocks):
    if blocks.shape[2] == LANES:
        return blocks
    whole = jnp.swapaxes(blocks, 0, 1).reshape(blocks.shape[1], -1, LANES)
    return jnp.swapaxes(whole, 0, 1)


def place_kernel(at_ref, *refs):
    *blocks, out_ref = refs
    rows = blocks[0].shape[0]
    for at, ref in enumerate(blocks):
        start = pl.multiple_of(at_ref[at] * rows, rows)
        out_ref[pl.ds(start, rows), :] = ref[...].astype(full_type)


def place_rows(order, blocks):
    rows, width = blocks[0].shape
    outs = [shape_of((rows * len(blocks), width), full_type)]
    return ordered_call(place_kernel, outs, [], "place_rows", order, *blocks)[0]


def unproject_kernel(dqk_ref, dv_ref, a_ref, b_ref, *block_refs):
    total = low_dot(dqk_ref[...], a_ref[...], contract_cols)
    store_blocks(total + low_dot(dv_ref[...], b_ref[...], contract_cols), block_refs)


def unproject(dqk, dvalue, w_qk, w_v):
    outs = blocks_of(dqk.shape[0], w_qk.shape[0])
    return whole_call(unproject_kernel, outs, "unproject", dqk, dvalue, w_qk, w_v)


def fold_pair_kernel(keep_ref, got_ref, *low_refs):
    total = keep_ref[...] + got_ref[...].astype(full_type)
    rows = low_refs[0].shape[0]
    for at, ref in enumerate(low_refs):
        ref[...] = total[at * rows : (at + 1) * rows].astype(low_type)


def close_kernel(*refs):
    *terms, low_far, high_far, out_ref = refs
    total = add_up(terms)
    half = low_far.shape[0]
    for at, ref in enumerate((low_far, high_far)):
        place = pl.ds(at * half, half)
        part = total[at * half : (at + 1) * half] + ref[...].astype(full_type)
        out_ref[place, :] = part.astype(low_type)


def pack_kernel(order_ref, *refs):
    hidden_ref, q_ref, k_ref, v_ref, o_ref, up_ref, col_ref, *norm_refs = refs[:11]
    a_out, u_out, b_out, own_out, block_out = refs[11:]
    heads, units = q_ref.shape[1], up_ref.shape[1]
    a_out[:, :heads] = q_ref[...]
    a_out[:, heads:] = k_ref[...]
    u_out[:, :units] = up_ref[...]
    u_out[:, units:] = col_ref[...]
    row = 0
    for at in range(0, heads, LANES):
        b_out[row : row + v_ref.shape[0], :] = v_ref[:, at : at + LANES]
        row += v_ref.shape[0]
    b_out[row : row + o_ref.shape[0], :] = o_ref[...]
    row += o_ref.shape[0]
    norms = [ref[...].astype(full_type).reshape(1, -1) for ref in norm_refs]
    norms = jnp.concatenate(norms + [jnp.zeros((SPARE - 4, LANES), full_type)], axis=0)
    b_out[row : row + SPARE, :] = norms.astype(low_type)
    parts = order_ref.shape[0]
    rows = hidden_ref.shape[0] // parts
    for at in range(parts):
        own_out[at * rows : (at + 1) * rows, :] = rows_in(hidden_ref, order_ref[at], rows)
    block_out[...] = own_out[0:rows, :]


def pack_inputs(order, hidden, w_query, w_key, w_value, w_out, w_up, w_colbert, *norms):
    rows, heads = w_query.shape
    span = hidden.shape[0] // order.shape[0]
    if w_out.shape[1] == LANES and rows == LANES:
        packed = (rows * heads // LANES + w_out.shape[0] + SPARE, LANES)
        outs = [
            shape_of((rows, 2 * heads)),
            shape_of((rows, w_up.shape[1] + w_colbert.shape[1])),
            shape_of(packed),
            shape_of(hidden.shape),
            shape_of((span, hidden.shape[1])),
        ]
        args = (hidden, w_query, w_key, w_value, w_out, w_up, w_colbert) + norms
        return ordered_call(pack_kernel, outs, [], "pack", order, *args, grant=60)
    norms = jnp.concatenate([jnp.stack(norms), jnp.zeros((SPARE - 4, w_out.shape[1]), low_type)], 0)
    blocks = [
        lax.dynamic_slice_in_dim(hidden, order[at] * span, span, 0)
        for at in range(order.shape[0])
    ]
    return (
        jnp.concatenate([w_query, w_key], axis=1),
        jnp.concatenate([w_up, w_colbert], axis=1),
        pack_vo(w_value, jnp.concatenate([w_out, norms], axis=0)),
        jnp.concatenate(blocks),
        blocks[0],
    )


def body(
    hidden_in,
    w_query,
    w_key,
    w_value,
    w_out,
    w_up,
    w_down,
    w_colbert,
    norm1_gain,
    norm1_shift,
    norm2_gain,
    norm2_shift,
    queries,
    passage,
    live,
    score_grad,
):
    tok_rows, width = hidden_in.shape
    device = lax.axis_index("dp")
    column = lax.axis_index("mp")
    dp_size = lax.axis_size("dp")
    mp_size = lax.axis_size("mp")
    group_size = dp_size // NBUCKET
    group_levels = group_size.bit_length() - 1
    own_rows = tok_rows // mp_size
    head_width = w_query.shape[1]
    dp_up, dp_down = upward("dp"), downward("dp")
    turned = dp_up[:1] + dp_down[:-1]
    row_order = offsets_of(downward("mp"))

    def ordered(value, owner, span=own_rows):
        return jnp.concatenate(
            [
                lax.dynamic_slice_in_dim(value, (owner * mp_size + (column ^ at)) * span, span, 0)
                for at in row_order
            ]
        )

    def group_gather(value):
        for level in range(group_levels):
            value = jnp.concatenate([value, swap(value, "dp", 2**level)], 0)
        return value

    across = dp_up[-1:] + dp_up[:-1]
    turned_back, across_back = turned[::-1], across[::-1]
    col_order = column ^ jnp.asarray(row_order, jnp.int32)
    norms = (norm1_gain, norm1_shift, norm2_gain, norm2_shift)
    out_shape = (w_out.shape[0] + SPARE, w_out.shape[1])
    packed_a, packed_u, packed_b, hidden_own, own_hidden = pack_inputs(
        col_order, hidden_in, w_query, w_key, w_value, w_out, w_up, w_colbert, *norms
    )
    pack_a = Gather(packed_a, "dp", dp_down)
    pack_u = Gather(packed_u, "dp", dp_down)
    pack_b = Gather(packed_b, "dp", dp_down)
    pack_d = Gather(w_down, "dp", turned)

    main = (hidden_own, own_hidden)
    main = pack_a.start(main)
    main = pack_b.start(main)
    main = pack_u.start(main)
    main = pack_d.start(main)
    others = group_gather(main[1][None])[1:]
    seg_own = ordered(passage, device)
    live_own = ordered(live, device)
    seg_others = jnp.concatenate([ordered(passage, device ^ at) for at in range(1, group_size)])
    live_others = jnp.concatenate([ordered(live, device ^ at) for at in range(1, group_size)])
    slot_own = jnp.where(live_own == 1, seg_own, -1)
    slot_keys = jnp.concatenate([slot_own, jnp.where(live_others == 1, seg_others, -1)])
    seg_row = seg_own.astype(full_type)[None, :]
    slot_row = slot_keys.astype(full_type)[None, :]
    blocks = 2 ** (NBUCKET - 1)
    seg_block = seg_own.reshape(blocks, -1)[:, 0]
    live_bias = jnp.where(live_own == 1, 0.0, neg_big)[:, None]
    same = seg_block[:, None] == seg_block[None, :]
    passages = jnp.arange(NPASS, dtype=jnp.int32)
    place = (seg_block[:, None] == passages[None, :]).astype(full_type)
    grad_block = jnp.sum(place[:, None, :] * score_grad[None], axis=2)
    weight = jnp.repeat(grad_block / QLEN, QLEN, axis=1)
    same = same.astype(full_type)
    place = place / jnp.sum(same, axis=1, keepdims=True)
    slot_own = slot_own.astype(full_type)[None, :]
    early = (seg_row, slot_own, slot_row, live_bias, weight, same, place)
    early, main = tie(early, main)
    seg_row, slot_own, slot_row, live_bias, weight, same, place = early
    main = pack_a.step(main)
    main = pack_b.step(main)
    others, main = tie(others, main)
    far_others = swap(others, "mp", 2)
    main = pack_d.finish(main)
    main = pack_u.step(main)
    main = pack_d.start(main)
    main = pack_a.step(main)
    main = pack_b.step(main)
    far_others, main = tie(far_others, main)
    main = pack_u.step(main)
    others = [others, far_others]
    others = others + [swap(each, "mp", 1) for each in others]
    others = jnp.stack(others, 1).reshape(-1, width)
    hidden_own, own_hidden = main
    hidden_all = jnp.concatenate([hidden_own, others], 0)
    main = (hidden_own, own_hidden, hidden_all)
    main = pack_a.drain(main)
    full_a = pack_a.value().reshape(width, -1)
    full_a, main = tie(full_a, main)
    hidden_own, own_hidden, hidden_all = main

    query_key = low_dot(hidden_all, full_a).astype(low_type)
    main = (query_key, hidden_all)
    main = pack_b.drain(main)
    full_b, full_out = unpack_vo(pack_b.value(), w_value.shape[0], head_width, out_shape)
    full_b = full_b.reshape(width, head_width)
    full_out = to_lanes(full_out)
    (full_b, full_out), main = tie((full_b, full_out), main)
    main = pack_d.step(main)
    query_key, hidden_all = main
    value_rows = low_dot(hidden_all, full_b).astype(low_type)
    norm_rows = jnp.swapaxes(full_out[:, head_width : head_width + 4], 0, 1).reshape(4, width)
    norm_rows = norm_rows.astype(full_type)
    attended, lse = attend_forward(query_key, value_rows, seg_row, slot_row)
    norm_rows, attended = tie(norm_rows, attended)
    parts = whole_call(mix_kernel, blocks_of(tok_rows, width), "mix", attended, full_out)
    terms = rows_scatter(parts)
    units = w_up.shape[1]
    square = shape_of((own_rows, width), full_type)
    low_square = shape_of((own_rows, width))
    narrow = shape_of((own_rows, 1), full_type)
    normed_one, normed_low, unit_one, scale_one = whole_call(
        norm_one_kernel,
        [square, low_square, square, narrow],
        "norm_one",
        own_hidden,
        *terms,
        norm_rows,
    )

    rows_one = [normed_low, swap(normed_low, "mp", 2)]
    rows_one = pack_u.drain(rows_one)
    full_up = pack_u.value().reshape(width, -1)
    col_own = full_up[:, units:]
    (full_up, col_own), rows_one = tie((full_up, col_own), rows_one)
    rows_one = rows_one + [swap(each, "mp", 1) for each in rows_one]
    far_col = swap(col_own, "mp", 2)
    active, slope = feed_up(rows_one, full_up, units)
    active = pack_d.drain(active)
    full_down = to_lanes(pack_d.value())
    parts = feed_down(active, full_down)
    far_col, parts = tie(far_col, parts)
    terms = rows_scatter(parts)
    col_blocks = [col_own, far_col]
    col_blocks = col_blocks + [swap(each, "mp", 1) for each in col_blocks]
    normed_two_low, unit_two, scale_two, embedded, embed_low, inv_length = ordered_call(
        norm_two_kernel,
        [low_square, square, narrow, square, low_square, narrow],
        [],
        "norm_two",
        col_order,
        normed_one,
        *terms,
        norm_rows,
        *col_blocks,
    )

    (far, far_lse), embed_low = tie((attended, lse), embed_low)
    far = group_gather(far[None])[1:]
    far_lse = group_gather(far_lse[None])[1:]
    far_e = swap(embed_low, "mp", 2)
    (far, far_lse), far_e = tie((far, far_lse), far_e)
    e_blocks = [embed_low, far_e]
    e_blocks = e_blocks + [swap(each, "mp", 1) for each in e_blocks]
    sharp, soft_block = late_forward(e_blocks, queries, live_bias, blocks)
    two_low, soft_block = tie(normed_two_low, soft_block)
    far_two = swap(two_low, "mp", 2)
    soft_far = group_gather(soft_block[None])[1:]
    *parts, scores = late_backward(
        sharp, soft_block, soft_far, same, place, weight, queries
    )
    far_two, parts = tie(far_two, parts)
    far_attended = far.reshape(-1, head_width)
    far_lse = jnp.swapaxes(far_lse, 0, 1).reshape(8, -1)

    score_masks = dp_up[group_levels:]
    scores, parts = tie(scores, parts)
    scores_far = swap(scores, "dp", score_masks[0])
    terms = rows_scatter(parts)
    scores_far, terms = tie(scores_far, terms)
    scores, terms = tie(scores + scores_far, terms)
    scores_far = swap(scores, "dp", score_masks[1])
    low_half = shape_of((own_rows, width // 2))
    du_own, du_far, dresid_two, dresid_low, two_sums = ordered_call(
        norm_two_back_kernel,
        [low_half, low_half, square, low_square, shape_of((2, width), full_type)],
        [((own_rows, width), low_type)],
        "norm_two_back",
        col_order,
        *terms,
        norm_rows,
        unit_two,
        scale_two,
        embedded,
        inv_length,
        *col_blocks,
    )
    dresid_blocks = [dresid_low, swap(dresid_low, "mp", 2)]
    scores_far, dresid_blocks = tie(scores_far, dresid_blocks)
    dresid_blocks = dresid_blocks + [swap(each, "mp", 1) for each in dresid_blocks]
    two_blocks = [normed_two_low, far_two]
    two_blocks = two_blocks + [swap(each, "mp", 1) for each in two_blocks]
    two_blocks, dresid_blocks = tie(two_blocks, dresid_blocks)
    scores = scores + scores_far
    for mask in score_masks[2:]:
        scores = scores + swap(scores, "dp", mask)

    (du_own, du_far), dresid_blocks = tie((du_own, du_far), dresid_blocks)
    du_far = swap(du_far, "mp", 2)
    dinner = feed_inner(dresid_blocks, full_down, slope)
    du_far, dinner = tie(du_far, dinner)
    parts = feed_back(dinner, full_up)
    got_far, got = swap(parts[3], "mp", 1), swap(parts[2], "mp", 1)
    du_blocks = [du_own, du_far]
    du_blocks = du_blocks + [swap(each, "mp", 1) for each in du_blocks]
    low = rows_fold([parts[1], got_far])
    (active, dinner, got), low = tie((active, dinner, got), low)
    far_low = swap(low, "mp", 2)
    grad_d = Scatter(*grad_down(active, dresid_blocks, dp_up), "dp", dp_up)
    dinner = grad_d.start(dinner)
    grad_u = Scatter(
        *grad_up(dinner, rows_one, two_blocks, du_blocks, w_colbert.shape[1], across_back),
        "dp",
        across_back,
    )
    far_low = grad_u.start(far_low)
    dresid_one, mixed_pack = whole_call(
        norm_one_back_kernel,
        [square, shape_of((own_rows + SPARE, width))],
        "norm_one_back",
        dresid_two,
        parts[0],
        got,
        far_low,
        norm_rows,
        unit_one,
        scale_one,
        two_sums,
    )
    packs = rows_gather(mixed_pack)

    dattended, norm_sums = whole_call(
        unmix_kernel,
        [shape_of((tok_rows, head_width)), shape_of((SPARE, width))],
        "unmix",
        *packs,
        full_out,
    )
    far_grads = group_gather(dattended[None])[1:].reshape(-1, head_width)
    own_q = (query_key, 0, dattended, attended, lse)
    all_keys = (value_rows, slot_row, tok_rows)
    keys = value_rows.shape[0]
    *sums, dquery = attend_back(own_q, None, keys, all_keys, None, True)
    far_grads, dquery = tie(far_grads, dquery)
    dquery = grad_d.step(grad_u.step(dquery))
    far_q = (query_key, tok_rows, far_grads, far_attended, far_lse)
    own_keys = (value_rows, slot_own, tok_rows)
    dqk, dvalue_low = attend_back(far_q, None, tok_rows, own_keys, sums, False, (dquery,))
    parts = unproject(dqk, dvalue_low, full_a, full_b)
    got_far, got = swap(parts[3], "mp", 1), swap(parts[2], "mp", 1)
    low = whole_call(
        fold_pair_kernel,
        [shape_of((own_rows // 2, width))] * 2,
        "fold_pair",
        parts[1],
        got_far,
    )
    (dqk, dvalue_low), low = tie((dqk, dvalue_low), low)
    far_low = [swap(each, "mp", 2) for each in low]
    grad_b = Scatter(
        *grad_vo(hidden_own, dvalue_low, attended, packs, norm_sums, across_back),
        "dp",
        across_back,
    )
    dqk = grad_b.start(dqk)
    dqk = grad_d.step(dqk)
    grad_a = Scatter(*grad_qk(hidden_own, dqk, dp_up), "dp", dp_up)
    last = grad_a.start(parts[0])
    far_low = grad_u.step(far_low)
    terms = [dresid_one, last, got, *far_low]
    input_own = whole_call(close_kernel, [low_square], "close", *terms)[0]
    far_own = swap(input_own, "mp", 2)
    far_own = grad_a.step(grad_b.step(far_own))
    input_blocks = [input_own, far_own]
    input_blocks = input_blocks + [swap(each, "mp", 1) for each in input_blocks]
    input_grad = place_rows(col_order, input_blocks)
    input_grad = grad_b.step(grad_a.step(input_grad))
    input_grad = grad_d.finish(grad_u.finish(input_grad))
    down_grad = grad_d.value()
    up_grad, colbert_grad = finish_pair(grad_u, units)
    ends = (input_grad, down_grad, up_grad, colbert_grad)
    ends = grad_a.finish(ends)
    query_grad, key_grad = finish_pair(grad_a, head_width)
    ends, (query_grad, key_grad) = grad_b.finish((ends, (query_grad, key_grad)))
    input_grad, down_grad, up_grad, colbert_grad = ends
    value_grad, out_grad, norm_grads = finish_vo(
        grad_b.keep[0], grad_b.other[0], w_value.shape, w_out.shape
    )
    return (
        scores,
        input_grad,
        query_grad,
        key_grad,
        value_grad,
        out_grad,
        up_grad,
        down_grad,
        colbert_grad,
        norm_grads[0].reshape(-1),
        norm_grads[1].reshape(-1),
        norm_grads[2].reshape(-1),
        norm_grads[3].reshape(-1),
    )


def solution(mesh):
    rows, both, across = P("dp", None), P("dp", "mp"), P("mp", "dp")
    return jax.shard_map(
        body,
        mesh=mesh,
        in_specs=(
            (rows, both, both, both, across, both, across, both)
            + (P("dp"),) * 4
            + (P("mp", None), P(), P(), P("mp", None))
        ),
        out_specs=(
            (P("mp", None), rows, both, both, both, across, both, across, both)
            + (P("dp"),) * 4
        ),
        check_vma=False,
    )
```

```python
import jax
import jax.numpy as jnp
from jax import lax
from jax.experimental import pallas as pl
from jax.experimental.pallas import tpu as pltpu
from jax.sharding import PartitionSpec as P

HEAD_DIM = 64
QLEN = 32
NBUCKET = 4
NPASS = 15
LANES = 128
SPARE = 16

neg_big = -1e30
low_type = jnp.bfloat16
full_type = jnp.float32
contract_rows = (((0,), (0,)), ((), ()))
contract_cols = (((1,), (1,)), ((), ()))
contract_inner = (((1,), (0,)), ((), ()))


def room(mebibytes):
    return pltpu.CompilerParams(vmem_limit_bytes=mebibytes * 1024 * 1024)


def rows_for_keys(keys):
    return 256 if keys <= 2048 else LANES


def room_for_keys(keys):
    return room(min(56, 4 + keys * rows_for_keys(keys) // 16384))


brief = pl.CostEstimate(flops=1, bytes_accessed=1, transcendentals=0)


def low_dot(left, right, dims=contract_inner):
    return lax.dot_general(left, right, dims, preferred_element_type=full_type)


def shape_of(shape, dtype=low_type):
    return jax.ShapeDtypeStruct(shape, dtype)


def whole_block(shape):
    return pl.BlockSpec(shape, lambda i: (0,) * len(shape))


def whole_call(kernel, outs, name, *args):
    return pl.pallas_call(
        kernel,
        grid=(1,),
        in_specs=[whole_block(each.shape) for each in args],
        out_specs=[whole_block(each.shape) for each in outs],
        out_shape=outs,
        compiler_params=room(12),
        cost_estimate=brief,
        name=name,
    )(*args)


def swap(value, axis, mask):
    pairs = [(source, source ^ mask) for source in range(lax.axis_size(axis))]
    return lax.ppermute(value, axis, pairs)


def bits_of(axis):
    return lax.axis_size(axis).bit_length() - 1


def has_bit(axis, mask):
    return lax.axis_index(axis) // mask % 2 == 1


def upward(axis):
    return [2**level for level in range(bits_of(axis))]


def downward(axis):
    return upward(axis)[::-1]


def offsets_of(masks):
    order = [0]
    for mask in masks:
        order = order + [at ^ mask for at in order]
    return order


def arrange(blocks, axis, masks):
    levels = bits_of(axis)
    cube = blocks.reshape((2,) * levels + blocks.shape[1:])
    for mask in masks:
        at = levels - mask.bit_length()
        cube = jnp.where(has_bit(axis, mask), jnp.flip(cube, at), cube)
    front = [levels - mask.bit_length() for mask in masks]
    cube = jnp.transpose(cube, front + list(range(levels, cube.ndim)))
    return cube.reshape(blocks.shape)


def tie(*values):
    return lax.optimization_barrier(values)


class Gather:
    def __init__(self, value, axis, masks):
        self.axis, self.masks = axis, list(masks)
        self.levels, self.shape = bits_of(axis), value.shape
        self.whole = value.reshape((1,) * self.levels + value.shape)

    def start(self, main):
        if self.masks:
            self.whole, main = tie(self.whole, main)
            self.other = swap(self.whole, self.axis, self.masks[0])
        return main

    def finish(self, main):
        if self.masks:
            mask = self.masks.pop(0)
            other, main = tie(self.other, main)
            at = self.levels - mask.bit_length()
            self.whole = jnp.where(
                has_bit(self.axis, mask),
                jnp.concatenate([other, self.whole], at),
                jnp.concatenate([self.whole, other], at),
            )
        return main

    def step(self, main):
        return self.start(self.finish(main))

    def drain(self, main):
        main = self.finish(main)
        while self.masks:
            main = self.finish(self.start(main))
        return main

    def value(self):
        return self.whole.reshape((-1,) + self.shape)


class Scatter:
    def __init__(self, keep, send, axis, masks):
        self.axis, self.masks = axis, list(masks)
        self.keep, self.send = keep, send

    def start(self, main):
        if self.masks:
            self.send, main = tie(self.send, main)
            self.other = swap(self.send, self.axis, self.masks[0])
        return main

    def finish(self, main):
        if self.masks:
            self.masks.pop(0)
            other, main = tie(self.other, main)
            if self.masks:
                self.keep, self.send = halve(self.keep, other)
            else:
                self.other = other
        return main

    def step(self, main):
        return self.start(self.finish(main))

    def drain(self, main):
        main = self.finish(main)
        while self.masks:
            main = self.finish(self.start(main))
        return main

    def value(self):
        return self.keep[0].astype(full_type) + self.other[0].astype(full_type)


def halve_kernel(keep_low, keep_high, other_low, other_high, low_ref, high_ref):
    for keep, other, out in (
        (keep_low, other_low, low_ref),
        (keep_high, other_high, high_ref),
    ):
        total = keep[...].astype(full_type) + other[...].astype(full_type)
        out[...] = total.astype(low_type)


def halve(keep, other):
    half = keep.shape[0] // 2
    block = (1,) + keep.shape[1:]
    low = pl.BlockSpec(block, lambda i: (i, 0, 0))
    high = pl.BlockSpec(block, lambda i: (half + i, 0, 0))
    return pl.pallas_call(
        halve_kernel,
        grid=(half,),
        in_specs=[low, high, low, high],
        out_specs=[low, low],
        out_shape=[shape_of((half,) + keep.shape[1:])] * 2,
        compiler_params=room(8),
        cost_estimate=brief,
        name="halve",
    )(keep, keep, other, other)


def rows_gather(block):
    blocks = [block]
    for mask in downward("mp"):
        blocks = blocks + [swap(each, "mp", mask) for each in blocks]
    return blocks


def rows_scatter(blocks):
    masks = upward("mp")
    terms = [[block] for block in blocks]
    for mask in masks:
        half = len(terms) // 2
        sends = [each[0] if len(each) == 1 else rows_fold(each) for each in terms[half:]]
        order = range(half)[::-1]
        got = {at: swap(sends[at], "mp", mask) for at in order}
        terms = [terms[at] + [got[at]] for at in range(half)]
    return terms[0]


def add_up(refs):
    total = refs[0][...].astype(full_type)
    for ref in refs[1:]:
        total = total + ref[...].astype(full_type)
    return total


def head_mask(width, head):
    lane = lax.broadcasted_iota(jnp.int32, (1, width), 1)
    return lane // HEAD_DIM == head


def only_head(rows, head):
    return jnp.where(head_mask(rows.shape[1], head), rows, jnp.zeros_like(rows))


def attend_forward_kernel(q_ref, k_ref, v_ref, segq_ref, segk_ref, o_ref, stat_ref):
    tile, width = q_ref.shape
    stat = jnp.broadcast_to(segq_ref[...], (LANES, tile)).T
    bias = jnp.where(stat[:, 0:1] == segk_ref[...], 0.0, neg_big)
    out = jnp.zeros((tile, width), full_type)
    lane = lax.broadcasted_iota(jnp.int32, (1, LANES), 1)
    queries = q_ref[...] * jnp.asarray(0.125, low_type)
    for head in range(width // HEAD_DIM):
        raw = low_dot(only_head(queries, head), k_ref[...], contract_cols) + bias
        top = jnp.max(raw, axis=1, keepdims=True)
        terms = jnp.exp(raw - top)
        total = jnp.sum(terms, axis=1, keepdims=True)
        mixed = low_dot(terms.astype(low_type), v_ref[...]) * (1.0 / total)
        out = jnp.where(head_mask(width, head), mixed, out)
        stat = jnp.where(lane == head, top + jnp.log(total), stat)
    o_ref[...] = out.astype(low_type)
    stat_ref[...] = stat.T[: stat_ref.shape[0]]


def attend_forward(query_key, value_rows, seg_rows, seg_keys):
    rows = seg_rows.shape[1]
    keys, width = value_rows.shape
    tile = rows_for_keys(keys)
    return pl.pallas_call(
        attend_forward_kernel,
        grid=(rows // tile,),
        in_specs=[
            pl.BlockSpec((tile, width), lambda i: (i, 0)),
            pl.BlockSpec((keys, width), lambda i: (0, 1)),
            pl.BlockSpec((keys, width), lambda i: (0, 0)),
            pl.BlockSpec((1, tile), lambda i: (0, i)),
            pl.BlockSpec((1, keys), lambda i: (0, 0)),
        ],
        out_specs=[
            pl.BlockSpec((tile, width), lambda i: (i, 0)),
            pl.BlockSpec((8, tile), lambda i: (0, i)),
        ],
        out_shape=[shape_of((rows, width)), shape_of((8, rows), full_type)],
        compiler_params=room_for_keys(keys),
        cost_estimate=brief,
        name="attend_forward",
    )(query_key, query_key, value_rows, seg_rows, seg_keys)


def attend_terms(q_ref, k_ref, v_ref, do_ref, o_ref, segk_ref, lse_ref):
    tile, width = q_ref.shape
    pad = jnp.zeros((LANES - lse_ref.shape[0], tile), full_type)
    lse = jnp.concatenate([lse_ref[...], pad], 0).T
    heads = width // HEAD_DIM
    bias = jnp.where(lse[:, heads : heads + 1] == segk_ref[...], 0.0, neg_big)
    queries = q_ref[...] * jnp.asarray(0.125, low_type)
    grads = do_ref[...]
    both = grads.astype(full_type) * o_ref[...].astype(full_type)
    for head in range(width // HEAD_DIM):
        q_head = only_head(queries, head)
        g_head = only_head(grads, head)
        delta = jnp.sum(only_head(both, head), axis=1, keepdims=True)
        raw = low_dot(q_head, k_ref[...], contract_cols)
        probs = jnp.exp(raw + (bias - lse[:, head : head + 1]))
        dprobs = low_dot(g_head, v_ref[...], contract_cols)
        dscore = (probs * (dprobs - delta)).astype(low_type)
        yield head, q_head, g_head, probs.astype(low_type), dscore


def attend_back(rows_of_q, part, keys, masks, sums, wants_dq, dq_parts=()):
    query_key, first_row, grads, attended, lse = rows_of_q
    value_rows, seg_keys, own = masks
    width = value_rows.shape[1]
    tile = rows_for_keys(keys)
    parts_of = 1 if part is None else 2
    steps = grads.shape[0] // tile // parts_of
    shift = steps if part == 1 else 0
    first = first_row // tile + shift
    closing = len(dq_parts) > 0

    def kernel(*refs):
        base, refs = refs[:7], refs[7:]
        q_ref, k_ref = base[:2]
        before, refs = (refs[:2], refs[2:]) if sums else (None, refs)
        parts, refs = refs[: len(dq_parts)], refs[len(dq_parts) :]
        if closing:
            dqk_out, dv_out, dk_sum, dv_sum = refs
        else:
            dk_sum, dv_sum = refs[:2]
        step = pl.program_id(0)

        @pl.when(step == 0)
        def _():
            dk_sum[...] = before[0][...] if sums else jnp.zeros_like(dk_sum)
            dv_sum[...] = before[1][...] if sums else jnp.zeros_like(dv_sum)

        dquery = jnp.zeros((tile, width), full_type)
        for head, q_head, g_head, probs, dscore in attend_terms(*base):
            if wants_dq:
                dquery = jnp.where(head_mask(width, head), low_dot(dscore, k_ref[...]), dquery)
            dk_sum[...] += low_dot(dscore[:, :own], q_head, contract_rows)
            dv_sum[...] += low_dot(probs[:, :own], g_head, contract_rows)
        if wants_dq:
            refs[2][...] = (dquery * 0.125).astype(low_type)
        if closing:

            @pl.when(step == steps - 1)
            def _():
                rows = own // len(parts)
                for at, ref in enumerate(parts):
                    dqk_out[at * rows : (at + 1) * rows, :width] = ref[...]
                dqk_out[:, width:] = dk_sum[...].astype(low_type)
                dv_out[...] = dv_sum[...].astype(low_type)

    tile_rows = pl.BlockSpec((tile, width), lambda i: (shift + i, 0))
    held = whole_block((own, width))
    in_specs = [
        pl.BlockSpec((tile, width), lambda i: (first + i, 0)),
        pl.BlockSpec((keys, width), lambda i: (0, 1)),
        pl.BlockSpec((keys, width), lambda i: (0, 0)),
        tile_rows,
        tile_rows,
        pl.BlockSpec((1, keys), lambda i: (0, 0)),
        pl.BlockSpec((8, tile), lambda i: (0, shift + i)),
    ]
    args = [query_key, query_key, value_rows, grads, attended, seg_keys, lse]
    if sums:
        in_specs, args = in_specs + [held, held], args + list(sums)
    in_specs = in_specs + [whole_block(each.shape) for each in dq_parts]
    args = args + list(dq_parts)
    if closing:
        outs = [shape_of((own, 2 * width)), shape_of((own, width))]
        out_specs = [whole_block(each.shape) for each in outs]
        scratch = [pltpu.VMEM((own, width), full_type)] * 2
    else:
        outs = [shape_of((own, width), full_type)] * 2
        out_specs, scratch = [held, held], []
        if wants_dq:
            outs = outs + [shape_of((steps * tile, width))]
            out_specs = out_specs + [pl.BlockSpec((tile, width), lambda i: (i, 0))]
    return pl.pallas_call(
        kernel,
        grid=(steps,),
        in_specs=in_specs,
        out_specs=out_specs,
        out_shape=outs,
        scratch_shapes=scratch,
        compiler_params=room_for_keys(keys),
        cost_estimate=brief,
        name="attend_back",
    )(*args)


def lanes_of(ref):
    return jnp.concatenate([ref[at] for at in range(ref.shape[0])], axis=1)


def rows_of(refs):
    return jnp.concatenate([ref[...] for ref in refs], axis=0)


def gather_blocks(block_refs, rows):
    @pl.when(pl.program_id(0) == 0)
    def _():
        span = block_refs[0].shape[0]
        for at, ref in enumerate(block_refs):
            rows[at * span : (at + 1) * span, :] = ref[...]


def feed_up_kernel(*refs):
    *row_refs, up_ref, g_ref, slope_ref, rows = refs
    gather_blocks(row_refs, rows)
    whole = low_dot(rows[...], up_ref[...])
    span = row_refs[0].shape[0]
    for at in range(len(row_refs)):
        place = pl.ds(at * span, span)
        inner = whole[at * span : (at + 1) * span]
        normal = 0.5 * (1.0 + lax.erf(inner * 0.7071067811865476))
        g_ref[place, :] = (inner * normal).astype(low_type)
        slope = normal + inner * jnp.exp(-0.5 * inner * inner) * 0.3989422804014327
        slope_ref[place, :] = slope.astype(low_type)


def feed_up(blocks, w_up, units):
    own, width = blocks[0].shape
    rows = own * len(blocks)
    tile = 256
    return pl.pallas_call(
        feed_up_kernel,
        grid=(units // tile,),
        in_specs=[pl.BlockSpec((own, width), lambda i: (0, 0))] * len(blocks)
        + [pl.BlockSpec((width, tile), lambda i: (0, i))],
        out_specs=[pl.BlockSpec((rows, tile), lambda i: (0, i))] * 2,
        out_shape=[shape_of((rows, units))] * 2,
        scratch_shapes=[pltpu.VMEM((rows, width), low_type)],
        compiler_params=room(10),
        cost_estimate=brief,
        name="feed_up",
    )(*blocks, w_up)


def store_blocks(total, block_refs):
    rows = total.shape[0] // len(block_refs)
    for at, ref in enumerate(block_refs):
        ref[...] = total[at * rows : (at + 1) * rows].astype(ref.dtype)


def blocks_of(rows, width):
    count = lax.axis_size("mp")
    kept = [shape_of((rows // count, width), full_type)] * (count // 2)
    return kept + [shape_of((rows // count, width))] * (count // 2)


def feed_down_kernel(g_ref, down_ref, *block_refs):
    store_blocks(low_dot(g_ref[...], lanes_of(down_ref)), block_refs)


def feed_down(active, w_down):
    rows, units = active.shape
    blocks, _, lanes = w_down.shape
    tile = 2
    return pl.pallas_call(
        feed_down_kernel,
        grid=(blocks // tile,),
        in_specs=[
            pl.BlockSpec((rows, units), lambda i: (0, 0)),
            pl.BlockSpec((tile, units, lanes), lambda i: (i, 0, 0)),
        ],
        out_specs=[
            pl.BlockSpec((each.shape[0], tile * lanes), lambda i: (0, i))
            for each in blocks_of(rows, blocks * lanes)
        ],
        out_shape=blocks_of(rows, blocks * lanes),
        compiler_params=room(10),
        cost_estimate=brief,
        name="feed_down",
    )(active, w_down)


def feed_inner_kernel(*refs):
    *row_refs, down_ref, slope_ref, dz_ref, rows = refs
    gather_blocks(row_refs, rows)
    dactive = low_dot(rows[...], lanes_of(down_ref), contract_cols)
    dz_ref[...] = (dactive * slope_ref[...].astype(full_type)).astype(low_type)


def feed_inner(blocks, w_down, slope):
    own, width = blocks[0].shape
    rows, units = slope.shape
    tile = 256
    lanes = w_down.shape[2]
    return pl.pallas_call(
        feed_inner_kernel,
        grid=(units // tile,),
        in_specs=[pl.BlockSpec((own, width), lambda i: (0, 0))] * len(blocks)
        + [
            pl.BlockSpec((w_down.shape[0], tile, lanes), lambda i: (0, i, 0)),
            pl.BlockSpec((rows, tile), lambda i: (0, i)),
        ],
        out_specs=pl.BlockSpec((rows, tile), lambda i: (0, i)),
        out_shape=shape_of((rows, units)),
        scratch_shapes=[pltpu.VMEM((rows, width), low_type)],
        compiler_params=room(10),
        cost_estimate=brief,
        name="feed_inner",
    )(*blocks, w_down, slope)


def feed_back_kernel(dz_ref, up_ref, *block_refs):
    store_blocks(low_dot(dz_ref[...], up_ref[...], contract_cols), block_refs)


def feed_back(dinner, w_up):
    rows, units = dinner.shape
    width = w_up.shape[0]
    tile = 256
    return pl.pallas_call(
        feed_back_kernel,
        grid=(width // tile,),
        in_specs=[
            pl.BlockSpec((rows, units), lambda i: (0, 0)),
            pl.BlockSpec((tile, units), lambda i: (i, 0)),
        ],
        out_specs=[
            pl.BlockSpec((each.shape[0], tile), lambda i: (0, i))
            for each in blocks_of(rows, width)
        ],
        out_shape=blocks_of(rows, width),
        compiler_params=room(10),
        cost_estimate=brief,
        name="feed_back",
    )(dinner, w_up)


def late_forward_kernel(*refs):
    *e_refs, q_ref, live_ref, sharp_ref, soft_ref, e_rows = refs
    gather_blocks(e_refs, e_rows)
    blocks = soft_ref.shape[0]
    per = blocks // len(e_refs)
    whole = low_dot(e_rows[...], q_ref[...], contract_cols)
    rows = e_refs[0].shape[0]
    for at in range(len(e_refs)):
        place = pl.ds(at * rows, rows)
        sharp = whole[at * rows : (at + 1) * rows] * 2.0 + live_ref[place, :]
        sharp_ref[place, :] = sharp
        cube = sharp.reshape(per, rows // per, sharp.shape[1])
        top = jnp.max(cube, axis=1)
        total = jnp.sum(jnp.exp(cube - top[:, None, :]), axis=1)
        soft = jnp.where(top > 0.5 * neg_big, top + jnp.log(total), neg_big)
        soft_ref[pl.ds(at * per, per), :] = soft


def late_forward(e_blocks, queries, live_bias, blocks):
    own, width = e_blocks[0].shape
    rows = own * len(e_blocks)
    count = queries.shape[0]
    tile = 512
    return pl.pallas_call(
        late_forward_kernel,
        grid=(count // tile,),
        in_specs=[pl.BlockSpec((own, width), lambda i: (0, 0))] * len(e_blocks)
        + [
            pl.BlockSpec((tile, width), lambda i: (i, 0)),
            pl.BlockSpec((rows, 1), lambda i: (0, 0)),
        ],
        out_specs=[
            pl.BlockSpec((rows, tile), lambda i: (0, i)),
            pl.BlockSpec((blocks, tile), lambda i: (0, i)),
        ],
        out_shape=[shape_of((rows, count), full_type), shape_of((blocks, count), full_type)],
        scratch_shapes=[pltpu.VMEM((rows, width), low_type)],
        compiler_params=room(14),
        cost_estimate=brief,
        name="late_forward",
    )(*e_blocks, queries, live_bias)


def join_soft(soft, far, same):
    top = soft
    for at in range(far.shape[0]):
        top = jnp.maximum(top, far[at])
    total = jnp.exp(soft - top)
    for at in range(far.shape[0]):
        total = total + jnp.exp(far[at] - top)
    blocks = soft.shape[0]
    most = jnp.full(soft.shape, neg_big, full_type)
    for at in range(blocks):
        shared = same[:, at : at + 1] > 0.0
        most = jnp.maximum(most, jnp.where(shared, top[at : at + 1], neg_big))
    sums = jnp.zeros(soft.shape, full_type)
    for at in range(blocks):
        shared = same[:, at : at + 1] > 0.0
        term = jnp.where(shared, top[at : at + 1], neg_big)
        sums = sums + jnp.exp(term - most) * total[at : at + 1]
    return most + jnp.log(sums)


def late_backward_kernel(
    sharp_ref, soft_ref, far_ref, same_ref, place_ref, weight_ref, q_ref, *refs
):
    *block_refs, score_ref, total = refs
    step = pl.program_id(0)
    blocks = soft_ref.shape[0]
    rows, tile = sharp_ref.shape
    soft = join_soft(soft_ref[...], far_ref[...], same_ref[...])
    cube = sharp_ref[...].reshape(blocks, rows // blocks, tile)
    pulled = weight_ref[...][:, None, :] * jnp.exp(cube - soft[:, None, :])
    term = low_dot(pulled.reshape(rows, tile).astype(low_type), q_ref[...])
    query = lax.broadcasted_iota(jnp.int32, (tile, score_ref.shape[0]), 0) // QLEN
    count = lax.broadcasted_iota(jnp.int32, (tile, score_ref.shape[0]), 1)
    pool = jnp.where(query == count, 0.5 / QLEN, 0.0)
    exact = lax.Precision.HIGHEST
    means = lax.dot_general(pool, soft, (((0,), (1,)), ((), ())), precision=exact)
    score_ref[...] = lax.dot_general(means, place_ref[...], contract_inner, precision=exact)

    @pl.when(step == 0)
    def _():
        total[...] = term

    @pl.when(step > 0)
    def _():
        total[...] += term

    @pl.when(step == pl.num_programs(0) - 1)
    def _():
        store_blocks(total[...], block_refs)


def late_backward(sharp, soft, far, same, place, weight, queries):
    rows, count = sharp.shape
    width = queries.shape[1]
    blocks = soft.shape[0]
    tile = min(1024, count)
    outs = blocks_of(rows, width)
    return pl.pallas_call(
        late_backward_kernel,
        grid=(count // tile,),
        in_specs=[
            pl.BlockSpec((rows, tile), lambda i: (0, i)),
            pl.BlockSpec((blocks, tile), lambda i: (0, i)),
            pl.BlockSpec((far.shape[0], blocks, tile), lambda i: (0, 0, i)),
            whole_block(same.shape),
            whole_block(place.shape),
            pl.BlockSpec((blocks, tile), lambda i: (0, i)),
            pl.BlockSpec((tile, width), lambda i: (i, 0)),
        ],
        out_specs=[whole_block(each.shape) for each in outs]
        + [pl.BlockSpec((tile // QLEN, NPASS), lambda i: (i, 0))],
        out_shape=outs + [shape_of((count // QLEN, NPASS), full_type)],
        scratch_shapes=[pltpu.VMEM((rows, width), full_type)],
        compiler_params=room(24),
        cost_estimate=brief,
        name="late_backward",
    )(sharp, soft, far, same, place, weight, queries)


def norm_stats(values):
    centre = values - jnp.mean(values, axis=-1, keepdims=True)
    spread = jnp.mean(centre * centre, axis=-1, keepdims=True)
    scale = lax.rsqrt(spread + 1e-05)
    return centre * scale, scale


def norm_backward(unit, scale, gain, grad):
    dunit = grad * gain
    dvalues = scale * (
        dunit
        - jnp.mean(dunit, axis=-1, keepdims=True)
        - unit * jnp.mean(dunit * unit, axis=-1, keepdims=True)
    )
    return (
        dvalues,
        jnp.sum(grad * unit, axis=0, keepdims=True),
        jnp.sum(grad, axis=0, keepdims=True),
    )


def norm_one_kernel(*refs):
    *terms, norm_ref, h_ref, low_ref, unit_ref, scale_ref = refs
    unit, scale = norm_stats(add_up(terms))
    normed = unit * norm_ref[0:1] + norm_ref[1:2]
    h_ref[...] = normed
    low_ref[...] = normed.astype(low_type)
    unit_ref[...] = unit
    scale_ref[...] = scale


def lanes_at(order_ref, at, span):
    return pl.ds(pl.multiple_of(order_ref[at] * span, span), span)


def norm_two_kernel(order_ref, *refs):
    *rest, low_ref, unit_ref, scale_ref, e_ref, elow_ref, inv_ref = refs
    parts = order_ref.shape[0]
    *terms, norm_ref = rest[:-parts]
    col_refs = rest[-parts:]
    unit, scale = norm_stats(add_up(terms))
    normed_low = (unit * norm_ref[2:3] + norm_ref[3:4]).astype(low_type)
    low_ref[...] = normed_low
    unit_ref[...] = unit
    scale_ref[...] = scale
    span = col_refs[0].shape[1]
    squares = 0.0
    for at, ref in enumerate(col_refs):
        projected = low_dot(normed_low, ref[...])
        e_ref[:, lanes_at(order_ref, at, span)] = projected
        squares = squares + jnp.sum(projected * projected, axis=-1, keepdims=True)
    inv = lax.rsqrt(squares + 1e-06)
    embedded = e_ref[...] * inv
    e_ref[...] = embedded
    elow_ref[...] = embedded.astype(low_type)
    inv_ref[...] = inv


def norm_two_back_kernel(order_ref, *refs):
    *rest, own_ref, far_ref, dr_ref, low_ref, g_ref, du_ref = refs
    parts = order_ref.shape[0]
    *terms, norm_ref, unit_ref, scale_ref, e_ref, inv_ref = rest[:-parts]
    col_refs = rest[-parts:]
    dembed = add_up(terms)
    embedded = e_ref[...]
    along = jnp.sum(embedded * dembed, axis=-1, keepdims=True)
    du_ref[...] = (inv_ref[...] * (dembed - embedded * along)).astype(low_type)
    span = col_refs[0].shape[1]
    dnormed = 0.0
    for at, ref in enumerate(col_refs):
        dproj = du_ref[:, lanes_at(order_ref, at, span)]
        dnormed = dnormed + low_dot(dproj, ref[...], contract_cols)
    half = own_ref.shape[1]
    mine = order_ref[0] // (parts // 2)
    own_ref[...] = du_ref[:, pl.ds(pl.multiple_of(mine * half, half), half)]
    far_ref[...] = du_ref[:, pl.ds(pl.multiple_of((1 - mine) * half, half), half)]
    dresid, dgain, dshift = norm_backward(
        unit_ref[...], scale_ref[...], norm_ref[2:3], dnormed
    )
    dr_ref[...] = dresid
    low_ref[...] = dresid.astype(low_type)
    g_ref[...] = jnp.concatenate([dgain, dshift], 0)


def split_sums(sums):
    high = sums.astype(low_type).astype(full_type)
    zeros = jnp.zeros((SPARE - 8, sums.shape[1]), full_type)
    return jnp.concatenate([high, sums - high, zeros], 0).astype(low_type)


def norm_one_back_kernel(*refs):
    *terms, norm_ref, unit_ref, scale_ref, two_ref, dr_ref, pack_ref = refs
    dresid, dgain, dshift = norm_backward(
        unit_ref[...], scale_ref[...], norm_ref[0:1], add_up(terms)
    )
    dr_ref[...] = dresid
    rows = dresid.shape[0]
    pack_ref[0:rows, :] = dresid.astype(low_type)
    pack_ref[rows : rows + SPARE, :] = split_sums(
        jnp.concatenate([dgain, dshift, two_ref[...]], 0)
    )


def fold_kernel(*refs):
    *terms, low_ref = refs
    low_ref[...] = add_up(terms).astype(low_type)


def rows_fold(terms):
    return whole_call(fold_kernel, [shape_of(terms[0].shape)], "fold", *terms)[0]


def mix_kernel(o_ref, out_ref, *block_refs):
    rows = o_ref.shape[1]
    weight = jnp.concatenate([out_ref[at, 0:rows, :] for at in range(out_ref.shape[0])], axis=1)
    store_blocks(low_dot(o_ref[...], weight), block_refs)


def unmix_kernel(*refs):
    *packs, out_ref, do_ref, sums_ref = refs
    rows = do_ref.shape[1]
    weight = jnp.concatenate([out_ref[at, 0:rows, :] for at in range(out_ref.shape[0])], axis=1)
    own = packs[0].shape[0] - SPARE
    sums = jnp.zeros((8, weight.shape[1]), full_type)
    mixed = jnp.concatenate([ref[0:own, :] for ref in packs], axis=0)
    do_ref[...] = low_dot(mixed, weight, contract_cols).astype(low_type)
    for ref in packs:
        sums = sums + ref[own : own + SPARE, :].astype(full_type)[:8]
    sums_ref[...] = split_sums(sums[:4] + sums[4:])


def block_order(masks):
    return lax.axis_index("dp") ^ jnp.asarray(offsets_of(masks[::-1]), jnp.int32)


def ordered_call(kernel, outs, scratch, name, order, *args, grant=20):
    return pl.pallas_call(
        kernel,
        grid=(1,),
        in_specs=[pl.BlockSpec(memory_space=pltpu.SMEM)]
        + [whole_block(each.shape) for each in args],
        out_specs=[whole_block(each.shape) for each in outs],
        out_shape=outs,
        scratch_shapes=[pltpu.VMEM(*each) for each in scratch],
        compiler_params=room(grant),
        cost_estimate=brief,
        name=name,
    )(order, *args)


def stored(place_ref, left, right):
    turned = left.T
    cols = right.shape[1]
    for start in range(0, cols, 256):
        stop = min(start + 256, cols)
        place_ref[:, start:stop] = low_dot(turned, right[:, start:stop]).astype(low_type)


def deal(order_ref, keep_ref, send_ref, write):
    half = keep_ref.shape[0]
    for at in range(2 * half):
        write(keep_ref.at[at] if at < half else send_ref.at[at - half], order_ref[at])


def rows_in(ref, block, count):
    return ref[pl.ds(pl.multiple_of(block * count, count), count), :]


def lanes_in(ref, block):
    return ref[:, pl.ds(pl.multiple_of(block * LANES, LANES), LANES)]


def halves_like(count, block):
    return [shape_of((count // 2,) + block)] * 2


def grad_down_kernel(order_ref, active_ref, *refs):
    *row_refs, keep_ref, send_ref, total = refs
    stored(total, active_ref[...], rows_of(row_refs))

    def write(ref, block):
        ref[...] = lanes_in(total, block)

    deal(order_ref, keep_ref, send_ref, write)


def grad_down(active, row_blocks, masks):
    count = lax.axis_size("dp")
    units, width = active.shape[1], row_blocks[0].shape[1]
    if width // count == LANES:
        return ordered_call(
            grad_down_kernel,
            halves_like(count, (units, LANES)),
            [((units, width), low_type)],
            "grad_down",
            block_order(masks),
            active,
            *row_blocks,
        )
    whole = low_dot(active, jnp.concatenate(row_blocks, 0), contract_rows).astype(low_type)
    return halves(arrange(jnp.swapaxes(whole.reshape(units, count, -1), 0, 1), "dp", masks))


def halves(blocks):
    half = blocks.shape[0] // 2
    return blocks[:half], blocks[half:]


def grad_up_kernel(order_ref, dinner_ref, *refs):
    *row_refs, keep_ref, send_ref, total = refs
    parts = len(row_refs) // 3
    units = dinner_ref.shape[1]
    block_rows = keep_ref.shape[1]
    cols = keep_ref.shape[2] - units
    stored(total.at[:, 0:units], rows_of(row_refs[:parts]), dinner_ref[...])
    mine = order_ref[order_ref.shape[0] - 1] % (row_refs[-1].shape[1] // cols)
    mine = pl.ds(pl.multiple_of(mine * cols, cols), cols)
    dproj = jnp.concatenate([ref[:, mine] for ref in row_refs[2 * parts :]], axis=0)
    stored(total.at[:, units:], rows_of(row_refs[parts : 2 * parts]), dproj)

    def write(ref, block):
        ref[...] = rows_in(total, block, block_rows)

    deal(order_ref, keep_ref, send_ref, write)


def grad_up(dinner, one_blocks, two_blocks, du_blocks, col_width, masks):
    count = lax.axis_size("dp")
    units, width = dinner.shape[1], one_blocks[0].shape[1]
    column = lax.axis_index("mp")
    rows = width // count
    if rows == LANES:
        order = jnp.concatenate([block_order(masks), column.reshape(1)])
        return ordered_call(
            grad_up_kernel,
            halves_like(count, (rows, units + col_width)),
            [((width, units + col_width), low_type)],
            "grad_up",
            order,
            dinner,
            *one_blocks,
            *two_blocks,
            *du_blocks,
        )
    column = column % (du_blocks[0].shape[1] // col_width)
    dproj = lax.dynamic_slice_in_dim(
        jnp.concatenate(du_blocks, 0), column * col_width, col_width, 1
    )
    up = low_dot(jnp.concatenate(one_blocks, 0), dinner, contract_rows)
    col = low_dot(jnp.concatenate(two_blocks, 0), dproj, contract_rows)
    whole = jnp.concatenate([up, col], 1).astype(low_type)
    return halves(arrange(whole.reshape(count, rows, -1), "dp", masks))


def grad_qk_kernel(order_ref, left_ref, right_ref, keep_ref, send_ref, total):
    block_rows = keep_ref.shape[1]
    stored(total, left_ref[...], right_ref[...])

    def write(ref, block):
        ref[...] = rows_in(total, block, block_rows)

    deal(order_ref, keep_ref, send_ref, write)


def grad_qk(left, right, masks):
    count = lax.axis_size("dp")
    width, cols = left.shape[1], right.shape[1]
    rows = width // count
    if rows == LANES:
        return ordered_call(
            grad_qk_kernel,
            halves_like(count, (rows, cols)),
            [((width, cols), low_type)],
            "grad_qk",
            block_order(masks),
            left,
            right,
        )
    whole = low_dot(left, right, contract_rows).astype(low_type)
    return halves(arrange(whole.reshape(count, rows, cols), "dp", masks))


def grad_vo_kernel(order_ref, hidden_ref, dv_ref, o_ref, *refs):
    *packs, sums_ref, keep_ref, send_ref, total_v, total_o = refs
    rows = packs[0].shape[0] - SPARE
    cols = dv_ref.shape[1]
    heads = o_ref.shape[1]
    stored(total_v, hidden_ref[...], dv_ref[...])
    mixed = jnp.concatenate([ref[0:rows, :] for ref in packs], axis=0)
    stored(total_o.at[0:heads, :], o_ref[...], mixed)
    total_o[heads : heads + SPARE, :] = sums_ref[...]

    def write(ref, block):
        value = rows_in(total_v, block, LANES)
        for at in range(cols // LANES):
            ref[at * LANES : (at + 1) * LANES, :] = value[:, at * LANES : (at + 1) * LANES]
        ref[cols:, :] = lanes_in(total_o, block)

    deal(order_ref, keep_ref, send_ref, write)


def finish_pair_kernel(keep_ref, other_ref, left_ref, right_ref):
    total = keep_ref[...].astype(full_type) + other_ref[...].astype(full_type)
    cols = left_ref.shape[1]
    left_ref[...] = total[:, :cols]
    right_ref[...] = total[:, cols:]


def finish_pair(scatter, cols):
    rows, both = scatter.keep.shape[1:]
    outs = [shape_of((rows, cols), full_type), shape_of((rows, both - cols), full_type)]
    return whole_call(finish_pair_kernel, outs, "finish_pair", scatter.keep[0], scatter.other[0])


def finish_vo_kernel(keep_ref, other_ref, value_ref, out_ref, *norm_refs):
    total = keep_ref[...].astype(full_type) + other_ref[...].astype(full_type)
    rows, cols = value_ref.shape
    row = 0
    for at in range(0, cols, LANES):
        value_ref[:, at : at + LANES] = total[row : row + rows]
        row += rows
    out_ref[...] = total[row : row + out_ref.shape[0]]
    row += out_ref.shape[0]
    for at, ref in enumerate(norm_refs):
        ref[...] = total[row + at : row + at + 1] + total[row + 4 + at : row + 5 + at]


def finish_vo(keep, other, value_shape, out_shape):
    rows, cols = out_shape
    if cols == LANES:
        outs = [shape_of(value_shape, full_type), shape_of(out_shape, full_type)]
        outs = outs + [shape_of((1, cols), full_type)] * 4
        value, out, *norms = whole_call(finish_vo_kernel, outs, "finish_vo", keep, other)
        return value, out, norms
    total = keep.astype(full_type) + other.astype(full_type)
    value, out = unpack_vo(total, *value_shape, (rows + SPARE, cols))
    return value, out[:rows], out[rows : rows + 4] + out[rows + 4 : rows + 8]


def pack_vo(value, out):
    cols = value.shape[-1]
    parts = [value[..., at : at + LANES] for at in range(0, cols, LANES)]
    return jnp.concatenate(parts + [out.reshape(out.shape[:-2] + (-1, LANES))], axis=-2)


def unpack_vo(packed, rows, cols, out_shape):
    high = rows * cols // LANES
    value = jnp.concatenate(
        [packed[..., at : at + rows, :] for at in range(0, high, rows)], axis=-1
    )
    return value, packed[..., high:, :].reshape(packed.shape[:-2] + out_shape)


def grad_vo(hidden, dvalue, attended, packs, sums, masks):
    count = lax.axis_size("dp")
    width, cols = hidden.shape[1], dvalue.shape[1]
    heads = attended.shape[1]
    rows = width // count
    if rows == LANES:
        block = (cols * rows // LANES + heads + SPARE, LANES)
        return ordered_call(
            grad_vo_kernel,
            halves_like(count, block),
            [((width, cols), low_type), ((heads + SPARE, width), low_type)],
            "grad_vo",
            block_order(masks),
            hidden,
            dvalue,
            attended,
            *packs,
            sums,
        )
    value = low_dot(hidden, dvalue, contract_rows).astype(low_type).reshape(count, rows, cols)
    mixed = jnp.concatenate([each[:-SPARE] for each in packs], 0)
    out = low_dot(attended, mixed, contract_rows).astype(low_type)
    out = jnp.concatenate([out, sums], 0).reshape(heads + SPARE, count, rows)
    return halves(arrange(pack_vo(value, jnp.swapaxes(out, 0, 1)), "dp", masks))


def to_lanes(blocks):
    if blocks.shape[2] == LANES:
        return blocks
    whole = jnp.swapaxes(blocks, 0, 1).reshape(blocks.shape[1], -1, LANES)
    return jnp.swapaxes(whole, 0, 1)


def place_kernel(at_ref, *refs):
    *blocks, out_ref = refs
    rows = blocks[0].shape[0]
    for at, ref in enumerate(blocks):
        start = pl.multiple_of(at_ref[at] * rows, rows)
        out_ref[pl.ds(start, rows), :] = ref[...].astype(full_type)


def place_rows(order, blocks):
    rows, width = blocks[0].shape
    outs = [shape_of((rows * len(blocks), width), full_type)]
    return ordered_call(place_kernel, outs, [], "place_rows", order, *blocks)[0]


def unproject_kernel(dqk_ref, dv_ref, a_ref, b_ref, *block_refs):
    total = low_dot(dqk_ref[...], a_ref[...], contract_cols)
    store_blocks(total + low_dot(dv_ref[...], b_ref[...], contract_cols), block_refs)


def unproject(dqk, dvalue, w_qk, w_v):
    outs = blocks_of(dqk.shape[0], w_qk.shape[0])
    return whole_call(unproject_kernel, outs, "unproject", dqk, dvalue, w_qk, w_v)


def fold_pair_kernel(keep_ref, got_ref, *low_refs):
    total = keep_ref[...] + got_ref[...].astype(full_type)
    rows = low_refs[0].shape[0]
    for at, ref in enumerate(low_refs):
        ref[...] = total[at * rows : (at + 1) * rows].astype(low_type)


def close_kernel(*refs):
    *terms, low_far, high_far, out_ref = refs
    total = add_up(terms)
    half = low_far.shape[0]
    for at, ref in enumerate((low_far, high_far)):
        place = pl.ds(at * half, half)
        part = total[at * half : (at + 1) * half] + ref[...].astype(full_type)
        out_ref[place, :] = part.astype(low_type)


def pack_kernel(order_ref, *refs):
    hidden_ref, q_ref, k_ref, v_ref, o_ref, up_ref, col_ref, *norm_refs = refs[:11]
    a_out, u_out, b_out, own_out, block_out = refs[11:]
    heads, units = q_ref.shape[1], up_ref.shape[1]
    a_out[:, :heads] = q_ref[...]
    a_out[:, heads:] = k_ref[...]
    u_out[:, :units] = up_ref[...]
    u_out[:, units:] = col_ref[...]
    row = 0
    for at in range(0, heads, LANES):
        b_out[row : row + v_ref.shape[0], :] = v_ref[:, at : at + LANES]
        row += v_ref.shape[0]
    b_out[row : row + o_ref.shape[0], :] = o_ref[...]
    row += o_ref.shape[0]
    norms = [ref[...].astype(full_type).reshape(1, -1) for ref in norm_refs]
    norms = jnp.concatenate(norms + [jnp.zeros((SPARE - 4, LANES), full_type)], axis=0)
    b_out[row : row + SPARE, :] = norms.astype(low_type)
    parts = order_ref.shape[0]
    rows = hidden_ref.shape[0] // parts
    for at in range(parts):
        own_out[at * rows : (at + 1) * rows, :] = rows_in(hidden_ref, order_ref[at], rows)
    block_out[...] = own_out[0:rows, :]


def pack_inputs(order, hidden, w_query, w_key, w_value, w_out, w_up, w_colbert, *norms):
    rows, heads = w_query.shape
    span = hidden.shape[0] // order.shape[0]
    if w_out.shape[1] == LANES and rows == LANES:
        packed = (rows * heads // LANES + w_out.shape[0] + SPARE, LANES)
        outs = [
            shape_of((rows, 2 * heads)),
            shape_of((rows, w_up.shape[1] + w_colbert.shape[1])),
            shape_of(packed),
            shape_of(hidden.shape),
            shape_of((span, hidden.shape[1])),
        ]
        args = (hidden, w_query, w_key, w_value, w_out, w_up, w_colbert) + norms
        return ordered_call(pack_kernel, outs, [], "pack", order, *args, grant=60)
    norms = jnp.concatenate([jnp.stack(norms), jnp.zeros((SPARE - 4, w_out.shape[1]), low_type)], 0)
    blocks = [
        lax.dynamic_slice_in_dim(hidden, order[at] * span, span, 0)
        for at in range(order.shape[0])
    ]
    return (
        jnp.concatenate([w_query, w_key], axis=1),
        jnp.concatenate([w_up, w_colbert], axis=1),
        pack_vo(w_value, jnp.concatenate([w_out, norms], axis=0)),
        jnp.concatenate(blocks),
        blocks[0],
    )


def body(
    hidden_in,
    w_query,
    w_key,
    w_value,
    w_out,
    w_up,
    w_down,
    w_colbert,
    norm1_gain,
    norm1_shift,
    norm2_gain,
    norm2_shift,
    queries,
    passage,
    live,
    score_grad,
):
    tok_rows, width = hidden_in.shape
    device = lax.axis_index("dp")
    column = lax.axis_index("mp")
    dp_size = lax.axis_size("dp")
    mp_size = lax.axis_size("mp")
    group_size = dp_size // NBUCKET
    group_levels = group_size.bit_length() - 1
    own_rows = tok_rows // mp_size
    head_width = w_query.shape[1]
    dp_up, dp_down = upward("dp"), downward("dp")
    turned = dp_up[:1] + dp_down[:-1]
    row_order = offsets_of(downward("mp"))

    def ordered(value, owner, span=own_rows):
        return jnp.concatenate(
            [
                lax.dynamic_slice_in_dim(value, (owner * mp_size + (column ^ at)) * span, span, 0)
                for at in row_order
            ]
        )

    def group_gather(value):
        for level in range(group_levels):
            value = jnp.concatenate([value, swap(value, "dp", 2**level)], 0)
        return value

    across = dp_up[-1:] + dp_up[:-1]
    turned_back, across_back = turned[::-1], across[::-1]
    col_order = column ^ jnp.asarray(row_order, jnp.int32)
    norms = (norm1_gain, norm1_shift, norm2_gain, norm2_shift)
    out_shape = (w_out.shape[0] + SPARE, w_out.shape[1])
    packed_a, packed_u, packed_b, hidden_own, own_hidden = pack_inputs(
        col_order, hidden_in, w_query, w_key, w_value, w_out, w_up, w_colbert, *norms
    )
    pack_a = Gather(packed_a, "dp", dp_down)
    pack_u = Gather(packed_u, "dp", dp_down)
    pack_b = Gather(packed_b, "dp", dp_down)
    pack_d = Gather(w_down, "dp", turned)

    main = (hidden_own, own_hidden)
    main = pack_a.start(main)
    main = pack_b.start(main)
    main = pack_d.start(main)
    others = group_gather(main[1][None])[1:]
    seg_own = ordered(passage, device)
    live_own = ordered(live, device)
    seg_others = jnp.concatenate([ordered(passage, device ^ at) for at in range(1, group_size)])
    live_others = jnp.concatenate([ordered(live, device ^ at) for at in range(1, group_size)])
    slot_own = jnp.where(live_own == 1, seg_own, -1)
    slot_keys = jnp.concatenate([slot_own, jnp.where(live_others == 1, seg_others, -1)])
    seg_row = seg_own.astype(full_type)[None, :]
    slot_row = slot_keys.astype(full_type)[None, :]
    blocks = 2 ** (NBUCKET - 1)
    seg_block = seg_own.reshape(blocks, -1)[:, 0]
    live_bias = jnp.where(live_own == 1, 0.0, neg_big)[:, None]
    same = seg_block[:, None] == seg_block[None, :]
    passages = jnp.arange(NPASS, dtype=jnp.int32)
    place = (seg_block[:, None] == passages[None, :]).astype(full_type)
    grad_block = jnp.sum(place[:, None, :] * score_grad[None], axis=2)
    weight = jnp.repeat(grad_block / QLEN, QLEN, axis=1)
    same = same.astype(full_type)
    place = place / jnp.sum(same, axis=1, keepdims=True)
    slot_own = slot_own.astype(full_type)[None, :]
    early = (seg_row, slot_own, slot_row, live_bias, weight, same, place)
    early, main = tie(early, main)
    seg_row, slot_own, slot_row, live_bias, weight, same, place = early
    main = pack_a.step(main)
    main = pack_b.step(main)
    main = pack_u.start(main)
    others, main = tie(others, main)
    far_others = swap(others, "mp", 2)
    main = pack_d.finish(main)
    main = pack_a.step(main)
    main = pack_b.step(main)
    main = pack_u.step(main)
    main = pack_d.start(main)
    far_others, main = tie(far_others, main)
    main = pack_u.step(main)
    others = [others, far_others]
    others = others + [swap(each, "mp", 1) for each in others]
    others = jnp.stack(others, 1).reshape(-1, width)
    hidden_own, own_hidden = main
    hidden_all = jnp.concatenate([hidden_own, others], 0)
    main = (hidden_own, own_hidden, hidden_all)
    main = pack_a.drain(main)
    full_a = pack_a.value().reshape(width, -1)
    full_a, main = tie(full_a, main)
    hidden_own, own_hidden, hidden_all = main

    query_key = low_dot(hidden_all, full_a).astype(low_type)
    main = (query_key, hidden_all)
    main = pack_b.drain(main)
    full_b, full_out = unpack_vo(pack_b.value(), w_value.shape[0], head_width, out_shape)
    full_b = full_b.reshape(width, head_width)
    full_out = to_lanes(full_out)
    (full_b, full_out), main = tie((full_b, full_out), main)
    main = pack_d.step(main)
    query_key, hidden_all = main
    value_rows = low_dot(hidden_all, full_b).astype(low_type)
    norm_rows = jnp.swapaxes(full_out[:, head_width : head_width + 4], 0, 1).reshape(4, width)
    norm_rows = norm_rows.astype(full_type)
    attended, lse = attend_forward(query_key, value_rows, seg_row, slot_row)
    norm_rows, attended = tie(norm_rows, attended)
    parts = whole_call(mix_kernel, blocks_of(tok_rows, width), "mix", attended, full_out)
    terms = rows_scatter(parts)
    units = w_up.shape[1]
    square = shape_of((own_rows, width), full_type)
    low_square = shape_of((own_rows, width))
    narrow = shape_of((own_rows, 1), full_type)
    normed_one, normed_low, unit_one, scale_one = whole_call(
        norm_one_kernel,
        [square, low_square, square, narrow],
        "norm_one",
        own_hidden,
        *terms,
        norm_rows,
    )

    rows_one = [normed_low, swap(normed_low, "mp", 2)]
    rows_one = pack_u.drain(rows_one)
    full_up = pack_u.value().reshape(width, -1)
    col_own = full_up[:, units:]
    (full_up, col_own), rows_one = tie((full_up, col_own), rows_one)
    rows_one = rows_one + [swap(each, "mp", 1) for each in rows_one]
    far_col = swap(col_own, "mp", 2)
    active, slope = feed_up(rows_one, full_up, units)
    active = pack_d.drain(active)
    full_down = to_lanes(pack_d.value())
    parts = feed_down(active, full_down)
    far_col, parts = tie(far_col, parts)
    terms = rows_scatter(parts)
    col_blocks = [col_own, far_col]
    col_blocks = col_blocks + [swap(each, "mp", 1) for each in col_blocks]
    normed_two_low, unit_two, scale_two, embedded, embed_low, inv_length = ordered_call(
        norm_two_kernel,
        [low_square, square, narrow, square, low_square, narrow],
        [],
        "norm_two",
        col_order,
        normed_one,
        *terms,
        norm_rows,
        *col_blocks,
    )

    (far, far_lse), embed_low = tie((attended, lse), embed_low)
    far = group_gather(far[None])[1:]
    far_lse = group_gather(far_lse[None])[1:]
    far_e = swap(embed_low, "mp", 2)
    (far, far_lse), far_e = tie((far, far_lse), far_e)
    e_blocks = [embed_low, far_e]
    e_blocks = e_blocks + [swap(each, "mp", 1) for each in e_blocks]
    sharp, soft_block = late_forward(e_blocks, queries, live_bias, blocks)
    two_low, soft_block = tie(normed_two_low, soft_block)
    far_two = swap(two_low, "mp", 2)
    soft_far = group_gather(soft_block[None])[1:]
    *parts, scores = late_backward(
        sharp, soft_block, soft_far, same, place, weight, queries
    )
    far_two, parts = tie(far_two, parts)
    far_attended = far.reshape(-1, head_width)
    far_lse = jnp.swapaxes(far_lse, 0, 1).reshape(8, -1)

    score_masks = dp_up[group_levels:]
    scores, parts = tie(scores, parts)
    scores_far = swap(scores, "dp", score_masks[0])
    terms = rows_scatter(parts)
    scores_far, terms = tie(scores_far, terms)
    scores, terms = tie(scores + scores_far, terms)
    scores_far = swap(scores, "dp", score_masks[1])
    low_half = shape_of((own_rows, width // 2))
    du_own, du_far, dresid_two, dresid_low, two_sums = ordered_call(
        norm_two_back_kernel,
        [low_half, low_half, square, low_square, shape_of((2, width), full_type)],
        [((own_rows, width), low_type)],
        "norm_two_back",
        col_order,
        *terms,
        norm_rows,
        unit_two,
        scale_two,
        embedded,
        inv_length,
        *col_blocks,
    )
    dresid_blocks = [dresid_low, swap(dresid_low, "mp", 2)]
    scores_far, dresid_blocks = tie(scores_far, dresid_blocks)
    dresid_blocks = dresid_blocks + [swap(each, "mp", 1) for each in dresid_blocks]
    two_blocks = [normed_two_low, far_two]
    two_blocks = two_blocks + [swap(each, "mp", 1) for each in two_blocks]
    two_blocks, dresid_blocks = tie(two_blocks, dresid_blocks)
    scores = scores + scores_far
    for mask in score_masks[2:]:
        scores = scores + swap(scores, "dp", mask)

    (du_own, du_far), dresid_blocks = tie((du_own, du_far), dresid_blocks)
    du_far = swap(du_far, "mp", 2)
    dinner = feed_inner(dresid_blocks, full_down, slope)
    du_far, dinner = tie(du_far, dinner)
    parts = feed_back(dinner, full_up)
    got_far, got = swap(parts[3], "mp", 1), swap(parts[2], "mp", 1)
    du_blocks = [du_own, du_far]
    du_blocks = du_blocks + [swap(each, "mp", 1) for each in du_blocks]
    low = rows_fold([parts[1], got_far])
    (active, dinner, got), low = tie((active, dinner, got), low)
    far_low = swap(low, "mp", 2)
    grad_d = Scatter(*grad_down(active, dresid_blocks, dp_up), "dp", dp_up)
    dinner = grad_d.start(dinner)
    grad_u = Scatter(
        *grad_up(dinner, rows_one, two_blocks, du_blocks, w_colbert.shape[1], across_back),
        "dp",
        across_back,
    )
    far_low = grad_u.start(far_low)
    dresid_one, mixed_pack = whole_call(
        norm_one_back_kernel,
        [square, shape_of((own_rows + SPARE, width))],
        "norm_one_back",
        dresid_two,
        parts[0],
        got,
        far_low,
        norm_rows,
        unit_one,
        scale_one,
        two_sums,
    )
    packs = rows_gather(mixed_pack)

    dattended, norm_sums = whole_call(
        unmix_kernel,
        [shape_of((tok_rows, head_width)), shape_of((SPARE, width))],
        "unmix",
        *packs,
        full_out,
    )
    far_grads = group_gather(dattended[None])[1:].reshape(-1, head_width)
    own_q = (query_key, 0, dattended, attended, lse)
    all_keys = (value_rows, slot_row, tok_rows)
    keys = value_rows.shape[0]
    *sums, dquery = attend_back(own_q, None, keys, all_keys, None, True)
    far_grads, dquery = tie(far_grads, dquery)
    dquery = grad_d.step(grad_u.step(dquery))
    far_q = (query_key, tok_rows, far_grads, far_attended, far_lse)
    own_keys = (value_rows, slot_own, tok_rows)
    dqk, dvalue_low = attend_back(far_q, None, tok_rows, own_keys, sums, False, (dquery,))
    parts = unproject(dqk, dvalue_low, full_a, full_b)
    got_far, got = swap(parts[3], "mp", 1), swap(parts[2], "mp", 1)
    low = whole_call(
        fold_pair_kernel,
        [shape_of((own_rows // 2, width))] * 2,
        "fold_pair",
        parts[1],
        got_far,
    )
    (dqk, dvalue_low), low = tie((dqk, dvalue_low), low)
    far_low = [swap(each, "mp", 2) for each in low]
    grad_b = Scatter(
        *grad_vo(hidden_own, dvalue_low, attended, packs, norm_sums, across_back),
        "dp",
        across_back,
    )
    dqk = grad_b.start(dqk)
    dqk = grad_d.step(dqk)
    grad_a = Scatter(*grad_qk(hidden_own, dqk, dp_up), "dp", dp_up)
    last = grad_a.start(parts[0])
    far_low = grad_u.step(far_low)
    terms = [dresid_one, last, got, *far_low]
    input_own = whole_call(close_kernel, [low_square], "close", *terms)[0]
    far_own = swap(input_own, "mp", 2)
    far_own = grad_a.step(grad_b.step(far_own))
    input_blocks = [input_own, far_own]
    input_blocks = input_blocks + [swap(each, "mp", 1) for each in input_blocks]
    input_grad = place_rows(col_order, input_blocks)
    input_grad = grad_b.step(grad_a.step(input_grad))
    input_grad = grad_d.finish(grad_u.finish(input_grad))
    down_grad = grad_d.value()
    up_grad, colbert_grad = finish_pair(grad_u, units)
    ends = (input_grad, down_grad, up_grad, colbert_grad)
    ends = grad_a.finish(ends)
    query_grad, key_grad = finish_pair(grad_a, head_width)
    ends, (query_grad, key_grad) = grad_b.finish((ends, (query_grad, key_grad)))
    input_grad, down_grad, up_grad, colbert_grad = ends
    value_grad, out_grad, norm_grads = finish_vo(
        grad_b.keep[0], grad_b.other[0], w_value.shape, w_out.shape
    )
    return (
        scores,
        input_grad,
        query_grad,
        key_grad,
        value_grad,
        out_grad,
        up_grad,
        down_grad,
        colbert_grad,
        norm_grads[0].reshape(-1),
        norm_grads[1].reshape(-1),
        norm_grads[2].reshape(-1),
        norm_grads[3].reshape(-1),
    )


def solution(mesh):
    rows, both, across = P("dp", None), P("dp", "mp"), P("mp", "dp")
    return jax.shard_map(
        body,
        mesh=mesh,
        in_specs=(
            (rows, both, both, both, across, both, across, both)
            + (P("dp"),) * 4
            + (P("mp", None), P(), P(), P("mp", None))
        ),
        out_specs=(
            (P("mp", None), rows, both, both, both, across, both, across, both)
            + (P("dp"),) * 4
        ),
        check_vma=False,
    )
```

```python
import jax
import jax.numpy as jnp
from jax import lax
from jax.experimental import pallas as pl
from jax.experimental.pallas import tpu as pltpu
from jax.sharding import PartitionSpec as P

HEAD_DIM = 64
QLEN = 32
NBUCKET = 4
NPASS = 15
LANES = 128
SPARE = 16

neg_big = -1e30
low_type = jnp.bfloat16
full_type = jnp.float32
contract_rows = (((0,), (0,)), ((), ()))
contract_cols = (((1,), (1,)), ((), ()))
contract_inner = (((1,), (0,)), ((), ()))


def room(mebibytes):
    return pltpu.CompilerParams(vmem_limit_bytes=mebibytes * 1024 * 1024)


def rows_for_keys(keys):
    return 256 if keys <= 2048 else LANES


def room_for_keys(keys):
    return room(min(56, 4 + keys * rows_for_keys(keys) // 16384))


brief = pl.CostEstimate(flops=1, bytes_accessed=1, transcendentals=0)


def low_dot(left, right, dims=contract_inner):
    return lax.dot_general(left, right, dims, preferred_element_type=full_type)


def shape_of(shape, dtype=low_type):
    return jax.ShapeDtypeStruct(shape, dtype)


def whole_block(shape):
    return pl.BlockSpec(shape, lambda i: (0,) * len(shape))


def whole_call(kernel, outs, name, *args):
    return pl.pallas_call(
        kernel,
        grid=(1,),
        in_specs=[whole_block(each.shape) for each in args],
        out_specs=[whole_block(each.shape) for each in outs],
        out_shape=outs,
        compiler_params=room(12),
        cost_estimate=brief,
        name=name,
    )(*args)


def swap(value, axis, mask):
    pairs = [(source, source ^ mask) for source in range(lax.axis_size(axis))]
    return lax.ppermute(value, axis, pairs)


def bits_of(axis):
    return lax.axis_size(axis).bit_length() - 1


def has_bit(axis, mask):
    return lax.axis_index(axis) // mask % 2 == 1


def upward(axis):
    return [2**level for level in range(bits_of(axis))]


def downward(axis):
    return upward(axis)[::-1]


def offsets_of(masks):
    order = [0]
    for mask in masks:
        order = order + [at ^ mask for at in order]
    return order


def arrange(blocks, axis, masks):
    levels = bits_of(axis)
    cube = blocks.reshape((2,) * levels + blocks.shape[1:])
    for mask in masks:
        at = levels - mask.bit_length()
        cube = jnp.where(has_bit(axis, mask), jnp.flip(cube, at), cube)
    front = [levels - mask.bit_length() for mask in masks]
    cube = jnp.transpose(cube, front + list(range(levels, cube.ndim)))
    return cube.reshape(blocks.shape)


def tie(*values):
    return lax.optimization_barrier(values)


class Gather:
    def __init__(self, value, axis, masks):
        self.axis, self.masks = axis, list(masks)
        self.levels, self.shape = bits_of(axis), value.shape
        self.whole = value.reshape((1,) * self.levels + value.shape)

    def start(self, main):
        if self.masks:
            self.whole, main = tie(self.whole, main)
            self.other = swap(self.whole, self.axis, self.masks[0])
        return main

    def finish(self, main):
        if self.masks:
            mask = self.masks.pop(0)
            other, main = tie(self.other, main)
            at = self.levels - mask.bit_length()
            self.whole = jnp.where(
                has_bit(self.axis, mask),
                jnp.concatenate([other, self.whole], at),
                jnp.concatenate([self.whole, other], at),
            )
        return main

    def step(self, main):
        return self.start(self.finish(main))

    def drain(self, main):
        main = self.finish(main)
        while self.masks:
            main = self.finish(self.start(main))
        return main

    def value(self):
        return self.whole.reshape((-1,) + self.shape)


class Scatter:
    def __init__(self, keep, send, axis, masks):
        self.axis, self.masks = axis, list(masks)
        self.keep, self.send = keep, send

    def start(self, main):
        if self.masks:
            self.send, main = tie(self.send, main)
            self.other = swap(self.send, self.axis, self.masks[0])
        return main

    def finish(self, main):
        if self.masks:
            self.masks.pop(0)
            other, main = tie(self.other, main)
            if self.masks:
                self.keep, self.send = halve(self.keep, other)
            else:
                self.other = other
        return main

    def step(self, main):
        return self.start(self.finish(main))

    def drain(self, main):
        main = self.finish(main)
        while self.masks:
            main = self.finish(self.start(main))
        return main

    def value(self):
        return self.keep[0].astype(full_type) + self.other[0].astype(full_type)


def halve_kernel(keep_low, keep_high, other_low, other_high, low_ref, high_ref):
    for keep, other, out in (
        (keep_low, other_low, low_ref),
        (keep_high, other_high, high_ref),
    ):
        total = keep[...].astype(full_type) + other[...].astype(full_type)
        out[...] = total.astype(low_type)


def halve(keep, other):
    half = keep.shape[0] // 2
    block = (1,) + keep.shape[1:]
    low = pl.BlockSpec(block, lambda i: (i, 0, 0))
    high = pl.BlockSpec(block, lambda i: (half + i, 0, 0))
    return pl.pallas_call(
        halve_kernel,
        grid=(half,),
        in_specs=[low, high, low, high],
        out_specs=[low, low],
        out_shape=[shape_of((half,) + keep.shape[1:])] * 2,
        compiler_params=room(8),
        cost_estimate=brief,
        name="halve",
    )(keep, keep, other, other)


def rows_gather(block):
    blocks = [block]
    for mask in downward("mp"):
        blocks = blocks + [swap(each, "mp", mask) for each in blocks]
    return blocks


def rows_scatter(blocks):
    masks = upward("mp")
    terms = [[block] for block in blocks]
    for mask in masks:
        half = len(terms) // 2
        sends = [each[0] if len(each) == 1 else rows_fold(each) for each in terms[half:]]
        order = range(half)[::-1]
        got = {at: swap(sends[at], "mp", mask) for at in order}
        terms = [terms[at] + [got[at]] for at in range(half)]
    return terms[0]


def add_up(refs):
    total = refs[0][...].astype(full_type)
    for ref in refs[1:]:
        total = total + ref[...].astype(full_type)
    return total


def head_mask(width, head):
    lane = lax.broadcasted_iota(jnp.int32, (1, width), 1)
    return lane // HEAD_DIM == head


def only_head(rows, head):
    return jnp.where(head_mask(rows.shape[1], head), rows, jnp.zeros_like(rows))


def attend_forward_kernel(q_ref, k_ref, v_ref, segq_ref, segk_ref, o_ref, stat_ref):
    tile, width = q_ref.shape
    stat = jnp.broadcast_to(segq_ref[...], (LANES, tile)).T
    bias = jnp.where(stat[:, 0:1] == segk_ref[...], 0.0, neg_big)
    out = jnp.zeros((tile, width), full_type)
    lane = lax.broadcasted_iota(jnp.int32, (1, LANES), 1)
    queries = q_ref[...] * jnp.asarray(0.125, low_type)
    for head in range(width // HEAD_DIM):
        raw = low_dot(only_head(queries, head), k_ref[...], contract_cols) + bias
        top = jnp.max(raw, axis=1, keepdims=True)
        terms = jnp.exp(raw - top)
        total = jnp.sum(terms, axis=1, keepdims=True)
        mixed = low_dot(terms.astype(low_type), v_ref[...]) * (1.0 / total)
        out = jnp.where(head_mask(width, head), mixed, out)
        stat = jnp.where(lane == head, top + jnp.log(total), stat)
    o_ref[...] = out.astype(low_type)
    stat_ref[...] = stat.T[: stat_ref.shape[0]]


def attend_forward(query_key, value_rows, seg_rows, seg_keys):
    rows = seg_rows.shape[1]
    keys, width = value_rows.shape
    tile = rows_for_keys(keys)
    return pl.pallas_call(
        attend_forward_kernel,
        grid=(rows // tile,),
        in_specs=[
            pl.BlockSpec((tile, width), lambda i: (i, 0)),
            pl.BlockSpec((keys, width), lambda i: (0, 1)),
            pl.BlockSpec((keys, width), lambda i: (0, 0)),
            pl.BlockSpec((1, tile), lambda i: (0, i)),
            pl.BlockSpec((1, keys), lambda i: (0, 0)),
        ],
        out_specs=[
            pl.BlockSpec((tile, width), lambda i: (i, 0)),
            pl.BlockSpec((8, tile), lambda i: (0, i)),
        ],
        out_shape=[shape_of((rows, width)), shape_of((8, rows), full_type)],
        compiler_params=room_for_keys(keys),
        cost_estimate=brief,
        name="attend_forward",
    )(query_key, query_key, value_rows, seg_rows, seg_keys)


def attend_terms(q_ref, k_ref, v_ref, do_ref, o_ref, segk_ref, lse_ref):
    tile, width = q_ref.shape
    pad = jnp.zeros((LANES - lse_ref.shape[0], tile), full_type)
    lse = jnp.concatenate([lse_ref[...], pad], 0).T
    heads = width // HEAD_DIM
    bias = jnp.where(lse[:, heads : heads + 1] == segk_ref[...], 0.0, neg_big)
    queries = q_ref[...] * jnp.asarray(0.125, low_type)
    grads = do_ref[...]
    both = grads.astype(full_type) * o_ref[...].astype(full_type)
    for head in range(width // HEAD_DIM):
        q_head = only_head(queries, head)
        g_head = only_head(grads, head)
        delta = jnp.sum(only_head(both, head), axis=1, keepdims=True)
        raw = low_dot(q_head, k_ref[...], contract_cols)
        probs = jnp.exp(raw + (bias - lse[:, head : head + 1]))
        dprobs = low_dot(g_head, v_ref[...], contract_cols)
        dscore = (probs * (dprobs - delta)).astype(low_type)
        yield head, q_head, g_head, probs.astype(low_type), dscore


def attend_back(rows_of_q, part, keys, masks, sums, wants_dq, dq_parts=()):
    query_key, first_row, grads, attended, lse = rows_of_q
    value_rows, seg_keys, own = masks
    width = value_rows.shape[1]
    tile = rows_for_keys(keys)
    parts_of = 1 if part is None else 2
    steps = grads.shape[0] // tile // parts_of
    shift = steps if part == 1 else 0
    first = first_row // tile + shift
    closing = len(dq_parts) > 0

    def kernel(*refs):
        base, refs = refs[:7], refs[7:]
        q_ref, k_ref = base[:2]
        before, refs = (refs[:2], refs[2:]) if sums else (None, refs)
        parts, refs = refs[: len(dq_parts)], refs[len(dq_parts) :]
        if closing:
            dqk_out, dv_out, dk_sum, dv_sum = refs
        else:
            dk_sum, dv_sum = refs[:2]
        step = pl.program_id(0)

        @pl.when(step == 0)
        def _():
            dk_sum[...] = before[0][...] if sums else jnp.zeros_like(dk_sum)
            dv_sum[...] = before[1][...] if sums else jnp.zeros_like(dv_sum)

        dquery = jnp.zeros((tile, width), full_type)
        for head, q_head, g_head, probs, dscore in attend_terms(*base):
            if wants_dq:
                dquery = jnp.where(head_mask(width, head), low_dot(dscore, k_ref[...]), dquery)
            dk_sum[...] += low_dot(dscore[:, :own], q_head, contract_rows)
            dv_sum[...] += low_dot(probs[:, :own], g_head, contract_rows)
        if wants_dq:
            refs[2][...] = (dquery * 0.125).astype(low_type)
        if closing:

            @pl.when(step == steps - 1)
            def _():
                rows = own // len(parts)
                for at, ref in enumerate(parts):
                    dqk_out[at * rows : (at + 1) * rows, :width] = ref[...]
                dqk_out[:, width:] = dk_sum[...].astype(low_type)
                dv_out[...] = dv_sum[...].astype(low_type)

    tile_rows = pl.BlockSpec((tile, width), lambda i: (shift + i, 0))
    held = whole_block((own, width))
    in_specs = [
        pl.BlockSpec((tile, width), lambda i: (first + i, 0)),
        pl.BlockSpec((keys, width), lambda i: (0, 1)),
        pl.BlockSpec((keys, width), lambda i: (0, 0)),
        tile_rows,
        tile_rows,
        pl.BlockSpec((1, keys), lambda i: (0, 0)),
        pl.BlockSpec((8, tile), lambda i: (0, shift + i)),
    ]
    args = [query_key, query_key, value_rows, grads, attended, seg_keys, lse]
    if sums:
        in_specs, args = in_specs + [held, held], args + list(sums)
    in_specs = in_specs + [whole_block(each.shape) for each in dq_parts]
    args = args + list(dq_parts)
    if closing:
        outs = [shape_of((own, 2 * width)), shape_of((own, width))]
        out_specs = [whole_block(each.shape) for each in outs]
        scratch = [pltpu.VMEM((own, width), full_type)] * 2
    else:
        outs = [shape_of((own, width), full_type)] * 2
        out_specs, scratch = [held, held], []
        if wants_dq:
            outs = outs + [shape_of((steps * tile, width))]
            out_specs = out_specs + [pl.BlockSpec((tile, width), lambda i: (i, 0))]
    return pl.pallas_call(
        kernel,
        grid=(steps,),
        in_specs=in_specs,
        out_specs=out_specs,
        out_shape=outs,
        scratch_shapes=scratch,
        compiler_params=room_for_keys(keys),
        cost_estimate=brief,
        name="attend_back",
    )(*args)


def lanes_of(ref):
    return jnp.concatenate([ref[at] for at in range(ref.shape[0])], axis=1)


def rows_of(refs):
    return jnp.concatenate([ref[...] for ref in refs], axis=0)


def gather_blocks(block_refs, rows):
    @pl.when(pl.program_id(0) == 0)
    def _():
        span = block_refs[0].shape[0]
        for at, ref in enumerate(block_refs):
            rows[at * span : (at + 1) * span, :] = ref[...]


def feed_up_kernel(*refs):
    *row_refs, up_ref, g_ref, slope_ref, rows = refs
    gather_blocks(row_refs, rows)
    whole = low_dot(rows[...], up_ref[...])
    span = row_refs[0].shape[0]
    for at in range(len(row_refs)):
        place = pl.ds(at * span, span)
        inner = whole[at * span : (at + 1) * span]
        normal = 0.5 * (1.0 + lax.erf(inner * 0.7071067811865476))
        g_ref[place, :] = (inner * normal).astype(low_type)
        slope = normal + inner * jnp.exp(-0.5 * inner * inner) * 0.3989422804014327
        slope_ref[place, :] = slope.astype(low_type)


def feed_up(blocks, w_up, units):
    own, width = blocks[0].shape
    rows = own * len(blocks)
    tile = 256
    return pl.pallas_call(
        feed_up_kernel,
        grid=(units // tile,),
        in_specs=[pl.BlockSpec((own, width), lambda i: (0, 0))] * len(blocks)
        + [pl.BlockSpec((width, tile), lambda i: (0, i))],
        out_specs=[pl.BlockSpec((rows, tile), lambda i: (0, i))] * 2,
        out_shape=[shape_of((rows, units))] * 2,
        scratch_shapes=[pltpu.VMEM((rows, width), low_type)],
        compiler_params=room(10),
        cost_estimate=brief,
        name="feed_up",
    )(*blocks, w_up)


def store_blocks(total, block_refs):
    rows = total.shape[0] // len(block_refs)
    for at, ref in enumerate(block_refs):
        ref[...] = total[at * rows : (at + 1) * rows].astype(ref.dtype)


def blocks_of(rows, width):
    count = lax.axis_size("mp")
    kept = [shape_of((rows // count, width), full_type)] * (count // 2)
    return kept + [shape_of((rows // count, width))] * (count // 2)


def feed_down_kernel(g_ref, down_ref, *block_refs):
    store_blocks(low_dot(g_ref[...], lanes_of(down_ref)), block_refs)


def feed_down(active, w_down):
    rows, units = active.shape
    blocks, _, lanes = w_down.shape
    tile = 2
    return pl.pallas_call(
        feed_down_kernel,
        grid=(blocks // tile,),
        in_specs=[
            pl.BlockSpec((rows, units), lambda i: (0, 0)),
            pl.BlockSpec((tile, units, lanes), lambda i: (i, 0, 0)),
        ],
        out_specs=[
            pl.BlockSpec((each.shape[0], tile * lanes), lambda i: (0, i))
            for each in blocks_of(rows, blocks * lanes)
        ],
        out_shape=blocks_of(rows, blocks * lanes),
        compiler_params=room(10),
        cost_estimate=brief,
        name="feed_down",
    )(active, w_down)


def feed_inner_kernel(*refs):
    *row_refs, down_ref, slope_ref, dz_ref, rows = refs
    gather_blocks(row_refs, rows)
    dactive = low_dot(rows[...], lanes_of(down_ref), contract_cols)
    dz_ref[...] = (dactive * slope_ref[...].astype(full_type)).astype(low_type)


def feed_inner(blocks, w_down, slope):
    own, width = blocks[0].shape
    rows, units = slope.shape
    tile = 256
    lanes = w_down.shape[2]
    return pl.pallas_call(
        feed_inner_kernel,
        grid=(units // tile,),
        in_specs=[pl.BlockSpec((own, width), lambda i: (0, 0))] * len(blocks)
        + [
            pl.BlockSpec((w_down.shape[0], tile, lanes), lambda i: (0, i, 0)),
            pl.BlockSpec((rows, tile), lambda i: (0, i)),
        ],
        out_specs=pl.BlockSpec((rows, tile), lambda i: (0, i)),
        out_shape=shape_of((rows, units)),
        scratch_shapes=[pltpu.VMEM((rows, width), low_type)],
        compiler_params=room(10),
        cost_estimate=brief,
        name="feed_inner",
    )(*blocks, w_down, slope)


def feed_back_kernel(dz_ref, up_ref, *block_refs):
    store_blocks(low_dot(dz_ref[...], up_ref[...], contract_cols), block_refs)


def feed_back(dinner, w_up):
    rows, units = dinner.shape
    width = w_up.shape[0]
    tile = 256
    return pl.pallas_call(
        feed_back_kernel,
        grid=(width // tile,),
        in_specs=[
            pl.BlockSpec((rows, units), lambda i: (0, 0)),
            pl.BlockSpec((tile, units), lambda i: (i, 0)),
        ],
        out_specs=[
            pl.BlockSpec((each.shape[0], tile), lambda i: (0, i))
            for each in blocks_of(rows, width)
        ],
        out_shape=blocks_of(rows, width),
        compiler_params=room(10),
        cost_estimate=brief,
        name="feed_back",
    )(dinner, w_up)


def late_forward_kernel(*refs):
    *e_refs, q_ref, live_ref, sharp_ref, soft_ref, e_rows = refs
    gather_blocks(e_refs, e_rows)
    blocks = soft_ref.shape[0]
    per = blocks // len(e_refs)
    whole = low_dot(e_rows[...], q_ref[...], contract_cols)
    rows = e_refs[0].shape[0]
    for at in range(len(e_refs)):
        place = pl.ds(at * rows, rows)
        sharp = whole[at * rows : (at + 1) * rows] * 2.0 + live_ref[place, :]
        sharp_ref[place, :] = sharp
        cube = sharp.reshape(per, rows // per, sharp.shape[1])
        top = jnp.max(cube, axis=1)
        total = jnp.sum(jnp.exp(cube - top[:, None, :]), axis=1)
        soft = jnp.where(top > 0.5 * neg_big, top + jnp.log(total), neg_big)
        soft_ref[pl.ds(at * per, per), :] = soft


def late_forward(e_blocks, queries, live_bias, blocks):
    own, width = e_blocks[0].shape
    rows = own * len(e_blocks)
    count = queries.shape[0]
    tile = 512
    return pl.pallas_call(
        late_forward_kernel,
        grid=(count // tile,),
        in_specs=[pl.BlockSpec((own, width), lambda i: (0, 0))] * len(e_blocks)
        + [
            pl.BlockSpec((tile, width), lambda i: (i, 0)),
            pl.BlockSpec((rows, 1), lambda i: (0, 0)),
        ],
        out_specs=[
            pl.BlockSpec((rows, tile), lambda i: (0, i)),
            pl.BlockSpec((blocks, tile), lambda i: (0, i)),
        ],
        out_shape=[shape_of((rows, count), full_type), shape_of((blocks, count), full_type)],
        scratch_shapes=[pltpu.VMEM((rows, width), low_type)],
        compiler_params=room(14),
        cost_estimate=brief,
        name="late_forward",
    )(*e_blocks, queries, live_bias)


def join_soft(soft, far, same):
    top = soft
    for at in range(far.shape[0]):
        top = jnp.maximum(top, far[at])
    total = jnp.exp(soft - top)
    for at in range(far.shape[0]):
        total = total + jnp.exp(far[at] - top)
    blocks = soft.shape[0]
    most = jnp.full(soft.shape, neg_big, full_type)
    for at in range(blocks):
        shared = same[:, at : at + 1] > 0.0
        most = jnp.maximum(most, jnp.where(shared, top[at : at + 1], neg_big))
    sums = jnp.zeros(soft.shape, full_type)
    for at in range(blocks):
        shared = same[:, at : at + 1] > 0.0
        term = jnp.where(shared, top[at : at + 1], neg_big)
        sums = sums + jnp.exp(term - most) * total[at : at + 1]
    return most + jnp.log(sums)


def late_backward_kernel(
    sharp_ref, soft_ref, far_ref, same_ref, place_ref, weight_ref, q_ref, *refs
):
    *block_refs, score_ref, total = refs
    step = pl.program_id(0)
    blocks = soft_ref.shape[0]
    rows, tile = sharp_ref.shape
    soft = join_soft(soft_ref[...], far_ref[...], same_ref[...])
    cube = sharp_ref[...].reshape(blocks, rows // blocks, tile)
    pulled = weight_ref[...][:, None, :] * jnp.exp(cube - soft[:, None, :])
    term = low_dot(pulled.reshape(rows, tile).astype(low_type), q_ref[...])
    query = lax.broadcasted_iota(jnp.int32, (tile, score_ref.shape[0]), 0) // QLEN
    count = lax.broadcasted_iota(jnp.int32, (tile, score_ref.shape[0]), 1)
    pool = jnp.where(query == count, 0.5 / QLEN, 0.0)
    exact = lax.Precision.HIGHEST
    means = lax.dot_general(pool, soft, (((0,), (1,)), ((), ())), precision=exact)
    score_ref[...] = lax.dot_general(means, place_ref[...], contract_inner, precision=exact)

    @pl.when(step == 0)
    def _():
        total[...] = term

    @pl.when(step > 0)
    def _():
        total[...] += term

    @pl.when(step == pl.num_programs(0) - 1)
    def _():
        store_blocks(total[...], block_refs)


def late_backward(sharp, soft, far, same, place, weight, queries):
    rows, count = sharp.shape
    width = queries.shape[1]
    blocks = soft.shape[0]
    tile = min(1024, count)
    outs = blocks_of(rows, width)
    return pl.pallas_call(
        late_backward_kernel,
        grid=(count // tile,),
        in_specs=[
            pl.BlockSpec((rows, tile), lambda i: (0, i)),
            pl.BlockSpec((blocks, tile), lambda i: (0, i)),
            pl.BlockSpec((far.shape[0], blocks, tile), lambda i: (0, 0, i)),
            whole_block(same.shape),
            whole_block(place.shape),
            pl.BlockSpec((blocks, tile), lambda i: (0, i)),
            pl.BlockSpec((tile, width), lambda i: (i, 0)),
        ],
        out_specs=[whole_block(each.shape) for each in outs]
        + [pl.BlockSpec((tile // QLEN, NPASS), lambda i: (i, 0))],
        out_shape=outs + [shape_of((count // QLEN, NPASS), full_type)],
        scratch_shapes=[pltpu.VMEM((rows, width), full_type)],
        compiler_params=room(24),
        cost_estimate=brief,
        name="late_backward",
    )(sharp, soft, far, same, place, weight, queries)


def norm_stats(values):
    centre = values - jnp.mean(values, axis=-1, keepdims=True)
    spread = jnp.mean(centre * centre, axis=-1, keepdims=True)
    scale = lax.rsqrt(spread + 1e-05)
    return centre * scale, scale


def norm_backward(unit, scale, gain, grad):
    dunit = grad * gain
    dvalues = scale * (
        dunit
        - jnp.mean(dunit, axis=-1, keepdims=True)
        - unit * jnp.mean(dunit * unit, axis=-1, keepdims=True)
    )
    return (
        dvalues,
        jnp.sum(grad * unit, axis=0, keepdims=True),
        jnp.sum(grad, axis=0, keepdims=True),
    )


def norm_one_kernel(*refs):
    *terms, norm_ref, h_ref, low_ref, unit_ref, scale_ref = refs
    unit, scale = norm_stats(add_up(terms))
    normed = unit * norm_ref[0:1] + norm_ref[1:2]
    h_ref[...] = normed
    low_ref[...] = normed.astype(low_type)
    unit_ref[...] = unit
    scale_ref[...] = scale


def lanes_at(order_ref, at, span):
    return pl.ds(pl.multiple_of(order_ref[at] * span, span), span)


def norm_two_kernel(order_ref, *refs):
    *rest, low_ref, unit_ref, scale_ref, e_ref, elow_ref, inv_ref = refs
    parts = order_ref.shape[0]
    *terms, norm_ref = rest[:-parts]
    col_refs = rest[-parts:]
    unit, scale = norm_stats(add_up(terms))
    normed_low = (unit * norm_ref[2:3] + norm_ref[3:4]).astype(low_type)
    low_ref[...] = normed_low
    unit_ref[...] = unit
    scale_ref[...] = scale
    span = col_refs[0].shape[1]
    squares = 0.0
    for at, ref in enumerate(col_refs):
        projected = low_dot(normed_low, ref[...])
        e_ref[:, lanes_at(order_ref, at, span)] = projected
        squares = squares + jnp.sum(projected * projected, axis=-1, keepdims=True)
    inv = lax.rsqrt(squares + 1e-06)
    embedded = e_ref[...] * inv
    e_ref[...] = embedded
    elow_ref[...] = embedded.astype(low_type)
    inv_ref[...] = inv


def norm_two_back_kernel(order_ref, *refs):
    *rest, own_ref, far_ref, dr_ref, low_ref, g_ref, du_ref = refs
    parts = order_ref.shape[0]
    *terms, norm_ref, unit_ref, scale_ref, e_ref, inv_ref = rest[:-parts]
    col_refs = rest[-parts:]
    dembed = add_up(terms)
    embedded = e_ref[...]
    along = jnp.sum(embedded * dembed, axis=-1, keepdims=True)
    du_ref[...] = (inv_ref[...] * (dembed - embedded * along)).astype(low_type)
    span = col_refs[0].shape[1]
    dnormed = 0.0
    for at, ref in enumerate(col_refs):
        dproj = du_ref[:, lanes_at(order_ref, at, span)]
        dnormed = dnormed + low_dot(dproj, ref[...], contract_cols)
    half = own_ref.shape[1]
    mine = order_ref[0] // (parts // 2)
    own_ref[...] = du_ref[:, pl.ds(pl.multiple_of(mine * half, half), half)]
    far_ref[...] = du_ref[:, pl.ds(pl.multiple_of((1 - mine) * half, half), half)]
    dresid, dgain, dshift = norm_backward(
        unit_ref[...], scale_ref[...], norm_ref[2:3], dnormed
    )
    dr_ref[...] = dresid
    low_ref[...] = dresid.astype(low_type)
    g_ref[...] = jnp.concatenate([dgain, dshift], 0)


def split_sums(sums):
    high = sums.astype(low_type).astype(full_type)
    zeros = jnp.zeros((SPARE - 8, sums.shape[1]), full_type)
    return jnp.concatenate([high, sums - high, zeros], 0).astype(low_type)


def norm_one_back_kernel(*refs):
    *terms, norm_ref, unit_ref, scale_ref, two_ref, dr_ref, pack_ref = refs
    dresid, dgain, dshift = norm_backward(
        unit_ref[...], scale_ref[...], norm_ref[0:1], add_up(terms)
    )
    dr_ref[...] = dresid
    rows = dresid.shape[0]
    pack_ref[0:rows, :] = dresid.astype(low_type)
    pack_ref[rows : rows + SPARE, :] = split_sums(
        jnp.concatenate([dgain, dshift, two_ref[...]], 0)
    )


def fold_kernel(*refs):
    *terms, low_ref = refs
    low_ref[...] = add_up(terms).astype(low_type)


def rows_fold(terms):
    return whole_call(fold_kernel, [shape_of(terms[0].shape)], "fold", *terms)[0]


def mix_kernel(o_ref, out_ref, *block_refs):
    rows = o_ref.shape[1]
    weight = jnp.concatenate([out_ref[at, 0:rows, :] for at in range(out_ref.shape[0])], axis=1)
    store_blocks(low_dot(o_ref[...], weight), block_refs)


def unmix_kernel(*refs):
    *packs, out_ref, do_ref, sums_ref = refs
    rows = do_ref.shape[1]
    weight = jnp.concatenate([out_ref[at, 0:rows, :] for at in range(out_ref.shape[0])], axis=1)
    own = packs[0].shape[0] - SPARE
    sums = jnp.zeros((8, weight.shape[1]), full_type)
    mixed = jnp.concatenate([ref[0:own, :] for ref in packs], axis=0)
    do_ref[...] = low_dot(mixed, weight, contract_cols).astype(low_type)
    for ref in packs:
        sums = sums + ref[own : own + SPARE, :].astype(full_type)[:8]
    sums_ref[...] = split_sums(sums[:4] + sums[4:])


def block_order(masks):
    return lax.axis_index("dp") ^ jnp.asarray(offsets_of(masks[::-1]), jnp.int32)


def ordered_call(kernel, outs, scratch, name, order, *args, grant=20):
    return pl.pallas_call(
        kernel,
        grid=(1,),
        in_specs=[pl.BlockSpec(memory_space=pltpu.SMEM)]
        + [whole_block(each.shape) for each in args],
        out_specs=[whole_block(each.shape) for each in outs],
        out_shape=outs,
        scratch_shapes=[pltpu.VMEM(*each) for each in scratch],
        compiler_params=room(grant),
        cost_estimate=brief,
        name=name,
    )(order, *args)


def stored(place_ref, left, right):
    turned = left.T
    cols = right.shape[1]
    for start in range(0, cols, 256):
        stop = min(start + 256, cols)
        place_ref[:, start:stop] = low_dot(turned, right[:, start:stop]).astype(low_type)


def deal(order_ref, keep_ref, send_ref, write):
    half = keep_ref.shape[0]
    for at in range(2 * half):
        write(keep_ref.at[at] if at < half else send_ref.at[at - half], order_ref[at])


def rows_in(ref, block, count):
    return ref[pl.ds(pl.multiple_of(block * count, count), count), :]


def lanes_in(ref, block):
    return ref[:, pl.ds(pl.multiple_of(block * LANES, LANES), LANES)]


def halves_like(count, block):
    return [shape_of((count // 2,) + block)] * 2


def grad_down_kernel(order_ref, active_ref, *refs):
    *row_refs, keep_ref, send_ref, total = refs
    stored(total, active_ref[...], rows_of(row_refs))

    def write(ref, block):
        ref[...] = lanes_in(total, block)

    deal(order_ref, keep_ref, send_ref, write)


def grad_down(active, row_blocks, masks):
    count = lax.axis_size("dp")
    units, width = active.shape[1], row_blocks[0].shape[1]
    if width // count == LANES:
        return ordered_call(
            grad_down_kernel,
            halves_like(count, (units, LANES)),
            [((units, width), low_type)],
            "grad_down",
            block_order(masks),
            active,
            *row_blocks,
        )
    whole = low_dot(active, jnp.concatenate(row_blocks, 0), contract_rows).astype(low_type)
    return halves(arrange(jnp.swapaxes(whole.reshape(units, count, -1), 0, 1), "dp", masks))


def halves(blocks):
    half = blocks.shape[0] // 2
    return blocks[:half], blocks[half:]


def grad_up_kernel(order_ref, dinner_ref, *refs):
    *row_refs, keep_ref, send_ref, total = refs
    parts = len(row_refs) // 3
    units = dinner_ref.shape[1]
    block_rows = keep_ref.shape[1]
    cols = keep_ref.shape[2] - units
    stored(total.at[:, 0:units], rows_of(row_refs[:parts]), dinner_ref[...])
    mine = order_ref[order_ref.shape[0] - 1] % (row_refs[-1].shape[1] // cols)
    mine = pl.ds(pl.multiple_of(mine * cols, cols), cols)
    dproj = jnp.concatenate([ref[:, mine] for ref in row_refs[2 * parts :]], axis=0)
    stored(total.at[:, units:], rows_of(row_refs[parts : 2 * parts]), dproj)

    def write(ref, block):
        ref[...] = rows_in(total, block, block_rows)

    deal(order_ref, keep_ref, send_ref, write)


def grad_up(dinner, one_blocks, two_blocks, du_blocks, col_width, masks):
    count = lax.axis_size("dp")
    units, width = dinner.shape[1], one_blocks[0].shape[1]
    column = lax.axis_index("mp")
    rows = width // count
    if rows == LANES:
        order = jnp.concatenate([block_order(masks), column.reshape(1)])
        return ordered_call(
            grad_up_kernel,
            halves_like(count, (rows, units + col_width)),
            [((width, units + col_width), low_type)],
            "grad_up",
            order,
            dinner,
            *one_blocks,
            *two_blocks,
            *du_blocks,
        )
    column = column % (du_blocks[0].shape[1] // col_width)
    dproj = lax.dynamic_slice_in_dim(
        jnp.concatenate(du_blocks, 0), column * col_width, col_width, 1
    )
    up = low_dot(jnp.concatenate(one_blocks, 0), dinner, contract_rows)
    col = low_dot(jnp.concatenate(two_blocks, 0), dproj, contract_rows)
    whole = jnp.concatenate([up, col], 1).astype(low_type)
    return halves(arrange(whole.reshape(count, rows, -1), "dp", masks))


def grad_qk_kernel(order_ref, left_ref, right_ref, keep_ref, send_ref, total):
    block_rows = keep_ref.shape[1]
    stored(total, left_ref[...], right_ref[...])

    def write(ref, block):
        ref[...] = rows_in(total, block, block_rows)

    deal(order_ref, keep_ref, send_ref, write)


def grad_qk(left, right, masks):
    count = lax.axis_size("dp")
    width, cols = left.shape[1], right.shape[1]
    rows = width // count
    if rows == LANES:
        return ordered_call(
            grad_qk_kernel,
            halves_like(count, (rows, cols)),
            [((width, cols), low_type)],
            "grad_qk",
            block_order(masks),
            left,
            right,
        )
    whole = low_dot(left, right, contract_rows).astype(low_type)
    return halves(arrange(whole.reshape(count, rows, cols), "dp", masks))


def grad_vo_kernel(order_ref, hidden_ref, dv_ref, o_ref, *refs):
    *packs, sums_ref, keep_ref, send_ref, total_v, total_o = refs
    rows = packs[0].shape[0] - SPARE
    cols = dv_ref.shape[1]
    heads = o_ref.shape[1]
    stored(total_v, hidden_ref[...], dv_ref[...])
    mixed = jnp.concatenate([ref[0:rows, :] for ref in packs], axis=0)
    stored(total_o.at[0:heads, :], o_ref[...], mixed)
    total_o[heads : heads + SPARE, :] = sums_ref[...]

    def write(ref, block):
        value = rows_in(total_v, block, LANES)
        for at in range(cols // LANES):
            ref[at * LANES : (at + 1) * LANES, :] = value[:, at * LANES : (at + 1) * LANES]
        ref[cols:, :] = lanes_in(total_o, block)

    deal(order_ref, keep_ref, send_ref, write)


def finish_pair_kernel(keep_ref, other_ref, left_ref, right_ref):
    total = keep_ref[...].astype(full_type) + other_ref[...].astype(full_type)
    cols = left_ref.shape[1]
    left_ref[...] = total[:, :cols]
    right_ref[...] = total[:, cols:]


def finish_pair(scatter, cols):
    rows, both = scatter.keep.shape[1:]
    outs = [shape_of((rows, cols), full_type), shape_of((rows, both - cols), full_type)]
    return whole_call(finish_pair_kernel, outs, "finish_pair", scatter.keep[0], scatter.other[0])


def finish_vo_kernel(keep_ref, other_ref, value_ref, out_ref, *norm_refs):
    total = keep_ref[...].astype(full_type) + other_ref[...].astype(full_type)
    rows, cols = value_ref.shape
    row = 0
    for at in range(0, cols, LANES):
        value_ref[:, at : at + LANES] = total[row : row + rows]
        row += rows
    out_ref[...] = total[row : row + out_ref.shape[0]]
    row += out_ref.shape[0]
    for at, ref in enumerate(norm_refs):
        ref[...] = total[row + at : row + at + 1] + total[row + 4 + at : row + 5 + at]


def finish_vo(keep, other, value_shape, out_shape):
    rows, cols = out_shape
    if cols == LANES:
        outs = [shape_of(value_shape, full_type), shape_of(out_shape, full_type)]
        outs = outs + [shape_of((1, cols), full_type)] * 4
        value, out, *norms = whole_call(finish_vo_kernel, outs, "finish_vo", keep, other)
        return value, out, norms
    total = keep.astype(full_type) + other.astype(full_type)
    value, out = unpack_vo(total, *value_shape, (rows + SPARE, cols))
    return value, out[:rows], out[rows : rows + 4] + out[rows + 4 : rows + 8]


def pack_vo(value, out):
    cols = value.shape[-1]
    parts = [value[..., at : at + LANES] for at in range(0, cols, LANES)]
    return jnp.concatenate(parts + [out.reshape(out.shape[:-2] + (-1, LANES))], axis=-2)


def unpack_vo(packed, rows, cols, out_shape):
    high = rows * cols // LANES
    value = jnp.concatenate(
        [packed[..., at : at + rows, :] for at in range(0, high, rows)], axis=-1
    )
    return value, packed[..., high:, :].reshape(packed.shape[:-2] + out_shape)


def grad_vo(hidden, dvalue, attended, packs, sums, masks):
    count = lax.axis_size("dp")
    width, cols = hidden.shape[1], dvalue.shape[1]
    heads = attended.shape[1]
    rows = width // count
    if rows == LANES:
        block = (cols * rows // LANES + heads + SPARE, LANES)
        return ordered_call(
            grad_vo_kernel,
            halves_like(count, block),
            [((width, cols), low_type), ((heads + SPARE, width), low_type)],
            "grad_vo",
            block_order(masks),
            hidden,
            dvalue,
            attended,
            *packs,
            sums,
        )
    value = low_dot(hidden, dvalue, contract_rows).astype(low_type).reshape(count, rows, cols)
    mixed = jnp.concatenate([each[:-SPARE] for each in packs], 0)
    out = low_dot(attended, mixed, contract_rows).astype(low_type)
    out = jnp.concatenate([out, sums], 0).reshape(heads + SPARE, count, rows)
    return halves(arrange(pack_vo(value, jnp.swapaxes(out, 0, 1)), "dp", masks))


def to_lanes(blocks):
    if blocks.shape[2] == LANES:
        return blocks
    whole = jnp.swapaxes(blocks, 0, 1).reshape(blocks.shape[1], -1, LANES)
    return jnp.swapaxes(whole, 0, 1)


def place_kernel(at_ref, *refs):
    *blocks, out_ref = refs
    rows = blocks[0].shape[0]
    for at, ref in enumerate(blocks):
        start = pl.multiple_of(at_ref[at] * rows, rows)
        out_ref[pl.ds(start, rows), :] = ref[...].astype(full_type)


def place_rows(order, blocks):
    rows, width = blocks[0].shape
    outs = [shape_of((rows * len(blocks), width), full_type)]
    return ordered_call(place_kernel, outs, [], "place_rows", order, *blocks)[0]


def unproject_kernel(dqk_ref, dv_ref, a_ref, b_ref, *block_refs):
    total = low_dot(dqk_ref[...], a_ref[...], contract_cols)
    store_blocks(total + low_dot(dv_ref[...], b_ref[...], contract_cols), block_refs)


def unproject(dqk, dvalue, w_qk, w_v):
    outs = blocks_of(dqk.shape[0], w_qk.shape[0])
    return whole_call(unproject_kernel, outs, "unproject", dqk, dvalue, w_qk, w_v)


def close_kernel(*refs):
    *terms, out_ref = refs
    out_ref[...] = add_up(terms).astype(low_type)


def pack_kernel(order_ref, *refs):
    hidden_ref, q_ref, k_ref, v_ref, o_ref, up_ref, col_ref, *norm_refs = refs[:11]
    a_out, u_out, b_out, own_out, block_out = refs[11:]
    heads, units = q_ref.shape[1], up_ref.shape[1]
    a_out[:, :heads] = q_ref[...]
    a_out[:, heads:] = k_ref[...]
    u_out[:, :units] = up_ref[...]
    u_out[:, units:] = col_ref[...]
    row = 0
    for at in range(0, heads, LANES):
        b_out[row : row + v_ref.shape[0], :] = v_ref[:, at : at + LANES]
        row += v_ref.shape[0]
    b_out[row : row + o_ref.shape[0], :] = o_ref[...]
    row += o_ref.shape[0]
    norms = [ref[...].astype(full_type).reshape(1, -1) for ref in norm_refs]
    norms = jnp.concatenate(norms + [jnp.zeros((SPARE - 4, LANES), full_type)], axis=0)
    b_out[row : row + SPARE, :] = norms.astype(low_type)
    parts = order_ref.shape[0]
    rows = hidden_ref.shape[0] // parts
    for at in range(parts):
        own_out[at * rows : (at + 1) * rows, :] = rows_in(hidden_ref, order_ref[at], rows)
    block_out[...] = own_out[0:rows, :]


def pack_inputs(order, hidden, w_query, w_key, w_value, w_out, w_up, w_colbert, *norms):
    rows, heads = w_query.shape
    span = hidden.shape[0] // order.shape[0]
    if w_out.shape[1] == LANES and rows == LANES:
        packed = (rows * heads // LANES + w_out.shape[0] + SPARE, LANES)
        outs = [
            shape_of((rows, 2 * heads)),
            shape_of((rows, w_up.shape[1] + w_colbert.shape[1])),
            shape_of(packed),
            shape_of(hidden.shape),
            shape_of((span, hidden.shape[1])),
        ]
        args = (hidden, w_query, w_key, w_value, w_out, w_up, w_colbert) + norms
        return ordered_call(pack_kernel, outs, [], "pack", order, *args, grant=60)
    norms = jnp.concatenate([jnp.stack(norms), jnp.zeros((SPARE - 4, w_out.shape[1]), low_type)], 0)
    blocks = [
        lax.dynamic_slice_in_dim(hidden, order[at] * span, span, 0)
        for at in range(order.shape[0])
    ]
    return (
        jnp.concatenate([w_query, w_key], axis=1),
        jnp.concatenate([w_up, w_colbert], axis=1),
        pack_vo(w_value, jnp.concatenate([w_out, norms], axis=0)),
        jnp.concatenate(blocks),
        blocks[0],
    )


def body(
    hidden_in,
    w_query,
    w_key,
    w_value,
    w_out,
    w_up,
    w_down,
    w_colbert,
    norm1_gain,
    norm1_shift,
    norm2_gain,
    norm2_shift,
    queries,
    passage,
    live,
    score_grad,
):
    tok_rows, width = hidden_in.shape
    device = lax.axis_index("dp")
    column = lax.axis_index("mp")
    dp_size = lax.axis_size("dp")
    mp_size = lax.axis_size("mp")
    group_size = dp_size // NBUCKET
    group_levels = group_size.bit_length() - 1
    own_rows = tok_rows // mp_size
    head_width = w_query.shape[1]
    dp_up, dp_down = upward("dp"), downward("dp")
    turned = dp_up[:1] + dp_down[:-1]
    row_order = offsets_of(downward("mp"))

    def ordered(value, owner, span=own_rows):
        return jnp.concatenate(
            [
                lax.dynamic_slice_in_dim(value, (owner * mp_size + (column ^ at)) * span, span, 0)
                for at in row_order
            ]
        )

    def group_gather(value):
        for level in range(group_levels):
            value = jnp.concatenate([value, swap(value, "dp", 2**level)], 0)
        return value

    across = dp_up[-1:] + dp_up[:-1]
    turned_back, across_back = turned[::-1], across[::-1]
    col_order = column ^ jnp.asarray(row_order, jnp.int32)
    norms = (norm1_gain, norm1_shift, norm2_gain, norm2_shift)
    out_shape = (w_out.shape[0] + SPARE, w_out.shape[1])
    packed_a, packed_u, packed_b, hidden_own, own_hidden = pack_inputs(
        col_order, hidden_in, w_query, w_key, w_value, w_out, w_up, w_colbert, *norms
    )
    pack_a = Gather(packed_a, "dp", dp_down)
    pack_u = Gather(packed_u, "dp", dp_down)
    pack_b = Gather(packed_b, "dp", dp_down)
    pack_d = Gather(w_down, "dp", turned)

    main = (hidden_own, own_hidden)
    main = pack_a.start(main)
    main = pack_b.start(main)
    main = pack_d.start(main)
    others = group_gather(main[1][None])[1:]
    seg_own = ordered(passage, device)
    live_own = ordered(live, device)
    seg_others = jnp.concatenate([ordered(passage, device ^ at) for at in range(1, group_size)])
    live_others = jnp.concatenate([ordered(live, device ^ at) for at in range(1, group_size)])
    slot_own = jnp.where(live_own == 1, seg_own, -1)
    slot_keys = jnp.concatenate([slot_own, jnp.where(live_others == 1, seg_others, -1)])
    seg_row = seg_own.astype(full_type)[None, :]
    slot_row = slot_keys.astype(full_type)[None, :]
    blocks = 2 ** (NBUCKET - 1)
    seg_block = seg_own.reshape(blocks, -1)[:, 0]
    live_bias = jnp.where(live_own == 1, 0.0, neg_big)[:, None]
    same = seg_block[:, None] == seg_block[None, :]
    passages = jnp.arange(NPASS, dtype=jnp.int32)
    place = (seg_block[:, None] == passages[None, :]).astype(full_type)
    grad_block = jnp.sum(place[:, None, :] * score_grad[None], axis=2)
    weight = jnp.repeat(grad_block / QLEN, QLEN, axis=1)
    same = same.astype(full_type)
    place = place / jnp.sum(same, axis=1, keepdims=True)
    slot_own = slot_own.astype(full_type)[None, :]
    early = (seg_row, slot_own, slot_row, live_bias, weight, same, place)
    early, main = tie(early, main)
    seg_row, slot_own, slot_row, live_bias, weight, same, place = early
    main = pack_a.step(main)
    main = pack_b.step(main)
    main = pack_u.start(main)
    others, main = tie(others, main)
    far_others = swap(others, "mp", 2)
    main = pack_d.finish(main)
    main = pack_a.step(main)
    main = pack_b.step(main)
    main = pack_u.step(main)
    main = pack_d.start(main)
    far_others, main = tie(far_others, main)
    main = pack_u.step(main)
    others = [others, far_others]
    others = others + [swap(each, "mp", 1) for each in others]
    others = jnp.stack(others, 1).reshape(-1, width)
    hidden_own, own_hidden = main
    hidden_all = jnp.concatenate([hidden_own, others], 0)
    main = (hidden_own, own_hidden, hidden_all)
    main = pack_a.drain(main)
    full_a = pack_a.value().reshape(width, -1)
    full_a, main = tie(full_a, main)
    hidden_own, own_hidden, hidden_all = main

    query_key = low_dot(hidden_all, full_a).astype(low_type)
    main = (query_key, hidden_all)
    main = pack_b.drain(main)
    full_b, full_out = unpack_vo(pack_b.value(), w_value.shape[0], head_width, out_shape)
    full_b = full_b.reshape(width, head_width)
    full_out = to_lanes(full_out)
    (full_b, full_out), main = tie((full_b, full_out), main)
    main = pack_d.step(main)
    query_key, hidden_all = main
    value_rows = low_dot(hidden_all, full_b).astype(low_type)
    norm_rows = jnp.swapaxes(full_out[:, head_width : head_width + 4], 0, 1).reshape(4, width)
    norm_rows = norm_rows.astype(full_type)
    attended, lse = attend_forward(query_key, value_rows, seg_row, slot_row)
    norm_rows, attended = tie(norm_rows, attended)
    parts = whole_call(mix_kernel, blocks_of(tok_rows, width), "mix", attended, full_out)
    terms = rows_scatter(parts)
    units = w_up.shape[1]
    square = shape_of((own_rows, width), full_type)
    low_square = shape_of((own_rows, width))
    narrow = shape_of((own_rows, 1), full_type)
    normed_one, normed_low, unit_one, scale_one = whole_call(
        norm_one_kernel,
        [square, low_square, square, narrow],
        "norm_one",
        own_hidden,
        *terms,
        norm_rows,
    )

    rows_one = [normed_low, swap(normed_low, "mp", 2)]
    rows_one = pack_u.drain(rows_one)
    full_up = pack_u.value().reshape(width, -1)
    col_own = full_up[:, units:]
    (full_up, col_own), rows_one = tie((full_up, col_own), rows_one)
    rows_one = rows_one + [swap(each, "mp", 1) for each in rows_one]
    far_col = swap(col_own, "mp", 2)
    active, slope = feed_up(rows_one, full_up, units)
    active = pack_d.drain(active)
    full_down = to_lanes(pack_d.value())
    parts = feed_down(active, full_down)
    far_col, parts = tie(far_col, parts)
    terms = rows_scatter(parts)
    col_blocks = [col_own, far_col]
    col_blocks = col_blocks + [swap(each, "mp", 1) for each in col_blocks]
    normed_two_low, unit_two, scale_two, embedded, embed_low, inv_length = ordered_call(
        norm_two_kernel,
        [low_square, square, narrow, square, low_square, narrow],
        [],
        "norm_two",
        col_order,
        normed_one,
        *terms,
        norm_rows,
        *col_blocks,
    )

    (far, far_lse), embed_low = tie((attended, lse), embed_low)
    far = group_gather(far[None])[1:]
    far_lse = group_gather(far_lse[None])[1:]
    far_e = swap(embed_low, "mp", 2)
    (far, far_lse), far_e = tie((far, far_lse), far_e)
    e_blocks = [embed_low, far_e]
    e_blocks = e_blocks + [swap(each, "mp", 1) for each in e_blocks]
    sharp, soft_block = late_forward(e_blocks, queries, live_bias, blocks)
    two_low, soft_block = tie(normed_two_low, soft_block)
    far_two = swap(two_low, "mp", 2)
    soft_far = group_gather(soft_block[None])[1:]
    *parts, scores = late_backward(
        sharp, soft_block, soft_far, same, place, weight, queries
    )
    far_two, parts = tie(far_two, parts)
    far_attended = far.reshape(-1, head_width)
    far_lse = jnp.swapaxes(far_lse, 0, 1).reshape(8, -1)

    score_masks = dp_up[group_levels:]
    scores, parts = tie(scores, parts)
    scores_far = swap(scores, "dp", score_masks[0])
    terms = rows_scatter(parts)
    scores_far, terms = tie(scores_far, terms)
    scores, terms = tie(scores + scores_far, terms)
    scores_far = swap(scores, "dp", score_masks[1])
    low_half = shape_of((own_rows, width // 2))
    du_own, du_far, dresid_two, dresid_low, two_sums = ordered_call(
        norm_two_back_kernel,
        [low_half, low_half, square, low_square, shape_of((2, width), full_type)],
        [((own_rows, width), low_type)],
        "norm_two_back",
        col_order,
        *terms,
        norm_rows,
        unit_two,
        scale_two,
        embedded,
        inv_length,
        *col_blocks,
    )
    dresid_blocks = [dresid_low, swap(dresid_low, "mp", 2)]
    scores_far, dresid_blocks = tie(scores_far, dresid_blocks)
    dresid_blocks = dresid_blocks + [swap(each, "mp", 1) for each in dresid_blocks]
    two_blocks = [normed_two_low, far_two]
    two_blocks = two_blocks + [swap(each, "mp", 1) for each in two_blocks]
    two_blocks, dresid_blocks = tie(two_blocks, dresid_blocks)
    scores = scores + scores_far
    for mask in score_masks[2:]:
        scores = scores + swap(scores, "dp", mask)

    (du_own, du_far), dresid_blocks = tie((du_own, du_far), dresid_blocks)
    du_far = swap(du_far, "mp", 2)
    dinner = feed_inner(dresid_blocks, full_down, slope)
    du_far, dinner = tie(du_far, dinner)
    parts = feed_back(dinner, full_up)
    got_far, got = swap(parts[3], "mp", 1), swap(parts[2], "mp", 1)
    du_blocks = [du_own, du_far]
    du_blocks = du_blocks + [swap(each, "mp", 1) for each in du_blocks]
    low = rows_fold([parts[1], got_far])
    (active, dinner, got), low = tie((active, dinner, got), low)
    far_low = swap(low, "mp", 2)
    grad_d = Scatter(*grad_down(active, dresid_blocks, dp_up), "dp", dp_up)
    dinner = grad_d.start(dinner)
    grad_u = Scatter(
        *grad_up(dinner, rows_one, two_blocks, du_blocks, w_colbert.shape[1], across_back),
        "dp",
        across_back,
    )
    far_low = grad_u.start(far_low)
    dresid_one, mixed_pack = whole_call(
        norm_one_back_kernel,
        [square, shape_of((own_rows + SPARE, width))],
        "norm_one_back",
        dresid_two,
        parts[0],
        got,
        far_low,
        norm_rows,
        unit_one,
        scale_one,
        two_sums,
    )
    packs = rows_gather(mixed_pack)

    dattended, norm_sums = whole_call(
        unmix_kernel,
        [shape_of((tok_rows, head_width)), shape_of((SPARE, width))],
        "unmix",
        *packs,
        full_out,
    )
    far_grads = group_gather(dattended[None])[1:].reshape(-1, head_width)
    own_q = (query_key, 0, dattended, attended, lse)
    all_keys = (value_rows, slot_row, tok_rows)
    keys = value_rows.shape[0]
    *sums, dquery = attend_back(own_q, None, keys, all_keys, None, True)
    far_grads, dquery = tie(far_grads, dquery)
    dquery = grad_d.step(grad_u.step(dquery))
    far_q = (query_key, tok_rows, far_grads, far_attended, far_lse)
    own_keys = (value_rows, slot_own, tok_rows)
    dqk, dvalue_low = attend_back(far_q, None, tok_rows, own_keys, sums, False, (dquery,))
    parts = unproject(dqk, dvalue_low, full_a, full_b)
    got_far, got = swap(parts[3], "mp", 1), swap(parts[2], "mp", 1)
    low = rows_fold([parts[1], got_far])
    (dqk, dvalue_low), low = tie((dqk, dvalue_low), low)
    far_low = swap(low, "mp", 2)
    grad_b = Scatter(
        *grad_vo(hidden_own, dvalue_low, attended, packs, norm_sums, across_back),
        "dp",
        across_back,
    )
    dqk = grad_b.start(dqk)
    grad_a = Scatter(*grad_qk(hidden_own, dqk, dp_up), "dp", dp_up)
    dqk = grad_a.start(dqk)
    dqk, last = tie(dqk, parts[0])
    last = grad_d.step(last)
    far_low = grad_u.step(far_low)
    terms = [dresid_one, last, got, far_low]
    input_own = whole_call(close_kernel, [low_square], "close", *terms)[0]
    far_own = swap(input_own, "mp", 2)
    far_own = grad_a.step(grad_b.step(far_own))
    input_blocks = [input_own, far_own]
    input_blocks = input_blocks + [swap(each, "mp", 1) for each in input_blocks]
    input_grad = place_rows(col_order, input_blocks)
    input_grad = grad_b.step(grad_a.step(input_grad))
    input_grad = grad_d.finish(grad_u.finish(input_grad))
    down_grad = grad_d.value()
    up_grad, colbert_grad = finish_pair(grad_u, units)
    ends = (input_grad, down_grad, up_grad, colbert_grad)
    ends = grad_a.finish(ends)
    query_grad, key_grad = finish_pair(grad_a, head_width)
    ends, (query_grad, key_grad) = grad_b.finish((ends, (query_grad, key_grad)))
    input_grad, down_grad, up_grad, colbert_grad = ends
    value_grad, out_grad, norm_grads = finish_vo(
        grad_b.keep[0], grad_b.other[0], w_value.shape, w_out.shape
    )
    return (
        scores,
        input_grad,
        query_grad,
        key_grad,
        value_grad,
        out_grad,
        up_grad,
        down_grad,
        colbert_grad,
        norm_grads[0].reshape(-1),
        norm_grads[1].reshape(-1),
        norm_grads[2].reshape(-1),
        norm_grads[3].reshape(-1),
    )


def solution(mesh):
    rows, both, across = P("dp", None), P("dp", "mp"), P("mp", "dp")
    return jax.shard_map(
        body,
        mesh=mesh,
        in_specs=(
            (rows, both, both, both, across, both, across, both)
            + (P("dp"),) * 4
            + (P("mp", None), P(), P(), P("mp", None))
        ),
        out_specs=(
            (P("mp", None), rows, both, both, both, across, both, across, both)
            + (P("dp"),) * 4
        ),
        check_vma=False,
    )
```
